256 devices in a mesh: lat: 8 (over z_hi, x), lon: 16 (over z_lo, y), grp: 2 (over core).
Axes of the slice: x: 4, y: 4, z: 8 (z_hi: 2, z_lo: 4; z = z_hi * 4 + z_lo), core: 2. Of those that a mesh axis runs over, the one named last changes fastest.
Arguments:
- teacher_in: bfloat16 [2, 192, 192, 512], P('grp', 'lat', 'lon'), may hold values from -6 to 6
- student_in: bfloat16 [2, 192, 192, 256], P('grp', 'lat', 'lon'), may hold values from -6 to 6
- regions: int32 [2, 192, 192], P(None, 'lat', 'lon'), may hold values from 0 to 2
- t_qkv: bfloat16 [2, 512, 1536], replicated, may hold values from -0.25 to 0.25
- t_out: bfloat16 [2, 512, 512], replicated, may hold values from -0.25 to 0.25
- s_qkv: bfloat16 [2, 256, 768], replicated, may hold values from -0.375 to 0.375
- s_out: bfloat16 [2, 256, 256], replicated, may hold values from -0.375 to 0.375
- s_proj: bfloat16 [256, 512], replicated, may hold values from -0.375 to 0.375
Outputs:
- teacher_out: bfloat16 [2, 192, 192, 512], P('grp', 'lat', 'lon')
- student_grad: float32 [2, 192, 192, 256], P('grp', 'lat', 'lon')
The draws below stay inside these ranges and needn't reach their ends.
All inputs are finite; a program needn't handle non-finite values.
Results may differ from the reference program's by a relative error of at most 0.02.
Values may be sent and summed in bfloat16 or wider, within the bound.
No kernel may reach another device: no remote copies, remote signals or barrier semaphores. Data moves between devices by JAX's collectives and lax.ppermute only.
A program may use at most 128 MiB of HBM per device.

```python
import jax
import jax.numpy as jnp
from jax import lax

D_T = 512
HEADS_T = 8
D_S = 256
HEADS_S = 4
LEV = 2
LAYERS = 2
LAT = 192
LON = 192


def place_ends(drawn, stream_key, smallest, top_value):
    spot = [jax.random.randint(jax.random.fold_in(stream_key, axis), (), 0, length) for axis, length in enumerate(drawn.shape)]
    main_axis = drawn.shape.index(max(drawn.shape))
    next_to = spot[:main_axis] + [(spot[main_axis] + 1) % drawn.shape[main_axis]] + spot[main_axis + 1:]
    return drawn.at[tuple(spot)].set(smallest).at[tuple(next_to)].set(top_value)


def level_of(stream_key, dims, cuts, low, largest):
    factor_of = 1.0
    for position, parts in cuts:
        steps = jax.random.uniform(jax.random.fold_in(jax.random.fold_in(stream_key, 6), position), (parts,), jnp.float32, low / len(cuts), largest / len(cuts))
        factor_of = factor_of * jnp.repeat(jnp.exp(steps), dims[position] // parts).reshape((-1,) + (1,) * (len(dims) - 1 - position))
    return factor_of


def centred(stream_key, dims, deviation, bound, pieces=(), kind=jnp.bfloat16):
    factor_of = level_of(stream_key, dims, pieces, -0.22, 0.18) if pieces else 1.0
    values = jax.random.normal(stream_key, dims, jnp.float32) * deviation * factor_of
    return jnp.minimum(jnp.maximum(values, -bound), bound).astype(kind)


def setup_inputs(seed: int = 0) -> dict:
    keys = jax.random.split(jax.random.key(seed), 9)
    return {
        "teacher_in": centred(keys[0], (LEV, LAT, LON, D_T), 1.0, 6.0, ((0, 2), (1, 8), (2, 16))),
        "student_in": centred(keys[1], (LEV, LAT, LON, D_S), 1.0, 6.0, ((0, 2), (1, 8), (2, 16))),
        "regions": place_ends(jax.random.randint(keys[2], (LEV, LAT, LON), 0, 3), jax.random.fold_in(keys[2], 1), 0, 2).astype(jnp.int32),
        "t_qkv": centred(keys[3], (LAYERS, D_T, 3 * D_T), D_T ** -0.5, 0.25),
        "t_out": centred(keys[4], (LAYERS, D_T, D_T), D_T ** -0.5, 0.25),
        "s_qkv": centred(keys[5], (LAYERS, D_S, 3 * D_S), D_S ** -0.5, 0.375),
        "s_out": centred(keys[6], (LAYERS, D_S, D_S), D_S ** -0.5, 0.375),
        "s_proj": centred(keys[7], (D_S, D_T), D_S ** -0.5, 0.375),
    }


logit_scale = 10.0
eps = 1e-06

def windows(source, win_rows, win_cols):
    levels, height, breadth = (source.shape[0], source.shape[1], source.shape[2])
    trailing = source.shape[3:]
    shaped = source.reshape((levels, height // win_rows, win_rows, breadth // win_cols, win_cols) + trailing)
    permute = (1, 3, 0, 2, 4) + tuple(range(5, 5 + len(trailing)))
    shaped = shaped.transpose(permute)
    return shaped.reshape((height // win_rows * (breadth // win_cols), levels * win_rows * win_cols) + trailing)

def unwindows(windowed, levels, height, breadth, win_rows, win_cols):
    trailing = windowed.shape[2:]
    shaped = windowed.reshape((height // win_rows, breadth // win_cols, levels, win_rows, win_cols) + trailing)
    permute = (2, 0, 3, 1, 4) + tuple(range(5, 5 + len(trailing)))
    return shaped.transpose(permute).reshape((levels, height, breadth) + trailing)

def attend(queries, key_rows, value_rows, reg_query, reg_key, head_count):
    nwin, nquery, channels = queries.shape
    nkey = key_rows.shape[1]
    head_size = channels // head_count
    q_heads = queries.reshape(nwin, nquery, head_count, head_size).astype(jnp.float32)
    k_heads = key_rows.reshape(nwin, nkey, head_count, head_size).astype(jnp.float32)
    v_heads = value_rows.reshape(nwin, nkey, head_count, head_size).astype(jnp.float32)
    products = jnp.einsum('wqhd,wkhd->whqk', q_heads, k_heads)
    query_sq = lax.optimization_barrier(jnp.sum(q_heads * q_heads, axis=3))
    key_sq = lax.optimization_barrier(jnp.sum(k_heads * k_heads, axis=3))
    scale_q = lax.rsqrt(query_sq + eps).transpose(0, 2, 1)[:, :, :, None]
    scale_k = lax.rsqrt(key_sq + eps).transpose(0, 2, 1)[:, :, None, :]
    scores = logit_scale * products * scale_q * scale_k
    allowed = reg_query[:, :, None] == reg_key[:, None, :]
    exponent = jnp.where(allowed[:, None], jnp.exp(scores), jnp.zeros((), jnp.float32))
    denominator = lax.optimization_barrier(jnp.sum(exponent, axis=3, keepdims=True))
    weights = (exponent / jnp.where(denominator > 0, denominator, jnp.ones((), jnp.float32))).astype(jnp.bfloat16)
    blended = jnp.einsum('whqk,wkhd->wqhd', weights.astype(jnp.float32), v_heads)
    return blended.astype(jnp.bfloat16).reshape(nwin, nquery, channels)

def project(source, matrix):
    channels = source.shape[-1]
    flat = source.reshape(-1, channels).astype(jnp.bfloat16)
    result = jnp.dot(flat, matrix, preferred_element_type=jnp.float32).astype(jnp.bfloat16)
    return result.reshape(source.shape[:-1] + (matrix.shape[1],))

def finish(source, attended, w_output):
    channels = source.shape[-1]
    output = jnp.dot(attended.reshape(-1, channels), w_output, preferred_element_type=jnp.float32)
    normed = output * lax.rsqrt(lax.optimization_barrier(jnp.mean(output * output, axis=-1, keepdims=True)) + eps)
    return (source.reshape(-1, channels).astype(jnp.float32) + normed).astype(jnp.bfloat16).reshape(source.shape)

def student_grad(student_in, reg_own, target, s_qkv, s_out, s_proj, head_count):
    levels, height, breadth, channels = student_in.shape
    reg_win = windows(reg_own.reshape(1, levels * height, breadth), 12, 6)

    def loss_fn(inputs):
        hidden = inputs
        for layer_idx in range(s_qkv.shape[0]):
            projected = project(hidden, s_qkv[layer_idx]).reshape(1, levels * height, breadth, 3 * channels)
            queries = windows(projected[..., :channels], 12, 6)
            key_rows = windows(projected[..., channels:2 * channels], 12, 6)
            value_rows = windows(projected[..., 2 * channels:], 12, 6)
            attended = attend(queries, key_rows, value_rows, reg_win, reg_win, head_count)
            attended = unwindows(attended, 1, levels * height, breadth, 12, 6).reshape(levels, height, breadth, channels)
            hidden = finish(hidden, attended, s_out[layer_idx])
        predicted = jnp.dot(hidden.reshape(-1, channels), s_proj, preferred_element_type=jnp.float32)
        residual = predicted - target.reshape(-1, target.shape[-1]).astype(jnp.float32)
        return 0.5 * jnp.sum(residual * residual)
    loss_value, pullback = jax.vjp(loss_fn, student_in.astype(jnp.float32))
    return pullback(jnp.ones((), jnp.float32))[0]

def place(source, filler):
    rolled = jnp.roll(source, 3, axis=2)
    widths = ((0, 0), (6, 6), (0, 0)) + ((0, 0),) * (source.ndim - 3)
    return jnp.pad(rolled, widths, constant_values=filler)

def reference(teacher_in, student_in, regions, t_qkv, t_out, s_qkv, s_out, s_proj):
    levels, height, breadth, channels = teacher_in.shape
    projected = project(teacher_in, t_qkv[0])
    queries = windows(projected[..., :channels], 12, 6)
    key_rows = windows(projected[..., channels:2 * channels], 12, 6)
    value_rows = windows(projected[..., 2 * channels:], 12, 6)
    reg_win = windows(regions, 12, 6)
    attended = attend(queries, key_rows, value_rows, reg_win, reg_win, HEADS_T)
    attended = unwindows(attended, levels, height, breadth, 12, 6)
    hidden_a = finish(teacher_in, attended, t_out[0])
    projected = project(hidden_a, t_qkv[1])
    tall = height + 12
    placed = place(projected, 0.0).reshape(1, levels * tall, breadth, 3 * channels)
    reg_placed = place(regions, -1).reshape(1, levels * tall, breadth)
    queries = windows(placed[..., :channels], 12, 6)
    key_rows = windows(placed[..., channels:2 * channels], 12, 6)
    value_rows = windows(placed[..., 2 * channels:], 12, 6)
    reg_win = windows(reg_placed, 12, 6)
    attended = attend(queries, key_rows, value_rows, reg_win, reg_win, HEADS_T)
    attended = unwindows(attended, 1, levels * tall, breadth, 12, 6).reshape(levels, tall, breadth, channels)
    attended = jnp.roll(attended[:, 6:6 + height], -3, axis=2)
    teacher_out = finish(hidden_a, attended, t_out[1])
    gradient = student_grad(student_in, regions, teacher_out, s_qkv, s_out, s_proj, HEADS_S)
    return (teacher_out, gradient)
```

```python
import functools

import jax
import jax.numpy as jnp
import ml_dtypes
import numpy as np
from jax import lax
from jax.experimental import pallas as pl
from jax.experimental.pallas import tpu as pltpu
from jax.sharding import PartitionSpec as P

HEADS_T = 8
HEADS_S = 4
EPS = 1e-06
LOG2E = 1.4426950408889634
SCALE = 10.0 * LOG2E
BF = jnp.bfloat16
F32 = jnp.float32

ROWS, COLS = 24, 12
WIN = 80
NA = 4 * WIN
NAT = ROWS * 16
QUAD = 256

PARTS = (
    ("nw", (0, 6), (0, 3), 32),
    ("n", (0, 6), (3, 9), 48),
    ("ne", (0, 6), (9, 12), 32),
    ("e", (6, 18), (9, 12), 48),
    ("se", (18, 24), (9, 12), 32),
    ("s", (18, 24), (3, 9), 48),
    ("sw", (18, 24), (0, 3), 32),
    ("w", (6, 18), (0, 3), 48),
    ("c", (6, 18), (3, 9), 80),
)
AT = {}
NG = 0
for _name, _r, _c, _kept in PARTS:
    AT[_name] = (NG, _kept)
    NG += _kept


def _a_slot(r, c):
    return (2 * (r // 12) + c // 6) * WIN + (r % 12) * 6 + c % 6


def _tables():
    to_a = np.zeros((NA, NAT), ml_dtypes.bfloat16)
    a_row = np.zeros((NA, ROWS), ml_dtypes.bfloat16)
    a_col = np.zeros((NA, COLS), ml_dtypes.bfloat16)
    for r in range(ROWS):
        for c in range(COLS):
            slot = _a_slot(r, c)
            to_a[slot, r * 16 + c] = 1
            a_row[slot, r] = 1
            a_col[slot, c] = 1
    a_to_g = np.zeros((NG, NA), ml_dtypes.bfloat16)
    for name, (r0, r1), (c0, c1), _ in PARTS:
        spot = AT[name][0]
        for r in range(r0, r1):
            for c in range(c0, c1):
                a_to_g[spot, _a_slot(r, c)] = 1
                spot += 1
    return to_a, a_row, a_col, a_to_g


TO_A, A_ROW, A_COL, A_TO_G = _tables()
FROM_A = np.ascontiguousarray(TO_A.T)
G_TO_A = np.ascontiguousarray(A_TO_G.T)


def dot(a, b):
    return jnp.dot(a, b, preferred_element_type=F32)


def dot_nt(a, b):
    return lax.dot_general(a, b, (((1,), (1,)), ((), ())), preferred_element_type=F32)


def dot_tn(a, b):
    return lax.dot_general(a, b, (((0,), (0,)), ((), ())), preferred_element_type=F32)


def head_lanes(rows, h):
    lane = lax.broadcasted_iota(jnp.int32, (rows, QUAD), 1)
    return jnp.where((lane >> 6) == h, 1.0, 0.0).astype(BF)


def head_blocks():
    row = lax.broadcasted_iota(jnp.int32, (QUAD, QUAD), 0)
    lane = lax.broadcasted_iota(jnp.int32, (QUAD, QUAD), 1)
    return jnp.where((row >> 6) == (lane >> 6), 1.0, 0.0).astype(BF)


def stack_heads(x):
    return jnp.concatenate([x * head_lanes(1, h) for h in range(4)], axis=0)


def stack_values(v):
    rows = v.shape[0]
    ones = jnp.concatenate([head_lanes(rows, h) for h in range(4)], axis=0)
    return jnp.concatenate([stack_heads(v), ones], axis=1)


def unstack_heads(x):
    n = x.shape[0] // 4
    lane = lax.broadcasted_iota(jnp.int32, (1, QUAD), 1) >> 6
    total = x[:n]
    for h in range(1, 4):
        total = jnp.where(lane == h, x[h * n : (h + 1) * n], total)
    return total


def head_sums(x, blocks):
    groups = [dot(x[:, i : i + QUAD].astype(BF), blocks) for i in range(0, x.shape[1], QUAD)]
    return groups[0] if len(groups) == 1 else jnp.concatenate(groups, axis=1)


def unit(x, blocks):
    scale = lax.rsqrt(head_sums(x * x, blocks) + EPS)
    return x * scale, scale


def id_mask(id_query, id_keys):
    keys = jnp.concatenate([id_keys] * 4, axis=0)
    row = dot_nt(jnp.full((8, 128), 1.0 / 128, BF), keys)[0:1]
    return id_query.astype(F32)[:, 0:1] == row


def attend(q, k, v, mask):
    scores = dot_nt(q, stack_heads(k))
    e = jnp.where(mask, jnp.exp2(scores), 0.0).astype(BF)
    both = dot(e, stack_values(v))
    return both[:, :QUAD], both[:, QUAD:], e


def to_window_order(x_ref, pad_ref, to_a):
    pad_ref[...] = jnp.zeros_like(pad_ref)
    pad_ref[:, 0:COLS, :] = x_ref[0]
    natural = pad_ref[...].reshape(NAT, x_ref.shape[3])
    return dot(to_a, natural).astype(BF)


def window_ids(reg, a_row, a_col):
    table = (reg + 1).astype(F32).astype(BF)
    picked = (dot(a_row, table) * a_col.astype(F32)).astype(BF)
    return dot(picked, jnp.ones((COLS, 128), BF)).astype(BF)


def residual(x, att, w):
    y = dot(att, w)
    r = lax.rsqrt(jnp.mean(y * y, axis=1, keepdims=True) + EPS)
    n = y * r
    return (x.astype(F32) + n).astype(BF), n, r


SAVE = 9 * QUAD + 384


def student_layer(x, w_qkv, w_out, ids, save_ref):
    blocks = head_blocks()
    qkv = dot(x, w_qkv)
    q, sq = unit(qkv[:, :QUAD], blocks)
    k, sk = unit(qkv[:, QUAD : 2 * QUAD], blocks)
    q = (q * SCALE).astype(BF)
    k = k.astype(BF)
    v = qkv[:, 2 * QUAD :].astype(BF)
    atts = []
    for w in range(4):
        rows = slice(w * WIN, (w + 1) * WIN)
        mask = id_mask(ids[rows], ids[rows])
        num, den, e = attend(q[rows], k[rows], v[rows], mask)
        z = 1.0 / den
        att = num * z
        save_ref[rows, 4 * QUAD : 5 * QUAD] = z.astype(BF)
        save_ref[rows, 9 * QUAD : 9 * QUAD + 4 * WIN] = e
        atts.append(att.astype(BF))
    att = jnp.concatenate(atts, axis=0)
    h, n, r = residual(x, att, w_out)
    for i, part in ((0, q), (1, k), (2, v), (3, att), (5, sq), (6, sk), (7, n)):
        save_ref[:, i * QUAD : (i + 1) * QUAD] = part.astype(BF)
    save_ref[:, 8 * QUAD : 9 * QUAD] = jnp.broadcast_to(r, (NA, QUAD)).astype(BF)
    return h


def fetch(*pairs):
    copies = [pltpu.make_async_copy(*pair) for pair in pairs]
    for copy in copies:
        copy.start()
    return copies


def student_first(
    x_ref, reg_ref, to_a, a_row, a_col, s_qkv, s_out, h_ref, id_ref, save_ref,
    pad_ref, wqkv, wout, sems,
):
    weights = fetch((s_qkv.at[0], wqkv, sems.at[0]), (s_out.at[0], wout, sems.at[1]))
    level = lax.axis_index("grp")
    x = to_window_order(x_ref, pad_ref, to_a[...])
    ids = window_ids(reg_ref[level], a_row[...], a_col[...])
    id_ref[...] = ids
    for copy in weights:
        copy.wait()
    h_ref[...] = student_layer(x, wqkv[...], wout[...], ids, save_ref)


def student_second(
    h_ref, id_ref, s_qkv, s_out, proj, after_ref, g_ref, save_ref, wqkv, wout, sems
):
    weights = fetch((s_qkv.at[1], wqkv, sems.at[0]), (s_out.at[1], wout, sems.at[1]))
    for copy in weights:
        copy.wait()
    h = student_layer(h_ref[...], wqkv[...], wout[...], id_ref[...], save_ref)
    predicted = dot(h, proj[...])
    g_ref[...] = dot_nt(predicted.astype(BF), proj[...])


def student_back(g, save_ref, w_qkv, w_out):
    blocks = head_blocks()
    part = lambda i: save_ref[:, i * QUAD : (i + 1) * QUAD]
    n, r = part(7).astype(F32), part(8).astype(F32)
    dy = r * (g - n * jnp.mean(g * n, axis=1, keepdims=True))
    datt = dot_nt(dy.astype(BF), w_out) * part(4).astype(F32)
    drop = (datt * part(3).astype(F32)).astype(BF) * jnp.asarray(-1.0, BF)
    datt = datt.astype(BF)
    q, k, v = part(0), part(1), part(2)
    dqs, dks, dvs = [], [], []
    for w in range(4):
        rows = slice(w * WIN, (w + 1) * WIN)
        e = save_ref[rows, 9 * QUAD : 9 * QUAD + 4 * WIN]
        both = jnp.concatenate([datt[rows], drop[rows]], axis=1)
        ds = (e.astype(F32) * dot_nt(both, stack_values(v[rows]))).astype(BF)
        dqs.append(dot(ds, stack_heads(k[rows])))
        dks.append(unstack_heads(dot_tn(ds, q[rows])))
        dvs.append(unstack_heads(dot_tn(e, datt[rows])))
    dq = 10.0 * jnp.concatenate(dqs, axis=0)
    dk = (1.0 / LOG2E) * jnp.concatenate(dks, axis=0)
    dv = jnp.concatenate(dvs, axis=0)
    q_unit = q.astype(F32) * (1.0 / SCALE)
    k_unit = k.astype(F32)
    dq = part(5).astype(F32) * (dq - q_unit * head_sums(q_unit * dq, blocks))
    dk = part(6).astype(F32) * (dk - k_unit * head_sums(k_unit * dk, blocks))
    dqkv = jnp.concatenate([dq.astype(BF), dk.astype(BF), dv.astype(BF)], axis=1)
    return g + dot_nt(dqkv, w_qkv)


def teacher_first(
    x_ref, far_ref, reg_ref, to_a, a_row, a_col, a_to_g, t_qkv, t_out, *refs
):
    h_ref, g_ref, sends, pad_ref, wqkv, wout, sems = *refs[:2], refs[2:10], *refs[10:]
    weights = fetch((t_qkv.at[0], wqkv, sems.at[0]), (t_out.at[0], wout, sems.at[1]))
    level = lax.axis_index("grp")
    width = x_ref.shape[3]
    blocks = head_blocks()
    x = to_window_order(x_ref, pad_ref, to_a[...])
    far = to_window_order(far_ref, pad_ref, to_a[...])
    ids = window_ids(reg_ref[level], a_row[...], a_col[...])
    ids_far = window_ids(reg_ref[1 - level], a_row[...], a_col[...])
    weights[0].wait()
    q = (unit(dot(x, wqkv[:, :width]), blocks)[0] * SCALE).astype(BF)
    rows = jnp.concatenate([x, far], axis=0)
    k = unit(dot(rows, wqkv[:, width : 2 * width]), blocks)[0].astype(BF)
    v = dot(rows, wqkv[:, 2 * width :]).astype(BF)
    atts = []
    for w in range(4):
        near_rows = slice(w * WIN, (w + 1) * WIN)
        far_rows = slice(NA + w * WIN, NA + (w + 1) * WIN)
        id_keys = jnp.concatenate([ids[near_rows], ids_far[near_rows]], axis=0)
        mask = id_mask(ids[near_rows], id_keys)
        quads = []
        for i in range(0, width, QUAD):
            lanes = slice(i, i + QUAD)
            num, den, _ = attend(
                q[near_rows, lanes],
                jnp.concatenate([k[near_rows, lanes], k[far_rows, lanes]], axis=0),
                jnp.concatenate([v[near_rows, lanes], v[far_rows, lanes]], axis=0),
                mask,
            )
            quads.append((num / den).astype(BF))
        atts.append(jnp.concatenate(quads, axis=1))
    weights[1].wait()
    h = residual(x, jnp.concatenate(atts, axis=0), wout[...])[0]
    h_ref[...] = h
    spread = dot(a_to_g[...], jnp.concatenate([h, ids], axis=1)).astype(BF)
    g_ref[...] = spread
    for ref, names in zip(sends, SENDS):
        spot = 0
        for name in names:
            start, kept = AT[name]
            ref[spot : spot + kept] = spread[start : start + kept]
            spot += kept


SENDS = (
    ("nw", "n", "ne"),
    ("ne", "e", "se"),
    ("sw", "s", "se"),
    ("nw", "w", "sw"),
    ("nw",),
    ("ne",),
    ("se",),
    ("sw",),
)
STEPS = ((-1, 0), (0, 1), (1, 0), (0, -1), (-1, -1), (-1, 1), (1, 1), (1, -1))
SIDES = ("N", "E", "S", "W", "NW", "NE", "SE", "SW")
OPPOSITE = {"N": "S", "S": "N", "E": "W", "W": "E", "NW": "SE", "SE": "NW", "NE": "SW", "SW": "NE"}
EXTRA = {
    "nw": (("N", "sw"), ("W", "ne"), ("NW", "se")),
    "n": (("N", "s"),),
    "ne": (("N", "se"), ("E", "nw"), ("NE", "sw")),
    "e": (("E", "w"),),
    "se": (("S", "ne"), ("E", "sw"), ("SE", "nw")),
    "s": (("S", "n"),),
    "sw": (("S", "nw"), ("W", "se"), ("SW", "ne")),
    "w": (("W", "e"),),
    "c": (),
}


def _arrivals():
    spots, spot = {}, NG
    for side in SIDES:
        for name in SENDS[SIDES.index(OPPOSITE[side])]:
            spots[side, name] = spot
            spot += AT[name][1]
    return spots, spot


ARRIVE, NX = _arrivals()


def teacher_second(
    h_ref, g_ref, r0, r1, r2, r3, r4, r5, r6, r7, from_a, g_to_a, t_qkv, t_out,
    proj, s_qkv, s_out, g0_ref, save0_ref, save1_ref, out_ref, grad_ref,
    wqkv, wout, w_proj, w_sqkv, w_sout, save0, save1, sems,
):
    later = fetch(
        (t_qkv.at[1], wqkv, sems.at[0]),
        (t_out.at[1], wout, sems.at[1]),
        (proj, w_proj, sems.at[2]),
        (save1_ref, save1, sems.at[3]),
        (s_qkv, w_sqkv, sems.at[4]),
        (s_out, w_sout, sems.at[5]),
        (save0_ref, save0, sems.at[6]),
    )
    lat = lax.axis_index("lat")
    last = lax.axis_size("lat") - 1
    width = h_ref.shape[1]
    blocks = head_blocks()
    own = g_ref[...]
    arrived = []
    ids = [own[:, width:]]
    for side, ref in zip(SIDES, (r0, r1, r2, r3, r4, r5, r6, r7)):
        arrived.append(ref[:, :width])
        tag = ref[:, width:]
        if "N" in side:
            tag = tag * jnp.where(lat > 0, 1.0, 0.0).astype(BF)
        if "S" in side:
            tag = tag * jnp.where(lat < last, 1.0, 0.0).astype(BF)
        ids.append(tag)
    ids = jnp.concatenate(ids, axis=0)
    later[0].wait()
    q = (unit(dot(own[:, :width], wqkv[:, :width]), blocks)[0] * SCALE).astype(BF)
    rows = jnp.concatenate([own[:, :width]] + arrived, axis=0)
    k = unit(dot(rows, wqkv[:, width : 2 * width]), blocks)[0].astype(BF)
    v = dot(rows, wqkv[:, 2 * width :]).astype(BF)
    atts = []
    for name, _, _, kept in PARTS:
        start = AT[name][0]
        spans = [slice(start, start + kept)]
        for side, part in EXTRA[name]:
            spot = ARRIVE[side, part]
            spans.append(slice(spot, spot + AT[part][1]))
        gather = lambda x: jnp.concatenate([x[s] for s in spans], axis=0) if len(spans) > 1 else x[spans[0]]
        mask = id_mask(ids[spans[0]], gather(ids))
        k_rows, v_rows = gather(k), gather(v)
        quads = []
        for i in range(0, width, QUAD):
            lanes = slice(i, i + QUAD)
            num, den, _ = attend(q[spans[0], lanes], k_rows[:, lanes], v_rows[:, lanes], mask)
            quads.append((num / den).astype(BF))
        atts.append(jnp.concatenate(quads, axis=1))
    att = dot(g_to_a[...], jnp.concatenate(atts, axis=0)).astype(BF)
    later[1].wait()
    teacher = residual(h_ref[...], att, wout[...])[0]
    natural = dot(from_a[...], teacher).astype(BF)
    out_ref[0] = natural.reshape(ROWS, 16, width)[:, :COLS, :]

    for copy in later[2:]:
        copy.wait()
    g = g0_ref[...] - dot_nt(teacher, w_proj[...])
    g = student_back(g, save1, w_sqkv[1], w_sout[1])
    g = student_back(g, save0, w_sqkv[0], w_sout[0])
    high = g.astype(BF)
    low = (g - high.astype(F32)).astype(BF)
    natural = dot(from_a[...], high) + dot(from_a[...], low)
    grad_ref[0] = natural.reshape(ROWS, 16, g.shape[1])[:, :COLS, :]


VMEM = pl.BlockSpec(memory_space=pltpu.VMEM)
ANY = pl.BlockSpec(memory_space=pl.ANY)


def call(kernel, name, outs, specs, args, scratch=(), flops=0):
    shapes = [jax.ShapeDtypeStruct(s, d) for s, d in outs]
    touched = sum(a.size * a.dtype.itemsize for a in args)
    return pl.pallas_call(
        kernel,
        name=name,
        out_shape=shapes,
        in_specs=specs,
        out_specs=[VMEM] * len(outs),
        scratch_shapes=list(scratch),
        compiler_params=pltpu.CompilerParams(vmem_limit_bytes=40 << 20),
        cost_estimate=pl.CostEstimate(flops=flops, bytes_accessed=touched, transcendentals=0),
    )(*args)


def neighbour_routes(step, lat_size, lon_size):
    di, dj = step
    route = []
    for i in range(lat_size):
        for j in range(lon_size):
            to = ((i + di) % lat_size) * lon_size + (j + dj) % lon_size
            route.append((i * lon_size + j, to))
    return route


def shards(teacher_in, student_in, regions, t_qkv, t_out, s_qkv, s_out, s_proj):
    width, narrow = teacher_in.shape[3], student_in.shape[3]
    lat_size, lon_size = lax.axis_size("lat"), lax.axis_size("lon")
    far = lax.ppermute(teacher_in, "grp", [(0, 1), (1, 0)])

    def buffers(*arrays):
        return [pltpu.VMEM(a, BF) for a in arrays] + [pltpu.SemaphoreType.DMA((len(arrays),))]

    layer_t, layer_s = t_qkv.shape[1:], s_qkv.shape[1:]
    out_t, out_s = t_out.shape[1:], s_out.shape[1:]

    args = [student_in, regions, TO_A, A_ROW, A_COL, s_qkv, s_out]
    h1, ids, save0 = call(
        student_first, "student_first",
        [((NA, narrow), BF), ((NA, 128), BF), ((NA, SAVE), BF)],
        [VMEM] * 5 + [ANY] * 2,
        args, [pltpu.VMEM((ROWS, 16, narrow), BF)] + buffers(layer_s, out_s), 10**9,
    )

    args = [teacher_in, far, regions, TO_A, A_ROW, A_COL, A_TO_G, t_qkv, t_out]
    pieces = [sum(AT[n][1] for n in names) for names in SENDS]
    hidden, spread, *sends = call(
        teacher_first, "teacher_first",
        [((NA, width), BF), ((NG, width + 128), BF)] + [((n, width + 128), BF) for n in pieces],
        [VMEM] * 7 + [ANY] * 2,
        args, [pltpu.VMEM((ROWS, 16, width), BF)] + buffers(layer_t, out_t), 4 * 10**9,
    )
    came = {}
    for side, step, piece in zip(SIDES, STEPS, sends):
        came[OPPOSITE[side]] = lax.ppermute(
            piece, ("lat", "lon"), neighbour_routes(step, lat_size, lon_size)
        )

    args = [h1, ids, s_qkv, s_out, s_proj, spread]
    g0, save1 = call(
        student_second, "student_second",
        [((NA, narrow), F32), ((NA, SAVE), BF)],
        [VMEM] * 2 + [ANY, ANY, VMEM, ANY],
        args, buffers(layer_s, out_s), 10**9,
    )

    args = [hidden, spread] + [came[s] for s in SIDES] + [FROM_A, G_TO_A, t_qkv, t_out]
    args += [s_proj, s_qkv, s_out, g0, save0, save1]
    specs = [VMEM] * 12 + [ANY] * 5 + [VMEM] + [ANY] * 2
    scratch = buffers(
        layer_t, out_t, s_proj.shape, s_qkv.shape, s_out.shape, save0.shape, save1.shape
    )
    return tuple(
        call(
            teacher_second, "teacher_second",
            [(teacher_in.shape, BF), (student_in.shape, F32)],
            specs, args, scratch, 6 * 10**9,
        )
    )


def solution(mesh):
    tiles = P("grp", "lat", "lon", None)
    return jax.shard_map(
        shards,
        mesh=mesh,
        in_specs=(tiles, tiles, P(None, "lat", "lon"), P(), P(), P(), P(), P()),
        out_specs=(tiles, tiles),
        check_vma=False,
    )
```

```python
import functools

import jax
import jax.numpy as jnp
import ml_dtypes
import numpy as np
from jax import lax
from jax.experimental import pallas as pl
from jax.experimental.pallas import tpu as pltpu
from jax.sharding import PartitionSpec as P

HEADS_T = 8
HEADS_S = 4
EPS = 1e-06
LOG2E = 1.4426950408889634
SCALE = 10.0 * LOG2E
BF = jnp.bfloat16
F32 = jnp.float32

ROWS, COLS = 24, 12
WIN = 80
NA = 4 * WIN
TALL = 32
NAT = COLS * TALL
QUAD = 256

PARTS = (
    ("nw", (0, 6), (0, 3), 32),
    ("n", (0, 6), (3, 9), 48),
    ("ne", (0, 6), (9, 12), 32),
    ("e", (6, 18), (9, 12), 48),
    ("se", (18, 24), (9, 12), 32),
    ("s", (18, 24), (3, 9), 48),
    ("sw", (18, 24), (0, 3), 32),
    ("w", (6, 18), (0, 3), 48),
    ("c", (6, 18), (3, 9), 80),
)
AT = {}
NG = 0
for _name, _r, _c, _kept in PARTS:
    AT[_name] = (NG, _kept)
    NG += _kept


def _a_slot(r, c):
    return (2 * (r // 12) + c // 6) * WIN + (r % 12) * 6 + c % 6


def _tables():
    to_a = np.zeros((NA, NAT), ml_dtypes.bfloat16)
    a_row = np.zeros((NA, ROWS), ml_dtypes.bfloat16)
    a_col = np.zeros((NA, COLS), ml_dtypes.bfloat16)
    for r in range(ROWS):
        for c in range(COLS):
            slot = _a_slot(r, c)
            to_a[slot, c * TALL + r] = 1
            a_row[slot, r] = 1
            a_col[slot, c] = 1
    a_to_g = np.zeros((NG, NA), ml_dtypes.bfloat16)
    for name, (r0, r1), (c0, c1), _ in PARTS:
        spot = AT[name][0]
        for r in range(r0, r1):
            for c in range(c0, c1):
                a_to_g[spot, _a_slot(r, c)] = 1
                spot += 1
    return to_a, a_row, a_col, a_to_g


TO_A, A_ROW, A_COL, A_TO_G = _tables()
FROM_A = np.ascontiguousarray(TO_A.T)
G_TO_A = np.ascontiguousarray(A_TO_G.T)


def dot(a, b):
    return jnp.dot(a, b, preferred_element_type=F32)


def dot_nt(a, b):
    return lax.dot_general(a, b, (((1,), (1,)), ((), ())), preferred_element_type=F32)


def dot_tn(a, b):
    return lax.dot_general(a, b, (((0,), (0,)), ((), ())), preferred_element_type=F32)


def head_lanes(rows, h):
    lane = lax.broadcasted_iota(jnp.int32, (rows, QUAD), 1)
    return jnp.where((lane >> 6) == h, 1.0, 0.0).astype(BF)


def head_blocks():
    row = lax.broadcasted_iota(jnp.int32, (QUAD, QUAD), 0)
    lane = lax.broadcasted_iota(jnp.int32, (QUAD, QUAD), 1)
    return jnp.where((row >> 6) == (lane >> 6), 1.0, 0.0).astype(BF)


def stack_heads(x):
    return jnp.concatenate([x * head_lanes(1, h) for h in range(4)], axis=0)


def stack_values(v):
    rows = v.shape[0]
    ones = jnp.concatenate([head_lanes(rows, h) for h in range(4)], axis=0)
    return jnp.concatenate([stack_heads(v), ones], axis=1)


def unstack_heads(x):
    n = x.shape[0] // 4
    lane = lax.broadcasted_iota(jnp.int32, (1, QUAD), 1) >> 6
    total = x[:n]
    for h in range(1, 4):
        total = jnp.where(lane == h, x[h * n : (h + 1) * n], total)
    return total


def head_sums(x, blocks):
    groups = [dot(x[:, i : i + QUAD].astype(BF), blocks) for i in range(0, x.shape[1], QUAD)]
    return groups[0] if len(groups) == 1 else jnp.concatenate(groups, axis=1)


def unit(x, blocks):
    scale = lax.rsqrt(head_sums(x * x, blocks) + EPS)
    return x * scale, scale


def id_mask(id_query, id_keys):
    keys = jnp.concatenate([id_keys] * 4, axis=0)
    row = dot_nt(jnp.full((8, 128), 1.0 / 128, BF), keys)[0:1]
    return id_query.astype(F32)[:, 0:1] == row


def attend(q, k, v, mask):
    scores = dot_nt(q, stack_heads(k))
    e = jnp.where(mask, jnp.exp2(scores), 0.0).astype(BF)
    both = dot(e, stack_values(v))
    return both[:, :QUAD], both[:, QUAD:], e


def to_window_order(x_ref, pad_ref, to_a):
    pad_ref[...] = jnp.zeros_like(pad_ref)
    pad_ref[:, 0:ROWS, :] = x_ref[0]
    natural = pad_ref[...].reshape(NAT, x_ref.shape[3])
    return dot(to_a, natural).astype(BF)


def window_ids(reg, a_row, a_col):
    table = (reg + 1).astype(F32).astype(BF)
    picked = (dot(a_col, table) * a_row.astype(F32)).astype(BF)
    return dot(picked, jnp.ones((ROWS, 128), BF)).astype(BF)


def by_level(reg_ref):
    level = lax.axis_index("grp")
    low, high = reg_ref[:, 0, :], reg_ref[:, 1, :]
    own = jnp.where(level == 0, low, high)
    return own, low + high - own


def residual(x, att, w):
    y = dot(att, w)
    r = lax.rsqrt(jnp.mean(y * y, axis=1, keepdims=True) + EPS)
    n = y * r
    return (x.astype(F32) + n).astype(BF), n, r


SAVE = 9 * QUAD + 384


def student_layer(x, w_qkv, w_out, ids, save_ref):
    blocks = head_blocks()
    qkv = dot(x, w_qkv)
    q, sq = unit(qkv[:, :QUAD], blocks)
    k, sk = unit(qkv[:, QUAD : 2 * QUAD], blocks)
    q = (q * SCALE).astype(BF)
    k = k.astype(BF)
    v = qkv[:, 2 * QUAD :].astype(BF)
    atts = []
    for w in range(4):
        rows = slice(w * WIN, (w + 1) * WIN)
        mask = id_mask(ids[rows], ids[rows])
        num, den, e = attend(q[rows], k[rows], v[rows], mask)
        z = 1.0 / den
        att = num * z
        save_ref[rows, 4 * QUAD : 5 * QUAD] = z.astype(BF)
        save_ref[rows, 9 * QUAD : 9 * QUAD + 4 * WIN] = e
        atts.append(att.astype(BF))
    att = jnp.concatenate(atts, axis=0)
    h, n, r = residual(x, att, w_out)
    for i, part in ((0, q), (1, k), (2, v), (3, att), (5, sq), (6, sk), (7, n)):
        save_ref[:, i * QUAD : (i + 1) * QUAD] = part.astype(BF)
    save_ref[:, 8 * QUAD : 9 * QUAD] = jnp.broadcast_to(r, (NA, QUAD)).astype(BF)
    return h


def fetch(*pairs):
    copies = [pltpu.make_async_copy(*pair) for pair in pairs]
    for copy in copies:
        copy.start()
    return copies


def student_first(x_ref, id_ref, to_a, s_qkv, s_out, after_ref, h_ref, save_ref, pad_ref):
    x = to_window_order(x_ref, pad_ref, to_a[...])
    h_ref[...] = student_layer(x, s_qkv[0], s_out[0], id_ref[...], save_ref)


def student_back(g, save_ref, w_qkv, w_out):
    blocks = head_blocks()
    part = lambda i: save_ref[:, i * QUAD : (i + 1) * QUAD]
    n, r = part(7).astype(F32), part(8).astype(F32)
    dy = r * (g - n * jnp.mean(g * n, axis=1, keepdims=True))
    datt = dot_nt(dy.astype(BF), w_out) * part(4).astype(F32)
    drop = (datt * part(3).astype(F32)).astype(BF) * jnp.asarray(-1.0, BF)
    datt = datt.astype(BF)
    q, k, v = part(0), part(1), part(2)
    dqs, dks, dvs = [], [], []
    for w in range(4):
        rows = slice(w * WIN, (w + 1) * WIN)
        e = save_ref[rows, 9 * QUAD : 9 * QUAD + 4 * WIN]
        both = jnp.concatenate([datt[rows], drop[rows]], axis=1)
        ds = (e.astype(F32) * dot_nt(both, stack_values(v[rows]))).astype(BF)
        dqs.append(dot(ds, stack_heads(k[rows])))
        dks.append(unstack_heads(dot_tn(ds, q[rows])))
        dvs.append(unstack_heads(dot_tn(e, datt[rows])))
    dq = 10.0 * jnp.concatenate(dqs, axis=0)
    dk = (1.0 / LOG2E) * jnp.concatenate(dks, axis=0)
    dv = jnp.concatenate(dvs, axis=0)
    q_unit = q.astype(F32) * (1.0 / SCALE)
    k_unit = k.astype(F32)
    dq = part(5).astype(F32) * (dq - q_unit * head_sums(q_unit * dq, blocks))
    dk = part(6).astype(F32) * (dk - k_unit * head_sums(k_unit * dk, blocks))
    dqkv = jnp.concatenate([dq.astype(BF), dk.astype(BF), dv.astype(BF)], axis=1)
    return g + dot_nt(dqkv, w_qkv)


def teacher_first(
    x_hbm, far_ref, reg_ref, to_a_hbm, a_row_hbm, a_col_hbm, a_to_g_hbm, t_qkv, t_out,
    h_ref, id_ref, g_ref, north_ref, south_ref,
    pad_ref, x_ref, to_a, a_row, a_col, a_to_g, wqkv, wout, sems,
):
    copies = fetch(
        (x_hbm, x_ref, sems.at[0]),
        (to_a_hbm, to_a, sems.at[1]),
        (t_qkv.at[0], wqkv, sems.at[2]),
        (a_row_hbm, a_row, sems.at[3]),
        (a_col_hbm, a_col, sems.at[4]),
        (t_out.at[0], wout, sems.at[5]),
        (a_to_g_hbm, a_to_g, sems.at[6]),
    )
    width = x_ref.shape[3]
    blocks = head_blocks()
    copies[0].wait()
    copies[1].wait()
    x = to_window_order(x_ref, pad_ref, to_a[...])
    far = to_window_order(far_ref, pad_ref, to_a[...])
    copies[3].wait()
    copies[4].wait()
    reg, reg_far = by_level(reg_ref)
    ids = window_ids(reg, a_row[...], a_col[...])
    ids_far = window_ids(reg_far, a_row[...], a_col[...])
    id_ref[...] = ids
    copies[2].wait()
    q = (unit(dot(x, wqkv[:, :width]), blocks)[0] * SCALE).astype(BF)
    rows = jnp.concatenate([x, far], axis=0)
    k = unit(dot(rows, wqkv[:, width : 2 * width]), blocks)[0].astype(BF)
    v = dot(rows, wqkv[:, 2 * width :]).astype(BF)
    atts = []
    for w in range(4):
        near_rows = slice(w * WIN, (w + 1) * WIN)
        far_rows = slice(NA + w * WIN, NA + (w + 1) * WIN)
        id_keys = jnp.concatenate([ids[near_rows], ids_far[near_rows]], axis=0)
        mask = id_mask(ids[near_rows], id_keys)
        quads = []
        for i in range(0, width, QUAD):
            lanes = slice(i, i + QUAD)
            num, den, _ = attend(
                q[near_rows, lanes],
                jnp.concatenate([k[near_rows, lanes], k[far_rows, lanes]], axis=0),
                jnp.concatenate([v[near_rows, lanes], v[far_rows, lanes]], axis=0),
                mask,
            )
            quads.append((num / den).astype(BF))
        atts.append(jnp.concatenate(quads, axis=1))
    copies[5].wait()
    h = residual(x, jnp.concatenate(atts, axis=0), wout[...])[0]
    h_ref[...] = h
    copies[6].wait()
    spread = dot(a_to_g[...], jnp.concatenate([h, ids], axis=1)).astype(BF)
    g_ref[...] = spread
    put(north_ref, [part(spread, n) for n in TO_NORTH])
    put(south_ref, [part(spread, n) for n in TO_SOUTH])


def part(x, name):
    start, kept = AT[name]
    return x[start : start + kept]


def put(ref, blocks):
    spot = 0
    for block in blocks:
        ref[spot : spot + block.shape[0]] = block
        spot += block.shape[0]


TO_NORTH = ("nw", "n", "ne")
TO_SOUTH = ("sw", "s", "se")
TO_WEST = (("N", "sw"), ("", "nw"), ("", "w"), ("", "sw"), ("S", "nw"))
TO_EAST = (("N", "se"), ("", "ne"), ("", "e"), ("", "se"), ("S", "ne"))
EXTRA = {
    "nw": (("N", "sw"), ("W", "ne"), ("NW", "se")),
    "n": (("N", "s"),),
    "ne": (("N", "se"), ("E", "nw"), ("NE", "sw")),
    "e": (("E", "w"),),
    "se": (("S", "ne"), ("E", "sw"), ("SE", "nw")),
    "s": (("S", "n"),),
    "sw": (("S", "nw"), ("W", "se"), ("SW", "ne")),
    "w": (("W", "e"),),
    "c": (),
}
EARLY = ("n", "c", "s")
LATE = ("nw", "ne", "e", "se", "sw", "w")
ORDER = [name for name, *_ in PARTS]


def _spots(items, start):
    spots = {}
    for side, name in items:
        spots[side, name] = start
        start += AT[name][1]
    return spots, start


KNOWN, NK = _spots([("N", n) for n in TO_SOUTH] + [("S", n) for n in TO_NORTH], NG)
KNOWN.update({("", n): AT[n][0] for n in ORDER})
_come = [((s + "E"), n) for s, n in TO_WEST] + [((s + "W"), n) for s, n in TO_EAST]
COME, NC = _spots(_come, 0)


def send_columns(g_ref, north_ref, south_ref, after_ref, west_ref, east_ref):
    def block(side, name):
        spot = KNOWN[side, name]
        kept = AT[name][1]
        if side == "N":
            return north_ref[spot - NG : spot - NG + kept]
        if side == "S":
            spot = spot - NG - north_ref.shape[0]
            return south_ref[spot : spot + kept]
        return g_ref[spot : spot + kept]

    put(west_ref, [block(*item) for item in TO_WEST])
    put(east_ref, [block(*item) for item in TO_EAST])


def window_attention(name, q, keys, mask_ids):
    k, v = keys
    mask = id_mask(*mask_ids)
    quads = []
    for i in range(0, q.shape[1], QUAD):
        lanes = slice(i, i + QUAD)
        num, den, _ = attend(q[:, lanes], k[:, lanes], v[:, lanes], mask)
        quads.append((num / den).astype(BF))
    return jnp.concatenate(quads, axis=1)


def gather(sources, items):
    blocks = []
    for side, name in items:
        for array, spots in sources:
            if (side, name) in spots:
                spot = spots[side, name]
                blocks.append(array[spot : spot + AT[name][1]])
                break
    return blocks[0] if len(blocks) == 1 else jnp.concatenate(blocks, axis=0)


def middle(
    h_ref, id_ref, s_qkv, s_out, proj, g_ref, north_ref, south_ref, t_qkv, after_ref,
    g0_ref, save_ref, q_ref, k_ref, v_ref, att_ref,
):
    width = g_ref.shape[1] - 128
    blocks = head_blocks()
    known = jnp.concatenate([g_ref[...], north_ref[...], south_ref[...]], axis=0)
    rows, ids = known[:, :width], known[:, width:]
    q = (unit(dot(rows[:NG], t_qkv[1, :, :width]), blocks)[0] * SCALE).astype(BF)
    k = unit(dot(rows, t_qkv[1, :, width : 2 * width]), blocks)[0].astype(BF)
    v = dot(rows, t_qkv[1, :, 2 * width :]).astype(BF)
    q_ref[...] = q
    k_ref[...] = k
    v_ref[...] = v
    for name in EARLY:
        items = (("", name),) + EXTRA[name]
        keys = [gather([(x, KNOWN)], items) for x in (k, v)]
        start, kept = AT[name]
        att_ref[start : start + kept] = window_attention(
            name, part(q, name), keys, (part(ids, name), gather([(ids, KNOWN)], items))
        )
    for name in LATE:
        start, kept = AT[name]
        att_ref[start : start + kept] = jnp.zeros((kept, width), BF)

    h = student_layer(h_ref[...], s_qkv[1], s_out[1], id_ref[...], save_ref)
    predicted = dot(h, proj[...])
    g0_ref[...] = dot_nt(predicted.astype(BF), proj[...])


def teacher_second(
    h_ref, g_ref, north_ref, south_ref, east_ref, west_ref, q_ref, k_ref, v_ref, att_ref,
    from_a, g_to_a, t_qkv, t_out, proj, s_qkv, s_out, g0_ref, save0, save1, out_ref, grad_ref,
):
    width = h_ref.shape[1]
    blocks = head_blocks()
    came = jnp.concatenate([east_ref[...], west_ref[...]], axis=0)
    rows = came[:, :width]
    k = unit(dot(rows, t_qkv[1, :, width : 2 * width]), blocks)[0].astype(BF)
    v = dot(rows, t_qkv[1, :, 2 * width :]).astype(BF)
    known_ids = jnp.concatenate(
        [g_ref[:, width:], north_ref[:, width:], south_ref[:, width:]], axis=0
    )
    atts = {name: part(att_ref, name) for name in EARLY}
    for name in LATE:
        items = (("", name),) + EXTRA[name]
        keys = [gather([(x, COME), (y, KNOWN)], items) for x, y in ((k, k_ref), (v, v_ref))]
        id_keys = gather([(came[:, width:], COME), (known_ids, KNOWN)], items)
        atts[name] = window_attention(
            name, part(q_ref, name), keys, (part(known_ids, name), id_keys)
        )
    att = jnp.concatenate([atts[name] for name in ORDER], axis=0)
    att = dot(g_to_a[...], att).astype(BF)
    teacher = residual(h_ref[...], att, t_out[1])[0]
    natural = dot(from_a[...], teacher).astype(BF)
    out_ref[0] = natural.reshape(COLS, TALL, width)[:, :ROWS, :]

    g = g0_ref[...] - dot_nt(teacher, proj[...])
    g = student_back(g, save1, s_qkv[1], s_out[1])
    g = student_back(g, save0, s_qkv[0], s_out[0])
    high = g.astype(BF)
    low = (g - high.astype(F32)).astype(BF)
    natural = dot(from_a[...], high) + dot(from_a[...], low)
    grad_ref[0] = natural.reshape(COLS, TALL, g.shape[1])[:, :ROWS, :]


VMEM = pl.BlockSpec(memory_space=pltpu.VMEM)
ANY = pl.BlockSpec(memory_space=pl.ANY)
HBM = pl.BlockSpec(memory_space=pltpu.HBM)


def call(kernel, name, outs, specs, args, scratch=(), flops=0):
    shapes = [jax.ShapeDtypeStruct(s, d) for s, d in outs]
    touched = sum(a.size * a.dtype.itemsize for a in args)
    return pl.pallas_call(
        kernel,
        name=name,
        out_shape=shapes,
        in_specs=specs,
        out_specs=[VMEM] * len(outs),
        scratch_shapes=list(scratch),
        compiler_params=pltpu.CompilerParams(vmem_limit_bytes=28 << 20),
        cost_estimate=pl.CostEstimate(flops=flops, bytes_accessed=touched, transcendentals=0),
    )(*args)


def buffers(*arrays):
    return [pltpu.VMEM(a.shape, a.dtype) for a in arrays] + [
        pltpu.SemaphoreType.DMA((len(arrays),))
    ]


def shards(teacher_in, student_in, regions, t_qkv, t_out, s_qkv, s_out, s_proj):
    width, narrow = teacher_in.shape[3], student_in.shape[3]
    lat_size, lon_size = lax.axis_size("lat"), lax.axis_size("lon")
    wide = width + 128
    teacher_in = teacher_in.transpose(0, 2, 1, 3)
    student_in = student_in.transpose(0, 2, 1, 3)
    regions = regions.transpose(2, 0, 1)
    far = lax.ppermute(teacher_in, "grp", [(0, 1), (1, 0)])

    args = [teacher_in, far, regions, TO_A, A_ROW, A_COL, A_TO_G, t_qkv, t_out]
    row_count = sum(AT[n][1] for n in TO_NORTH)
    hidden, ids, spread, to_north, to_south = call(
        teacher_first, "teacher_first",
        [((NA, width), BF), ((NA, 128), BF), ((NG, wide), BF)] + [((row_count, wide), BF)] * 2,
        [HBM, VMEM, VMEM] + [HBM] * 6,
        args,
        [pltpu.VMEM((COLS, TALL, width), BF)]
        + buffers(teacher_in, TO_A, A_ROW, A_COL, A_TO_G, t_qkv[0], t_out[0]),
        4 * 10**9,
    )
    north = lax.ppermute(to_south, "lat", [(i, i + 1) for i in range(lat_size - 1)])
    south = lax.ppermute(to_north, "lat", [(i + 1, i) for i in range(lat_size - 1)])

    h1, save0 = call(
        student_first, "student_first",
        [((NA, narrow), BF), ((NA, SAVE), BF)],
        [VMEM] * 5 + [ANY],
        [student_in, ids, TO_A, s_qkv, s_out, to_north],
        [pltpu.VMEM((COLS, TALL, narrow), BF)], 10**9,
    )

    to_west, to_east = call(
        send_columns, "send_columns",
        [((NC // 2, wide), BF)] * 2,
        [VMEM] * 3 + [ANY],
        [spread, north, south, h1], (), 10**6,
    )
    east = lax.ppermute(to_west, "lon", [((j + 1) % lon_size, j) for j in range(lon_size)])
    west = lax.ppermute(to_east, "lon", [(j, (j + 1) % lon_size) for j in range(lon_size)])

    g0, save1, q, k, v, att = call(
        middle, "middle",
        [((NA, narrow), F32), ((NA, SAVE), BF)]
        + [((NG, width), BF), ((NK, width), BF), ((NK, width), BF), ((NG, width), BF)],
        [VMEM] * 9 + [ANY],
        [h1, ids, s_qkv, s_out, s_proj, spread, north, south, t_qkv, to_west],
        (), 4 * 10**9,
    )

    args = [hidden, spread, north, south, east, west, q, k, v, att, FROM_A, G_TO_A]
    args += [t_qkv, t_out, s_proj, s_qkv, s_out, g0, save0, save1]
    out, grad = call(
        teacher_second, "teacher_second",
        [(teacher_in.shape, BF), (student_in.shape, F32)],
        [VMEM] * len(args), args, (), 6 * 10**9,
    )
    return out.transpose(0, 2, 1, 3), grad.transpose(0, 2, 1, 3)


def solution(mesh):
    tiles = P("grp", "lat", "lon", None)
    return jax.shard_map(
        shards,
        mesh=mesh,
        in_specs=(tiles, tiles, P(None, "lat", "lon"), P(), P(), P(), P(), P()),
        out_specs=(tiles, tiles),
        check_vma=False,
    )
```

```python
import functools

import jax
import jax.numpy as jnp
import ml_dtypes
import numpy as np
from jax import lax
from jax.experimental import pallas as pl
from jax.experimental.pallas import tpu as pltpu
from jax.sharding import PartitionSpec as P

HEADS_T = 8
HEADS_S = 4
EPS = 1e-06
LOG2E = 1.4426950408889634
SCALE = 10.0 * LOG2E
BF = jnp.bfloat16
F32 = jnp.float32

ROWS, COLS = 24, 12
WIN = 80
NA = 4 * WIN
TALL = 32
NAT = COLS * TALL
QUAD = 256

PARTS = (
    ("nw", (0, 6), (0, 3), 32),
    ("n", (0, 6), (3, 9), 48),
    ("ne", (0, 6), (9, 12), 32),
    ("e", (6, 18), (9, 12), 48),
    ("se", (18, 24), (9, 12), 32),
    ("s", (18, 24), (3, 9), 48),
    ("sw", (18, 24), (0, 3), 32),
    ("w", (6, 18), (0, 3), 48),
    ("c", (6, 18), (3, 9), 80),
)
AT = {}
NG = 0
for _name, _r, _c, _kept in PARTS:
    AT[_name] = (NG, _kept)
    NG += _kept


def _a_slot(r, c):
    return (2 * (r // 12) + c // 6) * WIN + (r % 12) * 6 + c % 6


def _tables():
    to_a = np.zeros((NA, NAT), ml_dtypes.bfloat16)
    a_row = np.zeros((NA, ROWS), ml_dtypes.bfloat16)
    a_col = np.zeros((NA, COLS), ml_dtypes.bfloat16)
    for r in range(ROWS):
        for c in range(COLS):
            slot = _a_slot(r, c)
            to_a[slot, c * TALL + r] = 1
            a_row[slot, r] = 1
            a_col[slot, c] = 1
    a_to_g = np.zeros((NG, NA), ml_dtypes.bfloat16)
    for name, (r0, r1), (c0, c1), _ in PARTS:
        spot = AT[name][0]
        for r in range(r0, r1):
            for c in range(c0, c1):
                a_to_g[spot, _a_slot(r, c)] = 1
                spot += 1
    return to_a, a_row, a_col, a_to_g


TO_A, A_ROW, A_COL, A_TO_G = _tables()
FROM_A = np.ascontiguousarray(TO_A.T)
G_TO_A = np.ascontiguousarray(A_TO_G.T)


def _packing(kept):
    table = np.zeros((128, sum(kept)), ml_dtypes.bfloat16)
    token, start = 0, 0
    for rows in kept:
        count = {32: 18, 48: 36}[rows]
        for i in range(count):
            table[token + i, start + i] = 1
        token, start = token + count, start + rows
    return table


PACK_ROWS = _packing((32, 48, 32))
PACK_COLS = _packing((32, 32, 48, 32, 32))
ROW_TOKENS, ROW_SENT = 72, 80
COL_TOKENS, COL_SENT = 108, 112
OPEN_ROWS = np.ascontiguousarray(PACK_ROWS.T[:, :ROW_SENT])
OPEN_COLS = np.ascontiguousarray(PACK_COLS.T[:, :COL_SENT])


def dot(a, b):
    return jnp.dot(a, b, preferred_element_type=F32)


def dot_nt(a, b):
    return lax.dot_general(a, b, (((1,), (1,)), ((), ())), preferred_element_type=F32)


def dot_tn(a, b):
    return lax.dot_general(a, b, (((0,), (0,)), ((), ())), preferred_element_type=F32)


def head_lanes(rows, h):
    lane = lax.broadcasted_iota(jnp.int32, (rows, QUAD), 1)
    return jnp.where((lane >> 6) == h, 1.0, 0.0).astype(BF)


def head_blocks():
    row = lax.broadcasted_iota(jnp.int32, (QUAD, QUAD), 0)
    lane = lax.broadcasted_iota(jnp.int32, (QUAD, QUAD), 1)
    return jnp.where((row >> 6) == (lane >> 6), 1.0, 0.0).astype(BF)


def stack_heads(x):
    return jnp.concatenate([x * head_lanes(1, h) for h in range(4)], axis=0)


def stack_values(v):
    rows = v.shape[0]
    ones = jnp.concatenate([head_lanes(rows, h) for h in range(4)], axis=0)
    return jnp.concatenate([stack_heads(v), ones], axis=1)


def unstack_heads(x):
    n = x.shape[0] // 4
    lane = lax.broadcasted_iota(jnp.int32, (1, QUAD), 1) >> 6
    total = x[:n]
    for h in range(1, 4):
        total = jnp.where(lane == h, x[h * n : (h + 1) * n], total)
    return total


def head_sums(x, blocks):
    groups = [dot(x[:, i : i + QUAD].astype(BF), blocks) for i in range(0, x.shape[1], QUAD)]
    return groups[0] if len(groups) == 1 else jnp.concatenate(groups, axis=1)


def unit(x, blocks):
    scale = lax.rsqrt(head_sums(x * x, blocks) + EPS)
    return x * scale, scale


def id_mask(id_query, id_keys):
    keys = jnp.concatenate([id_keys] * 4, axis=0)
    row = dot_nt(jnp.full((8, 128), 1.0 / 128, BF), keys)[0:1]
    return id_query.astype(F32)[:, 0:1] == row


def attend(q, k, v, mask):
    scores = dot_nt(q, stack_heads(k))
    e = jnp.where(mask, jnp.exp2(scores), 0.0).astype(BF)
    both = dot(e, stack_values(v))
    return both[:, :QUAD], both[:, QUAD:], e


def to_window_order(x_ref, pad_ref, to_a):
    pad_ref[...] = jnp.zeros_like(pad_ref)
    pad_ref[:, 0:ROWS, :] = x_ref[0]
    natural = pad_ref[...].reshape(NAT, x_ref.shape[3])
    return dot(to_a, natural).astype(BF)


def window_ids(reg, a_row, a_col):
    table = (reg + 1).astype(F32).astype(BF)
    picked = (dot(a_col, table) * a_row.astype(F32)).astype(BF)
    return dot(picked, jnp.ones((ROWS, 128), BF)).astype(BF)


def by_level(reg_ref):
    level = lax.axis_index("grp")
    low, high = reg_ref[:, 0, :], reg_ref[:, 1, :]
    own = jnp.where(level == 0, low, high)
    return own, low + high - own


def residual(x, att, w):
    y = dot(att, w)
    r = lax.rsqrt(jnp.mean(y * y, axis=1, keepdims=True) + EPS)
    n = y * r
    return (x.astype(F32) + n).astype(BF), n, r


SAVE = 9 * QUAD + 384


def student_layer(x, w_qkv, w_out, ids, save_ref):
    blocks = head_blocks()
    qkv = dot(x, w_qkv)
    q, sq = unit(qkv[:, :QUAD], blocks)
    k, sk = unit(qkv[:, QUAD : 2 * QUAD], blocks)
    q = (q * SCALE).astype(BF)
    k = k.astype(BF)
    v = qkv[:, 2 * QUAD :].astype(BF)
    atts = []
    for w in range(4):
        rows = slice(w * WIN, (w + 1) * WIN)
        mask = id_mask(ids[rows], ids[rows])
        num, den, e = attend(q[rows], k[rows], v[rows], mask)
        z = 1.0 / den
        att = num * z
        save_ref[rows, 4 * QUAD : 5 * QUAD] = z.astype(BF)
        save_ref[rows, 9 * QUAD : 9 * QUAD + 4 * WIN] = e
        atts.append(att.astype(BF))
    att = jnp.concatenate(atts, axis=0)
    h, n, r = residual(x, att, w_out)
    for i, part in ((0, q), (1, k), (2, v), (3, att), (5, sq), (6, sk), (7, n)):
        save_ref[:, i * QUAD : (i + 1) * QUAD] = part.astype(BF)
    save_ref[:, 8 * QUAD : 9 * QUAD] = jnp.broadcast_to(r, (NA, QUAD)).astype(BF)
    return h


def fetch(*pairs):
    copies = [pltpu.make_async_copy(*pair) for pair in pairs]
    for copy in copies:
        copy.start()
    return copies


def student_back(g, save_ref, w_qkv, w_out):
    blocks = head_blocks()
    part = lambda i: save_ref[:, i * QUAD : (i + 1) * QUAD]
    n, r = part(7).astype(F32), part(8).astype(F32)
    dy = r * (g - n * jnp.mean(g * n, axis=1, keepdims=True))
    datt = dot_nt(dy.astype(BF), w_out) * part(4).astype(F32)
    drop = (datt * part(3).astype(F32)).astype(BF) * jnp.asarray(-1.0, BF)
    datt = datt.astype(BF)
    q, k, v = part(0), part(1), part(2)
    dqs, dks, dvs = [], [], []
    for w in range(4):
        rows = slice(w * WIN, (w + 1) * WIN)
        e = save_ref[rows, 9 * QUAD : 9 * QUAD + 4 * WIN]
        both = jnp.concatenate([datt[rows], drop[rows]], axis=1)
        ds = (e.astype(F32) * dot_nt(both, stack_values(v[rows]))).astype(BF)
        dqs.append(dot(ds, stack_heads(k[rows])))
        dks.append(unstack_heads(dot_tn(ds, q[rows])))
        dvs.append(unstack_heads(dot_tn(e, datt[rows])))
    dq = 10.0 * jnp.concatenate(dqs, axis=0)
    dk = (1.0 / LOG2E) * jnp.concatenate(dks, axis=0)
    dv = jnp.concatenate(dvs, axis=0)
    q_unit = q.astype(F32) * (1.0 / SCALE)
    k_unit = k.astype(F32)
    dq = part(5).astype(F32) * (dq - q_unit * head_sums(q_unit * dq, blocks))
    dk = part(6).astype(F32) * (dk - k_unit * head_sums(k_unit * dk, blocks))
    dqkv = jnp.concatenate([dq.astype(BF), dk.astype(BF), dv.astype(BF)], axis=1)
    return g + dot_nt(dqkv, w_qkv)


def teacher_own(
    x_hbm, reg_hbm, to_a_hbm, a_row_hbm, a_col_hbm, t_qkv,
    x_out, id_ref, far_id_ref, q_ref, k_ref, v_ref,
    pad_ref, x_ref, reg_ref, to_a, a_row, a_col, wqkv, sems,
):
    copies = fetch(
        (x_hbm, x_ref, sems.at[0]),
        (to_a_hbm, to_a, sems.at[2]),
        (reg_hbm, reg_ref, sems.at[1]),
        (a_row_hbm, a_row, sems.at[3]),
        (a_col_hbm, a_col, sems.at[4]),
        (t_qkv.at[0], wqkv, sems.at[5]),
    )
    width = x_ref.shape[3]
    blocks = head_blocks()
    copies[0].wait()
    copies[1].wait()
    x = to_window_order(x_ref, pad_ref, to_a[...])
    x_out[...] = x
    for copy in copies[2:5]:
        copy.wait()
    reg, reg_far = by_level(reg_ref)
    id_ref[...] = window_ids(reg, a_row[...], a_col[...])
    far_id_ref[...] = window_ids(reg_far, a_row[...], a_col[...])
    copies[5].wait()
    q_ref[...] = (unit(dot(x, wqkv[:, :width]), blocks)[0] * SCALE).astype(BF)
    k_ref[...] = unit(dot(x, wqkv[:, width : 2 * width]), blocks)[0].astype(BF)
    v_ref[...] = dot(x, wqkv[:, 2 * width :]).astype(BF)


def teacher_first(
    far_ref, x_ref, id_ref, far_id_ref, q_ref, k_ref, v_ref, to_a, a_to_g, pack, t_qkv, t_out,
    h_ref, g_ref, north_ref, south_ref, pad_ref, wout, sems,
):
    copies = fetch((t_out.at[0], wout, sems.at[0]))
    width = x_ref.shape[1]
    blocks = head_blocks()
    far = to_window_order(far_ref, pad_ref, to_a[...])
    k_far = unit(dot(far, t_qkv[0, :, width : 2 * width]), blocks)[0].astype(BF)
    v_far = dot(far, t_qkv[0, :, 2 * width :]).astype(BF)
    atts = []
    for w in range(4):
        rows = slice(w * WIN, (w + 1) * WIN)
        id_keys = jnp.concatenate([id_ref[rows], far_id_ref[rows]], axis=0)
        keys = [
            jnp.concatenate([near[rows], away[rows]], axis=0)
            for near, away in ((k_ref, k_far), (v_ref, v_far))
        ]
        atts.append(window_attention(q_ref[rows], keys, (id_ref[rows], id_keys)))
    copies[0].wait()
    h = residual(x_ref[...], jnp.concatenate(atts, axis=0), wout[...])[0]
    h_ref[...] = h
    spread = dot(a_to_g[...], jnp.concatenate([h, id_ref[...]], axis=1)).astype(BF)
    g_ref[...] = spread
    for ref, names in ((north_ref, TO_NORTH), (south_ref, TO_SOUTH)):
        rows = jnp.concatenate([part(spread, n) for n in names], axis=0)
        ref[...] = packed(rows, pack[...], ROW_TOKENS, ROW_SENT)


def packed(rows, table, tokens, sent):
    width = rows.shape[1] - 128
    values = dot(table[:sent], rows[:, :width])
    ids = dot(table, rows[:, width:]).astype(BF)
    row = dot_nt(jnp.full((8, 128), 1.0 / 128, BF), ids)[0:1]
    row = jnp.concatenate([row, jnp.zeros((1, width - 128), F32)], axis=1)
    at = lax.broadcasted_iota(jnp.int32, (sent, 1), 0)
    return jnp.where(at == tokens, row, values).astype(BF)


def opened(sent, table, tokens):
    values = dot(table, sent).astype(BF)
    row = sent.astype(F32)[tokens : tokens + 1, : table.shape[1]]
    ids = dot((table.astype(F32) * row).astype(BF), jnp.ones((table.shape[1], 128), BF))
    return jnp.concatenate([values, ids.astype(BF)], axis=1)


def part(x, name):
    start, kept = AT[name]
    return x[start : start + kept]


TO_NORTH = ("nw", "n", "ne")
TO_SOUTH = ("sw", "s", "se")
TO_WEST = (("N", "sw"), ("", "nw"), ("", "w"), ("", "sw"), ("S", "nw"))
TO_EAST = (("N", "se"), ("", "ne"), ("", "e"), ("", "se"), ("S", "ne"))
EXTRA = {
    "nw": (("N", "sw"), ("W", "ne"), ("NW", "se")),
    "n": (("N", "s"),),
    "ne": (("N", "se"), ("E", "nw"), ("NE", "sw")),
    "e": (("E", "w"),),
    "se": (("S", "ne"), ("E", "sw"), ("SE", "nw")),
    "s": (("S", "n"),),
    "sw": (("S", "nw"), ("W", "se"), ("SW", "ne")),
    "w": (("W", "e"),),
    "c": (),
}
LATE = ("nw", "ne", "e", "se", "sw", "w")
ORDER = [name for name, *_ in PARTS]


def _spots(items):
    spots, start = {}, 0
    for side, name in items:
        spots[side, name] = start
        start += AT[name][1]
    return spots


OWN = {("", name): AT[name][0] for name in ORDER}
EDGE = _spots([("N", n) for n in TO_SOUTH] + [("S", n) for n in TO_NORTH])
COME = _spots([(s + "E", n) for s, n in TO_WEST] + [(s + "W", n) for s, n in TO_EAST])
NE_ROWS = 2 * sum(AT[n][1] for n in TO_NORTH)


def gather(sources, items):
    blocks = []
    for item in items:
        for array, spots in sources:
            if item in spots:
                spot = spots[item]
                blocks.append(array[spot : spot + AT[item[1]][1]])
                break
    return blocks[0] if len(blocks) == 1 else jnp.concatenate(blocks, axis=0)


def window_attention(q, keys, ids):
    k, v = keys
    mask = id_mask(*ids)
    quads = []
    for i in range(0, q.shape[1], QUAD):
        lanes = slice(i, i + QUAD)
        num, den, _ = attend(q[:, lanes], k[:, lanes], v[:, lanes], mask)
        quads.append((num / den).astype(BF))
    return jnp.concatenate(quads, axis=1)


def beside_rows(
    x_ref, id_ref, to_a, s_qkv, s_out, proj, g_ref, t_qkv, after_ref,
    g0_ref, save0, save1, q_ref, k_ref, v_ref, att_ref, pad_ref,
):
    width = g_ref.shape[1] - 128
    blocks = head_blocks()
    x = to_window_order(x_ref, pad_ref, to_a[...])
    h = student_layer(x, s_qkv[0], s_out[0], id_ref[...], save0)
    h = student_layer(h, s_qkv[1], s_out[1], id_ref[...], save1)
    predicted = dot(h, proj[...])
    g0_ref[...] = dot_nt(predicted.astype(BF), proj[...])

    rows = g_ref[:, :width]
    q = (unit(dot(rows, t_qkv[1, :, :width]), blocks)[0] * SCALE).astype(BF)
    k = unit(dot(rows, t_qkv[1, :, width : 2 * width]), blocks)[0].astype(BF)
    v = dot(rows, t_qkv[1, :, 2 * width :]).astype(BF)
    q_ref[...] = q
    k_ref[...] = k
    v_ref[...] = v
    ids = part(g_ref, "c")[:, width:]
    att_ref[...] = window_attention(part(q, "c"), [part(k, "c"), part(v, "c")], (ids, ids))


def send_columns(
    g_ref, north_ref, south_ref, open_rows, pack, after_ref, edge_ref, west_ref, east_ref
):
    width = north_ref.shape[1]
    lat = lax.axis_index("lat")
    blocks = []
    inside = (lat > 0, lat < lax.axis_size("lat") - 1)
    for ref, there in zip((north_ref, south_ref), inside):
        rows = opened(ref[...], open_rows[...], ROW_TOKENS)
        ids = rows[:, width:] * jnp.where(there, 1.0, 0.0).astype(BF)
        blocks.append(jnp.concatenate([rows[:, :width], ids], axis=1))
    edge = jnp.concatenate(blocks, axis=0)
    edge_ref[...] = edge
    for ref, items in ((west_ref, TO_WEST), (east_ref, TO_EAST)):
        rows = gather([(g_ref, OWN), (edge, EDGE)], items)
        ref[...] = packed(rows, pack[...], COL_TOKENS, COL_SENT)


def beside_columns(
    g_ref, edge_ref, t_qkv, q_ref, k_ref, v_ref, after_ref, k_out, v_out, n_ref, s_ref
):
    width = g_ref.shape[1] - 128
    blocks = head_blocks()
    rows = edge_ref[:, :width]
    k = unit(dot(rows, t_qkv[1, :, width : 2 * width]), blocks)[0].astype(BF)
    v = dot(rows, t_qkv[1, :, 2 * width :]).astype(BF)
    k_out[...] = k
    v_out[...] = v
    for name, ref in (("n", n_ref), ("s", s_ref)):
        items = (("", name),) + EXTRA[name]
        keys = [gather([(own, OWN), (edge, EDGE)], items) for own, edge in ((k_ref, k), (v_ref, v))]
        ids = [gather([(g_ref, OWN), (edge_ref, EDGE)], some)[:, width:] for some in (items[:1], items)]
        ref[...] = window_attention(part(q_ref, name), keys, ids)


def teacher_second(
    h_ref, g_ref, edge_ref, east_ref, west_ref, q_ref, k_ref, v_ref, k_edge, v_edge,
    c_ref, n_ref, s_ref, open_cols, from_a, g_to_a, t_qkv, t_out, proj, s_qkv, s_out,
    g0_ref, save0, save1, out_ref, grad_ref,
):
    width = h_ref.shape[1]
    blocks = head_blocks()
    came = [opened(ref[...], open_cols[...], COL_TOKENS) for ref in (east_ref, west_ref)]
    came = jnp.concatenate(came, axis=0)
    rows = came[:, :width]
    k = unit(dot(rows, t_qkv[1, :, width : 2 * width]), blocks)[0].astype(BF)
    v = dot(rows, t_qkv[1, :, 2 * width :]).astype(BF)
    atts = {"c": c_ref[...], "n": n_ref[...], "s": s_ref[...]}
    for name in LATE:
        items = (("", name),) + EXTRA[name]
        keys = [
            gather([(own, OWN), (edge, EDGE), (new, COME)], items)
            for own, edge, new in ((k_ref, k_edge, k), (v_ref, v_edge, v))
        ]
        ids = [
            gather([(g_ref, OWN), (edge_ref, EDGE), (came, COME)], some)[:, width:]
            for some in (items[:1], items)
        ]
        atts[name] = window_attention(part(q_ref, name), keys, ids)
    att = jnp.concatenate([atts[name] for name in ORDER], axis=0)
    att = dot(g_to_a[...], att).astype(BF)
    teacher = residual(h_ref[...], att, t_out[1])[0]
    natural = dot(from_a[...], teacher).astype(BF)
    out_ref[0] = natural.reshape(COLS, TALL, width)[:, :ROWS, :]

    g = g0_ref[...] - dot_nt(teacher, proj[...])
    g = student_back(g, save1, s_qkv[1], s_out[1])
    g = student_back(g, save0, s_qkv[0], s_out[0])
    high = g.astype(BF)
    low = (g - high.astype(F32)).astype(BF)
    natural = dot(from_a[...], high) + dot(from_a[...], low)
    grad_ref[0] = natural.reshape(COLS, TALL, g.shape[1])[:, :ROWS, :]


VMEM = pl.BlockSpec(memory_space=pltpu.VMEM)
ANY = pl.BlockSpec(memory_space=pl.ANY)
HBM = pl.BlockSpec(memory_space=pltpu.HBM)


def call(kernel, name, outs, specs, args, scratch=(), flops=0):
    shapes = [jax.ShapeDtypeStruct(s, d) for s, d in outs]
    touched = sum(a.size * a.dtype.itemsize for a in args)
    return pl.pallas_call(
        kernel,
        name=name,
        out_shape=shapes,
        in_specs=specs,
        out_specs=[VMEM] * len(outs),
        scratch_shapes=list(scratch),
        compiler_params=pltpu.CompilerParams(vmem_limit_bytes=28 << 20),
        cost_estimate=pl.CostEstimate(flops=flops, bytes_accessed=touched, transcendentals=0),
    )(*args)


def buffers(*arrays):
    return [pltpu.VMEM(a.shape, a.dtype) for a in arrays] + [
        pltpu.SemaphoreType.DMA((len(arrays),))
    ]


def shards(teacher_in, student_in, regions, t_qkv, t_out, s_qkv, s_out, s_proj):
    width, narrow = teacher_in.shape[3], student_in.shape[3]
    lat_size, lon_size = lax.axis_size("lat"), lax.axis_size("lon")
    wide = width + 128
    teacher_in = teacher_in.transpose(0, 2, 1, 3)
    student_in = student_in.transpose(0, 2, 1, 3)
    regions = regions.transpose(2, 0, 1)
    far = lax.ppermute(teacher_in, "grp", [(0, 1), (1, 0)])

    pinned = [
        pltpu.with_memory_space_constraint(jnp.asarray(a), pltpu.HBM)
        for a in (teacher_in, regions, TO_A, A_ROW, A_COL, t_qkv)
    ]
    x, ids, far_ids, q, k, v = call(
        teacher_own, "teacher_own",
        [((NA, width), BF), ((NA, 128), BF), ((NA, 128), BF)] + [((NA, width), BF)] * 3,
        [HBM] * 6, pinned,
        [pltpu.VMEM((COLS, TALL, width), BF)]
        + buffers(teacher_in, regions, TO_A, A_ROW, A_COL, t_qkv[0]),
        10**9,
    )
    hidden, spread, to_north, to_south = call(
        teacher_first, "teacher_first",
        [((NA, width), BF), ((NG, wide), BF)] + [((ROW_SENT, width), BF)] * 2,
        [VMEM] * 11 + [HBM],
        [far, x, ids, far_ids, q, k, v, TO_A, A_TO_G, PACK_ROWS, t_qkv]
        + [pltpu.with_memory_space_constraint(t_out, pltpu.HBM)],
        [pltpu.VMEM((COLS, TALL, width), BF)] + buffers(t_out[0]), 3 * 10**9,
    )
    north = lax.ppermute(to_south, "lat", [(i, (i + 1) % lat_size) for i in range(lat_size)])
    south = lax.ppermute(to_north, "lat", [((i + 1) % lat_size, i) for i in range(lat_size)])

    g0, save0, save1, q, k, v, c_att = call(
        beside_rows, "beside_rows",
        [((NA, narrow), F32), ((NA, SAVE), BF), ((NA, SAVE), BF)]
        + [((NG, width), BF)] * 3 + [((AT["c"][1], width), BF)],
        [VMEM] * 8 + [ANY],
        [student_in, ids, TO_A, s_qkv, s_out, s_proj, spread, t_qkv, to_north],
        [pltpu.VMEM((COLS, TALL, narrow), BF)], 5 * 10**9,
    )
    edge, to_west, to_east = call(
        send_columns, "send_columns",
        [((NE_ROWS, wide), BF)] + [((COL_SENT, width), BF)] * 2,
        [VMEM] * 5 + [ANY],
        [spread, north, south, OPEN_ROWS, PACK_COLS, g0], (), 10**7,
    )
    east = lax.ppermute(to_west, "lon", [((j + 1) % lon_size, j) for j in range(lon_size)])
    west = lax.ppermute(to_east, "lon", [(j, (j + 1) % lon_size) for j in range(lon_size)])

    k_edge, v_edge, n_att, s_att = call(
        beside_columns, "beside_columns",
        [((NE_ROWS, width), BF)] * 2 + [((AT["n"][1], width), BF)] * 2,
        [VMEM] * 6 + [ANY],
        [spread, edge, t_qkv, q, k, v, to_west], (), 2 * 10**9,
    )
    args = [hidden, spread, edge, east, west, q, k, v, k_edge, v_edge, c_att, n_att, s_att]
    args += [OPEN_COLS, FROM_A, G_TO_A, t_qkv, t_out, s_proj, s_qkv, s_out, g0, save0, save1]
    out, grad = call(
        teacher_second, "teacher_second",
        [(teacher_in.shape, BF), (student_in.shape, F32)],
        [VMEM] * len(args), args, (), 6 * 10**9,
    )
    return out.transpose(0, 2, 1, 3), grad.transpose(0, 2, 1, 3)


def solution(mesh):
    tiles = P("grp", "lat", "lon", None)
    return jax.shard_map(
        shards,
        mesh=mesh,
        in_specs=(tiles, tiles, P(None, "lat", "lon"), P(), P(), P(), P(), P()),
        out_specs=(tiles, tiles),
        check_vma=False,
    )
```

```python
import functools

import jax
import jax.numpy as jnp
import ml_dtypes
import numpy as np
from jax import lax
from jax.experimental import pallas as pl
from jax.experimental.pallas import tpu as pltpu
from jax.sharding import PartitionSpec as P

HEADS_T = 8
HEADS_S = 4
EPS = 1e-06
LOG2E = 1.4426950408889634
SCALE = 10.0 * LOG2E
BF = jnp.bfloat16
F32 = jnp.float32

ROWS, COLS = 24, 12
WIN = 80
NA = 4 * WIN
TALL = 32
NAT = COLS * TALL
QUAD = 256

PARTS = (
    ("nw", (0, 6), (0, 3), 32),
    ("n", (0, 6), (3, 9), 48),
    ("ne", (0, 6), (9, 12), 32),
    ("e", (6, 18), (9, 12), 48),
    ("se", (18, 24), (9, 12), 32),
    ("s", (18, 24), (3, 9), 48),
    ("sw", (18, 24), (0, 3), 32),
    ("w", (6, 18), (0, 3), 48),
    ("c", (6, 18), (3, 9), 80),
)
AT = {}
NG = 0
for _name, _r, _c, _kept in PARTS:
    AT[_name] = (NG, _kept)
    NG += _kept


def _a_slot(r, c):
    return (2 * (r // 12) + c // 6) * WIN + (r % 12) * 6 + c % 6


def _tables():
    to_a = np.zeros((NA, NAT), ml_dtypes.bfloat16)
    a_row = np.zeros((NA, ROWS), ml_dtypes.bfloat16)
    a_col = np.zeros((NA, COLS), ml_dtypes.bfloat16)
    for r in range(ROWS):
        for c in range(COLS):
            slot = _a_slot(r, c)
            to_a[slot, c * TALL + r] = 1
            a_row[slot, r] = 1
            a_col[slot, c] = 1
    a_to_g = np.zeros((NG, NA), ml_dtypes.bfloat16)
    for name, (r0, r1), (c0, c1), _ in PARTS:
        spot = AT[name][0]
        for r in range(r0, r1):
            for c in range(c0, c1):
                a_to_g[spot, _a_slot(r, c)] = 1
                spot += 1
    return to_a, a_row, a_col, a_to_g


TO_A, A_ROW, A_COL, A_TO_G = _tables()
FROM_A = np.ascontiguousarray(TO_A.T)
G_TO_A = np.ascontiguousarray(A_TO_G.T)


def _packing(kept):
    table = np.zeros((128, sum(kept)), ml_dtypes.bfloat16)
    token, start = 0, 0
    for rows in kept:
        count = {32: 18, 48: 36}[rows]
        for i in range(count):
            table[token + i, start + i] = 1
        token, start = token + count, start + rows
    return table


PACK_ROWS = _packing((32, 48, 32))
PACK_COLS = _packing((32, 32, 48, 32, 32))
ROW_TOKENS, ROW_SENT = 72, 80
COL_TOKENS, COL_SENT = 108, 112
OPEN_ROWS = np.ascontiguousarray(PACK_ROWS.T[:, :ROW_SENT])
OPEN_COLS = np.ascontiguousarray(PACK_COLS.T[:, :COL_SENT])


def dot(a, b):
    return jnp.dot(a, b, preferred_element_type=F32)


def dot_nt(a, b):
    return lax.dot_general(a, b, (((1,), (1,)), ((), ())), preferred_element_type=F32)


def dot_tn(a, b):
    return lax.dot_general(a, b, (((0,), (0,)), ((), ())), preferred_element_type=F32)


def head_lanes(rows, h):
    lane = lax.broadcasted_iota(jnp.int32, (rows, QUAD), 1)
    return jnp.where((lane >> 6) == h, 1.0, 0.0).astype(BF)


def head_blocks():
    row = lax.broadcasted_iota(jnp.int32, (QUAD, QUAD), 0)
    lane = lax.broadcasted_iota(jnp.int32, (QUAD, QUAD), 1)
    return jnp.where((row >> 6) == (lane >> 6), 1.0, 0.0).astype(BF)


def stack_heads(x):
    return jnp.concatenate([x * head_lanes(1, h) for h in range(4)], axis=0)


def stack_values(v):
    rows = v.shape[0]
    ones = jnp.concatenate([head_lanes(rows, h) for h in range(4)], axis=0)
    return jnp.concatenate([stack_heads(v), ones], axis=1)


def unstack_heads(x):
    n = x.shape[0] // 4
    lane = lax.broadcasted_iota(jnp.int32, (1, QUAD), 1) >> 6
    total = x[:n]
    for h in range(1, 4):
        total = jnp.where(lane == h, x[h * n : (h + 1) * n], total)
    return total


def head_sums(x, blocks):
    groups = [dot(x[:, i : i + QUAD].astype(BF), blocks) for i in range(0, x.shape[1], QUAD)]
    return groups[0] if len(groups) == 1 else jnp.concatenate(groups, axis=1)


def unit(x, blocks):
    scale = lax.rsqrt(head_sums(x * x, blocks) + EPS)
    return x * scale, scale


def id_mask(id_query, id_keys):
    keys = jnp.concatenate([id_keys] * 4, axis=0)
    row = dot_nt(jnp.full((8, 128), 1.0 / 128, BF), keys)[0:1]
    return id_query.astype(F32)[:, 0:1] == row


def attend(q, k, v, mask):
    scores = dot_nt(q, stack_heads(k))
    e = jnp.where(mask, jnp.exp2(scores), 0.0).astype(BF)
    both = dot(e, stack_values(v))
    return both[:, :QUAD], both[:, QUAD:], e


def to_window_order(x_ref, pad_ref, to_a):
    pad_ref[...] = jnp.zeros_like(pad_ref)
    pad_ref[:, 0:ROWS, :] = x_ref[0]
    natural = pad_ref[...].reshape(NAT, x_ref.shape[3])
    return dot(to_a, natural).astype(BF)


def window_ids(reg, a_row, a_col):
    table = (reg + 1).astype(F32).astype(BF)
    picked = (dot(a_col, table) * a_row.astype(F32)).astype(BF)
    return dot(picked, jnp.ones((ROWS, 128), BF)).astype(BF)


def by_level(reg_ref):
    level = lax.axis_index("grp")
    low, high = reg_ref[:, 0, :], reg_ref[:, 1, :]
    own = jnp.where(level == 0, low, high)
    return own, low + high - own


def residual(x, att, w):
    y = dot(att, w)
    r = lax.rsqrt(jnp.mean(y * y, axis=1, keepdims=True) + EPS)
    n = y * r
    return (x.astype(F32) + n).astype(BF), n, r


SAVE = 9 * QUAD + 384


def student_layer(x, w_qkv, w_out, ids, save_ref):
    blocks = head_blocks()
    qkv = dot(x, w_qkv)
    q, sq = unit(qkv[:, :QUAD], blocks)
    k, sk = unit(qkv[:, QUAD : 2 * QUAD], blocks)
    q = (q * SCALE).astype(BF)
    k = k.astype(BF)
    v = qkv[:, 2 * QUAD :].astype(BF)
    atts = []
    for w in range(4):
        rows = slice(w * WIN, (w + 1) * WIN)
        mask = id_mask(ids[rows], ids[rows])
        num, den, e = attend(q[rows], k[rows], v[rows], mask)
        z = 1.0 / den
        att = num * z
        save_ref[rows, 4 * QUAD : 5 * QUAD] = z.astype(BF)
        save_ref[rows, 9 * QUAD : 9 * QUAD + 4 * WIN] = e
        atts.append(att.astype(BF))
    att = jnp.concatenate(atts, axis=0)
    h, n, r = residual(x, att, w_out)
    for i, part in ((0, q), (1, k), (2, v), (3, att), (5, sq), (6, sk), (7, n)):
        save_ref[:, i * QUAD : (i + 1) * QUAD] = part.astype(BF)
    save_ref[:, 8 * QUAD : 9 * QUAD] = jnp.broadcast_to(r, (NA, QUAD)).astype(BF)
    return h


def fetch(*pairs):
    copies = [pltpu.make_async_copy(*pair) for pair in pairs]
    for copy in copies:
        copy.start()
    return copies


def student_back(g, save_ref, w_qkv, w_out):
    blocks = head_blocks()
    part = lambda i: save_ref[:, i * QUAD : (i + 1) * QUAD]
    n, r = part(7).astype(F32), part(8).astype(F32)
    dy = r * (g - n * jnp.mean(g * n, axis=1, keepdims=True))
    datt = dot_nt(dy.astype(BF), w_out) * part(4).astype(F32)
    drop = (datt * part(3).astype(F32)).astype(BF) * jnp.asarray(-1.0, BF)
    datt = datt.astype(BF)
    q, k, v = part(0), part(1), part(2)
    dqs, dks, dvs = [], [], []
    for w in range(4):
        rows = slice(w * WIN, (w + 1) * WIN)
        e = save_ref[rows, 9 * QUAD : 9 * QUAD + 4 * WIN]
        both = jnp.concatenate([datt[rows], drop[rows]], axis=1)
        ds = (e.astype(F32) * dot_nt(both, stack_values(v[rows]))).astype(BF)
        dqs.append(dot(ds, stack_heads(k[rows])))
        dks.append(unstack_heads(dot_tn(ds, q[rows])))
        dvs.append(unstack_heads(dot_tn(e, datt[rows])))
    dq = 10.0 * jnp.concatenate(dqs, axis=0)
    dk = (1.0 / LOG2E) * jnp.concatenate(dks, axis=0)
    dv = jnp.concatenate(dvs, axis=0)
    q_unit = q.astype(F32) * (1.0 / SCALE)
    k_unit = k.astype(F32)
    dq = part(5).astype(F32) * (dq - q_unit * head_sums(q_unit * dq, blocks))
    dk = part(6).astype(F32) * (dk - k_unit * head_sums(k_unit * dk, blocks))
    dqkv = jnp.concatenate([dq.astype(BF), dk.astype(BF), dv.astype(BF)], axis=1)
    return g + dot_nt(dqkv, w_qkv)


def teacher_own(
    x_hbm, reg_hbm, to_a_hbm, a_row_hbm, a_col_hbm, t_qkv,
    x_out, id_ref, far_id_ref, q_ref, k_ref, v_ref,
    pad_ref, x_ref, reg_ref, to_a, a_row, a_col, wqkv, sems,
):
    copies = fetch(
        (x_hbm, x_ref, sems.at[0]),
        (to_a_hbm, to_a, sems.at[2]),
        (reg_hbm, reg_ref, sems.at[1]),
        (a_row_hbm, a_row, sems.at[3]),
        (a_col_hbm, a_col, sems.at[4]),
        (t_qkv.at[0], wqkv, sems.at[5]),
    )
    width = x_ref.shape[3]
    blocks = head_blocks()
    copies[0].wait()
    copies[1].wait()
    x = to_window_order(x_ref, pad_ref, to_a[...])
    x_out[...] = x
    for copy in copies[2:5]:
        copy.wait()
    reg, reg_far = by_level(reg_ref)
    id_ref[...] = window_ids(reg, a_row[...], a_col[...])
    far_id_ref[...] = window_ids(reg_far, a_row[...], a_col[...])
    copies[5].wait()
    q_ref[...] = (unit(dot(x, wqkv[:, :width]), blocks)[0] * SCALE).astype(BF)
    k_ref[...] = unit(dot(x, wqkv[:, width : 2 * width]), blocks)[0].astype(BF)
    v_ref[...] = dot(x, wqkv[:, 2 * width :]).astype(BF)


def teacher_first(
    far_ref, x_ref, id_ref, far_id_ref, q_ref, k_ref, v_ref, to_a, a_to_g, pack, t_qkv, t_out,
    h_ref, g_ref, first_ref, second_ref, pad_ref, wout, sems,
):
    copies = fetch((t_out.at[0], wout, sems.at[0]))
    width = x_ref.shape[1]
    blocks = head_blocks()
    far = to_window_order(far_ref, pad_ref, to_a[...])
    k_far = unit(dot(far, t_qkv[0, :, width : 2 * width]), blocks)[0].astype(BF)
    v_far = dot(far, t_qkv[0, :, 2 * width :]).astype(BF)
    atts = []
    for w in range(4):
        rows = slice(w * WIN, (w + 1) * WIN)
        id_keys = jnp.concatenate([id_ref[rows], far_id_ref[rows]], axis=0)
        keys = [
            jnp.concatenate([near[rows], away[rows]], axis=0)
            for near, away in ((k_ref, k_far), (v_ref, v_far))
        ]
        atts.append(window_attention(q_ref[rows], keys, (id_ref[rows], id_keys)))
    copies[0].wait()
    h = residual(x_ref[...], jnp.concatenate(atts, axis=0), wout[...])[0]
    h_ref[...] = h
    spread = dot(a_to_g[...], jnp.concatenate([h, id_ref[...]], axis=1)).astype(BF)
    g_ref[...] = spread
    north, south = [
        packed(
            jnp.concatenate([part(spread, n) for n in names], axis=0),
            pack[...], ROW_TOKENS, ROW_SENT,
        )
        for names in (TO_NORTH, TO_SOUTH)
    ]
    first_ref[...], second_ref[...] = swapped("lat", north, south)


def swapped(axis, low, high):
    even = lax.rem(lax.axis_index(axis), 2) == 0
    low, high = low.astype(F32), high.astype(F32)
    return jnp.where(even, low, high).astype(BF), jnp.where(even, high, low).astype(BF)


def packed(rows, table, tokens, sent):
    width = rows.shape[1] - 128
    values = dot(table[:sent], rows[:, :width])
    ids = dot(table, rows[:, width:]).astype(BF)
    row = dot_nt(jnp.full((8, 128), 1.0 / 128, BF), ids)[0:1]
    row = jnp.concatenate([row, jnp.zeros((1, width - 128), F32)], axis=1)
    at = lax.broadcasted_iota(jnp.int32, (sent, 1), 0)
    return jnp.where(at == tokens, row, values).astype(BF)


def opened(sent, table, tokens):
    values = dot(table, sent).astype(BF)
    row = sent.astype(F32)[tokens : tokens + 1, : table.shape[1]]
    ids = dot((table.astype(F32) * row).astype(BF), jnp.ones((table.shape[1], 128), BF))
    return jnp.concatenate([values, ids.astype(BF)], axis=1)


def part(x, name):
    start, kept = AT[name]
    return x[start : start + kept]


TO_NORTH = ("nw", "n", "ne")
TO_SOUTH = ("sw", "s", "se")
TO_WEST = (("N", "sw"), ("", "nw"), ("", "w"), ("", "sw"), ("S", "nw"))
TO_EAST = (("N", "se"), ("", "ne"), ("", "e"), ("", "se"), ("S", "ne"))
EXTRA = {
    "nw": (("N", "sw"), ("W", "ne"), ("NW", "se")),
    "n": (("N", "s"),),
    "ne": (("N", "se"), ("E", "nw"), ("NE", "sw")),
    "e": (("E", "w"),),
    "se": (("S", "ne"), ("E", "sw"), ("SE", "nw")),
    "s": (("S", "n"),),
    "sw": (("S", "nw"), ("W", "se"), ("SW", "ne")),
    "w": (("W", "e"),),
    "c": (),
}
LATE = ("nw", "ne", "e", "se", "sw", "w")
ORDER = [name for name, *_ in PARTS]


def _spots(items):
    spots, start = {}, 0
    for side, name in items:
        spots[side, name] = start
        start += AT[name][1]
    return spots


OWN = {("", name): AT[name][0] for name in ORDER}
EDGE = _spots([("N", n) for n in TO_SOUTH] + [("S", n) for n in TO_NORTH])
COME = _spots([(s + "E", n) for s, n in TO_WEST] + [(s + "W", n) for s, n in TO_EAST])
NE_ROWS = 2 * sum(AT[n][1] for n in TO_NORTH)


def gather(sources, items):
    blocks = []
    for item in items:
        for array, spots in sources:
            if item in spots:
                spot = spots[item]
                blocks.append(array[spot : spot + AT[item[1]][1]])
                break
    return blocks[0] if len(blocks) == 1 else jnp.concatenate(blocks, axis=0)


def window_attention(q, keys, ids):
    k, v = keys
    mask = id_mask(*ids)
    quads = []
    for i in range(0, q.shape[1], QUAD):
        lanes = slice(i, i + QUAD)
        num, den, _ = attend(q[:, lanes], k[:, lanes], v[:, lanes], mask)
        quads.append((num / den).astype(BF))
    return jnp.concatenate(quads, axis=1)


def beside_rows(
    x_ref, id_ref, to_a, s_qkv, s_out, proj, g_ref, t_qkv, after_ref,
    g0_ref, save0, save1, q_ref, k_ref, v_ref, att_ref, pad_ref,
):
    width = g_ref.shape[1] - 128
    blocks = head_blocks()
    x = to_window_order(x_ref, pad_ref, to_a[...])
    h = student_layer(x, s_qkv[0], s_out[0], id_ref[...], save0)
    h = student_layer(h, s_qkv[1], s_out[1], id_ref[...], save1)
    predicted = dot(h, proj[...])
    g0_ref[...] = dot_nt(predicted.astype(BF), proj[...])

    rows = g_ref[:, :width]
    q = (unit(dot(rows, t_qkv[1, :, :width]), blocks)[0] * SCALE).astype(BF)
    k = unit(dot(rows, t_qkv[1, :, width : 2 * width]), blocks)[0].astype(BF)
    v = dot(rows, t_qkv[1, :, 2 * width :]).astype(BF)
    q_ref[...] = q
    k_ref[...] = k
    v_ref[...] = v
    ids = part(g_ref, "c")[:, width:]
    att_ref[...] = window_attention(part(q, "c"), [part(k, "c"), part(v, "c")], (ids, ids))


def send_columns(
    g_ref, first_ref, second_ref, open_rows, pack, after_ref, edge_ref, out_first, out_second
):
    width = first_ref.shape[1]
    lat = lax.axis_index("lat")
    blocks = []
    inside = (lat > 0, lat < lax.axis_size("lat") - 1)
    for sent, there in zip(swapped("lat", first_ref[...], second_ref[...]), inside):
        rows = opened(sent, open_rows[...], ROW_TOKENS)
        ids = rows[:, width:] * jnp.where(there, 1.0, 0.0).astype(BF)
        blocks.append(jnp.concatenate([rows[:, :width], ids], axis=1))
    edge = jnp.concatenate(blocks, axis=0)
    edge_ref[...] = edge
    west, east = [
        packed(
            gather([(g_ref, OWN), (edge, EDGE)], items), pack[...], COL_TOKENS, COL_SENT
        )
        for items in (TO_WEST, TO_EAST)
    ]
    out_first[...], out_second[...] = swapped("lon", west, east)


def beside_columns(
    g_ref, edge_ref, t_qkv, q_ref, k_ref, v_ref, k_out, v_out, n_ref, s_ref
):
    width = g_ref.shape[1] - 128
    blocks = head_blocks()
    rows = edge_ref[:, :width]
    k = unit(dot(rows, t_qkv[1, :, width : 2 * width]), blocks)[0].astype(BF)
    v = dot(rows, t_qkv[1, :, 2 * width :]).astype(BF)
    k_out[...] = k
    v_out[...] = v
    for name, ref in (("n", n_ref), ("s", s_ref)):
        items = (("", name),) + EXTRA[name]
        keys = [gather([(own, OWN), (edge, EDGE)], items) for own, edge in ((k_ref, k), (v_ref, v))]
        ids = [gather([(g_ref, OWN), (edge_ref, EDGE)], some)[:, width:] for some in (items[:1], items)]
        ref[...] = window_attention(part(q_ref, name), keys, ids)


def teacher_second(
    h_ref, g_ref, edge_ref, first_ref, second_ref, q_ref, k_ref, v_ref, k_edge, v_edge,
    c_ref, n_ref, s_ref, open_cols, from_a, g_to_a, t_qkv, t_out, proj, s_qkv, s_out,
    g0_ref, save0, save1, out_ref, grad_ref,
):
    width = h_ref.shape[1]
    blocks = head_blocks()
    west, east = swapped("lon", first_ref[...], second_ref[...])
    came = [opened(sent, open_cols[...], COL_TOKENS) for sent in (east, west)]
    came = jnp.concatenate(came, axis=0)
    rows = came[:, :width]
    k = unit(dot(rows, t_qkv[1, :, width : 2 * width]), blocks)[0].astype(BF)
    v = dot(rows, t_qkv[1, :, 2 * width :]).astype(BF)
    atts = {"c": c_ref[...], "n": n_ref[...], "s": s_ref[...]}
    for name in LATE:
        items = (("", name),) + EXTRA[name]
        keys = [
            gather([(own, OWN), (edge, EDGE), (new, COME)], items)
            for own, edge, new in ((k_ref, k_edge, k), (v_ref, v_edge, v))
        ]
        ids = [
            gather([(g_ref, OWN), (edge_ref, EDGE), (came, COME)], some)[:, width:]
            for some in (items[:1], items)
        ]
        atts[name] = window_attention(part(q_ref, name), keys, ids)
    att = jnp.concatenate([atts[name] for name in ORDER], axis=0)
    att = dot(g_to_a[...], att).astype(BF)
    teacher = residual(h_ref[...], att, t_out[1])[0]
    natural = dot(from_a[...], teacher).astype(BF)
    out_ref[0] = natural.reshape(COLS, TALL, width)[:, :ROWS, :]

    g = g0_ref[...] - dot_nt(teacher, proj[...])
    g = student_back(g, save1, s_qkv[1], s_out[1])
    g = student_back(g, save0, s_qkv[0], s_out[0])
    high = g.astype(BF)
    low = (g - high.astype(F32)).astype(BF)
    natural = dot(from_a[...], high) + dot(from_a[...], low)
    grad_ref[0] = natural.reshape(COLS, TALL, g.shape[1])[:, :ROWS, :]


VMEM = pl.BlockSpec(memory_space=pltpu.VMEM)
ANY = pl.BlockSpec(memory_space=pl.ANY)
HBM = pl.BlockSpec(memory_space=pltpu.HBM)


def call(kernel, name, outs, specs, args, scratch=(), flops=0):
    shapes = [jax.ShapeDtypeStruct(s, d) for s, d in outs]
    touched = sum(a.size * a.dtype.itemsize for a in args)
    return pl.pallas_call(
        kernel,
        name=name,
        out_shape=shapes,
        in_specs=specs,
        out_specs=[VMEM] * len(outs),
        scratch_shapes=list(scratch),
        compiler_params=pltpu.CompilerParams(vmem_limit_bytes=28 << 20),
        cost_estimate=pl.CostEstimate(flops=flops, bytes_accessed=touched, transcendentals=0),
    )(*args)


def buffers(*arrays):
    return [pltpu.VMEM(a.shape, a.dtype) for a in arrays] + [
        pltpu.SemaphoreType.DMA((len(arrays),))
    ]


def swaps(size, start, closed):
    route = {i: i for i in range(size)}
    for i in range(start, size if closed else size - 1, 2):
        j = (i + 1) % size
        route[i], route[j] = j, i
    return sorted(route.items())


def shards(teacher_in, student_in, regions, t_qkv, t_out, s_qkv, s_out, s_proj):
    width, narrow = teacher_in.shape[3], student_in.shape[3]
    lat_size, lon_size = lax.axis_size("lat"), lax.axis_size("lon")
    wide = width + 128
    teacher_in = teacher_in.transpose(0, 2, 1, 3)
    student_in = student_in.transpose(0, 2, 1, 3)
    regions = regions.transpose(2, 0, 1)
    far = lax.ppermute(teacher_in, "grp", [(0, 1), (1, 0)])

    pinned = [
        pltpu.with_memory_space_constraint(jnp.asarray(a), pltpu.HBM)
        for a in (teacher_in, regions, TO_A, A_ROW, A_COL, t_qkv)
    ]
    x, ids, far_ids, q, k, v = call(
        teacher_own, "teacher_own",
        [((NA, width), BF), ((NA, 128), BF), ((NA, 128), BF)] + [((NA, width), BF)] * 3,
        [HBM] * 6, pinned,
        [pltpu.VMEM((COLS, TALL, width), BF)]
        + buffers(teacher_in, regions, TO_A, A_ROW, A_COL, t_qkv[0]),
        10**9,
    )
    hidden, spread, rows_1, rows_2 = call(
        teacher_first, "teacher_first",
        [((NA, width), BF), ((NG, wide), BF)] + [((ROW_SENT, width), BF)] * 2,
        [VMEM] * 11 + [HBM],
        [far, x, ids, far_ids, q, k, v, TO_A, A_TO_G, PACK_ROWS, t_qkv]
        + [pltpu.with_memory_space_constraint(t_out, pltpu.HBM)],
        [pltpu.VMEM((COLS, TALL, width), BF)] + buffers(t_out[0]), 3 * 10**9,
    )
    rows_1 = lax.ppermute(rows_1, "lat", swaps(lat_size, 1, False))
    rows_2 = lax.ppermute(rows_2, "lat", swaps(lat_size, 0, False))

    g0, save0, save1, q, k, v, c_att = call(
        beside_rows, "beside_rows",
        [((NA, narrow), F32), ((NA, SAVE), BF), ((NA, SAVE), BF)]
        + [((NG, width), BF)] * 3 + [((AT["c"][1], width), BF)],
        [VMEM] * 8 + [ANY],
        [student_in, ids, TO_A, s_qkv, s_out, s_proj, spread, t_qkv, hidden],
        [pltpu.VMEM((COLS, TALL, narrow), BF)], 5 * 10**9,
    )
    edge, cols_1, cols_2 = call(
        send_columns, "send_columns",
        [((NE_ROWS, wide), BF)] + [((COL_SENT, width), BF)] * 2,
        [VMEM] * 5 + [ANY],
        [spread, rows_1, rows_2, OPEN_ROWS, PACK_COLS, g0], (), 10**7,
    )
    cols_1 = lax.ppermute(cols_1, "lon", swaps(lon_size, 1, True))
    cols_2 = lax.ppermute(cols_2, "lon", swaps(lon_size, 0, True))

    k_edge, v_edge, n_att, s_att = call(
        beside_columns, "beside_columns",
        [((NE_ROWS, width), BF)] * 2 + [((AT["n"][1], width), BF)] * 2,
        [VMEM] * 6,
        [spread, edge, t_qkv, q, k, v], (), 2 * 10**9,
    )
    args = [hidden, spread, edge, cols_1, cols_2, q, k, v, k_edge, v_edge, c_att, n_att, s_att]
    args += [OPEN_COLS, FROM_A, G_TO_A, t_qkv, t_out, s_proj, s_qkv, s_out, g0, save0, save1]
    out, grad = call(
        teacher_second, "teacher_second",
        [(teacher_in.shape, BF), (student_in.shape, F32)],
        [VMEM] * len(args), args, (), 6 * 10**9,
    )
    return out.transpose(0, 2, 1, 3), grad.transpose(0, 2, 1, 3)


def solution(mesh):
    tiles = P("grp", "lat", "lon", None)
    return jax.shard_map(
        shards,
        mesh=mesh,
        in_specs=(tiles, tiles, P(None, "lat", "lon"), P(), P(), P(), P(), P()),
        out_specs=(tiles, tiles),
        check_vma=False,
    )
```

```python
import functools

import jax
import jax.numpy as jnp
import ml_dtypes
import numpy as np
from jax import lax
from jax.experimental import pallas as pl
from jax.experimental.pallas import tpu as pltpu
from jax.sharding import PartitionSpec as P

HEADS_T = 8
HEADS_S = 4
EPS = 1e-06
LOG2E = 1.4426950408889634
SCALE = 10.0 * LOG2E
BF = jnp.bfloat16
F32 = jnp.float32

ROWS, COLS = 24, 12
WIN = 80
NA = 4 * WIN
TALL = 32
NAT = COLS * TALL
PAIR = 128

PARTS = (
    ("nw", (0, 6), (0, 3), 32),
    ("n", (0, 6), (3, 9), 48),
    ("ne", (0, 6), (9, 12), 32),
    ("e", (6, 18), (9, 12), 48),
    ("se", (18, 24), (9, 12), 32),
    ("s", (18, 24), (3, 9), 48),
    ("sw", (18, 24), (0, 3), 32),
    ("w", (6, 18), (0, 3), 48),
    ("c", (6, 18), (3, 9), 80),
)
AT = {}
NG = 0
for _name, _r, _c, _kept in PARTS:
    AT[_name] = (NG, _kept)
    NG += _kept


def _a_slot(r, c):
    return (2 * (r // 12) + c // 6) * WIN + (r % 12) * 6 + c % 6


def _tables():
    to_a = np.zeros((NA, NAT), ml_dtypes.bfloat16)
    a_row = np.zeros((NA, ROWS), ml_dtypes.bfloat16)
    a_col = np.zeros((NA, COLS), ml_dtypes.bfloat16)
    for r in range(ROWS):
        for c in range(COLS):
            slot = _a_slot(r, c)
            to_a[slot, c * TALL + r] = 1
            a_row[slot, r] = 1
            a_col[slot, c] = 1
    a_to_g = np.zeros((NG, NA), ml_dtypes.bfloat16)
    for name, (r0, r1), (c0, c1), _ in PARTS:
        spot = AT[name][0]
        for r in range(r0, r1):
            for c in range(c0, c1):
                a_to_g[spot, _a_slot(r, c)] = 1
                spot += 1
    return to_a, a_row, a_col, a_to_g


TO_A, A_ROW, A_COL, A_TO_G = _tables()
FROM_A = np.ascontiguousarray(TO_A.T)
G_TO_A = np.ascontiguousarray(A_TO_G.T)


def _packing(kept):
    table = np.zeros((128, sum(kept)), ml_dtypes.bfloat16)
    token, start = 0, 0
    for rows in kept:
        count = {32: 18, 48: 36}[rows]
        for i in range(count):
            table[token + i, start + i] = 1
        token, start = token + count, start + rows
    return table


PACK_ROWS = _packing((32, 48, 32))
PACK_COLS = _packing((32, 32, 48, 32, 32))
ROW_TOKENS, ROW_SENT = 72, 80
COL_TOKENS, COL_SENT = 108, 112
OPEN_ROWS = np.ascontiguousarray(PACK_ROWS.T[:, :ROW_SENT])
OPEN_COLS = np.ascontiguousarray(PACK_COLS.T[:, :COL_SENT])


def dot(a, b):
    return jnp.dot(a, b, preferred_element_type=F32)


def dot_nt(a, b):
    return lax.dot_general(a, b, (((1,), (1,)), ((), ())), preferred_element_type=F32)


def dot_tn(a, b):
    return lax.dot_general(a, b, (((0,), (0,)), ((), ())), preferred_element_type=F32)


def head_lanes(rows, h):
    lane = lax.broadcasted_iota(jnp.int32, (rows, PAIR), 1)
    return jnp.where((lane >> 6) == h, 1.0, 0.0).astype(BF)


def head_blocks():
    row = lax.broadcasted_iota(jnp.int32, (2 * PAIR, 2 * PAIR), 0)
    lane = lax.broadcasted_iota(jnp.int32, (2 * PAIR, 2 * PAIR), 1)
    return jnp.where((row >> 6) == (lane >> 6), 1.0, 0.0).astype(BF)


def stack_heads(x):
    return jnp.concatenate([x * head_lanes(1, h) for h in range(2)], axis=0)


def stack_values(v):
    rows = v.shape[0]
    ones = jnp.concatenate([head_lanes(rows, h) for h in range(2)], axis=0)
    return jnp.concatenate([stack_heads(v), ones], axis=1)


def unstack_heads(x):
    n = x.shape[0] // 2
    lane = lax.broadcasted_iota(jnp.int32, (1, PAIR), 1) >> 6
    return jnp.where(lane == 0, x[:n], x[n:])


def head_sums(x, blocks):
    step = blocks.shape[0]
    groups = [dot(x[:, i : i + step].astype(BF), blocks) for i in range(0, x.shape[1], step)]
    return groups[0] if len(groups) == 1 else jnp.concatenate(groups, axis=1)


def unit(x, blocks):
    scale = lax.rsqrt(head_sums(x * x, blocks) + EPS)
    return x * scale, scale


def id_mask(id_query, id_keys):
    keys = jnp.concatenate([id_keys] * 2, axis=0)
    row = dot_nt(jnp.full((8, 128), 1.0 / 128, BF), keys)[0:1]
    return id_query.astype(F32)[:, 0:1] == row


def attend(q, k, v, mask):
    pairs = [slice(i, i + PAIR) for i in range(0, q.shape[1], PAIR)]
    scores = [dot_nt(q[:, p], stack_heads(k[:, p])) for p in pairs]
    es = [jnp.where(mask, jnp.exp2(s), 0.0).astype(BF) for s in scores]
    both = [dot(e, stack_values(v[:, p])) for e, p in zip(es, pairs)]
    return [b[:, :PAIR] for b in both], [b[:, PAIR:] for b in both], es


def to_window_order(x_ref, pad_ref, to_a):
    pad_ref[...] = jnp.zeros_like(pad_ref)
    pad_ref[:, 0:ROWS, :] = x_ref[0]
    natural = pad_ref[...].reshape(NAT, x_ref.shape[3])
    return dot(to_a, natural).astype(BF)


def window_ids(reg, a_row, a_col):
    table = (reg + 1).astype(F32).astype(BF)
    picked = (dot(a_col, table) * a_row.astype(F32)).astype(BF)
    return dot(picked, jnp.ones((ROWS, 128), BF)).astype(BF)


def by_level(reg_ref):
    level = lax.axis_index("grp")
    low, high = reg_ref[:, 0, :], reg_ref[:, 1, :]
    own = jnp.where(level == 0, low, high)
    return own, low + high - own


def residual(x, att, w):
    y = dot(att, w)
    r = lax.rsqrt(jnp.mean(y * y, axis=1, keepdims=True) + EPS)
    n = y * r
    return (x.astype(F32) + n).astype(BF), n, r


WIDE = 2 * PAIR
SAVE = 11 * WIDE


def student_layer(x, w_qkv, w_out, ids, save_ref):
    blocks = head_blocks()
    qkv = dot(x, w_qkv)
    q, sq = unit(qkv[:, :WIDE], blocks)
    k, sk = unit(qkv[:, WIDE : 2 * WIDE], blocks)
    q = (q * SCALE).astype(BF)
    k = k.astype(BF)
    v = qkv[:, 2 * WIDE :].astype(BF)
    atts = []
    for w in range(4):
        rows = slice(w * WIN, (w + 1) * WIN)
        mask = id_mask(ids[rows], ids[rows])
        nums, dens, es = attend(q[rows], k[rows], v[rows], mask)
        z = 1.0 / jnp.concatenate(dens, axis=1)
        att = jnp.concatenate(nums, axis=1) * z
        save_ref[rows, 4 * WIDE : 5 * WIDE] = z.astype(BF)
        for i, e in enumerate(es):
            save_ref[rows, (9 + i) * WIDE : (9 + i) * WIDE + 2 * WIN] = e
        atts.append(att.astype(BF))
    att = jnp.concatenate(atts, axis=0)
    h, n, r = residual(x, att, w_out)
    for i, part in ((0, q), (1, k), (2, v), (3, att), (5, sq), (6, sk), (7, n)):
        save_ref[:, i * WIDE : (i + 1) * WIDE] = part.astype(BF)
    save_ref[:, 8 * WIDE : 9 * WIDE] = jnp.broadcast_to(r, (NA, WIDE)).astype(BF)
    return h


def fetch(*pairs):
    copies = [pltpu.make_async_copy(*pair) for pair in pairs]
    for copy in copies:
        copy.start()
    return copies


def student_back(g, save_ref, w_qkv, w_out):
    blocks = head_blocks()
    part = lambda i: save_ref[:, i * WIDE : (i + 1) * WIDE]
    n, r = part(7).astype(F32), part(8).astype(F32)
    dy = r * (g - n * jnp.mean(g * n, axis=1, keepdims=True))
    datt = dot_nt(dy.astype(BF), w_out) * part(4).astype(F32)
    drop = (datt * part(3).astype(F32)).astype(BF) * jnp.asarray(-1.0, BF)
    datt = datt.astype(BF)
    q, k, v = part(0), part(1), part(2)
    dqs, dks, dvs = [], [], []
    for w in range(4):
        rows = slice(w * WIN, (w + 1) * WIN)
        pairs = [slice(i, i + PAIR) for i in range(0, WIDE, PAIR)]
        es = [save_ref[rows, (9 + i) * WIDE : (9 + i) * WIDE + 2 * WIN] for i in range(2)]
        dws = [
            dot_nt(
                jnp.concatenate([datt[rows, p], drop[rows, p]], axis=1), stack_values(v[rows, p])
            )
            for p in pairs
        ]
        dvs.append([unstack_heads(dot_tn(e, datt[rows, p])) for e, p in zip(es, pairs)])
        dss = [(e.astype(F32) * dw).astype(BF) for e, dw in zip(es, dws)]
        dqs.append([dot(ds, stack_heads(k[rows, p])) for ds, p in zip(dss, pairs)])
        dks.append([unstack_heads(dot_tn(ds, q[rows, p])) for ds, p in zip(dss, pairs)])
    dqs, dks, dvs = [[jnp.concatenate(x, axis=1) for x in y] for y in (dqs, dks, dvs)]
    dq = 10.0 * jnp.concatenate(dqs, axis=0)
    dk = (1.0 / LOG2E) * jnp.concatenate(dks, axis=0)
    dv = jnp.concatenate(dvs, axis=0)
    q_unit = q.astype(F32) * (1.0 / SCALE)
    k_unit = k.astype(F32)
    dq = part(5).astype(F32) * (dq - q_unit * head_sums(q_unit * dq, blocks))
    dk = part(6).astype(F32) * (dk - k_unit * head_sums(k_unit * dk, blocks))
    dqkv = jnp.concatenate([dq.astype(BF), dk.astype(BF), dv.astype(BF)], axis=1)
    return g + dot_nt(dqkv, w_qkv)


def teacher_own(
    x_hbm, reg_hbm, to_a_hbm, a_row_hbm, a_col_hbm, t_qkv,
    x_out, id_ref, far_id_ref, q_ref, k_ref, v_ref,
    pad_ref, x_ref, reg_ref, to_a, a_row, a_col, wqkv, sems,
):
    copies = fetch(
        (x_hbm, x_ref, sems.at[0]),
        (to_a_hbm, to_a, sems.at[2]),
        (reg_hbm, reg_ref, sems.at[1]),
        (a_row_hbm, a_row, sems.at[3]),
        (a_col_hbm, a_col, sems.at[4]),
        (t_qkv.at[0], wqkv, sems.at[5]),
    )
    width = x_ref.shape[3]
    blocks = head_blocks()
    copies[0].wait()
    copies[1].wait()
    x = to_window_order(x_ref, pad_ref, to_a[...])
    x_out[...] = x
    for copy in copies[2:5]:
        copy.wait()
    reg, reg_far = by_level(reg_ref)
    id_ref[...] = window_ids(reg, a_row[...], a_col[...])
    far_id_ref[...] = window_ids(reg_far, a_row[...], a_col[...])
    copies[5].wait()
    q_ref[...] = (unit(dot(x, wqkv[:, :width]), blocks)[0] * SCALE).astype(BF)
    k_ref[...] = unit(dot(x, wqkv[:, width : 2 * width]), blocks)[0].astype(BF)
    v_ref[...] = dot(x, wqkv[:, 2 * width :]).astype(BF)


def teacher_first(
    far_ref, x_ref, id_ref, far_id_ref, q_ref, k_ref, v_ref, to_a, a_to_g, pack, t_qkv, t_out,
    h_ref, g_ref, first_ref, second_ref, pad_ref, wout, sems,
):
    copies = fetch((t_out.at[0], wout, sems.at[0]))
    width = x_ref.shape[1]
    blocks = head_blocks()
    far = to_window_order(far_ref, pad_ref, to_a[...])
    k_far = unit(dot(far, t_qkv[0, :, width : 2 * width]), blocks)[0].astype(BF)
    v_far = dot(far, t_qkv[0, :, 2 * width :]).astype(BF)
    atts = []
    for w in range(4):
        rows = slice(w * WIN, (w + 1) * WIN)
        id_keys = jnp.concatenate([id_ref[rows], far_id_ref[rows]], axis=0)
        keys = [
            jnp.concatenate([near[rows], away[rows]], axis=0)
            for near, away in ((k_ref, k_far), (v_ref, v_far))
        ]
        atts.append(window_attention(q_ref[rows], keys, (id_ref[rows], id_keys)))
    copies[0].wait()
    h = residual(x_ref[...], jnp.concatenate(atts, axis=0), wout[...])[0]
    h_ref[...] = h
    spread = dot(a_to_g[...], jnp.concatenate([h, id_ref[...]], axis=1)).astype(BF)
    g_ref[...] = spread
    north, south = [
        packed(
            jnp.concatenate([part(spread, n) for n in names], axis=0),
            pack[...], ROW_TOKENS, ROW_SENT,
        )
        for names in (TO_NORTH, TO_SOUTH)
    ]
    first_ref[...], second_ref[...] = swapped("lat", north, south)


def swapped(axis, low, high):
    even = lax.rem(lax.axis_index(axis), 2) == 0
    low, high = low.astype(F32), high.astype(F32)
    return jnp.where(even, low, high).astype(BF), jnp.where(even, high, low).astype(BF)


def packed(rows, table, tokens, sent):
    width = rows.shape[1] - 128
    values = dot(table[:sent], rows[:, :width])
    ids = dot(table, rows[:, width:]).astype(BF)
    row = dot_nt(jnp.full((8, 128), 1.0 / 128, BF), ids)[0:1]
    row = jnp.concatenate([row, jnp.zeros((1, width - 128), F32)], axis=1)
    at = lax.broadcasted_iota(jnp.int32, (sent, 1), 0)
    return jnp.where(at == tokens, row, values).astype(BF)


def opened(sent, table, tokens):
    values = dot(table, sent).astype(BF)
    row = sent.astype(F32)[tokens : tokens + 1, : table.shape[1]]
    ids = dot((table.astype(F32) * row).astype(BF), jnp.ones((table.shape[1], 128), BF))
    return jnp.concatenate([values, ids.astype(BF)], axis=1)


def part(x, name):
    start, kept = AT[name]
    return x[start : start + kept]


TO_NORTH = ("nw", "n", "ne")
TO_SOUTH = ("sw", "s", "se")
TO_WEST = (("N", "sw"), ("", "nw"), ("", "w"), ("", "sw"), ("S", "nw"))
TO_EAST = (("N", "se"), ("", "ne"), ("", "e"), ("", "se"), ("S", "ne"))
EXTRA = {
    "nw": (("N", "sw"), ("W", "ne"), ("NW", "se")),
    "n": (("N", "s"),),
    "ne": (("N", "se"), ("E", "nw"), ("NE", "sw")),
    "e": (("E", "w"),),
    "se": (("S", "ne"), ("E", "sw"), ("SE", "nw")),
    "s": (("S", "n"),),
    "sw": (("S", "nw"), ("W", "se"), ("SW", "ne")),
    "w": (("W", "e"),),
    "c": (),
}
LATE = ("nw", "ne", "e", "se", "sw", "w")
ORDER = [name for name, *_ in PARTS]


def _spots(items):
    spots, start = {}, 0
    for side, name in items:
        spots[side, name] = start
        start += AT[name][1]
    return spots


OWN = {("", name): AT[name][0] for name in ORDER}
EDGE = _spots([("N", n) for n in TO_SOUTH] + [("S", n) for n in TO_NORTH])
COME = _spots([(s + "E", n) for s, n in TO_WEST] + [(s + "W", n) for s, n in TO_EAST])
NE_ROWS = 2 * sum(AT[n][1] for n in TO_NORTH)


def gather(sources, items):
    blocks = []
    for item in items:
        for array, spots in sources:
            if item in spots:
                spot = spots[item]
                blocks.append(array[spot : spot + AT[item[1]][1]])
                break
    return blocks[0] if len(blocks) == 1 else jnp.concatenate(blocks, axis=0)


def window_attention(q, keys, ids):
    nums, dens, _ = attend(q, *keys, id_mask(*ids))
    return jnp.concatenate([(n / d).astype(BF) for n, d in zip(nums, dens)], axis=1)


def beside_rows(
    x_ref, id_ref, to_a, s_qkv, s_out, proj, g_ref, t_qkv, after_ref,
    g0_ref, save0, save1, q_ref, k_ref, v_ref, att_ref, pad_ref,
):
    width = g_ref.shape[1] - 128
    blocks = head_blocks()
    x = to_window_order(x_ref, pad_ref, to_a[...])
    h = student_layer(x, s_qkv[0], s_out[0], id_ref[...], save0)
    h = student_layer(h, s_qkv[1], s_out[1], id_ref[...], save1)
    predicted = dot(h, proj[...])
    g0_ref[...] = dot_nt(predicted.astype(BF), proj[...])

    rows = g_ref[:, :width]
    q = (unit(dot(rows, t_qkv[1, :, :width]), blocks)[0] * SCALE).astype(BF)
    k = unit(dot(rows, t_qkv[1, :, width : 2 * width]), blocks)[0].astype(BF)
    v = dot(rows, t_qkv[1, :, 2 * width :]).astype(BF)
    q_ref[...] = q
    k_ref[...] = k
    v_ref[...] = v
    ids = part(g_ref, "c")[:, width:]
    att_ref[...] = window_attention(part(q, "c"), [part(k, "c"), part(v, "c")], (ids, ids))


def send_columns(
    g_ref, first_ref, second_ref, open_rows, pack, after_ref, edge_ref, out_first, out_second
):
    width = first_ref.shape[1]
    lat = lax.axis_index("lat")
    blocks = []
    inside = (lat > 0, lat < lax.axis_size("lat") - 1)
    for sent, there in zip(swapped("lat", first_ref[...], second_ref[...]), inside):
        rows = opened(sent, open_rows[...], ROW_TOKENS)
        ids = rows[:, width:] * jnp.where(there, 1.0, 0.0).astype(BF)
        blocks.append(jnp.concatenate([rows[:, :width], ids], axis=1))
    edge = jnp.concatenate(blocks, axis=0)
    edge_ref[...] = edge
    west, east = [
        packed(
            gather([(g_ref, OWN), (edge, EDGE)], items), pack[...], COL_TOKENS, COL_SENT
        )
        for items in (TO_WEST, TO_EAST)
    ]
    out_first[...], out_second[...] = swapped("lon", west, east)


def beside_columns(
    g_ref, edge_ref, t_qkv, q_ref, k_ref, v_ref, k_out, v_out, n_ref, s_ref
):
    width = g_ref.shape[1] - 128
    blocks = head_blocks()
    rows = edge_ref[:, :width]
    k = unit(dot(rows, t_qkv[1, :, width : 2 * width]), blocks)[0].astype(BF)
    v = dot(rows, t_qkv[1, :, 2 * width :]).astype(BF)
    k_out[...] = k
    v_out[...] = v
    for name, ref in (("n", n_ref), ("s", s_ref)):
        items = (("", name),) + EXTRA[name]
        keys = [gather([(own, OWN), (edge, EDGE)], items) for own, edge in ((k_ref, k), (v_ref, v))]
        ids = [gather([(g_ref, OWN), (edge_ref, EDGE)], some)[:, width:] for some in (items[:1], items)]
        ref[...] = window_attention(part(q_ref, name), keys, ids)


def teacher_second(
    h_ref, g_ref, edge_ref, first_ref, second_ref, q_ref, k_ref, v_ref, k_edge, v_edge,
    c_ref, n_ref, s_ref, open_cols, from_a, g_to_a, t_qkv, t_out, proj, s_qkv, s_out,
    g0_ref, save0, save1, out_ref, grad_ref,
):
    width = h_ref.shape[1]
    blocks = head_blocks()
    west, east = swapped("lon", first_ref[...], second_ref[...])
    came = [opened(sent, open_cols[...], COL_TOKENS) for sent in (east, west)]
    came = jnp.concatenate(came, axis=0)
    rows = came[:, :width]
    k = unit(dot(rows, t_qkv[1, :, width : 2 * width]), blocks)[0].astype(BF)
    v = dot(rows, t_qkv[1, :, 2 * width :]).astype(BF)
    atts = {"c": c_ref[...], "n": n_ref[...], "s": s_ref[...]}
    for name in LATE:
        items = (("", name),) + EXTRA[name]
        keys = [
            gather([(own, OWN), (edge, EDGE), (new, COME)], items)
            for own, edge, new in ((k_ref, k_edge, k), (v_ref, v_edge, v))
        ]
        ids = [
            gather([(g_ref, OWN), (edge_ref, EDGE), (came, COME)], some)[:, width:]
            for some in (items[:1], items)
        ]
        atts[name] = window_attention(part(q_ref, name), keys, ids)
    att = jnp.concatenate([atts[name] for name in ORDER], axis=0)
    att = dot(g_to_a[...], att).astype(BF)
    teacher = residual(h_ref[...], att, t_out[1])[0]
    natural = dot(from_a[...], teacher).astype(BF)
    out_ref[0] = natural.reshape(COLS, TALL, width)[:, :ROWS, :]

    g = g0_ref[...] - dot_nt(teacher, proj[...])
    g = student_back(g, save1, s_qkv[1], s_out[1])
    g = student_back(g, save0, s_qkv[0], s_out[0])
    high = g.astype(BF)
    low = (g - high.astype(F32)).astype(BF)
    natural = dot(from_a[...], high) + dot(from_a[...], low)
    grad_ref[0] = natural.reshape(COLS, TALL, g.shape[1])[:, :ROWS, :]


VMEM = pl.BlockSpec(memory_space=pltpu.VMEM)
ANY = pl.BlockSpec(memory_space=pl.ANY)
HBM = pl.BlockSpec(memory_space=pltpu.HBM)


def call(kernel, name, outs, specs, args, scratch=(), flops=0):
    shapes = [jax.ShapeDtypeStruct(s, d) for s, d in outs]
    touched = sum(a.size * a.dtype.itemsize for a in args)
    return pl.pallas_call(
        kernel,
        name=name,
        out_shape=shapes,
        in_specs=specs,
        out_specs=[VMEM] * len(outs),
        scratch_shapes=list(scratch),
        compiler_params=pltpu.CompilerParams(vmem_limit_bytes=28 << 20),
        cost_estimate=pl.CostEstimate(flops=flops, bytes_accessed=touched, transcendentals=0),
    )(*args)


def buffers(*arrays):
    return [pltpu.VMEM(a.shape, a.dtype) for a in arrays] + [
        pltpu.SemaphoreType.DMA((len(arrays),))
    ]


def swaps(size, start, closed):
    route = {i: i for i in range(size)}
    for i in range(start, size if closed else size - 1, 2):
        j = (i + 1) % size
        route[i], route[j] = j, i
    return sorted(route.items())


def shards(teacher_in, student_in, regions, t_qkv, t_out, s_qkv, s_out, s_proj):
    width, narrow = teacher_in.shape[3], student_in.shape[3]
    lat_size, lon_size = lax.axis_size("lat"), lax.axis_size("lon")
    wide = width + 128
    teacher_in = teacher_in.transpose(0, 2, 1, 3)
    student_in = student_in.transpose(0, 2, 1, 3)
    regions = regions.transpose(2, 0, 1)
    far = lax.ppermute(teacher_in, "grp", [(0, 1), (1, 0)])

    pinned = [
        pltpu.with_memory_space_constraint(jnp.asarray(a), pltpu.HBM)
        for a in (teacher_in, regions, TO_A, A_ROW, A_COL, t_qkv)
    ]
    x, ids, far_ids, q, k, v = call(
        teacher_own, "teacher_own",
        [((NA, width), BF), ((NA, 128), BF), ((NA, 128), BF)] + [((NA, width), BF)] * 3,
        [HBM] * 6, pinned,
        [pltpu.VMEM((COLS, TALL, width), BF)]
        + buffers(teacher_in, regions, TO_A, A_ROW, A_COL, t_qkv[0]),
        10**9,
    )
    hidden, spread, rows_1, rows_2 = call(
        teacher_first, "teacher_first",
        [((NA, width), BF), ((NG, wide), BF)] + [((ROW_SENT, width), BF)] * 2,
        [VMEM] * 11 + [HBM],
        [far, x, ids, far_ids, q, k, v, TO_A, A_TO_G, PACK_ROWS, t_qkv]
        + [pltpu.with_memory_space_constraint(t_out, pltpu.HBM)],
        [pltpu.VMEM((COLS, TALL, width), BF)] + buffers(t_out[0]), 3 * 10**9,
    )
    rows_1 = lax.ppermute(rows_1, "lat", swaps(lat_size, 1, False))
    rows_2 = lax.ppermute(rows_2, "lat", swaps(lat_size, 0, False))

    g0, save0, save1, q, k, v, c_att = call(
        beside_rows, "beside_rows",
        [((NA, narrow), F32), ((NA, SAVE), BF), ((NA, SAVE), BF)]
        + [((NG, width), BF)] * 3 + [((AT["c"][1], width), BF)],
        [VMEM] * 8 + [ANY],
        [student_in, ids, TO_A, s_qkv, s_out, s_proj, spread, t_qkv, hidden],
        [pltpu.VMEM((COLS, TALL, narrow), BF)], 5 * 10**9,
    )
    edge, cols_1, cols_2 = call(
        send_columns, "send_columns",
        [((NE_ROWS, wide), BF)] + [((COL_SENT, width), BF)] * 2,
        [VMEM] * 5 + [ANY],
        [spread, rows_1, rows_2, OPEN_ROWS, PACK_COLS, g0], (), 10**7,
    )
    cols_1 = lax.ppermute(cols_1, "lon", swaps(lon_size, 1, True))
    cols_2 = lax.ppermute(cols_2, "lon", swaps(lon_size, 0, True))

    k_edge, v_edge, n_att, s_att = call(
        beside_columns, "beside_columns",
        [((NE_ROWS, width), BF)] * 2 + [((AT["n"][1], width), BF)] * 2,
        [VMEM] * 6,
        [spread, edge, t_qkv, q, k, v], (), 2 * 10**9,
    )
    args = [hidden, spread, edge, cols_1, cols_2, q, k, v, k_edge, v_edge, c_att, n_att, s_att]
    args += [OPEN_COLS, FROM_A, G_TO_A, t_qkv, t_out, s_proj, s_qkv, s_out, g0, save0, save1]
    out, grad = call(
        teacher_second, "teacher_second",
        [(teacher_in.shape, BF), (student_in.shape, F32)],
        [VMEM] * len(args), args, (), 6 * 10**9,
    )
    return out.transpose(0, 2, 1, 3), grad.transpose(0, 2, 1, 3)


def solution(mesh):
    tiles = P("grp", "lat", "lon", None)
    return jax.shard_map(
        shards,
        mesh=mesh,
        in_specs=(tiles, tiles, P(None, "lat", "lon"), P(), P(), P(), P(), P()),
        out_specs=(tiles, tiles),
        check_vma=False,
    )
```

```python
import functools

import jax
import jax.numpy as jnp
import ml_dtypes
import numpy as np
from jax import lax
from jax.experimental import pallas as pl
from jax.experimental.pallas import tpu as pltpu
from jax.sharding import PartitionSpec as P

HEADS_T = 8
HEADS_S = 4
EPS = 1e-06
LOG2E = 1.4426950408889634
SCALE = 10.0 * LOG2E
BF = jnp.bfloat16
F32 = jnp.float32

ROWS, COLS = 24, 12
WIN = 80
NA = 4 * WIN
TALL = 32
NAT = COLS * TALL
PAIR = 128

PARTS = (
    ("nw", (0, 6), (0, 3), 32),
    ("n", (0, 6), (3, 9), 48),
    ("ne", (0, 6), (9, 12), 32),
    ("e", (6, 18), (9, 12), 48),
    ("se", (18, 24), (9, 12), 32),
    ("s", (18, 24), (3, 9), 48),
    ("sw", (18, 24), (0, 3), 32),
    ("w", (6, 18), (0, 3), 48),
    ("c", (6, 18), (3, 9), 80),
)
AT = {}
NG = 0
for _name, _r, _c, _kept in PARTS:
    AT[_name] = (NG, _kept)
    NG += _kept


def _a_slot(r, c):
    return (2 * (r // 12) + c // 6) * WIN + (r % 12) * 6 + c % 6


def _tables():
    to_a = np.zeros((NA, NAT), ml_dtypes.bfloat16)
    a_row = np.zeros((NA, ROWS), ml_dtypes.bfloat16)
    a_col = np.zeros((NA, COLS), ml_dtypes.bfloat16)
    for r in range(ROWS):
        for c in range(COLS):
            slot = _a_slot(r, c)
            to_a[slot, c * TALL + r] = 1
            a_row[slot, r] = 1
            a_col[slot, c] = 1
    a_to_g = np.zeros((NG, NA), ml_dtypes.bfloat16)
    for name, (r0, r1), (c0, c1), _ in PARTS:
        spot = AT[name][0]
        for r in range(r0, r1):
            for c in range(c0, c1):
                a_to_g[spot, _a_slot(r, c)] = 1
                spot += 1
    return to_a, a_row, a_col, a_to_g


TO_A, A_ROW, A_COL, A_TO_G = _tables()
FROM_A = np.ascontiguousarray(TO_A.T)
G_TO_A = np.ascontiguousarray(A_TO_G.T)


def _packing(kept):
    table = np.zeros((128, sum(kept)), ml_dtypes.bfloat16)
    token, start = 0, 0
    for rows in kept:
        count = {32: 18, 48: 36}[rows]
        for i in range(count):
            table[token + i, start + i] = 1
        token, start = token + count, start + rows
    return table


PACK_ROWS = _packing((32, 48, 32))
PACK_COLS = _packing((32, 32, 48, 32, 32))
ROW_TOKENS, ROW_SENT = 72, 80
COL_TOKENS, COL_SENT = 108, 112
OPEN_ROWS = np.ascontiguousarray(PACK_ROWS.T[:, :ROW_SENT])
OPEN_COLS = np.ascontiguousarray(PACK_COLS.T[:, :COL_SENT])


def dot(a, b):
    return jnp.dot(a, b, preferred_element_type=F32)


def dot_nt(a, b):
    return lax.dot_general(a, b, (((1,), (1,)), ((), ())), preferred_element_type=F32)


def dot_tn(a, b):
    return lax.dot_general(a, b, (((0,), (0,)), ((), ())), preferred_element_type=F32)


def head_lanes(rows, h):
    lane = lax.broadcasted_iota(jnp.int32, (rows, PAIR), 1)
    return jnp.where((lane >> 6) == h, 1.0, 0.0).astype(BF)


def head_blocks():
    row = lax.broadcasted_iota(jnp.int32, (2 * PAIR, 2 * PAIR), 0)
    lane = lax.broadcasted_iota(jnp.int32, (2 * PAIR, 2 * PAIR), 1)
    return jnp.where((row >> 6) == (lane >> 6), 1.0, 0.0).astype(BF)


def stack_heads(x):
    return jnp.concatenate([x * head_lanes(1, h) for h in range(2)], axis=0)


def stack_values(v):
    rows = v.shape[0]
    ones = jnp.concatenate([head_lanes(rows, h) for h in range(2)], axis=0)
    return jnp.concatenate([stack_heads(v), ones], axis=1)


def unstack_heads(x):
    n = x.shape[0] // 2
    lane = lax.broadcasted_iota(jnp.int32, (1, PAIR), 1) >> 6
    return jnp.where(lane == 0, x[:n], x[n:])


def head_sums(x, blocks):
    step = blocks.shape[0]
    groups = [dot(x[:, i : i + step].astype(BF), blocks) for i in range(0, x.shape[1], step)]
    return groups[0] if len(groups) == 1 else jnp.concatenate(groups, axis=1)


def unit(x, blocks):
    scale = lax.rsqrt(head_sums(x * x, blocks) + EPS)
    return x * scale, scale


def id_mask(id_query, id_keys):
    keys = jnp.concatenate([id_keys] * 2, axis=0)
    row = dot_nt(jnp.full((8, 128), 1.0 / 128, BF), keys)[0:1]
    return id_query.astype(F32)[:, 0:1] == row


def attend(q, k, v, mask):
    pairs = [slice(i, i + PAIR) for i in range(0, q.shape[1], PAIR)]
    scores = [dot_nt(q[:, p], stack_heads(k[:, p])) for p in pairs]
    es = [jnp.where(mask, jnp.exp2(s), 0.0).astype(BF) for s in scores]
    both = [dot(e, stack_values(v[:, p])) for e, p in zip(es, pairs)]
    return [b[:, :PAIR] for b in both], [b[:, PAIR:] for b in both], es


def to_window_order(x_ref, pad_ref, to_a):
    pad_ref[...] = jnp.zeros_like(pad_ref)
    pad_ref[:, 0:ROWS, :] = x_ref[0]
    natural = pad_ref[...].reshape(NAT, x_ref.shape[3])
    return dot(to_a, natural).astype(BF)


def window_ids(reg, a_row, a_col):
    table = (reg + 1).astype(F32).astype(BF)
    picked = (dot(a_col, table) * a_row.astype(F32)).astype(BF)
    return dot(picked, jnp.ones((ROWS, 128), BF)).astype(BF)


def by_level(reg_ref):
    level = lax.axis_index("grp")
    low, high = reg_ref[:, 0, :], reg_ref[:, 1, :]
    own = jnp.where(level == 0, low, high)
    return own, low + high - own


def residual(x, att, w):
    y = dot(att, w)
    r = lax.rsqrt(jnp.mean(y * y, axis=1, keepdims=True) + EPS)
    n = y * r
    return (x.astype(F32) + n).astype(BF), n, r


WIDE = 2 * PAIR
SAVE = 11 * WIDE


def student_layer(x, w_qkv, w_out, ids, save_ref):
    blocks = head_blocks()
    qkv = dot(x, w_qkv)
    q, sq = unit(qkv[:, :WIDE], blocks)
    k, sk = unit(qkv[:, WIDE : 2 * WIDE], blocks)
    q = (q * SCALE).astype(BF)
    k = k.astype(BF)
    v = qkv[:, 2 * WIDE :].astype(BF)
    atts = []
    for w in range(4):
        rows = slice(w * WIN, (w + 1) * WIN)
        mask = id_mask(ids[rows], ids[rows])
        nums, dens, es = attend(q[rows], k[rows], v[rows], mask)
        z = 1.0 / jnp.concatenate(dens, axis=1)
        att = jnp.concatenate(nums, axis=1) * z
        save_ref[rows, 4 * WIDE : 5 * WIDE] = z.astype(BF)
        for i, e in enumerate(es):
            save_ref[rows, (9 + i) * WIDE : (9 + i) * WIDE + 2 * WIN] = e
        atts.append(att.astype(BF))
    att = jnp.concatenate(atts, axis=0)
    h, n, r = residual(x, att, w_out)
    for i, part in ((0, q), (1, k), (2, v), (3, att), (5, sq), (6, sk), (7, n)):
        save_ref[:, i * WIDE : (i + 1) * WIDE] = part.astype(BF)
    save_ref[:, 8 * WIDE : 9 * WIDE] = jnp.broadcast_to(r, (NA, WIDE)).astype(BF)
    return h


def fetch(*pairs):
    copies = [pltpu.make_async_copy(*pair) for pair in pairs]
    for copy in copies:
        copy.start()
    return copies


def student_back(g, save_ref, w_qkv, w_out):
    blocks = head_blocks()
    part = lambda i: save_ref[:, i * WIDE : (i + 1) * WIDE]
    n, r = part(7).astype(F32), part(8).astype(F32)
    dy = r * (g - n * jnp.mean(g * n, axis=1, keepdims=True))
    datt = dot_nt(dy.astype(BF), w_out) * part(4).astype(F32)
    drop = (datt * part(3).astype(F32)).astype(BF) * jnp.asarray(-1.0, BF)
    datt = datt.astype(BF)
    q, k, v = part(0), part(1), part(2)
    dqs, dks, dvs = [], [], []
    for w in range(4):
        rows = slice(w * WIN, (w + 1) * WIN)
        pairs = [slice(i, i + PAIR) for i in range(0, WIDE, PAIR)]
        es = [save_ref[rows, (9 + i) * WIDE : (9 + i) * WIDE + 2 * WIN] for i in range(2)]
        dws = [
            dot_nt(
                jnp.concatenate([datt[rows, p], drop[rows, p]], axis=1), stack_values(v[rows, p])
            )
            for p in pairs
        ]
        dvs.append([unstack_heads(dot_tn(e, datt[rows, p])) for e, p in zip(es, pairs)])
        dss = [(e.astype(F32) * dw).astype(BF) for e, dw in zip(es, dws)]
        dqs.append([dot(ds, stack_heads(k[rows, p])) for ds, p in zip(dss, pairs)])
        dks.append([unstack_heads(dot_tn(ds, q[rows, p])) for ds, p in zip(dss, pairs)])
    dqs, dks, dvs = [[jnp.concatenate(x, axis=1) for x in y] for y in (dqs, dks, dvs)]
    dq = 10.0 * jnp.concatenate(dqs, axis=0)
    dk = (1.0 / LOG2E) * jnp.concatenate(dks, axis=0)
    dv = jnp.concatenate(dvs, axis=0)
    q_unit = q.astype(F32) * (1.0 / SCALE)
    k_unit = k.astype(F32)
    dq = part(5).astype(F32) * (dq - q_unit * head_sums(q_unit * dq, blocks))
    dk = part(6).astype(F32) * (dk - k_unit * head_sums(k_unit * dk, blocks))
    dqkv = jnp.concatenate([dq.astype(BF), dk.astype(BF), dv.astype(BF)], axis=1)
    return g + dot_nt(dqkv, w_qkv)


def teacher_own(
    x_hbm, reg_hbm, to_a_hbm, a_row_hbm, a_col_hbm, t_qkv,
    x_out, id_ref, far_id_ref, q_ref, k_ref, v_ref,
    pad_ref, x_ref, reg_ref, to_a, a_row, a_col, wqkv, sems,
):
    copies = fetch(
        (x_hbm, x_ref, sems.at[0]),
        (to_a_hbm, to_a, sems.at[2]),
        (reg_hbm, reg_ref, sems.at[1]),
        (a_row_hbm, a_row, sems.at[3]),
        (a_col_hbm, a_col, sems.at[4]),
        (t_qkv.at[0], wqkv, sems.at[5]),
    )
    width = x_ref.shape[3]
    blocks = head_blocks()
    copies[0].wait()
    copies[1].wait()
    x = to_window_order(x_ref, pad_ref, to_a[...])
    x_out[...] = x
    for copy in copies[2:5]:
        copy.wait()
    reg, reg_far = by_level(reg_ref)
    id_ref[...] = window_ids(reg, a_row[...], a_col[...])
    far_id_ref[...] = window_ids(reg_far, a_row[...], a_col[...])
    copies[5].wait()
    q_ref[...] = (unit(dot(x, wqkv[:, :width]), blocks)[0] * SCALE).astype(BF)
    k_ref[...] = unit(dot(x, wqkv[:, width : 2 * width]), blocks)[0].astype(BF)
    v_ref[...] = dot(x, wqkv[:, 2 * width :]).astype(BF)


def teacher_first(
    far_ref, x_ref, id_ref, far_id_ref, q_ref, k_ref, v_ref, to_a, a_to_g, pack, t_qkv, t_out,
    h_ref, g_ref, first_ref, second_ref, pad_ref, wout, sems,
):
    copies = fetch((t_out.at[0], wout, sems.at[0]))
    width = x_ref.shape[1]
    blocks = head_blocks()
    far = to_window_order(far_ref, pad_ref, to_a[...])
    k_far = unit(dot(far, t_qkv[0, :, width : 2 * width]), blocks)[0].astype(BF)
    v_far = dot(far, t_qkv[0, :, 2 * width :]).astype(BF)
    atts = []
    for w in range(4):
        rows = slice(w * WIN, (w + 1) * WIN)
        id_keys = jnp.concatenate([id_ref[rows], far_id_ref[rows]], axis=0)
        keys = [
            jnp.concatenate([near[rows], away[rows]], axis=0)
            for near, away in ((k_ref, k_far), (v_ref, v_far))
        ]
        atts.append(window_attention(q_ref[rows], keys, (id_ref[rows], id_keys)))
    copies[0].wait()
    h = residual(x_ref[...], jnp.concatenate(atts, axis=0), wout[...])[0]
    h_ref[...] = h
    spread = dot(a_to_g[...], jnp.concatenate([h, id_ref[...]], axis=1)).astype(BF)
    g_ref[...] = spread
    north, south = [
        packed(
            jnp.concatenate([part(spread, n) for n in names], axis=0),
            pack[...], ROW_TOKENS, ROW_SENT,
        )
        for names in (TO_NORTH, TO_SOUTH)
    ]
    first_ref[...], second_ref[...] = swapped("lat", north, south)


def swapped(axis, low, high):
    even = lax.rem(lax.axis_index(axis), 2) == 0
    low, high = low.astype(F32), high.astype(F32)
    return jnp.where(even, low, high).astype(BF), jnp.where(even, high, low).astype(BF)


def packed(rows, table, tokens, sent):
    width = rows.shape[1] - 128
    values = dot(table[:sent], rows[:, :width])
    ids = dot(table, rows[:, width:]).astype(BF)
    row = dot_nt(jnp.full((8, 128), 1.0 / 128, BF), ids)[0:1]
    row = jnp.concatenate([row, jnp.zeros((1, width - 128), F32)], axis=1)
    at = lax.broadcasted_iota(jnp.int32, (sent, 1), 0)
    return jnp.where(at == tokens, row, values).astype(BF)


def opened(sent, table, tokens):
    values = dot(table, sent).astype(BF)
    row = sent.astype(F32)[tokens : tokens + 1, : table.shape[1]]
    ids = dot((table.astype(F32) * row).astype(BF), jnp.ones((table.shape[1], 128), BF))
    return jnp.concatenate([values, ids.astype(BF)], axis=1)


def part(x, name):
    start, kept = AT[name]
    return x[start : start + kept]


TO_NORTH = ("nw", "n", "ne")
TO_SOUTH = ("sw", "s", "se")
TO_WEST = (("N", "sw"), ("", "nw"), ("", "w"), ("", "sw"), ("S", "nw"))
TO_EAST = (("N", "se"), ("", "ne"), ("", "e"), ("", "se"), ("S", "ne"))
EXTRA = {
    "nw": (("N", "sw"), ("W", "ne"), ("NW", "se")),
    "n": (("N", "s"),),
    "ne": (("N", "se"), ("E", "nw"), ("NE", "sw")),
    "e": (("E", "w"),),
    "se": (("S", "ne"), ("E", "sw"), ("SE", "nw")),
    "s": (("S", "n"),),
    "sw": (("S", "nw"), ("W", "se"), ("SW", "ne")),
    "w": (("W", "e"),),
    "c": (),
}
LATE = ("nw", "ne", "e", "se", "sw", "w")
ORDER = [name for name, *_ in PARTS]


def _spots(items):
    spots, start = {}, 0
    for side, name in items:
        spots[side, name] = start
        start += AT[name][1]
    return spots


OWN = {("", name): AT[name][0] for name in ORDER}
EDGE = _spots([("N", n) for n in TO_SOUTH] + [("S", n) for n in TO_NORTH])
COME = _spots([(s + "E", n) for s, n in TO_WEST] + [(s + "W", n) for s, n in TO_EAST])
NE_ROWS = 2 * sum(AT[n][1] for n in TO_NORTH)


def gather(sources, items):
    blocks = []
    for item in items:
        for array, spots in sources:
            if item in spots:
                spot = spots[item]
                blocks.append(array[spot : spot + AT[item[1]][1]])
                break
    return blocks[0] if len(blocks) == 1 else jnp.concatenate(blocks, axis=0)


def window_attention(q, keys, ids):
    nums, dens, _ = attend(q, *keys, id_mask(*ids))
    return jnp.concatenate([(n / d).astype(BF) for n, d in zip(nums, dens)], axis=1)


def beside_rows(
    x_ref, id_ref, to_a, s_qkv, s_out, proj, g_ref, t_qkv, after_ref,
    g0_ref, save0, save1, q_ref, k_ref, v_ref, att_ref, pad_ref,
):
    width = g_ref.shape[1] - 128
    blocks = head_blocks()
    x = to_window_order(x_ref, pad_ref, to_a[...])
    h = student_layer(x, s_qkv[0], s_out[0], id_ref[...], save0)
    h = student_layer(h, s_qkv[1], s_out[1], id_ref[...], save1)
    predicted = dot(h, proj[...])
    g0_ref[...] = dot_nt(predicted.astype(BF), proj[...])

    rows = g_ref[:, :width]
    q = (unit(dot(rows, t_qkv[1, :, :width]), blocks)[0] * SCALE).astype(BF)
    k = unit(dot(rows, t_qkv[1, :, width : 2 * width]), blocks)[0].astype(BF)
    v = dot(rows, t_qkv[1, :, 2 * width :]).astype(BF)
    q_ref[...] = q
    k_ref[...] = k
    v_ref[...] = v
    ids = part(g_ref, "c")[:, width:]
    att_ref[...] = window_attention(part(q, "c"), [part(k, "c"), part(v, "c")], (ids, ids))


def send_columns(
    g_ref, first_ref, second_ref, open_rows, pack, after_ref, edge_ref, out_first, out_second
):
    width = first_ref.shape[1]
    lat = lax.axis_index("lat")
    blocks = []
    inside = (lat > 0, lat < lax.axis_size("lat") - 1)
    for sent, there in zip(swapped("lat", first_ref[...], second_ref[...]), inside):
        rows = opened(sent, open_rows[...], ROW_TOKENS)
        ids = rows[:, width:] * jnp.where(there, 1.0, 0.0).astype(BF)
        blocks.append(jnp.concatenate([rows[:, :width], ids], axis=1))
    edge = jnp.concatenate(blocks, axis=0)
    edge_ref[...] = edge
    west, east = [
        packed(
            gather([(g_ref, OWN), (edge, EDGE)], items), pack[...], COL_TOKENS, COL_SENT
        )
        for items in (TO_WEST, TO_EAST)
    ]
    out_first[...], out_second[...] = swapped("lon", west, east)


def beside_columns(
    g_ref, edge_ref, t_qkv, q_ref, k_ref, v_ref, k_out, v_out, n_ref, s_ref
):
    width = g_ref.shape[1] - 128
    blocks = head_blocks()
    rows = edge_ref[:, :width]
    k = unit(dot(rows, t_qkv[1, :, width : 2 * width]), blocks)[0].astype(BF)
    v = dot(rows, t_qkv[1, :, 2 * width :]).astype(BF)
    k_out[...] = k
    v_out[...] = v
    for name, ref in (("n", n_ref), ("s", s_ref)):
        items = (("", name),) + EXTRA[name]
        keys = [gather([(own, OWN), (edge, EDGE)], items) for own, edge in ((k_ref, k), (v_ref, v))]
        ids = [gather([(g_ref, OWN), (edge_ref, EDGE)], some)[:, width:] for some in (items[:1], items)]
        ref[...] = window_attention(part(q_ref, name), keys, ids)


def teacher_second(
    h_ref, g_ref, edge_ref, first_ref, second_ref, q_ref, k_ref, v_ref, k_edge, v_edge,
    c_ref, n_ref, s_ref, open_cols, from_a, g_to_a, t_qkv, t_out, proj, s_qkv, s_out,
    g0_ref, save0, save1, out_ref, grad_ref,
):
    width = h_ref.shape[1]
    blocks = head_blocks()
    west, east = swapped("lon", first_ref[...], second_ref[...])
    came = [opened(sent, open_cols[...], COL_TOKENS) for sent in (east, west)]
    came = jnp.concatenate(came, axis=0)
    rows = came[:, :width]
    k = unit(dot(rows, t_qkv[1, :, width : 2 * width]), blocks)[0].astype(BF)
    v = dot(rows, t_qkv[1, :, 2 * width :]).astype(BF)
    atts = {"c": c_ref[...], "n": n_ref[...], "s": s_ref[...]}
    for name in LATE:
        items = (("", name),) + EXTRA[name]
        keys = [
            gather([(own, OWN), (edge, EDGE), (new, COME)], items)
            for own, edge, new in ((k_ref, k_edge, k), (v_ref, v_edge, v))
        ]
        ids = [
            gather([(g_ref, OWN), (edge_ref, EDGE), (came, COME)], some)[:, width:]
            for some in (items[:1], items)
        ]
        atts[name] = window_attention(part(q_ref, name), keys, ids)
    att = jnp.concatenate([atts[name] for name in ORDER], axis=0)
    att = dot(g_to_a[...], att).astype(BF)
    teacher = residual(h_ref[...], att, t_out[1])[0]
    natural = dot(from_a[...], teacher).astype(BF)
    out_ref[0] = natural.reshape(COLS, TALL, width)[:, :ROWS, :]

    g = g0_ref[...] - dot_nt(teacher, proj[...])
    g = student_back(g, save1, s_qkv[1], s_out[1])
    g = student_back(g, save0, s_qkv[0], s_out[0])
    high = g.astype(BF)
    low = (g - high.astype(F32)).astype(BF)
    natural = dot(from_a[...], high) + dot(from_a[...], low)
    grad_ref[0] = natural.reshape(COLS, TALL, g.shape[1])[:, :ROWS, :]


VMEM = pl.BlockSpec(memory_space=pltpu.VMEM)
ANY = pl.BlockSpec(memory_space=pl.ANY)
HBM = pl.BlockSpec(memory_space=pltpu.HBM)


def call(kernel, name, outs, specs, args, scratch=(), flops=0):
    shapes = [jax.ShapeDtypeStruct(s, d) for s, d in outs]
    touched = sum(a.size * a.dtype.itemsize for a in args)
    return pl.pallas_call(
        kernel,
        name=name,
        out_shape=shapes,
        in_specs=specs,
        out_specs=[VMEM] * len(outs),
        scratch_shapes=list(scratch),
        compiler_params=pltpu.CompilerParams(vmem_limit_bytes=28 << 20),
        cost_estimate=pl.CostEstimate(flops=flops, bytes_accessed=touched, transcendentals=0),
    )(*args)


def buffers(*arrays):
    return [pltpu.VMEM(a.shape, a.dtype) for a in arrays] + [
        pltpu.SemaphoreType.DMA((len(arrays),))
    ]


def swaps(size, start):
    route = {}
    for i in range(start, size, 2):
        j = (i + 1) % size
        route[i], route[j] = j, i
    return sorted(route.items())


def shards(teacher_in, student_in, regions, t_qkv, t_out, s_qkv, s_out, s_proj):
    width, narrow = teacher_in.shape[3], student_in.shape[3]
    lat_size, lon_size = lax.axis_size("lat"), lax.axis_size("lon")
    wide = width + 128
    teacher_in = teacher_in.transpose(0, 2, 1, 3)
    student_in = student_in.transpose(0, 2, 1, 3)
    regions = regions.transpose(2, 0, 1)
    far = lax.ppermute(teacher_in, "grp", [(0, 1), (1, 0)])

    pinned = [
        pltpu.with_memory_space_constraint(jnp.asarray(a), pltpu.HBM)
        for a in (teacher_in, regions, TO_A, A_ROW, A_COL, t_qkv)
    ]
    x, ids, far_ids, q, k, v = call(
        teacher_own, "teacher_own",
        [((NA, width), BF), ((NA, 128), BF), ((NA, 128), BF)] + [((NA, width), BF)] * 3,
        [HBM] * 6, pinned,
        [pltpu.VMEM((COLS, TALL, width), BF)]
        + buffers(teacher_in, regions, TO_A, A_ROW, A_COL, t_qkv[0]),
        10**9,
    )
    hidden, spread, rows_1, rows_2 = call(
        teacher_first, "teacher_first",
        [((NA, width), BF), ((NG, wide), BF)] + [((ROW_SENT, width), BF)] * 2,
        [VMEM] * 11 + [HBM],
        [far, x, ids, far_ids, q, k, v, TO_A, A_TO_G, PACK_ROWS, t_qkv]
        + [pltpu.with_memory_space_constraint(t_out, pltpu.HBM)],
        [pltpu.VMEM((COLS, TALL, width), BF)] + buffers(t_out[0]), 3 * 10**9,
    )
    rows_2 = lax.ppermute(rows_2, "lat", swaps(lat_size, 0))
    rows_1 = lax.ppermute(rows_1, "lat", swaps(lat_size, 1))

    g0, save0, save1, q, k, v, c_att = call(
        beside_rows, "beside_rows",
        [((NA, narrow), F32), ((NA, SAVE), BF), ((NA, SAVE), BF)]
        + [((NG, width), BF)] * 3 + [((AT["c"][1], width), BF)],
        [VMEM] * 8 + [ANY],
        [student_in, ids, TO_A, s_qkv, s_out, s_proj, spread, t_qkv, hidden],
        [pltpu.VMEM((COLS, TALL, narrow), BF)], 5 * 10**9,
    )
    edge, cols_1, cols_2 = call(
        send_columns, "send_columns",
        [((NE_ROWS, wide), BF)] + [((COL_SENT, width), BF)] * 2,
        [VMEM] * 5 + [ANY],
        [spread, rows_1, rows_2, OPEN_ROWS, PACK_COLS, g0], (), 10**7,
    )
    cols_2 = lax.ppermute(cols_2, "lon", swaps(lon_size, 0))
    cols_1 = lax.ppermute(cols_1, "lon", swaps(lon_size, 1))

    k_edge, v_edge, n_att, s_att = call(
        beside_columns, "beside_columns",
        [((NE_ROWS, width), BF)] * 2 + [((AT["n"][1], width), BF)] * 2,
        [VMEM] * 6,
        [spread, edge, t_qkv, q, k, v], (), 2 * 10**9,
    )
    args = [hidden, spread, edge, cols_1, cols_2, q, k, v, k_edge, v_edge, c_att, n_att, s_att]
    args += [OPEN_COLS, FROM_A, G_TO_A, t_qkv, t_out, s_proj, s_qkv, s_out, g0, save0, save1]
    out, grad = call(
        teacher_second, "teacher_second",
        [(teacher_in.shape, BF), (student_in.shape, F32)],
        [VMEM] * len(args), args, (), 6 * 10**9,
    )
    return out.transpose(0, 2, 1, 3), grad.transpose(0, 2, 1, 3)


def solution(mesh):
    tiles = P("grp", "lat", "lon", None)
    return jax.shard_map(
        shards,
        mesh=mesh,
        in_specs=(tiles, tiles, P(None, "lat", "lon"), P(), P(), P(), P(), P()),
        out_specs=(tiles, tiles),
        check_vma=False,
    )
```

```python
import functools

import jax
import jax.numpy as jnp
import ml_dtypes
import numpy as np
from jax import lax
from jax.experimental import pallas as pl
from jax.experimental.pallas import tpu as pltpu
from jax.sharding import PartitionSpec as P

HEADS_T = 8
HEADS_S = 4
EPS = 1e-06
LOG2E = 1.4426950408889634
SCALE = 10.0 * LOG2E
BF = jnp.bfloat16
F32 = jnp.float32

ROWS, COLS = 24, 12
WIN = 80
NA = 4 * WIN
TALL = 32
NAT = COLS * TALL
PAIR = 128

PARTS = (
    ("nw", (0, 6), (0, 3), 32),
    ("n", (0, 6), (3, 9), 48),
    ("ne", (0, 6), (9, 12), 32),
    ("e", (6, 18), (9, 12), 48),
    ("se", (18, 24), (9, 12), 32),
    ("s", (18, 24), (3, 9), 48),
    ("sw", (18, 24), (0, 3), 32),
    ("w", (6, 18), (0, 3), 48),
    ("c", (6, 18), (3, 9), 80),
)
AT = {}
NG = 0
for _name, _r, _c, _kept in PARTS:
    AT[_name] = (NG, _kept)
    NG += _kept


def _a_slot(r, c):
    return (2 * (r // 12) + c // 6) * WIN + (r % 12) * 6 + c % 6


def _tables():
    to_a = np.zeros((NA, NAT), ml_dtypes.bfloat16)
    a_row = np.zeros((NA, ROWS), ml_dtypes.bfloat16)
    a_col = np.zeros((NA, COLS), ml_dtypes.bfloat16)
    for r in range(ROWS):
        for c in range(COLS):
            slot = _a_slot(r, c)
            to_a[slot, c * TALL + r] = 1
            a_row[slot, r] = 1
            a_col[slot, c] = 1
    a_to_g = np.zeros((NG, NA), ml_dtypes.bfloat16)
    for name, (r0, r1), (c0, c1), _ in PARTS:
        spot = AT[name][0]
        for r in range(r0, r1):
            for c in range(c0, c1):
                a_to_g[spot, _a_slot(r, c)] = 1
                spot += 1
    return to_a, a_row, a_col, a_to_g


TO_A, A_ROW, A_COL, A_TO_G = _tables()
FROM_A = np.ascontiguousarray(TO_A.T)
G_TO_A = np.ascontiguousarray(A_TO_G.T)


def _packing(kept):
    table = np.zeros((128, sum(kept)), ml_dtypes.bfloat16)
    token, start = 0, 0
    for rows in kept:
        count = {32: 18, 48: 36}[rows]
        for i in range(count):
            table[token + i, start + i] = 1
        token, start = token + count, start + rows
    return table


PACK_ROWS = _packing((32, 48, 32))
PACK_COLS = _packing((32, 32, 48, 32, 32))
ROW_TOKENS, ROW_SENT = 72, 80
COL_TOKENS, COL_SENT = 108, 112
OPEN_ROWS = np.ascontiguousarray(PACK_ROWS.T[:, :ROW_SENT])
OPEN_COLS = np.ascontiguousarray(PACK_COLS.T[:, :COL_SENT])


def dot(a, b):
    return jnp.dot(a, b, preferred_element_type=F32)


def dot_nt(a, b):
    return lax.dot_general(a, b, (((1,), (1,)), ((), ())), preferred_element_type=F32)


def dot_tn(a, b):
    return lax.dot_general(a, b, (((0,), (0,)), ((), ())), preferred_element_type=F32)


def head_lanes(rows, h):
    lane = lax.broadcasted_iota(jnp.int32, (rows, PAIR), 1)
    return jnp.where((lane >> 6) == h, 1.0, 0.0).astype(BF)


def head_blocks():
    row = lax.broadcasted_iota(jnp.int32, (2 * PAIR, 2 * PAIR), 0)
    lane = lax.broadcasted_iota(jnp.int32, (2 * PAIR, 2 * PAIR), 1)
    return jnp.where((row >> 6) == (lane >> 6), 1.0, 0.0).astype(BF)


def stack_heads(x):
    return jnp.concatenate([x * head_lanes(1, h) for h in range(2)], axis=0)


def stack_values(v):
    rows = v.shape[0]
    ones = jnp.concatenate([head_lanes(rows, h) for h in range(2)], axis=0)
    return jnp.concatenate([stack_heads(v), ones], axis=1)


def unstack_heads(x):
    n = x.shape[0] // 2
    lane = lax.broadcasted_iota(jnp.int32, (1, PAIR), 1) >> 6
    return jnp.where(lane == 0, x[:n], x[n:])


def head_sums(x, blocks):
    step = blocks.shape[0]
    groups = [dot(x[:, i : i + step].astype(BF), blocks) for i in range(0, x.shape[1], step)]
    return groups[0] if len(groups) == 1 else jnp.concatenate(groups, axis=1)


def unit(x, blocks):
    scale = lax.rsqrt(head_sums(x * x, blocks) + EPS)
    return x * scale, scale


def id_mask(id_query, id_keys):
    keys = jnp.concatenate([id_keys] * 2, axis=0)
    row = dot_nt(jnp.full((8, 128), 1.0 / 128, BF), keys)[0:1]
    return id_query.astype(F32)[:, 0:1] == row


def pairs_of(x):
    return [x[:, i : i + PAIR] for i in range(0, x.shape[1], PAIR)]


def attend(windows):
    scores = [
        [dot_nt(qp, stack_heads(kp)) for qp, kp in zip(pairs_of(q), pairs_of(k))]
        for q, k, _, _ in windows
    ]
    es = [
        [jnp.where(w[3], jnp.exp2(s), 0.0).astype(BF) for s in group]
        for w, group in zip(windows, scores)
    ]
    both = [
        [dot(e, stack_values(vp)) for e, vp in zip(group, pairs_of(w[2]))]
        for w, group in zip(windows, es)
    ]
    return [
        ([b[:, :PAIR] for b in group], [b[:, PAIR:] for b in group], e)
        for group, e in zip(both, es)
    ]


def to_window_order(x_ref, pad_ref, to_a):
    pad_ref[...] = jnp.zeros_like(pad_ref)
    pad_ref[:, 0:ROWS, :] = x_ref[0]
    natural = pad_ref[...].reshape(NAT, x_ref.shape[3])
    return dot(to_a, natural).astype(BF)


def window_ids(reg, a_row, a_col):
    table = (reg + 1).astype(F32).astype(BF)
    picked = (dot(a_col, table) * a_row.astype(F32)).astype(BF)
    return dot(picked, jnp.ones((ROWS, 128), BF)).astype(BF)


def by_level(reg_ref):
    level = lax.axis_index("grp")
    low, high = reg_ref[:, 0, :], reg_ref[:, 1, :]
    own = jnp.where(level == 0, low, high)
    return own, low + high - own


def residual(x, att, w):
    y = dot(att, w)
    r = lax.rsqrt(jnp.mean(y * y, axis=1, keepdims=True) + EPS)
    n = y * r
    return (x.astype(F32) + n).astype(BF), n, r


WIDE = 2 * PAIR
SAVE = 11 * WIDE


def student_layer(x, w_qkv, w_out, ids, save_ref):
    blocks = head_blocks()
    qkv = dot(x, w_qkv)
    q, sq = unit(qkv[:, :WIDE], blocks)
    k, sk = unit(qkv[:, WIDE : 2 * WIDE], blocks)
    q = (q * SCALE).astype(BF)
    k = k.astype(BF)
    v = qkv[:, 2 * WIDE :].astype(BF)
    atts = []
    windows = [slice(w * WIN, (w + 1) * WIN) for w in range(4)]
    found = attend([(q[r], k[r], v[r], id_mask(ids[r], ids[r])) for r in windows])
    for rows, (nums, dens, es) in zip(windows, found):
        z = 1.0 / jnp.concatenate(dens, axis=1)
        att = jnp.concatenate(nums, axis=1) * z
        save_ref[rows, 4 * WIDE : 5 * WIDE] = z.astype(BF)
        for i, e in enumerate(es):
            save_ref[rows, (9 + i) * WIDE : (9 + i) * WIDE + 2 * WIN] = e
        atts.append(att.astype(BF))
    att = jnp.concatenate(atts, axis=0)
    h, n, r = residual(x, att, w_out)
    for i, part in ((0, q), (1, k), (2, v), (3, att), (5, sq), (6, sk), (7, n)):
        save_ref[:, i * WIDE : (i + 1) * WIDE] = part.astype(BF)
    save_ref[:, 8 * WIDE : 9 * WIDE] = jnp.broadcast_to(r, (NA, WIDE)).astype(BF)
    return h


def fetch(*pairs):
    copies = [pltpu.make_async_copy(*pair) for pair in pairs]
    for copy in copies:
        copy.start()
    return copies


def student_back(g, save_ref, w_qkv, w_out):
    blocks = head_blocks()
    part = lambda i: save_ref[:, i * WIDE : (i + 1) * WIDE]
    n, r = part(7).astype(F32), part(8).astype(F32)
    dy = r * (g - n * jnp.mean(g * n, axis=1, keepdims=True))
    datt = dot_nt(dy.astype(BF), w_out) * part(4).astype(F32)
    drop = (datt * part(3).astype(F32)).astype(BF) * jnp.asarray(-1.0, BF)
    datt = datt.astype(BF)
    q, k, v = part(0), part(1), part(2)
    windows = [slice(w * WIN, (w + 1) * WIN) for w in range(4)]
    blocks_of = [(r, slice(i, i + PAIR)) for r in windows for i in range(0, WIDE, PAIR)]
    es = [
        save_ref[r, (9 + i) * WIDE : (9 + i) * WIDE + 2 * WIN] for r in windows for i in range(2)
    ]
    dws = [
        dot_nt(jnp.concatenate([datt[r, p], drop[r, p]], axis=1), stack_values(v[r, p]))
        for r, p in blocks_of
    ]
    dv = [unstack_heads(dot_tn(e, datt[r, p])) for e, (r, p) in zip(es, blocks_of)]
    dss = [(e.astype(F32) * dw).astype(BF) for e, dw in zip(es, dws)]
    dq = [dot(ds, stack_heads(k[r, p])) for ds, (r, p) in zip(dss, blocks_of)]
    dk = [unstack_heads(dot_tn(ds, q[r, p])) for ds, (r, p) in zip(dss, blocks_of)]
    dqs, dks, dvs = [[x[i : i + 2] for i in range(0, len(x), 2)] for x in (dq, dk, dv)]
    dqs, dks, dvs = [[jnp.concatenate(x, axis=1) for x in y] for y in (dqs, dks, dvs)]
    dq = 10.0 * jnp.concatenate(dqs, axis=0)
    dk = (1.0 / LOG2E) * jnp.concatenate(dks, axis=0)
    dv = jnp.concatenate(dvs, axis=0)
    q_unit = q.astype(F32) * (1.0 / SCALE)
    k_unit = k.astype(F32)
    dq = part(5).astype(F32) * (dq - q_unit * head_sums(q_unit * dq, blocks))
    dk = part(6).astype(F32) * (dk - k_unit * head_sums(k_unit * dk, blocks))
    dqkv = jnp.concatenate([dq.astype(BF), dk.astype(BF), dv.astype(BF)], axis=1)
    return g + dot_nt(dqkv, w_qkv)


def teacher_own(
    x_hbm, reg_hbm, to_a_hbm, a_row_hbm, a_col_hbm, t_qkv,
    x_out, id_ref, far_id_ref, q_ref, k_ref, v_ref,
    pad_ref, x_ref, reg_ref, to_a, a_row, a_col, wqkv, sems,
):
    copies = fetch(
        (x_hbm, x_ref, sems.at[0]),
        (to_a_hbm, to_a, sems.at[2]),
        (reg_hbm, reg_ref, sems.at[1]),
        (a_row_hbm, a_row, sems.at[3]),
        (a_col_hbm, a_col, sems.at[4]),
        (t_qkv.at[0], wqkv, sems.at[5]),
    )
    width = x_ref.shape[3]
    blocks = head_blocks()
    copies[0].wait()
    copies[1].wait()
    x = to_window_order(x_ref, pad_ref, to_a[...])
    x_out[...] = x
    for copy in copies[2:5]:
        copy.wait()
    reg, reg_far = by_level(reg_ref)
    id_ref[...] = window_ids(reg, a_row[...], a_col[...])
    far_id_ref[...] = window_ids(reg_far, a_row[...], a_col[...])
    copies[5].wait()
    q_ref[...] = (unit(dot(x, wqkv[:, :width]), blocks)[0] * SCALE).astype(BF)
    k_ref[...] = unit(dot(x, wqkv[:, width : 2 * width]), blocks)[0].astype(BF)
    v_ref[...] = dot(x, wqkv[:, 2 * width :]).astype(BF)


def teacher_first(
    far_ref, x_ref, id_ref, far_id_ref, q_ref, k_ref, v_ref, to_a, a_to_g, pack, t_qkv, t_out,
    h_ref, g_ref, first_ref, second_ref, pad_ref, wout, sems,
):
    copies = fetch((t_out.at[0], wout, sems.at[0]))
    width = x_ref.shape[1]
    blocks = head_blocks()
    far = to_window_order(far_ref, pad_ref, to_a[...])
    k_far = unit(dot(far, t_qkv[0, :, width : 2 * width]), blocks)[0].astype(BF)
    v_far = dot(far, t_qkv[0, :, 2 * width :]).astype(BF)
    windows = []
    for w in range(4):
        rows = slice(w * WIN, (w + 1) * WIN)
        id_keys = jnp.concatenate([id_ref[rows], far_id_ref[rows]], axis=0)
        keys = [
            jnp.concatenate([near[rows], away[rows]], axis=0)
            for near, away in ((k_ref, k_far), (v_ref, v_far))
        ]
        windows.append((q_ref[rows], keys, (id_ref[rows], id_keys)))
    atts = window_attention(windows)
    copies[0].wait()
    h = residual(x_ref[...], jnp.concatenate(atts, axis=0), wout[...])[0]
    h_ref[...] = h
    spread = dot(a_to_g[...], jnp.concatenate([h, id_ref[...]], axis=1)).astype(BF)
    g_ref[...] = spread
    north, south = [
        packed(
            jnp.concatenate([part(spread, n) for n in names], axis=0),
            pack[...], ROW_TOKENS, ROW_SENT,
        )
        for names in (TO_NORTH, TO_SOUTH)
    ]
    first_ref[...], second_ref[...] = swapped("lat", north, south)


def swapped(axis, low, high):
    even = lax.rem(lax.axis_index(axis), 2) == 0
    low, high = low.astype(F32), high.astype(F32)
    return jnp.where(even, low, high).astype(BF), jnp.where(even, high, low).astype(BF)


def packed(rows, table, tokens, sent):
    width = rows.shape[1] - 128
    values = dot(table[:sent], rows[:, :width])
    ids = dot(table, rows[:, width:]).astype(BF)
    row = dot_nt(jnp.full((8, 128), 1.0 / 128, BF), ids)[0:1]
    row = jnp.concatenate([row, jnp.zeros((1, width - 128), F32)], axis=1)
    at = lax.broadcasted_iota(jnp.int32, (sent, 1), 0)
    return jnp.where(at == tokens, row, values).astype(BF)


def opened(sent, table, tokens):
    values = dot(table, sent).astype(BF)
    row = sent.astype(F32)[tokens : tokens + 1, : table.shape[1]]
    ids = dot((table.astype(F32) * row).astype(BF), jnp.ones((table.shape[1], 128), BF))
    return jnp.concatenate([values, ids.astype(BF)], axis=1)


def part(x, name):
    start, kept = AT[name]
    return x[start : start + kept]


TO_NORTH = ("nw", "n", "ne")
TO_SOUTH = ("sw", "s", "se")
TO_WEST = (("N", "sw"), ("", "nw"), ("", "w"), ("", "sw"), ("S", "nw"))
TO_EAST = (("N", "se"), ("", "ne"), ("", "e"), ("", "se"), ("S", "ne"))
EXTRA = {
    "nw": (("N", "sw"), ("W", "ne"), ("NW", "se")),
    "n": (("N", "s"),),
    "ne": (("N", "se"), ("E", "nw"), ("NE", "sw")),
    "e": (("E", "w"),),
    "se": (("S", "ne"), ("E", "sw"), ("SE", "nw")),
    "s": (("S", "n"),),
    "sw": (("S", "nw"), ("W", "se"), ("SW", "ne")),
    "w": (("W", "e"),),
    "c": (),
}
LATE = ("nw", "ne", "e", "se", "sw", "w")
ORDER = [name for name, *_ in PARTS]


def _spots(items):
    spots, start = {}, 0
    for side, name in items:
        spots[side, name] = start
        start += AT[name][1]
    return spots


OWN = {("", name): AT[name][0] for name in ORDER}
EDGE = _spots([("N", n) for n in TO_SOUTH] + [("S", n) for n in TO_NORTH])
COME = _spots([(s + "E", n) for s, n in TO_WEST] + [(s + "W", n) for s, n in TO_EAST])
NE_ROWS = 2 * sum(AT[n][1] for n in TO_NORTH)


def gather(sources, items):
    blocks = []
    for item in items:
        for array, spots in sources:
            if item in spots:
                spot = spots[item]
                blocks.append(array[spot : spot + AT[item[1]][1]])
                break
    return blocks[0] if len(blocks) == 1 else jnp.concatenate(blocks, axis=0)


def window_attention(windows):
    found = attend([(q, k, v, id_mask(*ids)) for q, (k, v), ids in windows])
    return [
        jnp.concatenate([(n / d).astype(BF) for n, d in zip(nums, dens)], axis=1)
        for nums, dens, _ in found
    ]


def beside_rows(
    x_ref, id_ref, to_a, s_qkv, s_out, proj, g_ref, t_qkv, after_ref,
    g0_ref, save0, save1, q_ref, k_ref, v_ref, att_ref, pad_ref,
):
    width = g_ref.shape[1] - 128
    blocks = head_blocks()
    x = to_window_order(x_ref, pad_ref, to_a[...])
    h = student_layer(x, s_qkv[0], s_out[0], id_ref[...], save0)
    h = student_layer(h, s_qkv[1], s_out[1], id_ref[...], save1)
    predicted = dot(h, proj[...])
    g0_ref[...] = dot_nt(predicted.astype(BF), proj[...])

    rows = g_ref[:, :width]
    q = (unit(dot(rows, t_qkv[1, :, :width]), blocks)[0] * SCALE).astype(BF)
    k = unit(dot(rows, t_qkv[1, :, width : 2 * width]), blocks)[0].astype(BF)
    v = dot(rows, t_qkv[1, :, 2 * width :]).astype(BF)
    q_ref[...] = q
    k_ref[...] = k
    v_ref[...] = v
    ids = part(g_ref, "c")[:, width:]
    [att_ref[...]] = window_attention([(part(q, "c"), [part(k, "c"), part(v, "c")], (ids, ids))])


def send_columns(
    g_ref, second_ref, first_ref, open_rows, pack, after_ref, edge_ref, out_first, out_second
):
    width = first_ref.shape[1]
    lat = lax.axis_index("lat")
    blocks = []
    inside = (lat > 0, lat < lax.axis_size("lat") - 1)
    for sent, there in zip(swapped("lat", first_ref[...], second_ref[...]), inside):
        rows = opened(sent, open_rows[...], ROW_TOKENS)
        ids = rows[:, width:] * jnp.where(there, 1.0, 0.0).astype(BF)
        blocks.append(jnp.concatenate([rows[:, :width], ids], axis=1))
    edge = jnp.concatenate(blocks, axis=0)
    edge_ref[...] = edge
    west, east = [
        packed(
            gather([(g_ref, OWN), (edge, EDGE)], items), pack[...], COL_TOKENS, COL_SENT
        )
        for items in (TO_WEST, TO_EAST)
    ]
    out_first[...], out_second[...] = swapped("lon", west, east)


def beside_columns(
    g_ref, edge_ref, t_qkv, q_ref, k_ref, v_ref, k_out, v_out, n_ref, s_ref
):
    width = g_ref.shape[1] - 128
    blocks = head_blocks()
    rows = edge_ref[:, :width]
    k = unit(dot(rows, t_qkv[1, :, width : 2 * width]), blocks)[0].astype(BF)
    v = dot(rows, t_qkv[1, :, 2 * width :]).astype(BF)
    k_out[...] = k
    v_out[...] = v
    windows = []
    for name in ("n", "s"):
        items = (("", name),) + EXTRA[name]
        keys = [gather([(own, OWN), (edge, EDGE)], items) for own, edge in ((k_ref, k), (v_ref, v))]
        ids = [gather([(g_ref, OWN), (edge_ref, EDGE)], some)[:, width:] for some in (items[:1], items)]
        windows.append((part(q_ref, name), keys, ids))
    n_ref[...], s_ref[...] = window_attention(windows)


def teacher_second(
    h_ref, g_ref, edge_ref, second_ref, first_ref, q_ref, k_ref, v_ref, k_edge, v_edge,
    c_ref, n_ref, s_ref, open_cols, from_a, g_to_a, t_qkv, t_out, proj, s_qkv, s_out,
    g0_ref, save0, save1, out_ref, grad_ref,
):
    width = h_ref.shape[1]
    blocks = head_blocks()
    west, east = swapped("lon", first_ref[...], second_ref[...])
    came = [opened(sent, open_cols[...], COL_TOKENS) for sent in (east, west)]
    came = jnp.concatenate(came, axis=0)
    rows = came[:, :width]
    k = unit(dot(rows, t_qkv[1, :, width : 2 * width]), blocks)[0].astype(BF)
    v = dot(rows, t_qkv[1, :, 2 * width :]).astype(BF)
    atts = {"c": c_ref[...], "n": n_ref[...], "s": s_ref[...]}
    windows = []
    for name in LATE:
        items = (("", name),) + EXTRA[name]
        keys = [
            gather([(own, OWN), (edge, EDGE), (new, COME)], items)
            for own, edge, new in ((k_ref, k_edge, k), (v_ref, v_edge, v))
        ]
        ids = [
            gather([(g_ref, OWN), (edge_ref, EDGE), (came, COME)], some)[:, width:]
            for some in (items[:1], items)
        ]
        windows.append((part(q_ref, name), keys, ids))
    atts.update(zip(LATE, window_attention(windows)))
    att = jnp.concatenate([atts[name] for name in ORDER], axis=0)
    att = dot(g_to_a[...], att).astype(BF)
    teacher = residual(h_ref[...], att, t_out[1])[0]
    natural = dot(from_a[...], teacher).astype(BF)
    out_ref[0] = natural.reshape(COLS, TALL, width)[:, :ROWS, :]

    g = g0_ref[...] - dot_nt(teacher, proj[...])
    g = student_back(g, save1, s_qkv[1], s_out[1])
    g = student_back(g, save0, s_qkv[0], s_out[0])
    high = g.astype(BF)
    low = (g - high.astype(F32)).astype(BF)
    natural = dot(from_a[...], high) + dot(from_a[...], low)
    grad_ref[0] = natural.reshape(COLS, TALL, g.shape[1])[:, :ROWS, :]


VMEM = pl.BlockSpec(memory_space=pltpu.VMEM)
ANY = pl.BlockSpec(memory_space=pl.ANY)
HBM = pl.BlockSpec(memory_space=pltpu.HBM)


def call(kernel, name, outs, specs, args, scratch=(), flops=0):
    shapes = [jax.ShapeDtypeStruct(s, d) for s, d in outs]
    touched = sum(a.size * a.dtype.itemsize for a in args)
    return pl.pallas_call(
        kernel,
        name=name,
        out_shape=shapes,
        in_specs=specs,
        out_specs=[VMEM] * len(outs),
        scratch_shapes=list(scratch),
        compiler_params=pltpu.CompilerParams(vmem_limit_bytes=28 << 20),
        cost_estimate=pl.CostEstimate(flops=flops, bytes_accessed=touched, transcendentals=0),
    )(*args)


def buffers(*arrays):
    return [pltpu.VMEM(a.shape, a.dtype) for a in arrays] + [
        pltpu.SemaphoreType.DMA((len(arrays),))
    ]


def swaps(size, start):
    route = {}
    for i in range(start, size, 2):
        j = (i + 1) % size
        route[i], route[j] = j, i
    return sorted(route.items())


def shards(teacher_in, student_in, regions, t_qkv, t_out, s_qkv, s_out, s_proj):
    width, narrow = teacher_in.shape[3], student_in.shape[3]
    lat_size, lon_size = lax.axis_size("lat"), lax.axis_size("lon")
    wide = width + 128
    teacher_in = teacher_in.transpose(0, 2, 1, 3)
    student_in = student_in.transpose(0, 2, 1, 3)
    regions = regions.transpose(2, 0, 1)
    far = lax.ppermute(teacher_in, "grp", [(0, 1), (1, 0)])

    pinned = [
        pltpu.with_memory_space_constraint(jnp.asarray(a), pltpu.HBM)
        for a in (teacher_in, regions, TO_A, A_ROW, A_COL, t_qkv)
    ]
    x, ids, far_ids, q, k, v = call(
        teacher_own, "teacher_own",
        [((NA, width), BF), ((NA, 128), BF), ((NA, 128), BF)] + [((NA, width), BF)] * 3,
        [HBM] * 6, pinned,
        [pltpu.VMEM((COLS, TALL, width), BF)]
        + buffers(teacher_in, regions, TO_A, A_ROW, A_COL, t_qkv[0]),
        10**9,
    )
    hidden, spread, rows_1, rows_2 = call(
        teacher_first, "teacher_first",
        [((NA, width), BF), ((NG, wide), BF)] + [((ROW_SENT, width), BF)] * 2,
        [VMEM] * 11 + [HBM],
        [far, x, ids, far_ids, q, k, v, TO_A, A_TO_G, PACK_ROWS, t_qkv]
        + [pltpu.with_memory_space_constraint(t_out, pltpu.HBM)],
        [pltpu.VMEM((COLS, TALL, width), BF)] + buffers(t_out[0]), 3 * 10**9,
    )
    rows_2 = lax.ppermute(rows_2, "lat", swaps(lat_size, 0))
    rows_1 = lax.ppermute(rows_1, "lat", swaps(lat_size, 1))

    g0, save0, save1, q, k, v, c_att = call(
        beside_rows, "beside_rows",
        [((NA, narrow), F32), ((NA, SAVE), BF), ((NA, SAVE), BF)]
        + [((NG, width), BF)] * 3 + [((AT["c"][1], width), BF)],
        [VMEM] * 8 + [ANY],
        [student_in, ids, TO_A, s_qkv, s_out, s_proj, spread, t_qkv, hidden],
        [pltpu.VMEM((COLS, TALL, narrow), BF)], 5 * 10**9,
    )
    edge, cols_1, cols_2 = call(
        send_columns, "send_columns",
        [((NE_ROWS, wide), BF)] + [((COL_SENT, width), BF)] * 2,
        [VMEM] * 5 + [ANY],
        [spread, rows_2, rows_1, OPEN_ROWS, PACK_COLS, g0], (), 10**7,
    )
    cols_2 = lax.ppermute(cols_2, "lon", swaps(lon_size, 0))
    cols_1 = lax.ppermute(cols_1, "lon", swaps(lon_size, 1))

    k_edge, v_edge, n_att, s_att = call(
        beside_columns, "beside_columns",
        [((NE_ROWS, width), BF)] * 2 + [((AT["n"][1], width), BF)] * 2,
        [VMEM] * 6,
        [spread, edge, t_qkv, q, k, v], (), 2 * 10**9,
    )
    args = [hidden, spread, edge, cols_2, cols_1, q, k, v, k_edge, v_edge, c_att, n_att, s_att]
    args += [OPEN_COLS, FROM_A, G_TO_A, t_qkv, t_out, s_proj, s_qkv, s_out, g0, save0, save1]
    out, grad = call(
        teacher_second, "teacher_second",
        [(teacher_in.shape, BF), (student_in.shape, F32)],
        [VMEM] * len(args), args, (), 6 * 10**9,
    )
    return out.transpose(0, 2, 1, 3), grad.transpose(0, 2, 1, 3)


def solution(mesh):
    tiles = P("grp", "lat", "lon", None)
    return jax.shard_map(
        shards,
        mesh=mesh,
        in_specs=(tiles, tiles, P(None, "lat", "lon"), P(), P(), P(), P(), P()),
        out_specs=(tiles, tiles),
        check_vma=False,
    )
```

```python
import functools

import jax
import jax.numpy as jnp
import ml_dtypes
import numpy as np
from jax import lax
from jax.experimental import pallas as pl
from jax.experimental.pallas import tpu as pltpu
from jax.sharding import PartitionSpec as P

HEADS_T = 8
HEADS_S = 4
EPS = 1e-06
LOG2E = 1.4426950408889634
SCALE = 10.0 * LOG2E
BF = jnp.bfloat16
F32 = jnp.float32

ROWS, COLS = 24, 12
WIN = 80
NA = 4 * WIN
TALL = 32
NAT = COLS * TALL
PAIR = 128

PARTS = (
    ("nw", (0, 6), (0, 3), 32),
    ("n", (0, 6), (3, 9), 48),
    ("ne", (0, 6), (9, 12), 32),
    ("e", (6, 18), (9, 12), 48),
    ("se", (18, 24), (9, 12), 32),
    ("s", (18, 24), (3, 9), 48),
    ("sw", (18, 24), (0, 3), 32),
    ("w", (6, 18), (0, 3), 48),
    ("c", (6, 18), (3, 9), 80),
)
AT = {}
NG = 0
for _name, _r, _c, _kept in PARTS:
    AT[_name] = (NG, _kept)
    NG += _kept


def _a_slot(r, c):
    return (2 * (r // 12) + c // 6) * WIN + (r % 12) * 6 + c % 6


def _tables():
    to_a = np.zeros((NA, NAT), ml_dtypes.bfloat16)
    a_row = np.zeros((NA, ROWS), ml_dtypes.bfloat16)
    a_col = np.zeros((NA, COLS), ml_dtypes.bfloat16)
    for r in range(ROWS):
        for c in range(COLS):
            slot = _a_slot(r, c)
            to_a[slot, c * TALL + r] = 1
            a_row[slot, r] = 1
            a_col[slot, c] = 1
    a_to_g = np.zeros((NG, NA), ml_dtypes.bfloat16)
    for name, (r0, r1), (c0, c1), _ in PARTS:
        spot = AT[name][0]
        for r in range(r0, r1):
            for c in range(c0, c1):
                a_to_g[spot, _a_slot(r, c)] = 1
                spot += 1
    return to_a, a_row, a_col, a_to_g


TO_A, A_ROW, A_COL, A_TO_G = _tables()
FROM_A = np.ascontiguousarray(TO_A.T)
G_TO_A = np.ascontiguousarray(A_TO_G.T)


def _packing(kept):
    table = np.zeros((128, sum(kept)), ml_dtypes.bfloat16)
    token, start = 0, 0
    for rows in kept:
        count = {32: 18, 48: 36}[rows]
        for i in range(count):
            table[token + i, start + i] = 1
        token, start = token + count, start + rows
    return table


PACK_ROWS = _packing((32, 48, 32))
PACK_COLS = _packing((32, 32, 48, 32, 32))
ROW_TOKENS, ROW_SENT = 72, 80
COL_TOKENS, COL_SENT = 108, 112
OPEN_ROWS = np.ascontiguousarray(PACK_ROWS.T[:, :ROW_SENT])
OPEN_COLS = np.ascontiguousarray(PACK_COLS.T[:, :COL_SENT])


def dot(a, b):
    return jnp.dot(a, b, preferred_element_type=F32)


def dot_nt(a, b):
    return lax.dot_general(a, b, (((1,), (1,)), ((), ())), preferred_element_type=F32)


def dot_tn(a, b):
    return lax.dot_general(a, b, (((0,), (0,)), ((), ())), preferred_element_type=F32)


def head_lanes(rows, h):
    lane = lax.broadcasted_iota(jnp.int32, (rows, PAIR), 1)
    return jnp.where((lane >> 6) == h, 1.0, 0.0).astype(BF)


def head_blocks():
    row = lax.broadcasted_iota(jnp.int32, (2 * PAIR, 2 * PAIR), 0)
    lane = lax.broadcasted_iota(jnp.int32, (2 * PAIR, 2 * PAIR), 1)
    return jnp.where((row >> 6) == (lane >> 6), 1.0, 0.0).astype(BF)


def stack_heads(x):
    return jnp.concatenate([x * head_lanes(1, h) for h in range(2)], axis=0)


def stack_values(v):
    rows = v.shape[0]
    ones = jnp.concatenate([head_lanes(rows, h) for h in range(2)], axis=0)
    return jnp.concatenate([stack_heads(v), ones], axis=1)


def unstack_heads(x):
    n = x.shape[0] // 2
    lane = lax.broadcasted_iota(jnp.int32, (1, PAIR), 1) >> 6
    return jnp.where(lane == 0, x[:n], x[n:])


def head_sums(x, blocks):
    step = blocks.shape[0]
    groups = [dot(x[:, i : i + step].astype(BF), blocks) for i in range(0, x.shape[1], step)]
    return groups[0] if len(groups) == 1 else jnp.concatenate(groups, axis=1)


def unit(x, blocks):
    scale = lax.rsqrt(head_sums(x * x, blocks) + EPS)
    return x * scale, scale


def id_mask(id_query, id_keys):
    keys = jnp.concatenate([id_keys] * 2, axis=0)
    row = dot_nt(jnp.full((8, 128), 1.0 / 128, BF), keys)[0:1]
    return id_query.astype(F32)[:, 0:1] == row


def pairs_of(x):
    return [x[:, i : i + PAIR] for i in range(0, x.shape[1], PAIR)]


def attend(windows):
    scores = [
        [dot_nt(qp, stack_heads(kp)) for qp, kp in zip(pairs_of(q), pairs_of(k))]
        for q, k, _, _ in windows
    ]
    es = [
        [jnp.where(w[3], jnp.exp2(s), 0.0).astype(BF) for s in group]
        for w, group in zip(windows, scores)
    ]
    both = [
        [dot(e, stack_values(vp)) for e, vp in zip(group, pairs_of(w[2]))]
        for w, group in zip(windows, es)
    ]
    return [
        ([b[:, :PAIR] for b in group], [b[:, PAIR:] for b in group], e)
        for group, e in zip(both, es)
    ]


def to_window_order(x_ref, pad_ref, to_a):
    pad_ref[...] = jnp.zeros_like(pad_ref)
    pad_ref[:, 0:ROWS, :] = x_ref[0]
    natural = pad_ref[...].reshape(NAT, x_ref.shape[3])
    return dot(to_a, natural).astype(BF)


def window_ids(reg, a_row, a_col):
    table = (reg + 1).astype(F32).astype(BF)
    picked = (dot(a_col, table) * a_row.astype(F32)).astype(BF)
    return dot(picked, jnp.ones((ROWS, 128), BF)).astype(BF)


def by_level(reg_ref):
    level = lax.axis_index("grp")
    low, high = reg_ref[:, 0, :], reg_ref[:, 1, :]
    own = jnp.where(level == 0, low, high)
    return own, low + high - own


def residual(x, att, w):
    y = dot(att, w)
    r = lax.rsqrt(jnp.mean(y * y, axis=1, keepdims=True) + EPS)
    n = y * r
    return (x.astype(F32) + n).astype(BF), n, r


WIDE = 2 * PAIR
SAVE = 11 * WIDE


def student_layer(x, w_qkv, w_out, ids, save_ref):
    blocks = head_blocks()
    qkv = dot(x, w_qkv)
    q, sq = unit(qkv[:, :WIDE], blocks)
    k, sk = unit(qkv[:, WIDE : 2 * WIDE], blocks)
    q = (q * SCALE).astype(BF)
    k = k.astype(BF)
    v = qkv[:, 2 * WIDE :].astype(BF)
    atts = []
    windows = [slice(w * WIN, (w + 1) * WIN) for w in range(4)]
    found = attend([(q[r], k[r], v[r], id_mask(ids[r], ids[r])) for r in windows])
    for rows, (nums, dens, es) in zip(windows, found):
        z = 1.0 / jnp.concatenate(dens, axis=1)
        att = jnp.concatenate(nums, axis=1) * z
        save_ref[rows, 4 * WIDE : 5 * WIDE] = z.astype(BF)
        for i, e in enumerate(es):
            save_ref[rows, (9 + i) * WIDE : (9 + i) * WIDE + 2 * WIN] = e
        atts.append(att.astype(BF))
    att = jnp.concatenate(atts, axis=0)
    h, n, r = residual(x, att, w_out)
    for i, part in ((0, q), (1, k), (2, v), (3, att), (5, sq), (6, sk), (7, n)):
        save_ref[:, i * WIDE : (i + 1) * WIDE] = part.astype(BF)
    save_ref[:, 8 * WIDE : 9 * WIDE] = jnp.broadcast_to(r, (NA, WIDE)).astype(BF)
    return h


def fetch(*pairs):
    copies = [pltpu.make_async_copy(*pair) for pair in pairs]
    for copy in copies:
        copy.start()
    return copies


def student_back(g, save_ref, w_qkv, w_out):
    blocks = head_blocks()
    part = lambda i: save_ref[:, i * WIDE : (i + 1) * WIDE]
    n, r = part(7).astype(F32), part(8).astype(F32)
    dy = r * (g - n * jnp.mean(g * n, axis=1, keepdims=True))
    datt = dot_nt(dy.astype(BF), w_out) * part(4).astype(F32)
    drop = (datt * part(3).astype(F32)).astype(BF) * jnp.asarray(-1.0, BF)
    datt = datt.astype(BF)
    q, k, v = part(0), part(1), part(2)
    windows = [slice(w * WIN, (w + 1) * WIN) for w in range(4)]
    blocks_of = [(r, slice(i, i + PAIR)) for r in windows for i in range(0, WIDE, PAIR)]
    es = [
        save_ref[r, (9 + i) * WIDE : (9 + i) * WIDE + 2 * WIN] for r in windows for i in range(2)
    ]
    dws = [
        dot_nt(jnp.concatenate([datt[r, p], drop[r, p]], axis=1), stack_values(v[r, p]))
        for r, p in blocks_of
    ]
    dv = [unstack_heads(dot_tn(e, datt[r, p])) for e, (r, p) in zip(es, blocks_of)]
    dss = [(e.astype(F32) * dw).astype(BF) for e, dw in zip(es, dws)]
    dq = [dot(ds, stack_heads(k[r, p])) for ds, (r, p) in zip(dss, blocks_of)]
    dk = [unstack_heads(dot_tn(ds, q[r, p])) for ds, (r, p) in zip(dss, blocks_of)]
    dqs, dks, dvs = [[x[i : i + 2] for i in range(0, len(x), 2)] for x in (dq, dk, dv)]
    dqs, dks, dvs = [[jnp.concatenate(x, axis=1) for x in y] for y in (dqs, dks, dvs)]
    dq = 10.0 * jnp.concatenate(dqs, axis=0)
    dk = (1.0 / LOG2E) * jnp.concatenate(dks, axis=0)
    dv = jnp.concatenate(dvs, axis=0)
    q_unit = q.astype(F32) * (1.0 / SCALE)
    k_unit = k.astype(F32)
    dq = part(5).astype(F32) * (dq - q_unit * head_sums(q_unit * dq, blocks))
    dk = part(6).astype(F32) * (dk - k_unit * head_sums(k_unit * dk, blocks))
    dqkv = jnp.concatenate([dq.astype(BF), dk.astype(BF), dv.astype(BF)], axis=1)
    return g + dot_nt(dqkv, w_qkv)


def teacher_own(
    x_hbm, reg_hbm, to_a_hbm, a_row_hbm, a_col_hbm, t_qkv,
    x_out, id_ref, far_id_ref, q_ref, k_ref, v_ref,
    pad_ref, x_ref, reg_ref, to_a, a_row, a_col, wqkv, sems,
):
    copies = fetch(
        (x_hbm, x_ref, sems.at[0]),
        (to_a_hbm, to_a, sems.at[2]),
        (reg_hbm, reg_ref, sems.at[1]),
        (a_row_hbm, a_row, sems.at[3]),
        (a_col_hbm, a_col, sems.at[4]),
        (t_qkv.at[0], wqkv, sems.at[5]),
    )
    width = x_ref.shape[3]
    blocks = head_blocks()
    copies[0].wait()
    copies[1].wait()
    x = to_window_order(x_ref, pad_ref, to_a[...])
    x_out[...] = x
    for copy in copies[2:5]:
        copy.wait()
    reg, reg_far = by_level(reg_ref)
    id_ref[...] = window_ids(reg, a_row[...], a_col[...])
    far_id_ref[...] = window_ids(reg_far, a_row[...], a_col[...])
    copies[5].wait()
    q_ref[...] = (unit(dot(x, wqkv[:, :width]), blocks)[0] * SCALE).astype(BF)
    k_ref[...] = unit(dot(x, wqkv[:, width : 2 * width]), blocks)[0].astype(BF)
    v_ref[...] = dot(x, wqkv[:, 2 * width :]).astype(BF)


def teacher_first(
    far_ref, x_ref, id_ref, far_id_ref, q_ref, k_ref, v_ref, to_a, a_to_g, pack, t_qkv, t_out,
    h_ref, g_ref, first_ref, second_ref, pad_ref, wout, sems,
):
    copies = fetch((t_out.at[0], wout, sems.at[0]))
    width = x_ref.shape[1]
    blocks = head_blocks()
    far = to_window_order(far_ref, pad_ref, to_a[...])
    k_far = unit(dot(far, t_qkv[0, :, width : 2 * width]), blocks)[0].astype(BF)
    v_far = dot(far, t_qkv[0, :, 2 * width :]).astype(BF)
    windows = []
    for w in range(4):
        rows = slice(w * WIN, (w + 1) * WIN)
        id_keys = jnp.concatenate([id_ref[rows], far_id_ref[rows]], axis=0)
        keys = [
            jnp.concatenate([near[rows], away[rows]], axis=0)
            for near, away in ((k_ref, k_far), (v_ref, v_far))
        ]
        windows.append((q_ref[rows], keys, (id_ref[rows], id_keys)))
    atts = window_attention(windows)
    copies[0].wait()
    h = residual(x_ref[...], jnp.concatenate(atts, axis=0), wout[...])[0]
    h_ref[...] = h
    spread = dot(a_to_g[...], jnp.concatenate([h, id_ref[...]], axis=1)).astype(BF)
    g_ref[...] = spread
    north, south = [
        packed(
            jnp.concatenate([part(spread, n) for n in names], axis=0),
            pack[...], ROW_TOKENS, ROW_SENT,
        )
        for names in (TO_NORTH, TO_SOUTH)
    ]
    first_ref[...], second_ref[...] = swapped("lat", north, south)


def swapped(axis, low, high):
    even = lax.rem(lax.axis_index(axis), 2) == 0
    low, high = low.astype(F32), high.astype(F32)
    return jnp.where(even, low, high).astype(BF), jnp.where(even, high, low).astype(BF)


def packed(rows, table, tokens, sent):
    width = rows.shape[1] - 128
    values = dot(table[:sent], rows[:, :width])
    ids = dot(table, rows[:, width:]).astype(BF)
    row = dot_nt(jnp.full((8, 128), 1.0 / 128, BF), ids)[0:1]
    row = jnp.concatenate([row, jnp.zeros((1, width - 128), F32)], axis=1)
    at = lax.broadcasted_iota(jnp.int32, (sent, 1), 0)
    return jnp.where(at == tokens, row, values).astype(BF)


def opened(sent, table, tokens):
    values = dot(table, sent).astype(BF)
    row = sent.astype(F32)[tokens : tokens + 1, : table.shape[1]]
    ids = dot((table.astype(F32) * row).astype(BF), jnp.ones((table.shape[1], 128), BF))
    return jnp.concatenate([values, ids.astype(BF)], axis=1)


def part(x, name):
    start, kept = AT[name]
    return x[start : start + kept]


TO_NORTH = ("nw", "n", "ne")
TO_SOUTH = ("sw", "s", "se")
TO_WEST = (("N", "sw"), ("", "nw"), ("", "w"), ("", "sw"), ("S", "nw"))
TO_EAST = (("N", "se"), ("", "ne"), ("", "e"), ("", "se"), ("S", "ne"))
EXTRA = {
    "nw": (("N", "sw"), ("W", "ne"), ("NW", "se")),
    "n": (("N", "s"),),
    "ne": (("N", "se"), ("E", "nw"), ("NE", "sw")),
    "e": (("E", "w"),),
    "se": (("S", "ne"), ("E", "sw"), ("SE", "nw")),
    "s": (("S", "n"),),
    "sw": (("S", "nw"), ("W", "se"), ("SW", "ne")),
    "w": (("W", "e"),),
    "c": (),
}
LATE = ("nw", "ne", "e", "se", "sw", "w")
ORDER = [name for name, *_ in PARTS]


def _spots(items):
    spots, start = {}, 0
    for side, name in items:
        spots[side, name] = start
        start += AT[name][1]
    return spots


OWN = {("", name): AT[name][0] for name in ORDER}
EDGE = _spots([("N", n) for n in TO_SOUTH] + [("S", n) for n in TO_NORTH])
COME = _spots([(s + "E", n) for s, n in TO_WEST] + [(s + "W", n) for s, n in TO_EAST])
NE_ROWS = 2 * sum(AT[n][1] for n in TO_NORTH)


def gather(sources, items):
    blocks = []
    for item in items:
        for array, spots in sources:
            if item in spots:
                spot = spots[item]
                blocks.append(array[spot : spot + AT[item[1]][1]])
                break
    return blocks[0] if len(blocks) == 1 else jnp.concatenate(blocks, axis=0)


def window_attention(windows):
    found = attend([(q, k, v, id_mask(*ids)) for q, (k, v), ids in windows])
    return [
        jnp.concatenate([(n / d).astype(BF) for n, d in zip(nums, dens)], axis=1)
        for nums, dens, _ in found
    ]


def beside_rows(
    x_ref, id_ref, to_a, s_qkv, s_out, proj, g_ref, t_qkv, after_ref,
    g0_ref, save0, save1, q_ref, k_ref, v_ref, att_ref, pad_ref,
):
    width = g_ref.shape[1] - 128
    blocks = head_blocks()
    x = to_window_order(x_ref, pad_ref, to_a[...])
    h = student_layer(x, s_qkv[0], s_out[0], id_ref[...], save0)
    h = student_layer(h, s_qkv[1], s_out[1], id_ref[...], save1)
    predicted = dot(h, proj[...])
    g0_ref[...] = dot_nt(predicted.astype(BF), proj[...])

    rows = g_ref[:, :width]
    q = (unit(dot(rows, t_qkv[1, :, :width]), blocks)[0] * SCALE).astype(BF)
    k = unit(dot(rows, t_qkv[1, :, width : 2 * width]), blocks)[0].astype(BF)
    v = dot(rows, t_qkv[1, :, 2 * width :]).astype(BF)
    q_ref[...] = q
    k_ref[...] = k
    v_ref[...] = v
    ids = part(g_ref, "c")[:, width:]
    [att_ref[...]] = window_attention([(part(q, "c"), [part(k, "c"), part(v, "c")], (ids, ids))])


def send_columns(
    g_ref, first_ref, second_ref, open_rows, pack, after_ref, edge_ref, out_first, out_second
):
    width = first_ref.shape[1]
    lat = lax.axis_index("lat")
    blocks = []
    inside = (lat > 0, lat < lax.axis_size("lat") - 1)
    for sent, there in zip(swapped("lat", first_ref[...], second_ref[...]), inside):
        rows = opened(sent, open_rows[...], ROW_TOKENS)
        ids = rows[:, width:] * jnp.where(there, 1.0, 0.0).astype(BF)
        blocks.append(jnp.concatenate([rows[:, :width], ids], axis=1))
    edge = jnp.concatenate(blocks, axis=0)
    edge_ref[...] = edge
    west, east = [
        packed(
            gather([(g_ref, OWN), (edge, EDGE)], items), pack[...], COL_TOKENS, COL_SENT
        )
        for items in (TO_WEST, TO_EAST)
    ]
    out_first[...], out_second[...] = swapped("lon", west, east)


def beside_columns(
    g_ref, edge_ref, t_qkv, q_ref, k_ref, v_ref, k_out, v_out, n_ref, s_ref
):
    width = g_ref.shape[1] - 128
    blocks = head_blocks()
    rows = edge_ref[:, :width]
    k = unit(dot(rows, t_qkv[1, :, width : 2 * width]), blocks)[0].astype(BF)
    v = dot(rows, t_qkv[1, :, 2 * width :]).astype(BF)
    k_out[...] = k
    v_out[...] = v
    windows = []
    for name in ("n", "s"):
        items = (("", name),) + EXTRA[name]
        keys = [gather([(own, OWN), (edge, EDGE)], items) for own, edge in ((k_ref, k), (v_ref, v))]
        ids = [gather([(g_ref, OWN), (edge_ref, EDGE)], some)[:, width:] for some in (items[:1], items)]
        windows.append((part(q_ref, name), keys, ids))
    n_ref[...], s_ref[...] = window_attention(windows)


def teacher_second(
    h_ref, g_ref, edge_ref, first_ref, second_ref, q_ref, k_ref, v_ref, k_edge, v_edge,
    c_ref, n_ref, s_ref, open_cols, from_a, g_to_a, t_qkv, t_out, proj, s_qkv, s_out,
    g0_ref, save0, save1, out_hbm, grad_hbm, out_ref, grad_ref, sems,
):
    width = h_ref.shape[1]
    blocks = head_blocks()
    west, east = swapped("lon", first_ref[...], second_ref[...])
    came = [opened(sent, open_cols[...], COL_TOKENS) for sent in (east, west)]
    came = jnp.concatenate(came, axis=0)
    rows = came[:, :width]
    k = unit(dot(rows, t_qkv[1, :, width : 2 * width]), blocks)[0].astype(BF)
    v = dot(rows, t_qkv[1, :, 2 * width :]).astype(BF)
    atts = {"c": c_ref[...], "n": n_ref[...], "s": s_ref[...]}
    windows = []
    for name in LATE:
        items = (("", name),) + EXTRA[name]
        keys = [
            gather([(own, OWN), (edge, EDGE), (new, COME)], items)
            for own, edge, new in ((k_ref, k_edge, k), (v_ref, v_edge, v))
        ]
        ids = [
            gather([(g_ref, OWN), (edge_ref, EDGE), (came, COME)], some)[:, width:]
            for some in (items[:1], items)
        ]
        windows.append((part(q_ref, name), keys, ids))
    atts.update(zip(LATE, window_attention(windows)))
    att = jnp.concatenate([atts[name] for name in ORDER], axis=0)
    att = dot(g_to_a[...], att).astype(BF)
    teacher = residual(h_ref[...], att, t_out[1])[0]
    natural = dot(from_a[...], teacher).astype(BF)
    out_ref[0] = natural.reshape(COLS, TALL, width)[:, :ROWS, :]
    copies = fetch((out_ref, out_hbm, sems.at[0]))

    g = g0_ref[...] - dot_nt(teacher, proj[...])
    g = student_back(g, save1, s_qkv[1], s_out[1])
    g = student_back(g, save0, s_qkv[0], s_out[0])
    high = g.astype(BF)
    low = (g - high.astype(F32)).astype(BF)
    half = COLS // 2
    for i in range(2):
        table = from_a[i * half * TALL : (i + 1) * half * TALL]
        natural = dot(table, high) + dot(table, low)
        cols = pl.ds(i * half, half)
        grad_ref[0, cols] = natural.reshape(half, TALL, g.shape[1])[:, :ROWS, :]
        copies += fetch((grad_ref.at[0, cols], grad_hbm.at[0, cols], sems.at[1 + i]))
    for copy in copies:
        copy.wait()


VMEM = pl.BlockSpec(memory_space=pltpu.VMEM)
ANY = pl.BlockSpec(memory_space=pl.ANY)
HBM = pl.BlockSpec(memory_space=pltpu.HBM)


def call(kernel, name, outs, specs, args, scratch=(), flops=0, out_space=VMEM):
    shapes = [jax.ShapeDtypeStruct(s, d) for s, d in outs]
    touched = sum(a.size * a.dtype.itemsize for a in args)
    return pl.pallas_call(
        kernel,
        name=name,
        out_shape=shapes,
        in_specs=specs,
        out_specs=[out_space] * len(outs),
        scratch_shapes=list(scratch),
        compiler_params=pltpu.CompilerParams(vmem_limit_bytes=28 << 20),
        cost_estimate=pl.CostEstimate(flops=flops, bytes_accessed=touched, transcendentals=0),
    )(*args)


def buffers(*arrays):
    return [pltpu.VMEM(a.shape, a.dtype) for a in arrays] + [
        pltpu.SemaphoreType.DMA((len(arrays),))
    ]


def swaps(size, start):
    route = {}
    for i in range(start, size, 2):
        j = (i + 1) % size
        route[i], route[j] = j, i
    return sorted(route.items())


def shards(teacher_in, student_in, regions, t_qkv, t_out, s_qkv, s_out, s_proj):
    width, narrow = teacher_in.shape[3], student_in.shape[3]
    lat_size, lon_size = lax.axis_size("lat"), lax.axis_size("lon")
    wide = width + 128
    teacher_in = teacher_in.transpose(0, 2, 1, 3)
    student_in = student_in.transpose(0, 2, 1, 3)
    regions = regions.transpose(2, 0, 1)
    far = lax.ppermute(teacher_in, "grp", [(0, 1), (1, 0)])

    pinned = [
        pltpu.with_memory_space_constraint(jnp.asarray(a), pltpu.HBM)
        for a in (teacher_in, regions, TO_A, A_ROW, A_COL, t_qkv)
    ]
    x, ids, far_ids, q, k, v = call(
        teacher_own, "teacher_own",
        [((NA, width), BF), ((NA, 128), BF), ((NA, 128), BF)] + [((NA, width), BF)] * 3,
        [HBM] * 6, pinned,
        [pltpu.VMEM((COLS, TALL, width), BF)]
        + buffers(teacher_in, regions, TO_A, A_ROW, A_COL, t_qkv[0]),
        10**9,
    )
    hidden, spread, rows_1, rows_2 = call(
        teacher_first, "teacher_first",
        [((NA, width), BF), ((NG, wide), BF)] + [((ROW_SENT, width), BF)] * 2,
        [VMEM] * 11 + [HBM],
        [far, x, ids, far_ids, q, k, v, TO_A, A_TO_G, PACK_ROWS, t_qkv]
        + [pltpu.with_memory_space_constraint(t_out, pltpu.HBM)],
        [pltpu.VMEM((COLS, TALL, width), BF)] + buffers(t_out[0]), 3 * 10**9,
    )
    rows_2 = lax.ppermute(rows_2, "lat", swaps(lat_size, 0))
    rows_1 = lax.ppermute(rows_1, "lat", swaps(lat_size, 1))

    g0, save0, save1, q, k, v, c_att = call(
        beside_rows, "beside_rows",
        [((NA, narrow), F32), ((NA, SAVE), BF), ((NA, SAVE), BF)]
        + [((NG, width), BF)] * 3 + [((AT["c"][1], width), BF)],
        [VMEM] * 8 + [ANY],
        [student_in, ids, TO_A, s_qkv, s_out, s_proj, spread, t_qkv, hidden],
        [pltpu.VMEM((COLS, TALL, narrow), BF)], 5 * 10**9,
    )
    edge, cols_1, cols_2 = call(
        send_columns, "send_columns",
        [((NE_ROWS, wide), BF)] + [((COL_SENT, width), BF)] * 2,
        [VMEM] * 5 + [ANY],
        [spread, rows_1, rows_2, OPEN_ROWS, PACK_COLS, g0], (), 10**7,
    )
    cols_2 = lax.ppermute(cols_2, "lon", swaps(lon_size, 0))
    cols_1 = lax.ppermute(cols_1, "lon", swaps(lon_size, 1))

    k_edge, v_edge, n_att, s_att = call(
        beside_columns, "beside_columns",
        [((NE_ROWS, width), BF)] * 2 + [((AT["n"][1], width), BF)] * 2,
        [VMEM] * 6,
        [spread, edge, t_qkv, q, k, v], (), 2 * 10**9,
    )
    args = [hidden, spread, edge, cols_1, cols_2, q, k, v, k_edge, v_edge, c_att, n_att, s_att]
    args += [OPEN_COLS, FROM_A, G_TO_A, t_qkv, t_out, s_proj, s_qkv, s_out, g0, save0, save1]
    out, grad = call(
        teacher_second, "teacher_second",
        [(teacher_in.shape, BF), (student_in.shape, F32)],
        [VMEM] * len(args), args,
        [
            pltpu.VMEM(teacher_in.shape, BF),
            pltpu.VMEM(student_in.shape, F32),
            pltpu.SemaphoreType.DMA((3,)),
        ],
        6 * 10**9, ANY,
    )
    return out.transpose(0, 2, 1, 3), grad.transpose(0, 2, 1, 3)


def solution(mesh):
    tiles = P("grp", "lat", "lon", None)
    return jax.shard_map(
        shards,
        mesh=mesh,
        in_specs=(tiles, tiles, P(None, "lat", "lon"), P(), P(), P(), P(), P()),
        out_specs=(tiles, tiles),
        check_vma=False,
    )
```

```python
import functools

import jax
import jax.numpy as jnp
import ml_dtypes
import numpy as np
from jax import lax
from jax.experimental import pallas as pl
from jax.experimental.pallas import tpu as pltpu
from jax.sharding import PartitionSpec as P

HEADS_T = 8
HEADS_S = 4
EPS = 1e-06
LOG2E = 1.4426950408889634
SCALE = 10.0 * LOG2E
BF = jnp.bfloat16
F32 = jnp.float32

ROWS, COLS = 24, 12
WIN = 80
NA = 4 * WIN
TALL = 32
NAT = COLS * TALL
PAIR = 128

PARTS = (
    ("nw", (0, 6), (0, 3), 32),
    ("n", (0, 6), (3, 9), 48),
    ("ne", (0, 6), (9, 12), 32),
    ("e", (6, 18), (9, 12), 48),
    ("se", (18, 24), (9, 12), 32),
    ("s", (18, 24), (3, 9), 48),
    ("sw", (18, 24), (0, 3), 32),
    ("w", (6, 18), (0, 3), 48),
    ("c", (6, 18), (3, 9), 80),
)
AT = {}
NG = 0
for _name, _r, _c, _kept in PARTS:
    AT[_name] = (NG, _kept)
    NG += _kept


def _a_slot(r, c):
    return (2 * (r // 12) + c // 6) * WIN + (r % 12) * 6 + c % 6


def _tables():
    to_a = np.zeros((NA, NAT), ml_dtypes.bfloat16)
    a_row = np.zeros((NA, ROWS), ml_dtypes.bfloat16)
    a_col = np.zeros((NA, COLS), ml_dtypes.bfloat16)
    for r in range(ROWS):
        for c in range(COLS):
            slot = _a_slot(r, c)
            to_a[slot, c * TALL + r] = 1
            a_row[slot, r] = 1
            a_col[slot, c] = 1
    a_to_g = np.zeros((NG, NA), ml_dtypes.bfloat16)
    for name, (r0, r1), (c0, c1), _ in PARTS:
        spot = AT[name][0]
        for r in range(r0, r1):
            for c in range(c0, c1):
                a_to_g[spot, _a_slot(r, c)] = 1
                spot += 1
    return to_a, a_row, a_col, a_to_g


TO_A, A_ROW, A_COL, A_TO_G = _tables()
FROM_A = np.ascontiguousarray(TO_A.T)
G_TO_A = np.ascontiguousarray(A_TO_G.T)


def _packing(kept):
    table = np.zeros((128, sum(kept)), ml_dtypes.bfloat16)
    token, start = 0, 0
    for rows in kept:
        count = {32: 18, 48: 36}[rows]
        for i in range(count):
            table[token + i, start + i] = 1
        token, start = token + count, start + rows
    return table


def _corners(start, west, east):
    table = np.zeros((256, ROW_SENT), ml_dtypes.bfloat16)
    for i in range(18):
        table[start + i, west + i] = 1
        table[128 + start + i, east + i] = 1
    return table


PACK_ROWS = _packing((32, 48, 32))
PACK_OWN = np.roll(PACK_ROWS, 18, axis=0)
PACK_COLS = _packing((32, 32, 48, 32, 32))
ROW_TOKENS, ROW_SENT = 72, 80
COL_TOKENS, COL_SENT = 108, 112
FROM_NORTH = _corners(0, 0, 54)
FROM_SOUTH = _corners(90, 0, 54)
OPEN_ROWS = np.ascontiguousarray(PACK_ROWS.T[:, :ROW_SENT])
OPEN_COLS = np.ascontiguousarray(PACK_COLS.T[:, :COL_SENT])


def dot(a, b):
    return jnp.dot(a, b, preferred_element_type=F32)


def dot_nt(a, b):
    return lax.dot_general(a, b, (((1,), (1,)), ((), ())), preferred_element_type=F32)


def dot_tn(a, b):
    return lax.dot_general(a, b, (((0,), (0,)), ((), ())), preferred_element_type=F32)


def head_lanes(rows, h):
    lane = lax.broadcasted_iota(jnp.int32, (rows, PAIR), 1)
    return jnp.where((lane >> 6) == h, 1.0, 0.0).astype(BF)


def head_blocks():
    row = lax.broadcasted_iota(jnp.int32, (2 * PAIR, 2 * PAIR), 0)
    lane = lax.broadcasted_iota(jnp.int32, (2 * PAIR, 2 * PAIR), 1)
    return jnp.where((row >> 6) == (lane >> 6), 1.0, 0.0).astype(BF)


def stack_heads(x):
    return jnp.concatenate([x * head_lanes(1, h) for h in range(2)], axis=0)


def stack_values(v):
    rows = v.shape[0]
    ones = jnp.concatenate([head_lanes(rows, h) for h in range(2)], axis=0)
    return jnp.concatenate([stack_heads(v), ones], axis=1)


def unstack_heads(x):
    n = x.shape[0] // 2
    lane = lax.broadcasted_iota(jnp.int32, (1, PAIR), 1) >> 6
    return jnp.where(lane == 0, x[:n], x[n:])


def head_sums(x, blocks):
    step = blocks.shape[0]
    groups = [dot(x[:, i : i + step].astype(BF), blocks) for i in range(0, x.shape[1], step)]
    return groups[0] if len(groups) == 1 else jnp.concatenate(groups, axis=1)


def unit(x, blocks):
    scale = lax.rsqrt(head_sums(x * x, blocks) + EPS)
    return x * scale, scale


def id_mask(id_query, id_keys):
    keys = jnp.concatenate([id_keys] * 2, axis=0)
    row = dot_nt(jnp.full((8, 128), 1.0 / 128, BF), keys)[0:1]
    return id_query.astype(F32)[:, 0:1] == row


def pairs_of(x):
    return [x[:, i : i + PAIR] for i in range(0, x.shape[1], PAIR)]


def attend(windows):
    scores = [
        [dot_nt(qp, stack_heads(kp)) for qp, kp in zip(pairs_of(q), pairs_of(k))]
        for q, k, _, _ in windows
    ]
    es = [
        [jnp.where(w[3], jnp.exp2(s), 0.0).astype(BF) for s in group]
        for w, group in zip(windows, scores)
    ]
    both = [
        [dot(e, stack_values(vp)) for e, vp in zip(group, pairs_of(w[2]))]
        for w, group in zip(windows, es)
    ]
    return [
        ([b[:, :PAIR] for b in group], [b[:, PAIR:] for b in group], e)
        for group, e in zip(both, es)
    ]


def to_window_order(x_ref, pad_ref, to_a):
    pad_ref[...] = jnp.zeros_like(pad_ref)
    pad_ref[:, 0:ROWS, :] = x_ref[0]
    natural = pad_ref[...].reshape(NAT, x_ref.shape[3])
    return dot(to_a, natural).astype(BF)


def window_ids(reg, a_row, a_col):
    table = (reg + 1).astype(F32).astype(BF)
    picked = (dot(a_col, table) * a_row.astype(F32)).astype(BF)
    return dot(picked, jnp.ones((ROWS, 128), BF)).astype(BF)


def by_level(reg_ref):
    level = lax.axis_index("grp")
    low, high = reg_ref[:, 0, :], reg_ref[:, 1, :]
    own = jnp.where(level == 0, low, high)
    return own, low + high - own


def residual(x, att, w):
    y = dot(att, w)
    r = lax.rsqrt(jnp.mean(y * y, axis=1, keepdims=True) + EPS)
    n = y * r
    return (x.astype(F32) + n).astype(BF), n, r


WIDE = 2 * PAIR
SAVE = 11 * WIDE


def student_layer(x, w_qkv, w_out, ids, save_ref):
    blocks = head_blocks()
    qkv = dot(x, w_qkv)
    q, sq = unit(qkv[:, :WIDE], blocks)
    k, sk = unit(qkv[:, WIDE : 2 * WIDE], blocks)
    q = (q * SCALE).astype(BF)
    k = k.astype(BF)
    v = qkv[:, 2 * WIDE :].astype(BF)
    atts = []
    windows = [slice(w * WIN, (w + 1) * WIN) for w in range(4)]
    found = attend([(q[r], k[r], v[r], id_mask(ids[r], ids[r])) for r in windows])
    for rows, (nums, dens, es) in zip(windows, found):
        z = 1.0 / jnp.concatenate(dens, axis=1)
        att = jnp.concatenate(nums, axis=1) * z
        save_ref[rows, 4 * WIDE : 5 * WIDE] = z.astype(BF)
        for i, e in enumerate(es):
            save_ref[rows, (9 + i) * WIDE : (9 + i) * WIDE + 2 * WIN] = e
        atts.append(att.astype(BF))
    att = jnp.concatenate(atts, axis=0)
    h, n, r = residual(x, att, w_out)
    for i, part in ((0, q), (1, k), (2, v), (3, att), (5, sq), (6, sk), (7, n)):
        save_ref[:, i * WIDE : (i + 1) * WIDE] = part.astype(BF)
    save_ref[:, 8 * WIDE : 9 * WIDE] = jnp.broadcast_to(r, (NA, WIDE)).astype(BF)
    return h


def fetch(*pairs):
    copies = [pltpu.make_async_copy(*pair) for pair in pairs]
    for copy in copies:
        copy.start()
    return copies


def student_back(g, save_ref, w_qkv, w_out):
    blocks = head_blocks()
    part = lambda i: save_ref[:, i * WIDE : (i + 1) * WIDE]
    n, r = part(7).astype(F32), part(8).astype(F32)
    dy = r * (g - n * jnp.mean(g * n, axis=1, keepdims=True))
    datt = dot_nt(dy.astype(BF), w_out) * part(4).astype(F32)
    drop = (datt * part(3).astype(F32)).astype(BF) * jnp.asarray(-1.0, BF)
    datt = datt.astype(BF)
    q, k, v = part(0), part(1), part(2)
    windows = [slice(w * WIN, (w + 1) * WIN) for w in range(4)]
    blocks_of = [(r, slice(i, i + PAIR)) for r in windows for i in range(0, WIDE, PAIR)]
    es = [
        save_ref[r, (9 + i) * WIDE : (9 + i) * WIDE + 2 * WIN] for r in windows for i in range(2)
    ]
    dws = [
        dot_nt(jnp.concatenate([datt[r, p], drop[r, p]], axis=1), stack_values(v[r, p]))
        for r, p in blocks_of
    ]
    dv = [unstack_heads(dot_tn(e, datt[r, p])) for e, (r, p) in zip(es, blocks_of)]
    dss = [(e.astype(F32) * dw).astype(BF) for e, dw in zip(es, dws)]
    dq = [dot(ds, stack_heads(k[r, p])) for ds, (r, p) in zip(dss, blocks_of)]
    dk = [unstack_heads(dot_tn(ds, q[r, p])) for ds, (r, p) in zip(dss, blocks_of)]
    dqs, dks, dvs = [[x[i : i + 2] for i in range(0, len(x), 2)] for x in (dq, dk, dv)]
    dqs, dks, dvs = [[jnp.concatenate(x, axis=1) for x in y] for y in (dqs, dks, dvs)]
    dq = 10.0 * jnp.concatenate(dqs, axis=0)
    dk = (1.0 / LOG2E) * jnp.concatenate(dks, axis=0)
    dv = jnp.concatenate(dvs, axis=0)
    q_unit = q.astype(F32) * (1.0 / SCALE)
    k_unit = k.astype(F32)
    dq = part(5).astype(F32) * (dq - q_unit * head_sums(q_unit * dq, blocks))
    dk = part(6).astype(F32) * (dk - k_unit * head_sums(k_unit * dk, blocks))
    dqkv = jnp.concatenate([dq.astype(BF), dk.astype(BF), dv.astype(BF)], axis=1)
    return g + dot_nt(dqkv, w_qkv)


def teacher_own(
    x_hbm, reg_hbm, to_a_hbm, a_row_hbm, a_col_hbm, t_qkv,
    x_out, id_ref, far_id_ref, q_ref, k_ref, v_ref,
    pad_ref, x_ref, reg_ref, to_a, a_row, a_col, wqkv, sems,
):
    copies = fetch(
        (x_hbm, x_ref, sems.at[0]),
        (to_a_hbm, to_a, sems.at[2]),
        (reg_hbm, reg_ref, sems.at[1]),
        (a_row_hbm, a_row, sems.at[3]),
        (a_col_hbm, a_col, sems.at[4]),
        (t_qkv.at[0], wqkv, sems.at[5]),
    )
    width = x_ref.shape[3]
    blocks = head_blocks()
    copies[0].wait()
    copies[1].wait()
    x = to_window_order(x_ref, pad_ref, to_a[...])
    x_out[...] = x
    for copy in copies[2:5]:
        copy.wait()
    reg, reg_far = by_level(reg_ref)
    id_ref[...] = window_ids(reg, a_row[...], a_col[...])
    far_id_ref[...] = window_ids(reg_far, a_row[...], a_col[...])
    copies[5].wait()
    q_ref[...] = (unit(dot(x, wqkv[:, :width]), blocks)[0] * SCALE).astype(BF)
    k_ref[...] = unit(dot(x, wqkv[:, width : 2 * width]), blocks)[0].astype(BF)
    v_ref[...] = dot(x, wqkv[:, 2 * width :]).astype(BF)


def teacher_first(
    far_ref, x_ref, id_ref, far_id_ref, q_ref, k_ref, v_ref, to_a, a_to_g, pack, t_qkv, t_out,
    h_ref, g_ref, first_ref, second_ref, pad_ref, wout, sems,
):
    copies = fetch((t_out.at[0], wout, sems.at[0]))
    width = x_ref.shape[1]
    blocks = head_blocks()
    far = to_window_order(far_ref, pad_ref, to_a[...])
    k_far = unit(dot(far, t_qkv[0, :, width : 2 * width]), blocks)[0].astype(BF)
    v_far = dot(far, t_qkv[0, :, 2 * width :]).astype(BF)
    windows = []
    for w in range(4):
        rows = slice(w * WIN, (w + 1) * WIN)
        id_keys = jnp.concatenate([id_ref[rows], far_id_ref[rows]], axis=0)
        keys = [
            jnp.concatenate([near[rows], away[rows]], axis=0)
            for near, away in ((k_ref, k_far), (v_ref, v_far))
        ]
        windows.append((q_ref[rows], keys, (id_ref[rows], id_keys)))
    atts = window_attention(windows)
    copies[0].wait()
    h = residual(x_ref[...], jnp.concatenate(atts, axis=0), wout[...])[0]
    h_ref[...] = h
    spread = dot(a_to_g[...], jnp.concatenate([h, id_ref[...]], axis=1)).astype(BF)
    g_ref[...] = spread
    north, south = [
        packed(
            jnp.concatenate([part(spread, n) for n in names], axis=0),
            pack[...], ROW_TOKENS, ROW_SENT,
        )
        for names in (TO_NORTH, TO_SOUTH)
    ]
    first_ref[...], second_ref[...] = swapped("lat", north, south)


def swapped(axis, low, high):
    even = lax.rem(lax.axis_index(axis), 2) == 0
    low, high = low.astype(F32), high.astype(F32)
    return jnp.where(even, low, high).astype(BF), jnp.where(even, high, low).astype(BF)


def packed(rows, table, tokens, sent):
    width = rows.shape[1] - 128
    values = dot(table[:sent], rows[:, :width])
    ids = dot(table, rows[:, width:]).astype(BF)
    row = dot_nt(jnp.full((8, 128), 1.0 / 128, BF), ids)[0:1]
    row = jnp.concatenate([row, jnp.zeros((1, width - 128), F32)], axis=1)
    at = lax.broadcasted_iota(jnp.int32, (sent, 1), 0)
    return jnp.where(at == tokens, row, values).astype(BF)


def opened(sent, table, tokens):
    values = dot(table, sent).astype(BF)
    row = sent.astype(F32)[tokens : tokens + 1, : table.shape[1]]
    ids = dot((table.astype(F32) * row).astype(BF), jnp.ones((table.shape[1], 128), BF))
    return jnp.concatenate([values, ids.astype(BF)], axis=1)


def part(x, name):
    start, kept = AT[name]
    return x[start : start + kept]


TO_NORTH = ("nw", "n", "ne")
TO_SOUTH = ("sw", "s", "se")
TO_WEST = (("N", "sw"), ("", "nw"), ("", "w"), ("", "sw"), ("S", "nw"))
TO_EAST = (("N", "se"), ("", "ne"), ("", "e"), ("", "se"), ("S", "ne"))
EXTRA = {
    "nw": (("N", "sw"), ("W", "ne"), ("NW", "se")),
    "n": (("N", "s"),),
    "ne": (("N", "se"), ("E", "nw"), ("NE", "sw")),
    "e": (("E", "w"),),
    "se": (("S", "ne"), ("E", "sw"), ("SE", "nw")),
    "s": (("S", "n"),),
    "sw": (("S", "nw"), ("W", "se"), ("SW", "ne")),
    "w": (("W", "e"),),
    "c": (),
}
LATE = ("nw", "ne", "e", "se", "sw", "w")
ORDER = [name for name, *_ in PARTS]


def _spots(items):
    spots, start = {}, 0
    for side, name in items:
        spots[side, name] = start
        start += AT[name][1]
    return spots


OWN = {("", name): AT[name][0] for name in ORDER}
EDGE = _spots([("N", n) for n in TO_SOUTH] + [("S", n) for n in TO_NORTH])
COME = _spots([(s + "E", n) for s, n in TO_WEST] + [(s + "W", n) for s, n in TO_EAST])
NE_ROWS = 2 * sum(AT[n][1] for n in TO_NORTH)


def gather(sources, items):
    blocks = []
    for item in items:
        for array, spots in sources:
            if item in spots:
                spot = spots[item]
                blocks.append(array[spot : spot + AT[item[1]][1]])
                break
    return blocks[0] if len(blocks) == 1 else jnp.concatenate(blocks, axis=0)


def window_attention(windows):
    found = attend([(q, k, v, id_mask(*ids)) for q, (k, v), ids in windows])
    return [
        jnp.concatenate([(n / d).astype(BF) for n, d in zip(nums, dens)], axis=1)
        for nums, dens, _ in found
    ]


def beside_rows(
    x_ref, id_ref, to_a, s_qkv, s_out, proj, g_ref, t_qkv, pack, after_ref,
    g0_ref, save0, save1, q_ref, k_ref, v_ref, att_ref, west_ref, east_ref, pad_ref,
):
    width = g_ref.shape[1] - 128
    blocks = head_blocks()
    x = to_window_order(x_ref, pad_ref, to_a[...])
    h = student_layer(x, s_qkv[0], s_out[0], id_ref[...], save0)
    h = student_layer(h, s_qkv[1], s_out[1], id_ref[...], save1)
    predicted = dot(h, proj[...])
    g0_ref[...] = dot_nt(predicted.astype(BF), proj[...])

    for ref, items in ((west_ref, TO_WEST), (east_ref, TO_EAST)):
        rows = gather([(g_ref, OWN)], items[1:4])
        ref[...] = packed(rows, pack[...], COL_TOKENS, COL_SENT)

    rows = g_ref[:, :width]
    q = (unit(dot(rows, t_qkv[1, :, :width]), blocks)[0] * SCALE).astype(BF)
    k = unit(dot(rows, t_qkv[1, :, width : 2 * width]), blocks)[0].astype(BF)
    v = dot(rows, t_qkv[1, :, 2 * width :]).astype(BF)
    q_ref[...] = q
    k_ref[...] = k
    v_ref[...] = v
    ids = part(g_ref, "c")[:, width:]
    [att_ref[...]] = window_attention([(part(q, "c"), [part(k, "c"), part(v, "c")], (ids, ids))])


def on_map():
    lat = lax.axis_index("lat")
    inside = (lat > 0, lat < lax.axis_size("lat") - 1)
    return [jnp.where(x, 1.0, 0.0) for x in inside]


def send_columns(
    first_ref, second_ref, from_north, from_south, west_ref, east_ref, after_ref,
    out_first, out_second,
):
    rows = swapped("lat", first_ref[...], second_ref[...])
    tables = (from_north[...], from_south[...])
    values = sum(dot(table, sent) for table, sent in zip(tables, rows))
    ids = 0.0
    for table, sent, there in zip(tables, rows, on_map()):
        row = sent.astype(F32)[ROW_TOKENS : ROW_TOKENS + 1, :ROW_SENT] * there
        ids += dot_nt(jnp.broadcast_to(row, (8, ROW_SENT)).astype(BF), table)
    at = lax.broadcasted_iota(jnp.int32, (COL_SENT, 1), 0)
    empty = jnp.zeros((1, first_ref.shape[1] - 128), F32)
    payloads = []
    for i, ref in ((0, west_ref), (128, east_ref)):
        row = jnp.concatenate([ids[0:1, i : i + 128], empty], axis=1)
        corners = jnp.where(at == COL_TOKENS, row, values[i : i + COL_SENT])
        payloads.append((ref[...].astype(F32) + corners).astype(BF))
    out_first[...], out_second[...] = swapped("lon", *payloads)


def beside_columns(
    g_ref, first_ref, second_ref, open_rows, t_qkv, q_ref, k_ref, v_ref, after_ref,
    edge_ref, k_out, v_out, n_ref, s_ref,
):
    width = g_ref.shape[1] - 128
    blocks = head_blocks()
    edge = []
    for sent, there in zip(swapped("lat", first_ref[...], second_ref[...]), on_map()):
        rows = opened(sent, open_rows[...], ROW_TOKENS)
        edge.append(jnp.concatenate([rows[:, :width], rows[:, width:] * there.astype(BF)], axis=1))
    edge_ref[...] = jnp.concatenate(edge, axis=0)
    rows = edge_ref[:, :width]
    k = unit(dot(rows, t_qkv[1, :, width : 2 * width]), blocks)[0].astype(BF)
    v = dot(rows, t_qkv[1, :, 2 * width :]).astype(BF)
    k_out[...] = k
    v_out[...] = v
    windows = []
    for name in ("n", "s"):
        items = (("", name),) + EXTRA[name]
        keys = [gather([(own, OWN), (edge, EDGE)], items) for own, edge in ((k_ref, k), (v_ref, v))]
        ids = [gather([(g_ref, OWN), (edge_ref, EDGE)], some)[:, width:] for some in (items[:1], items)]
        windows.append((part(q_ref, name), keys, ids))
    n_ref[...], s_ref[...] = window_attention(windows)


def teacher_second(
    h_ref, g_ref, edge_ref, first_ref, second_ref, q_ref, k_ref, v_ref, k_edge, v_edge,
    c_ref, n_ref, s_ref, open_cols, from_a, g_to_a, t_qkv, t_out, proj, s_qkv, s_out,
    g0_ref, save0, save1, out_hbm, grad_hbm, out_ref, grad_ref, sems,
):
    width = h_ref.shape[1]
    blocks = head_blocks()
    west, east = swapped("lon", first_ref[...], second_ref[...])
    came = [opened(sent, open_cols[...], COL_TOKENS) for sent in (east, west)]
    came = jnp.concatenate(came, axis=0)
    rows = came[:, :width]
    k = unit(dot(rows, t_qkv[1, :, width : 2 * width]), blocks)[0].astype(BF)
    v = dot(rows, t_qkv[1, :, 2 * width :]).astype(BF)
    atts = {"c": c_ref[...], "n": n_ref[...], "s": s_ref[...]}
    windows = []
    for name in LATE:
        items = (("", name),) + EXTRA[name]
        keys = [
            gather([(own, OWN), (edge, EDGE), (new, COME)], items)
            for own, edge, new in ((k_ref, k_edge, k), (v_ref, v_edge, v))
        ]
        ids = [
            gather([(g_ref, OWN), (edge_ref, EDGE), (came, COME)], some)[:, width:]
            for some in (items[:1], items)
        ]
        windows.append((part(q_ref, name), keys, ids))
    atts.update(zip(LATE, window_attention(windows)))
    att = jnp.concatenate([atts[name] for name in ORDER], axis=0)
    att = dot(g_to_a[...], att).astype(BF)
    teacher = residual(h_ref[...], att, t_out[1])[0]
    natural = dot(from_a[...], teacher).astype(BF)
    out_ref[0] = natural.reshape(COLS, TALL, width)[:, :ROWS, :]
    copies = fetch((out_ref, out_hbm, sems.at[0]))

    g = g0_ref[...] - dot_nt(teacher, proj[...])
    g = student_back(g, save1, s_qkv[1], s_out[1])
    g = student_back(g, save0, s_qkv[0], s_out[0])
    high = g.astype(BF)
    low = (g - high.astype(F32)).astype(BF)
    half = COLS // 2
    for i in range(2):
        table = from_a[i * half * TALL : (i + 1) * half * TALL]
        natural = dot(table, high) + dot(table, low)
        cols = pl.ds(i * half, half)
        grad_ref[0, cols] = natural.reshape(half, TALL, g.shape[1])[:, :ROWS, :]
        copies += fetch((grad_ref.at[0, cols], grad_hbm.at[0, cols], sems.at[1 + i]))
    for copy in copies:
        copy.wait()


VMEM = pl.BlockSpec(memory_space=pltpu.VMEM)
ANY = pl.BlockSpec(memory_space=pl.ANY)
HBM = pl.BlockSpec(memory_space=pltpu.HBM)


def call(kernel, name, outs, specs, args, scratch=(), flops=0, out_space=VMEM):
    shapes = [jax.ShapeDtypeStruct(s, d) for s, d in outs]
    touched = sum(a.size * a.dtype.itemsize for a in args)
    return pl.pallas_call(
        kernel,
        name=name,
        out_shape=shapes,
        in_specs=specs,
        out_specs=[out_space] * len(outs),
        scratch_shapes=list(scratch),
        compiler_params=pltpu.CompilerParams(vmem_limit_bytes=28 << 20),
        cost_estimate=pl.CostEstimate(flops=flops, bytes_accessed=touched, transcendentals=0),
    )(*args)


def buffers(*arrays):
    return [pltpu.VMEM(a.shape, a.dtype) for a in arrays] + [
        pltpu.SemaphoreType.DMA((len(arrays),))
    ]


def swaps(size, start):
    route = {}
    for i in range(start, size, 2):
        j = (i + 1) % size
        route[i], route[j] = j, i
    return sorted(route.items())


def inner_swaps(lat_size, lon_size):
    route = []
    for i in range(lat_size):
        for j in range(lon_size):
            if 0 < i < lat_size - 1:
                to = (i - 1 + 2 * (i % 2)) * lon_size + j
            else:
                to = i * lon_size + (j ^ 1)
            route.append((i * lon_size + j, to))
    return route


def shards(teacher_in, student_in, regions, t_qkv, t_out, s_qkv, s_out, s_proj):
    width, narrow = teacher_in.shape[3], student_in.shape[3]
    lat_size, lon_size = lax.axis_size("lat"), lax.axis_size("lon")
    wide = width + 128
    teacher_in = teacher_in.transpose(0, 2, 1, 3)
    student_in = student_in.transpose(0, 2, 1, 3)
    regions = regions.transpose(2, 0, 1)
    far = lax.ppermute(teacher_in, "grp", [(0, 1), (1, 0)])

    pinned = [
        pltpu.with_memory_space_constraint(jnp.asarray(a), pltpu.HBM)
        for a in (teacher_in, regions, TO_A, A_ROW, A_COL, t_qkv)
    ]
    x, ids, far_ids, q, k, v = call(
        teacher_own, "teacher_own",
        [((NA, width), BF), ((NA, 128), BF), ((NA, 128), BF)] + [((NA, width), BF)] * 3,
        [HBM] * 6, pinned,
        [pltpu.VMEM((COLS, TALL, width), BF)]
        + buffers(teacher_in, regions, TO_A, A_ROW, A_COL, t_qkv[0]),
        10**9,
    )
    hidden, spread, rows_1, rows_2 = call(
        teacher_first, "teacher_first",
        [((NA, width), BF), ((NG, wide), BF)] + [((ROW_SENT, width), BF)] * 2,
        [VMEM] * 11 + [HBM],
        [far, x, ids, far_ids, q, k, v, TO_A, A_TO_G, PACK_ROWS, t_qkv]
        + [pltpu.with_memory_space_constraint(t_out, pltpu.HBM)],
        [pltpu.VMEM((COLS, TALL, width), BF)] + buffers(t_out[0]), 3 * 10**9,
    )
    rows_2 = lax.ppermute(rows_2, "lat", swaps(lat_size, 0))
    rows_1 = lax.ppermute(rows_1, ("lat", "lon"), inner_swaps(lat_size, lon_size))

    g0, save0, save1, q, k, v, c_att, west, east = call(
        beside_rows, "beside_rows",
        [((NA, narrow), F32), ((NA, SAVE), BF), ((NA, SAVE), BF)]
        + [((NG, width), BF)] * 3 + [((AT["c"][1], width), BF)] + [((COL_SENT, width), BF)] * 2,
        [VMEM] * 9 + [ANY],
        [student_in, ids, TO_A, s_qkv, s_out, s_proj, spread, t_qkv, PACK_OWN, hidden],
        [pltpu.VMEM((COLS, TALL, narrow), BF)], 5 * 10**9,
    )
    cols_1, cols_2 = call(
        send_columns, "send_columns",
        [((COL_SENT, width), BF)] * 2,
        [VMEM] * 6 + [ANY],
        [rows_1, rows_2, FROM_NORTH, FROM_SOUTH, west, east, g0], (), 10**7,
    )
    sent = cols_2
    cols_2 = lax.ppermute(cols_2, "lon", swaps(lon_size, 0))
    cols_1 = lax.ppermute(cols_1, "lon", swaps(lon_size, 1))

    edge, k_edge, v_edge, n_att, s_att = call(
        beside_columns, "beside_columns",
        [((NE_ROWS, wide), BF)] + [((NE_ROWS, width), BF)] * 2 + [((AT["n"][1], width), BF)] * 2,
        [VMEM] * 8 + [ANY],
        [spread, rows_1, rows_2, OPEN_ROWS, t_qkv, q, k, v, sent], (), 2 * 10**9,
    )
    args = [hidden, spread, edge, cols_1, cols_2, q, k, v, k_edge, v_edge, c_att, n_att, s_att]
    args += [OPEN_COLS, FROM_A, G_TO_A, t_qkv, t_out, s_proj, s_qkv, s_out, g0, save0, save1]
    out, grad = call(
        teacher_second, "teacher_second",
        [(teacher_in.shape, BF), (student_in.shape, F32)],
        [VMEM] * len(args), args,
        [
            pltpu.VMEM(teacher_in.shape, BF),
            pltpu.VMEM(student_in.shape, F32),
            pltpu.SemaphoreType.DMA((3,)),
        ],
        6 * 10**9, ANY,
    )
    return out.transpose(0, 2, 1, 3), grad.transpose(0, 2, 1, 3)


def solution(mesh):
    tiles = P("grp", "lat", "lon", None)
    return jax.shard_map(
        shards,
        mesh=mesh,
        in_specs=(tiles, tiles, P(None, "lat", "lon"), P(), P(), P(), P(), P()),
        out_specs=(tiles, tiles),
        check_vma=False,
    )
```

```python
import functools

import jax
import jax.numpy as jnp
import ml_dtypes
import numpy as np
from jax import lax
from jax.experimental import pallas as pl
from jax.experimental.pallas import tpu as pltpu
from jax.sharding import PartitionSpec as P

HEADS_T = 8
HEADS_S = 4
EPS = 1e-06
LOG2E = 1.4426950408889634
SCALE = 10.0 * LOG2E
BF = jnp.bfloat16
F32 = jnp.float32

ROWS, COLS = 24, 12
WIN = 80
NA = 4 * WIN
TALL = 32
NAT = COLS * TALL
PAIR = 128

PARTS = (
    ("nw", (0, 6), (0, 3), 32),
    ("n", (0, 6), (3, 9), 48),
    ("ne", (0, 6), (9, 12), 32),
    ("e", (6, 18), (9, 12), 48),
    ("se", (18, 24), (9, 12), 32),
    ("s", (18, 24), (3, 9), 48),
    ("sw", (18, 24), (0, 3), 32),
    ("w", (6, 18), (0, 3), 48),
    ("c", (6, 18), (3, 9), 80),
)
AT = {}
NG = 0
for _name, _r, _c, _kept in PARTS:
    AT[_name] = (NG, _kept)
    NG += _kept


def _a_slot(r, c):
    return (2 * (r // 12) + c // 6) * WIN + (r % 12) * 6 + c % 6


def _tables():
    to_a = np.zeros((NA, NAT), ml_dtypes.bfloat16)
    a_row = np.zeros((NA, ROWS), ml_dtypes.bfloat16)
    a_col = np.zeros((NA, COLS), ml_dtypes.bfloat16)
    for r in range(ROWS):
        for c in range(COLS):
            slot = _a_slot(r, c)
            to_a[slot, c * TALL + r] = 1
            a_row[slot, r] = 1
            a_col[slot, c] = 1
    a_to_g = np.zeros((NG, NA), ml_dtypes.bfloat16)
    for name, (r0, r1), (c0, c1), _ in PARTS:
        spot = AT[name][0]
        for r in range(r0, r1):
            for c in range(c0, c1):
                a_to_g[spot, _a_slot(r, c)] = 1
                spot += 1
    return to_a, a_row, a_col, a_to_g


TO_A, A_ROW, A_COL, A_TO_G = _tables()
FROM_A = np.ascontiguousarray(TO_A.T)
G_TO_A = np.ascontiguousarray(A_TO_G.T)


def _packing(kept):
    table = np.zeros((128, sum(kept)), ml_dtypes.bfloat16)
    token, start = 0, 0
    for rows in kept:
        count = {32: 18, 48: 36}[rows]
        for i in range(count):
            table[token + i, start + i] = 1
        token, start = token + count, start + rows
    return table


def _corners(start, west, east):
    table = np.zeros((256, ROW_SENT), ml_dtypes.bfloat16)
    for i in range(18):
        table[start + i, west + i] = 1
        table[128 + start + i, east + i] = 1
    return table


PACK_ROWS = _packing((32, 48, 32))
PACK_OWN = np.roll(PACK_ROWS, 18, axis=0)
PACK_COLS = _packing((32, 32, 48, 32, 32))
ROW_TOKENS, ROW_SENT = 72, 80
COL_TOKENS, COL_SENT = 108, 112
FROM_NORTH = _corners(0, 0, 54)
FROM_SOUTH = _corners(90, 0, 54)
OPEN_ROWS = np.ascontiguousarray(PACK_ROWS.T[:, :ROW_SENT])
OPEN_COLS = np.ascontiguousarray(PACK_COLS.T[:, :COL_SENT])


def dot(a, b):
    return jnp.dot(a, b, preferred_element_type=F32)


def dot_nt(a, b):
    return lax.dot_general(a, b, (((1,), (1,)), ((), ())), preferred_element_type=F32)


def dot_tn(a, b):
    return lax.dot_general(a, b, (((0,), (0,)), ((), ())), preferred_element_type=F32)


def head_lanes(rows, h):
    lane = lax.broadcasted_iota(jnp.int32, (rows, PAIR), 1)
    return jnp.where((lane >> 6) == h, 1.0, 0.0).astype(BF)


def head_blocks():
    row = lax.broadcasted_iota(jnp.int32, (2 * PAIR, 2 * PAIR), 0)
    lane = lax.broadcasted_iota(jnp.int32, (2 * PAIR, 2 * PAIR), 1)
    return jnp.where((row >> 6) == (lane >> 6), 1.0, 0.0).astype(BF)


def stack_heads(x):
    return jnp.concatenate([x * head_lanes(1, h) for h in range(2)], axis=0)


def stack_values(v):
    rows = v.shape[0]
    ones = jnp.concatenate([head_lanes(rows, h) for h in range(2)], axis=0)
    return jnp.concatenate([stack_heads(v), ones], axis=1)


def unstack_heads(x):
    n = x.shape[0] // 2
    lane = lax.broadcasted_iota(jnp.int32, (1, PAIR), 1) >> 6
    return jnp.where(lane == 0, x[:n], x[n:])


def head_sums(x, blocks):
    step = blocks.shape[0]
    groups = [dot(x[:, i : i + step].astype(BF), blocks) for i in range(0, x.shape[1], step)]
    return groups[0] if len(groups) == 1 else jnp.concatenate(groups, axis=1)


def unit(x, blocks):
    scale = lax.rsqrt(head_sums(x * x, blocks) + EPS)
    return x * scale, scale


def id_mask(id_query, id_keys):
    keys = jnp.concatenate([id_keys] * 2, axis=0)
    row = dot_nt(jnp.full((8, 128), 1.0 / 128, BF), keys)[0:1]
    return id_query.astype(F32)[:, 0:1] == row


def pairs_of(x):
    return [x[:, i : i + PAIR] for i in range(0, x.shape[1], PAIR)]


def attend(windows):
    scores = [
        [dot_nt(qp, stack_heads(kp)) for qp, kp in zip(pairs_of(q), pairs_of(k))]
        for q, k, _, _ in windows
    ]
    es = [
        [jnp.where(w[3], jnp.exp2(s), 0.0).astype(BF) for s in group]
        for w, group in zip(windows, scores)
    ]
    both = [
        [dot(e, stack_values(vp)) for e, vp in zip(group, pairs_of(w[2]))]
        for w, group in zip(windows, es)
    ]
    return [
        ([b[:, :PAIR] for b in group], [b[:, PAIR:] for b in group], e)
        for group, e in zip(both, es)
    ]


def to_window_order(x_ref, pad_ref, to_a):
    pad_ref[...] = jnp.zeros_like(pad_ref)
    pad_ref[:, 0:ROWS, :] = x_ref[0]
    natural = pad_ref[...].reshape(NAT, x_ref.shape[3])
    return dot(to_a, natural).astype(BF)


def window_ids(reg, a_row, a_col):
    table = (reg + 1).astype(F32).astype(BF)
    picked = (dot(a_col, table) * a_row.astype(F32)).astype(BF)
    return dot(picked, jnp.ones((ROWS, 128), BF)).astype(BF)


def by_level(reg_ref):
    level = lax.axis_index("grp")
    low, high = reg_ref[:, 0, :], reg_ref[:, 1, :]
    own = jnp.where(level == 0, low, high)
    return own, low + high - own


def residual(x, att, w):
    y = dot(att, w)
    r = lax.rsqrt(jnp.mean(y * y, axis=1, keepdims=True) + EPS)
    n = y * r
    return (x.astype(F32) + n).astype(BF), n, r


WIDE = 2 * PAIR
SAVE = 11 * WIDE


def student_layer(x, w_qkv, w_out, ids, save_ref):
    blocks = head_blocks()
    qkv = dot(x, w_qkv)
    q, sq = unit(qkv[:, :WIDE], blocks)
    k, sk = unit(qkv[:, WIDE : 2 * WIDE], blocks)
    q = (q * SCALE).astype(BF)
    k = k.astype(BF)
    v = qkv[:, 2 * WIDE :].astype(BF)
    atts = []
    windows = [slice(w * WIN, (w + 1) * WIN) for w in range(4)]
    found = attend([(q[r], k[r], v[r], id_mask(ids[r], ids[r])) for r in windows])
    for rows, (nums, dens, es) in zip(windows, found):
        z = 1.0 / jnp.concatenate(dens, axis=1)
        att = jnp.concatenate(nums, axis=1) * z
        save_ref[rows, 4 * WIDE : 5 * WIDE] = z.astype(BF)
        for i, e in enumerate(es):
            save_ref[rows, (9 + i) * WIDE : (9 + i) * WIDE + 2 * WIN] = e
        atts.append(att.astype(BF))
    att = jnp.concatenate(atts, axis=0)
    h, n, r = residual(x, att, w_out)
    for i, part in ((0, q), (1, k), (2, v), (3, att), (5, sq), (6, sk), (7, n)):
        save_ref[:, i * WIDE : (i + 1) * WIDE] = part.astype(BF)
    save_ref[:, 8 * WIDE : 9 * WIDE] = jnp.broadcast_to(r, (NA, WIDE)).astype(BF)
    return h


def fetch(*pairs):
    copies = [pltpu.make_async_copy(*pair) for pair in pairs]
    for copy in copies:
        copy.start()
    return copies


def student_back(g, save_ref, w_qkv, w_out):
    blocks = head_blocks()
    part = lambda i: save_ref[:, i * WIDE : (i + 1) * WIDE]
    n, r = part(7).astype(F32), part(8).astype(F32)
    dy = r * (g - n * jnp.mean(g * n, axis=1, keepdims=True))
    datt = dot_nt(dy.astype(BF), w_out) * part(4).astype(F32)
    drop = (datt * part(3).astype(F32)).astype(BF) * jnp.asarray(-1.0, BF)
    datt = datt.astype(BF)
    q, k, v = part(0), part(1), part(2)
    windows = [slice(w * WIN, (w + 1) * WIN) for w in range(4)]
    blocks_of = [(r, slice(i, i + PAIR)) for r in windows for i in range(0, WIDE, PAIR)]
    es = [
        save_ref[r, (9 + i) * WIDE : (9 + i) * WIDE + 2 * WIN] for r in windows for i in range(2)
    ]
    dws = [
        dot_nt(jnp.concatenate([datt[r, p], drop[r, p]], axis=1), stack_values(v[r, p]))
        for r, p in blocks_of
    ]
    dv = [unstack_heads(dot_tn(e, datt[r, p])) for e, (r, p) in zip(es, blocks_of)]
    dss = [(e.astype(F32) * dw).astype(BF) for e, dw in zip(es, dws)]
    dq = [dot(ds, stack_heads(k[r, p])) for ds, (r, p) in zip(dss, blocks_of)]
    dk = [unstack_heads(dot_tn(ds, q[r, p])) for ds, (r, p) in zip(dss, blocks_of)]
    dqs, dks, dvs = [[x[i : i + 2] for i in range(0, len(x), 2)] for x in (dq, dk, dv)]
    dqs, dks, dvs = [[jnp.concatenate(x, axis=1) for x in y] for y in (dqs, dks, dvs)]
    dq = 10.0 * jnp.concatenate(dqs, axis=0)
    dk = (1.0 / LOG2E) * jnp.concatenate(dks, axis=0)
    dv = jnp.concatenate(dvs, axis=0)
    q_unit = q.astype(F32) * (1.0 / SCALE)
    k_unit = k.astype(F32)
    dq = part(5).astype(F32) * (dq - q_unit * head_sums(q_unit * dq, blocks))
    dk = part(6).astype(F32) * (dk - k_unit * head_sums(k_unit * dk, blocks))
    dqkv = jnp.concatenate([dq.astype(BF), dk.astype(BF), dv.astype(BF)], axis=1)
    return g + dot_nt(dqkv, w_qkv)


def teacher_own(
    x_hbm, reg_hbm, to_a_hbm, a_row_hbm, a_col_hbm, t_qkv,
    x_out, id_ref, far_id_ref, q_ref, k_ref, v_ref, to_a, wqkv,
    pad_ref, x_ref, reg_ref, a_row, a_col, sems,
):
    width = x_ref.shape[3]
    thirds = [pl.ds(i * width, width) for i in range(3)]
    copies = fetch(
        (x_hbm, x_ref, sems.at[0]),
        (to_a_hbm, to_a, sems.at[1]),
        (t_qkv.at[0, :, thirds[0]], wqkv.at[:, thirds[0]], sems.at[2]),
        (t_qkv.at[0, :, thirds[1]], wqkv.at[:, thirds[1]], sems.at[3]),
        (t_qkv.at[0, :, thirds[2]], wqkv.at[:, thirds[2]], sems.at[4]),
        (reg_hbm, reg_ref, sems.at[5]),
        (a_row_hbm, a_row, sems.at[6]),
        (a_col_hbm, a_col, sems.at[7]),
    )
    blocks = head_blocks()
    copies[0].wait()
    copies[1].wait()
    x = to_window_order(x_ref, pad_ref, to_a[...])
    x_out[...] = x
    copies[2].wait()
    q_ref[...] = (unit(dot(x, wqkv[:, :width]), blocks)[0] * SCALE).astype(BF)
    copies[3].wait()
    k_ref[...] = unit(dot(x, wqkv[:, width : 2 * width]), blocks)[0].astype(BF)
    copies[4].wait()
    v_ref[...] = dot(x, wqkv[:, 2 * width :]).astype(BF)
    for copy in copies[5:]:
        copy.wait()
    reg, reg_far = by_level(reg_ref)
    id_ref[...] = window_ids(reg, a_row[...], a_col[...])
    far_id_ref[...] = window_ids(reg_far, a_row[...], a_col[...])


def teacher_first(
    far_ref, x_ref, id_ref, far_id_ref, q_ref, k_ref, v_ref, to_a, a_to_g, pack, wqkv, t_out,
    h_ref, g_ref, first_ref, second_ref, pad_ref, wout, sems,
):
    copies = fetch((t_out.at[0], wout, sems.at[0]))
    width = x_ref.shape[1]
    blocks = head_blocks()
    far = to_window_order(far_ref, pad_ref, to_a[...])
    k_far = unit(dot(far, wqkv[:, width : 2 * width]), blocks)[0].astype(BF)
    v_far = dot(far, wqkv[:, 2 * width :]).astype(BF)
    windows = []
    for w in range(4):
        rows = slice(w * WIN, (w + 1) * WIN)
        id_keys = jnp.concatenate([id_ref[rows], far_id_ref[rows]], axis=0)
        keys = [
            jnp.concatenate([near[rows], away[rows]], axis=0)
            for near, away in ((k_ref, k_far), (v_ref, v_far))
        ]
        windows.append((q_ref[rows], keys, (id_ref[rows], id_keys)))
    atts = window_attention(windows)
    copies[0].wait()
    h = residual(x_ref[...], jnp.concatenate(atts, axis=0), wout[...])[0]
    h_ref[...] = h
    spread = dot(a_to_g[...], jnp.concatenate([h, id_ref[...]], axis=1)).astype(BF)
    g_ref[...] = spread
    north, south = [
        packed(
            jnp.concatenate([part(spread, n) for n in names], axis=0),
            pack[...], ROW_TOKENS, ROW_SENT,
        )
        for names in (TO_NORTH, TO_SOUTH)
    ]
    first_ref[...], second_ref[...] = swapped("lat", north, south)


def swapped(axis, low, high):
    even = lax.rem(lax.axis_index(axis), 2) == 0
    low, high = low.astype(F32), high.astype(F32)
    return jnp.where(even, low, high).astype(BF), jnp.where(even, high, low).astype(BF)


def packed(rows, table, tokens, sent):
    width = rows.shape[1] - 128
    values = dot(table[:sent], rows[:, :width])
    ids = dot(table, rows[:, width:]).astype(BF)
    row = dot_nt(jnp.full((8, 128), 1.0 / 128, BF), ids)[0:1]
    row = jnp.concatenate([row, jnp.zeros((1, width - 128), F32)], axis=1)
    at = lax.broadcasted_iota(jnp.int32, (sent, 1), 0)
    return jnp.where(at == tokens, row, values).astype(BF)


def opened(sent, table, tokens):
    values = dot(table, sent).astype(BF)
    row = sent.astype(F32)[tokens : tokens + 1, : table.shape[1]]
    ids = dot((table.astype(F32) * row).astype(BF), jnp.ones((table.shape[1], 128), BF))
    return jnp.concatenate([values, ids.astype(BF)], axis=1)


def part(x, name):
    start, kept = AT[name]
    return x[start : start + kept]


TO_NORTH = ("nw", "n", "ne")
TO_SOUTH = ("sw", "s", "se")
TO_WEST = (("N", "sw"), ("", "nw"), ("", "w"), ("", "sw"), ("S", "nw"))
TO_EAST = (("N", "se"), ("", "ne"), ("", "e"), ("", "se"), ("S", "ne"))
EXTRA = {
    "nw": (("N", "sw"), ("W", "ne"), ("NW", "se")),
    "n": (("N", "s"),),
    "ne": (("N", "se"), ("E", "nw"), ("NE", "sw")),
    "e": (("E", "w"),),
    "se": (("S", "ne"), ("E", "sw"), ("SE", "nw")),
    "s": (("S", "n"),),
    "sw": (("S", "nw"), ("W", "se"), ("SW", "ne")),
    "w": (("W", "e"),),
    "c": (),
}
LATE = ("nw", "ne", "e", "se", "sw", "w")
ORDER = [name for name, *_ in PARTS]


def _spots(items):
    spots, start = {}, 0
    for side, name in items:
        spots[side, name] = start
        start += AT[name][1]
    return spots


OWN = {("", name): AT[name][0] for name in ORDER}
EDGE = _spots([("N", n) for n in TO_SOUTH] + [("S", n) for n in TO_NORTH])
COME = _spots([(s + "E", n) for s, n in TO_WEST] + [(s + "W", n) for s, n in TO_EAST])
NE_ROWS = 2 * sum(AT[n][1] for n in TO_NORTH)


def gather(sources, items):
    blocks = []
    for item in items:
        for array, spots in sources:
            if item in spots:
                spot = spots[item]
                blocks.append(array[spot : spot + AT[item[1]][1]])
                break
    return blocks[0] if len(blocks) == 1 else jnp.concatenate(blocks, axis=0)


def window_attention(windows):
    found = attend([(q, k, v, id_mask(*ids)) for q, (k, v), ids in windows])
    return [
        jnp.concatenate([(n / d).astype(BF) for n, d in zip(nums, dens)], axis=1)
        for nums, dens, _ in found
    ]


def beside_rows(
    x_ref, id_ref, to_a, s_qkv, s_out, proj, g_ref, t_qkv, pack, after_ref,
    g0_ref, save0, save1, q_ref, k_ref, v_ref, att_ref, west_ref, east_ref, pad_ref,
):
    width = g_ref.shape[1] - 128
    blocks = head_blocks()
    x = to_window_order(x_ref, pad_ref, to_a[...])
    h = student_layer(x, s_qkv[0], s_out[0], id_ref[...], save0)
    h = student_layer(h, s_qkv[1], s_out[1], id_ref[...], save1)
    predicted = dot(h, proj[...])
    g0_ref[...] = dot_nt(predicted.astype(BF), proj[...])

    for ref, items in ((west_ref, TO_WEST), (east_ref, TO_EAST)):
        rows = gather([(g_ref, OWN)], items[1:4])
        ref[...] = packed(rows, pack[...], COL_TOKENS, COL_SENT)

    rows = g_ref[:, :width]
    q = (unit(dot(rows, t_qkv[1, :, :width]), blocks)[0] * SCALE).astype(BF)
    k = unit(dot(rows, t_qkv[1, :, width : 2 * width]), blocks)[0].astype(BF)
    v = dot(rows, t_qkv[1, :, 2 * width :]).astype(BF)
    q_ref[...] = q
    k_ref[...] = k
    v_ref[...] = v
    ids = part(g_ref, "c")[:, width:]
    [att_ref[...]] = window_attention([(part(q, "c"), [part(k, "c"), part(v, "c")], (ids, ids))])


def on_map():
    lat = lax.axis_index("lat")
    inside = (lat > 0, lat < lax.axis_size("lat") - 1)
    return [jnp.where(x, 1.0, 0.0) for x in inside]


def send_columns(
    first_ref, second_ref, from_north, from_south, west_ref, east_ref, after_ref,
    out_first, out_second,
):
    rows = swapped("lat", first_ref[...], second_ref[...])
    tables = (from_north[...], from_south[...])
    values = sum(dot(table, sent) for table, sent in zip(tables, rows))
    ids = 0.0
    for table, sent, there in zip(tables, rows, on_map()):
        row = sent.astype(F32)[ROW_TOKENS : ROW_TOKENS + 1, :ROW_SENT] * there
        ids += dot_nt(jnp.broadcast_to(row, (8, ROW_SENT)).astype(BF), table)
    at = lax.broadcasted_iota(jnp.int32, (COL_SENT, 1), 0)
    empty = jnp.zeros((1, first_ref.shape[1] - 128), F32)
    payloads = []
    for i, ref in ((0, west_ref), (128, east_ref)):
        row = jnp.concatenate([ids[0:1, i : i + 128], empty], axis=1)
        corners = jnp.where(at == COL_TOKENS, row, values[i : i + COL_SENT])
        payloads.append((ref[...].astype(F32) + corners).astype(BF))
    out_first[...], out_second[...] = swapped("lon", *payloads)


def beside_columns(
    g_ref, first_ref, second_ref, open_rows, t_qkv, q_ref, k_ref, v_ref, after_ref,
    edge_ref, k_out, v_out, n_ref, s_ref,
):
    width = g_ref.shape[1] - 128
    blocks = head_blocks()
    edge = []
    for sent, there in zip(swapped("lat", first_ref[...], second_ref[...]), on_map()):
        rows = opened(sent, open_rows[...], ROW_TOKENS)
        edge.append(jnp.concatenate([rows[:, :width], rows[:, width:] * there.astype(BF)], axis=1))
    edge_ref[...] = jnp.concatenate(edge, axis=0)
    rows = edge_ref[:, :width]
    k = unit(dot(rows, t_qkv[1, :, width : 2 * width]), blocks)[0].astype(BF)
    v = dot(rows, t_qkv[1, :, 2 * width :]).astype(BF)
    k_out[...] = k
    v_out[...] = v
    windows = []
    for name in ("n", "s"):
        items = (("", name),) + EXTRA[name]
        keys = [gather([(own, OWN), (edge, EDGE)], items) for own, edge in ((k_ref, k), (v_ref, v))]
        ids = [gather([(g_ref, OWN), (edge_ref, EDGE)], some)[:, width:] for some in (items[:1], items)]
        windows.append((part(q_ref, name), keys, ids))
    n_ref[...], s_ref[...] = window_attention(windows)


def teacher_second(
    h_ref, g_ref, edge_ref, first_ref, second_ref, q_ref, k_ref, v_ref, k_edge, v_edge,
    c_ref, n_ref, s_ref, open_cols, from_a, g_to_a, t_qkv, t_out, proj, s_qkv, s_out,
    g0_ref, save0, save1, out_hbm, grad_hbm, out_ref, grad_ref, sems,
):
    width = h_ref.shape[1]
    blocks = head_blocks()
    west, east = swapped("lon", first_ref[...], second_ref[...])
    came = [opened(sent, open_cols[...], COL_TOKENS) for sent in (east, west)]
    came = jnp.concatenate(came, axis=0)
    rows = came[:, :width]
    k = unit(dot(rows, t_qkv[1, :, width : 2 * width]), blocks)[0].astype(BF)
    v = dot(rows, t_qkv[1, :, 2 * width :]).astype(BF)
    atts = {"c": c_ref[...], "n": n_ref[...], "s": s_ref[...]}
    windows = []
    for name in LATE:
        items = (("", name),) + EXTRA[name]
        keys = [
            gather([(own, OWN), (edge, EDGE), (new, COME)], items)
            for own, edge, new in ((k_ref, k_edge, k), (v_ref, v_edge, v))
        ]
        ids = [
            gather([(g_ref, OWN), (edge_ref, EDGE), (came, COME)], some)[:, width:]
            for some in (items[:1], items)
        ]
        windows.append((part(q_ref, name), keys, ids))
    atts.update(zip(LATE, window_attention(windows)))
    att = jnp.concatenate([atts[name] for name in ORDER], axis=0)
    att = dot(g_to_a[...], att).astype(BF)
    teacher = residual(h_ref[...], att, t_out[1])[0]
    natural = dot(from_a[...], teacher).astype(BF)
    out_ref[0] = natural.reshape(COLS, TALL, width)[:, :ROWS, :]
    copies = fetch((out_ref, out_hbm, sems.at[0]))

    g = g0_ref[...] - dot_nt(teacher, proj[...])
    g = student_back(g, save1, s_qkv[1], s_out[1])
    g = student_back(g, save0, s_qkv[0], s_out[0])
    high = g.astype(BF)
    low = (g - high.astype(F32)).astype(BF)
    half = COLS // 2
    for i in range(2):
        table = from_a[i * half * TALL : (i + 1) * half * TALL]
        natural = dot(table, high) + dot(table, low)
        cols = pl.ds(i * half, half)
        grad_ref[0, cols] = natural.reshape(half, TALL, g.shape[1])[:, :ROWS, :]
        copies += fetch((grad_ref.at[0, cols], grad_hbm.at[0, cols], sems.at[1 + i]))
    for copy in copies:
        copy.wait()


VMEM = pl.BlockSpec(memory_space=pltpu.VMEM)
ANY = pl.BlockSpec(memory_space=pl.ANY)
HBM = pl.BlockSpec(memory_space=pltpu.HBM)


def call(kernel, name, outs, specs, args, scratch=(), flops=0, out_space=VMEM):
    shapes = [jax.ShapeDtypeStruct(s, d) for s, d in outs]
    touched = sum(a.size * a.dtype.itemsize for a in args)
    return pl.pallas_call(
        kernel,
        name=name,
        out_shape=shapes,
        in_specs=specs,
        out_specs=[out_space] * len(outs),
        scratch_shapes=list(scratch),
        compiler_params=pltpu.CompilerParams(vmem_limit_bytes=28 << 20),
        cost_estimate=pl.CostEstimate(flops=flops, bytes_accessed=touched, transcendentals=0),
    )(*args)


def buffers(*arrays):
    return [pltpu.VMEM(a.shape, a.dtype) for a in arrays] + [
        pltpu.SemaphoreType.DMA((len(arrays),))
    ]


def swaps(size, start):
    route = {}
    for i in range(start, size, 2):
        j = (i + 1) % size
        route[i], route[j] = j, i
    return sorted(route.items())


def inner_swaps(lat_size, lon_size):
    route = []
    for i in range(lat_size):
        for j in range(lon_size):
            if 0 < i < lat_size - 1:
                to = (i - 1 + 2 * (i % 2)) * lon_size + j
            else:
                to = i * lon_size + (j ^ 1)
            route.append((i * lon_size + j, to))
    return route


def shards(teacher_in, student_in, regions, t_qkv, t_out, s_qkv, s_out, s_proj):
    width, narrow = teacher_in.shape[3], student_in.shape[3]
    lat_size, lon_size = lax.axis_size("lat"), lax.axis_size("lon")
    wide = width + 128
    teacher_in = teacher_in.transpose(0, 2, 1, 3)
    student_in = student_in.transpose(0, 2, 1, 3)
    regions = regions.transpose(2, 0, 1)
    far = lax.ppermute(teacher_in, "grp", [(0, 1), (1, 0)])

    pinned = [
        pltpu.with_memory_space_constraint(jnp.asarray(a), pltpu.HBM)
        for a in (teacher_in, regions, TO_A, A_ROW, A_COL, t_qkv)
    ]
    x, ids, far_ids, q, k, v, to_a, wqkv = call(
        teacher_own, "teacher_own",
        [((NA, width), BF), ((NA, 128), BF), ((NA, 128), BF)] + [((NA, width), BF)] * 3
        + [((NA, NAT), BF), (t_qkv.shape[1:], BF)],
        [HBM] * 6, pinned,
        [pltpu.VMEM((COLS, TALL, width), BF)]
        + buffers(teacher_in, regions, A_ROW, A_COL)[:-1]
        + [pltpu.SemaphoreType.DMA((8,))],
        10**9,
    )
    hidden, spread, rows_1, rows_2 = call(
        teacher_first, "teacher_first",
        [((NA, width), BF), ((NG, wide), BF)] + [((ROW_SENT, width), BF)] * 2,
        [VMEM] * 11 + [HBM],
        [far, x, ids, far_ids, q, k, v, to_a, A_TO_G, PACK_ROWS, wqkv]
        + [pltpu.with_memory_space_constraint(t_out, pltpu.HBM)],
        [pltpu.VMEM((COLS, TALL, width), BF)] + buffers(t_out[0]), 3 * 10**9,
    )
    rows_2 = lax.ppermute(rows_2, "lat", swaps(lat_size, 0))
    rows_1 = lax.ppermute(rows_1, ("lat", "lon"), inner_swaps(lat_size, lon_size))

    g0, save0, save1, q, k, v, c_att, west, east = call(
        beside_rows, "beside_rows",
        [((NA, narrow), F32), ((NA, SAVE), BF), ((NA, SAVE), BF)]
        + [((NG, width), BF)] * 3 + [((AT["c"][1], width), BF)] + [((COL_SENT, width), BF)] * 2,
        [VMEM] * 9 + [ANY],
        [student_in, ids, to_a, s_qkv, s_out, s_proj, spread, t_qkv, PACK_OWN, hidden],
        [pltpu.VMEM((COLS, TALL, narrow), BF)], 5 * 10**9,
    )
    cols_1, cols_2 = call(
        send_columns, "send_columns",
        [((COL_SENT, width), BF)] * 2,
        [VMEM] * 6 + [ANY],
        [rows_1, rows_2, FROM_NORTH, FROM_SOUTH, west, east, g0], (), 10**7,
    )
    sent = cols_2
    cols_2 = lax.ppermute(cols_2, "lon", swaps(lon_size, 0))
    cols_1 = lax.ppermute(cols_1, "lon", swaps(lon_size, 1))

    edge, k_edge, v_edge, n_att, s_att = call(
        beside_columns, "beside_columns",
        [((NE_ROWS, wide), BF)] + [((NE_ROWS, width), BF)] * 2 + [((AT["n"][1], width), BF)] * 2,
        [VMEM] * 8 + [ANY],
        [spread, rows_1, rows_2, OPEN_ROWS, t_qkv, q, k, v, sent], (), 2 * 10**9,
    )
    args = [hidden, spread, edge, cols_1, cols_2, q, k, v, k_edge, v_edge, c_att, n_att, s_att]
    args += [OPEN_COLS, FROM_A, G_TO_A, t_qkv, t_out, s_proj, s_qkv, s_out, g0, save0, save1]
    out, grad = call(
        teacher_second, "teacher_second",
        [(teacher_in.shape, BF), (student_in.shape, F32)],
        [VMEM] * len(args), args,
        [
            pltpu.VMEM(teacher_in.shape, BF),
            pltpu.VMEM(student_in.shape, F32),
            pltpu.SemaphoreType.DMA((3,)),
        ],
        6 * 10**9, ANY,
    )
    return out.transpose(0, 2, 1, 3), grad.transpose(0, 2, 1, 3)


def solution(mesh):
    tiles = P("grp", "lat", "lon", None)
    return jax.shard_map(
        shards,
        mesh=mesh,
        in_specs=(tiles, tiles, P(None, "lat", "lon"), P(), P(), P(), P(), P()),
        out_specs=(tiles, tiles),
        check_vma=False,
    )
```

```python
import functools

import jax
import jax.numpy as jnp
import ml_dtypes
import numpy as np
from jax import lax
from jax.experimental import pallas as pl
from jax.experimental.pallas import tpu as pltpu
from jax.sharding import PartitionSpec as P

HEADS_T = 8
HEADS_S = 4
EPS = 1e-06
LOG2E = 1.4426950408889634
SCALE = 10.0 * LOG2E
BF = jnp.bfloat16
F32 = jnp.float32

ROWS, COLS = 24, 12
WIN = 80
NA = 4 * WIN
TALL = 32
NAT = COLS * TALL
PAIR = 128

PARTS = (
    ("nw", (0, 6), (0, 3), 32),
    ("n", (0, 6), (3, 9), 48),
    ("ne", (0, 6), (9, 12), 32),
    ("e", (6, 18), (9, 12), 48),
    ("se", (18, 24), (9, 12), 32),
    ("s", (18, 24), (3, 9), 48),
    ("sw", (18, 24), (0, 3), 32),
    ("w", (6, 18), (0, 3), 48),
    ("c", (6, 18), (3, 9), 80),
)
AT = {}
NG = 0
for _name, _r, _c, _kept in PARTS:
    AT[_name] = (NG, _kept)
    NG += _kept


def _a_slot(r, c):
    return (2 * (r // 12) + c // 6) * WIN + (r % 12) * 6 + c % 6


def _tables():
    to_a = np.zeros((NA, NAT), ml_dtypes.bfloat16)
    a_row = np.zeros((NA, ROWS), ml_dtypes.bfloat16)
    a_col = np.zeros((NA, COLS), ml_dtypes.bfloat16)
    for r in range(ROWS):
        for c in range(COLS):
            slot = _a_slot(r, c)
            to_a[slot, c * TALL + r] = 1
            a_row[slot, r] = 1
            a_col[slot, c] = 1
    a_to_g = np.zeros((NG, NA), ml_dtypes.bfloat16)
    for name, (r0, r1), (c0, c1), _ in PARTS:
        spot = AT[name][0]
        for r in range(r0, r1):
            for c in range(c0, c1):
                a_to_g[spot, _a_slot(r, c)] = 1
                spot += 1
    return to_a, a_row, a_col, a_to_g


TO_A, A_ROW, A_COL, A_TO_G = _tables()
FROM_A = np.ascontiguousarray(TO_A.T)
G_TO_A = np.ascontiguousarray(A_TO_G.T)


def _packing(kept):
    table = np.zeros((128, sum(kept)), ml_dtypes.bfloat16)
    token, start = 0, 0
    for rows in kept:
        count = {32: 18, 48: 36}[rows]
        for i in range(count):
            table[token + i, start + i] = 1
        token, start = token + count, start + rows
    return table


def _corners(start, west, east):
    table = np.zeros((256, ROW_SENT), ml_dtypes.bfloat16)
    for i in range(18):
        table[start + i, west + i] = 1
        table[128 + start + i, east + i] = 1
    return table


PACK_ROWS = _packing((32, 48, 32))
PACK_OWN = np.roll(PACK_ROWS, 18, axis=0)
PACK_COLS = _packing((32, 32, 48, 32, 32))
ROW_TOKENS, ROW_SENT = 72, 80
COL_TOKENS, COL_SENT = 108, 112
FROM_NORTH = _corners(0, 0, 54)
FROM_SOUTH = _corners(90, 0, 54)
OPEN_ROWS = np.ascontiguousarray(PACK_ROWS.T[:, :ROW_SENT])
OPEN_COLS = np.ascontiguousarray(PACK_COLS.T[:, :COL_SENT])


def dot(a, b):
    return jnp.dot(a, b, preferred_element_type=F32)


def dot_nt(a, b):
    return lax.dot_general(a, b, (((1,), (1,)), ((), ())), preferred_element_type=F32)


def dot_tn(a, b):
    return lax.dot_general(a, b, (((0,), (0,)), ((), ())), preferred_element_type=F32)


def head_lanes(rows, h):
    lane = lax.broadcasted_iota(jnp.int32, (rows, PAIR), 1)
    return jnp.where((lane >> 6) == h, 1.0, 0.0).astype(BF)


def head_blocks():
    row = lax.broadcasted_iota(jnp.int32, (2 * PAIR, 2 * PAIR), 0)
    lane = lax.broadcasted_iota(jnp.int32, (2 * PAIR, 2 * PAIR), 1)
    return jnp.where((row >> 6) == (lane >> 6), 1.0, 0.0).astype(BF)


def stack_heads(x):
    return jnp.concatenate([x * head_lanes(1, h) for h in range(2)], axis=0)


def stack_values(v):
    rows = v.shape[0]
    ones = jnp.concatenate([head_lanes(rows, h) for h in range(2)], axis=0)
    return jnp.concatenate([stack_heads(v), ones], axis=1)


def unstack_heads(x):
    n = x.shape[0] // 2
    lane = lax.broadcasted_iota(jnp.int32, (1, PAIR), 1) >> 6
    return jnp.where(lane == 0, x[:n], x[n:])


def head_sums(x, blocks):
    step = blocks.shape[0]
    groups = [dot(x[:, i : i + step].astype(BF), blocks) for i in range(0, x.shape[1], step)]
    return groups[0] if len(groups) == 1 else jnp.concatenate(groups, axis=1)


def unit(x, blocks):
    scale = lax.rsqrt(head_sums(x * x, blocks) + EPS)
    return x * scale, scale


def id_mask(id_query, id_keys):
    keys = jnp.concatenate([id_keys] * 2, axis=0)
    row = dot_nt(jnp.full((8, 128), 1.0 / 128, BF), keys)[0:1]
    return id_query.astype(F32)[:, 0:1] == row


def pairs_of(x):
    return [x[:, i : i + PAIR] for i in range(0, x.shape[1], PAIR)]


def attend(windows):
    scores = [
        [dot_nt(qp, stack_heads(kp)) for qp, kp in zip(pairs_of(q), pairs_of(k))]
        for q, k, _, _ in windows
    ]
    es = [
        [jnp.where(w[3], jnp.exp2(s), 0.0).astype(BF) for s in group]
        for w, group in zip(windows, scores)
    ]
    both = [
        [dot(e, stack_values(vp)) for e, vp in zip(group, pairs_of(w[2]))]
        for w, group in zip(windows, es)
    ]
    return [
        ([b[:, :PAIR] for b in group], [b[:, PAIR:] for b in group], e)
        for group, e in zip(both, es)
    ]


def to_window_order(x_ref, pad_ref, to_a):
    pad_ref[...] = jnp.zeros_like(pad_ref)
    pad_ref[:, 0:ROWS, :] = x_ref[0]
    natural = pad_ref[...].reshape(NAT, x_ref.shape[3])
    return dot(to_a, natural).astype(BF)


def window_ids(reg, a_row, a_col):
    table = (reg + 1).astype(F32).astype(BF)
    picked = (dot(a_col, table) * a_row.astype(F32)).astype(BF)
    return dot(picked, jnp.ones((ROWS, 128), BF)).astype(BF)


def by_level(reg_ref):
    level = lax.axis_index("grp")
    low, high = reg_ref[:, 0, :], reg_ref[:, 1, :]
    own = jnp.where(level == 0, low, high)
    return own, low + high - own


def residual(x, att, w):
    y = dot(att, w)
    r = lax.rsqrt(jnp.mean(y * y, axis=1, keepdims=True) + EPS)
    n = y * r
    return (x.astype(F32) + n).astype(BF), n, r


WIDE = 2 * PAIR
SAVE = 11 * WIDE


def student_layer(x, w_qkv, w_out, ids, save_ref):
    blocks = head_blocks()
    qkv = dot(x, w_qkv)
    q, sq = unit(qkv[:, :WIDE], blocks)
    k, sk = unit(qkv[:, WIDE : 2 * WIDE], blocks)
    q = (q * SCALE).astype(BF)
    k = k.astype(BF)
    v = qkv[:, 2 * WIDE :].astype(BF)
    atts = []
    windows = [slice(w * WIN, (w + 1) * WIN) for w in range(4)]
    found = attend([(q[r], k[r], v[r], id_mask(ids[r], ids[r])) for r in windows])
    for rows, (nums, dens, es) in zip(windows, found):
        z = 1.0 / jnp.concatenate(dens, axis=1)
        att = jnp.concatenate(nums, axis=1) * z
        save_ref[rows, 4 * WIDE : 5 * WIDE] = z.astype(BF)
        for i, e in enumerate(es):
            save_ref[rows, (9 + i) * WIDE : (9 + i) * WIDE + 2 * WIN] = e
        atts.append(att.astype(BF))
    att = jnp.concatenate(atts, axis=0)
    h, n, r = residual(x, att, w_out)
    for i, part in ((0, q), (1, k), (2, v), (3, att), (5, sq), (6, sk), (7, n)):
        save_ref[:, i * WIDE : (i + 1) * WIDE] = part.astype(BF)
    save_ref[:, 8 * WIDE : 9 * WIDE] = jnp.broadcast_to(r, (NA, WIDE)).astype(BF)
    return h


def fetch(*pairs):
    copies = [pltpu.make_async_copy(*pair) for pair in pairs]
    for copy in copies:
        copy.start()
    return copies


def student_back(g, save_ref, w_qkv, w_out):
    blocks = head_blocks()
    part = lambda i: save_ref[:, i * WIDE : (i + 1) * WIDE]
    n, r = part(7).astype(F32), part(8).astype(F32)
    dy = r * (g - n * jnp.mean(g * n, axis=1, keepdims=True))
    datt = dot_nt(dy.astype(BF), w_out) * part(4).astype(F32)
    drop = (datt * part(3).astype(F32)).astype(BF) * jnp.asarray(-1.0, BF)
    datt = datt.astype(BF)
    q, k, v = part(0), part(1), part(2)
    windows = [slice(w * WIN, (w + 1) * WIN) for w in range(4)]
    blocks_of = [(r, slice(i, i + PAIR)) for r in windows for i in range(0, WIDE, PAIR)]
    es = [
        save_ref[r, (9 + i) * WIDE : (9 + i) * WIDE + 2 * WIN] for r in windows for i in range(2)
    ]
    dws = [
        dot_nt(jnp.concatenate([datt[r, p], drop[r, p]], axis=1), stack_values(v[r, p]))
        for r, p in blocks_of
    ]
    dv = [unstack_heads(dot_tn(e, datt[r, p])) for e, (r, p) in zip(es, blocks_of)]
    dss = [(e.astype(F32) * dw).astype(BF) for e, dw in zip(es, dws)]
    dq = [dot(ds, stack_heads(k[r, p])) for ds, (r, p) in zip(dss, blocks_of)]
    dk = [unstack_heads(dot_tn(ds, q[r, p])) for ds, (r, p) in zip(dss, blocks_of)]
    dqs, dks, dvs = [[x[i : i + 2] for i in range(0, len(x), 2)] for x in (dq, dk, dv)]
    dqs, dks, dvs = [[jnp.concatenate(x, axis=1) for x in y] for y in (dqs, dks, dvs)]
    dq = 10.0 * jnp.concatenate(dqs, axis=0)
    dk = (1.0 / LOG2E) * jnp.concatenate(dks, axis=0)
    dv = jnp.concatenate(dvs, axis=0)
    q_unit = q.astype(F32) * (1.0 / SCALE)
    k_unit = k.astype(F32)
    dq = part(5).astype(F32) * (dq - q_unit * head_sums(q_unit * dq, blocks))
    dk = part(6).astype(F32) * (dk - k_unit * head_sums(k_unit * dk, blocks))
    dqkv = jnp.concatenate([dq.astype(BF), dk.astype(BF), dv.astype(BF)], axis=1)
    return g + dot_nt(dqkv, w_qkv)


def teacher_own(
    x_hbm, reg_hbm, to_a_hbm, a_row_hbm, a_col_hbm, t_qkv,
    x_out, id_ref, far_id_ref, q_ref, k_ref, v_ref, to_a, wqkv,
    pad_ref, x_ref, reg_ref, a_row, a_col, sems,
):
    width = x_ref.shape[3]
    copies = fetch(
        (x_hbm, x_ref, sems.at[0]),
        (to_a_hbm, to_a, sems.at[1]),
        (reg_hbm, reg_ref, sems.at[2]),
        (a_row_hbm, a_row, sems.at[3]),
        (a_col_hbm, a_col, sems.at[4]),
        (t_qkv.at[0], wqkv, sems.at[5]),
    )
    blocks = head_blocks()
    copies[0].wait()
    copies[1].wait()
    x = to_window_order(x_ref, pad_ref, to_a[...])
    x_out[...] = x
    for copy in copies[2:5]:
        copy.wait()
    reg, reg_far = by_level(reg_ref)
    id_ref[...] = window_ids(reg, a_row[...], a_col[...])
    far_id_ref[...] = window_ids(reg_far, a_row[...], a_col[...])
    copies[5].wait()
    q_ref[...] = (unit(dot(x, wqkv[:, :width]), blocks)[0] * SCALE).astype(BF)
    k_ref[...] = unit(dot(x, wqkv[:, width : 2 * width]), blocks)[0].astype(BF)
    v_ref[...] = dot(x, wqkv[:, 2 * width :]).astype(BF)


def teacher_first(
    far_ref, x_ref, id_ref, far_id_ref, q_ref, k_ref, v_ref, to_a, rows_from_a, wqkv, t_out,
    h_ref, first_ref, second_ref, pad_ref, wout, sems,
):
    copies = fetch((t_out.at[0], wout, sems.at[0]))
    width = x_ref.shape[1]
    blocks = head_blocks()
    sent_ids = dot(rows_from_a[...], id_ref[...]).astype(BF)
    sent_ids = dot_nt(jnp.full((8, 128), 1.0 / 128, BF), sent_ids)[0:1]
    empty = jnp.zeros((1, width - 128), F32)
    id_rows = [jnp.concatenate([sent_ids[:, i : i + 128], empty], axis=1) for i in (0, 128)]
    far = to_window_order(far_ref, pad_ref, to_a[...])
    k_far = unit(dot(far, wqkv[:, width : 2 * width]), blocks)[0].astype(BF)
    v_far = dot(far, wqkv[:, 2 * width :]).astype(BF)
    windows = []
    for w in range(4):
        rows = slice(w * WIN, (w + 1) * WIN)
        id_keys = jnp.concatenate([id_ref[rows], far_id_ref[rows]], axis=0)
        keys = [
            jnp.concatenate([near[rows], away[rows]], axis=0)
            for near, away in ((k_ref, k_far), (v_ref, v_far))
        ]
        windows.append((q_ref[rows], keys, (id_ref[rows], id_keys)))
    atts = window_attention(windows)
    copies[0].wait()
    h = residual(x_ref[...], jnp.concatenate(atts, axis=0), wout[...])[0]
    h_ref[...] = h
    values = [dot(rows_from_a[i : i + ROW_SENT], h) for i in (0, 128)]
    at = lax.broadcasted_iota(jnp.int32, (ROW_SENT, 1), 0)
    payloads = [jnp.where(at == ROW_TOKENS, row, x) for row, x in zip(id_rows, values)]
    first_ref[...], second_ref[...] = swapped("lat", *payloads)


def swapped(axis, low, high):
    even = lax.rem(lax.axis_index(axis), 2) == 0
    low, high = low.astype(F32), high.astype(F32)
    return jnp.where(even, low, high).astype(BF), jnp.where(even, high, low).astype(BF)


def packed(rows, table, tokens, sent):
    width = rows.shape[1] - 128
    values = dot(table[:sent], rows[:, :width])
    ids = dot(table, rows[:, width:]).astype(BF)
    row = dot_nt(jnp.full((8, 128), 1.0 / 128, BF), ids)[0:1]
    row = jnp.concatenate([row, jnp.zeros((1, width - 128), F32)], axis=1)
    at = lax.broadcasted_iota(jnp.int32, (sent, 1), 0)
    return jnp.where(at == tokens, row, values).astype(BF)


def opened(sent, table, tokens):
    values = dot(table, sent).astype(BF)
    row = sent.astype(F32)[tokens : tokens + 1, : table.shape[1]]
    ids = dot((table.astype(F32) * row).astype(BF), jnp.ones((table.shape[1], 128), BF))
    return jnp.concatenate([values, ids.astype(BF)], axis=1)


def part(x, name):
    start, kept = AT[name]
    return x[start : start + kept]


TO_NORTH = ("nw", "n", "ne")
TO_SOUTH = ("sw", "s", "se")


def _row_table():
    table = np.zeros((256, NA), ml_dtypes.bfloat16)
    for start, names in ((0, TO_NORTH), (128, TO_SOUTH)):
        rows = np.concatenate([A_TO_G[AT[n][0] : AT[n][0] + AT[n][1]] for n in names])
        table[start : start + 128] = PACK_ROWS.astype(np.float32) @ rows.astype(np.float32)
    return table


ROWS_FROM_A = _row_table()
TO_WEST = (("N", "sw"), ("", "nw"), ("", "w"), ("", "sw"), ("S", "nw"))
TO_EAST = (("N", "se"), ("", "ne"), ("", "e"), ("", "se"), ("S", "ne"))
EXTRA = {
    "nw": (("N", "sw"), ("W", "ne"), ("NW", "se")),
    "n": (("N", "s"),),
    "ne": (("N", "se"), ("E", "nw"), ("NE", "sw")),
    "e": (("E", "w"),),
    "se": (("S", "ne"), ("E", "sw"), ("SE", "nw")),
    "s": (("S", "n"),),
    "sw": (("S", "nw"), ("W", "se"), ("SW", "ne")),
    "w": (("W", "e"),),
    "c": (),
}
LATE = ("nw", "ne", "e", "se", "sw", "w")
ORDER = [name for name, *_ in PARTS]


def _spots(items):
    spots, start = {}, 0
    for side, name in items:
        spots[side, name] = start
        start += AT[name][1]
    return spots


OWN = {("", name): AT[name][0] for name in ORDER}
EDGE = _spots([("N", n) for n in TO_SOUTH] + [("S", n) for n in TO_NORTH])
COME = _spots([(s + "E", n) for s, n in TO_WEST] + [(s + "W", n) for s, n in TO_EAST])
NE_ROWS = 2 * sum(AT[n][1] for n in TO_NORTH)


def gather(sources, items):
    blocks = []
    for item in items:
        for array, spots in sources:
            if item in spots:
                spot = spots[item]
                blocks.append(array[spot : spot + AT[item[1]][1]])
                break
    return blocks[0] if len(blocks) == 1 else jnp.concatenate(blocks, axis=0)


def window_attention(windows):
    found = attend([(q, k, v, id_mask(*ids)) for q, (k, v), ids in windows])
    return [
        jnp.concatenate([(n / d).astype(BF) for n, d in zip(nums, dens)], axis=1)
        for nums, dens, _ in found
    ]


def beside_rows(
    x_ref, id_ref, to_a, s_qkv, s_out, proj, hidden_ref, a_to_g, t_qkv, pack, after_ref,
    g_ref, g0_ref, save0, save1, q_ref, k_ref, v_ref, att_ref, west_ref, east_ref, pad_ref,
):
    width = hidden_ref.shape[1]
    blocks = head_blocks()
    spread = jnp.concatenate([hidden_ref[...], id_ref[...]], axis=1)
    spread = dot(a_to_g[...], spread).astype(BF)
    g_ref[...] = spread
    x = to_window_order(x_ref, pad_ref, to_a[...])
    h = student_layer(x, s_qkv[0], s_out[0], id_ref[...], save0)
    h = student_layer(h, s_qkv[1], s_out[1], id_ref[...], save1)
    predicted = dot(h, proj[...])
    g0_ref[...] = dot_nt(predicted.astype(BF), proj[...])

    for ref, items in ((west_ref, TO_WEST), (east_ref, TO_EAST)):
        rows = gather([(spread, OWN)], items[1:4])
        ref[...] = packed(rows, pack[...], COL_TOKENS, COL_SENT)

    rows = spread[:, :width]
    q = (unit(dot(rows, t_qkv[1, :, :width]), blocks)[0] * SCALE).astype(BF)
    k = unit(dot(rows, t_qkv[1, :, width : 2 * width]), blocks)[0].astype(BF)
    v = dot(rows, t_qkv[1, :, 2 * width :]).astype(BF)
    q_ref[...] = q
    k_ref[...] = k
    v_ref[...] = v
    ids = part(spread, "c")[:, width:]
    [att_ref[...]] = window_attention([(part(q, "c"), [part(k, "c"), part(v, "c")], (ids, ids))])


def on_map():
    lat = lax.axis_index("lat")
    inside = (lat > 0, lat < lax.axis_size("lat") - 1)
    return [jnp.where(x, 1.0, 0.0) for x in inside]


def send_columns(
    first_ref, second_ref, from_north, from_south, west_ref, east_ref, after_ref,
    out_first, out_second,
):
    rows = swapped("lat", first_ref[...], second_ref[...])
    tables = (from_north[...], from_south[...])
    values = sum(dot(table, sent) for table, sent in zip(tables, rows))
    ids = 0.0
    for table, sent, there in zip(tables, rows, on_map()):
        row = sent.astype(F32)[ROW_TOKENS : ROW_TOKENS + 1, :ROW_SENT] * there
        ids += dot_nt(jnp.broadcast_to(row, (8, ROW_SENT)).astype(BF), table)
    at = lax.broadcasted_iota(jnp.int32, (COL_SENT, 1), 0)
    empty = jnp.zeros((1, first_ref.shape[1] - 128), F32)
    payloads = []
    for i, ref in ((0, west_ref), (128, east_ref)):
        row = jnp.concatenate([ids[0:1, i : i + 128], empty], axis=1)
        corners = jnp.where(at == COL_TOKENS, row, values[i : i + COL_SENT])
        payloads.append((ref[...].astype(F32) + corners).astype(BF))
    out_first[...], out_second[...] = swapped("lon", *payloads)


def beside_columns(
    g_ref, first_ref, second_ref, open_rows, t_qkv, q_ref, k_ref, v_ref, after_ref,
    edge_ref, k_out, v_out, n_ref, s_ref,
):
    width = g_ref.shape[1] - 128
    blocks = head_blocks()
    edge = []
    for sent, there in zip(swapped("lat", first_ref[...], second_ref[...]), on_map()):
        rows = opened(sent, open_rows[...], ROW_TOKENS)
        edge.append(jnp.concatenate([rows[:, :width], rows[:, width:] * there.astype(BF)], axis=1))
    edge_ref[...] = jnp.concatenate(edge, axis=0)
    rows = edge_ref[:, :width]
    k = unit(dot(rows, t_qkv[1, :, width : 2 * width]), blocks)[0].astype(BF)
    v = dot(rows, t_qkv[1, :, 2 * width :]).astype(BF)
    k_out[...] = k
    v_out[...] = v
    windows = []
    for name in ("n", "s"):
        items = (("", name),) + EXTRA[name]
        keys = [gather([(own, OWN), (edge, EDGE)], items) for own, edge in ((k_ref, k), (v_ref, v))]
        ids = [gather([(g_ref, OWN), (edge_ref, EDGE)], some)[:, width:] for some in (items[:1], items)]
        windows.append((part(q_ref, name), keys, ids))
    n_ref[...], s_ref[...] = window_attention(windows)


def teacher_second(
    h_ref, g_ref, edge_ref, first_ref, second_ref, q_ref, k_ref, v_ref, k_edge, v_edge,
    c_ref, n_ref, s_ref, open_cols, from_a, g_to_a, t_qkv, t_out, proj, s_qkv, s_out,
    g0_ref, save0, save1, out_hbm, grad_hbm, out_ref, grad_ref, sems,
):
    width = h_ref.shape[1]
    blocks = head_blocks()
    west, east = swapped("lon", first_ref[...], second_ref[...])
    came = [opened(sent, open_cols[...], COL_TOKENS) for sent in (east, west)]
    came = jnp.concatenate(came, axis=0)
    rows = came[:, :width]
    k = unit(dot(rows, t_qkv[1, :, width : 2 * width]), blocks)[0].astype(BF)
    v = dot(rows, t_qkv[1, :, 2 * width :]).astype(BF)
    atts = {"c": c_ref[...], "n": n_ref[...], "s": s_ref[...]}
    windows = []
    for name in LATE:
        items = (("", name),) + EXTRA[name]
        keys = [
            gather([(own, OWN), (edge, EDGE), (new, COME)], items)
            for own, edge, new in ((k_ref, k_edge, k), (v_ref, v_edge, v))
        ]
        ids = [
            gather([(g_ref, OWN), (edge_ref, EDGE), (came, COME)], some)[:, width:]
            for some in (items[:1], items)
        ]
        windows.append((part(q_ref, name), keys, ids))
    atts.update(zip(LATE, window_attention(windows)))
    att = jnp.concatenate([atts[name] for name in ORDER], axis=0)
    att = dot(g_to_a[...], att).astype(BF)
    teacher = residual(h_ref[...], att, t_out[1])[0]
    natural = dot(from_a[...], teacher).astype(BF)
    out_ref[0] = natural.reshape(COLS, TALL, width)[:, :ROWS, :]
    copies = fetch((out_ref, out_hbm, sems.at[0]))

    g = g0_ref[...] - dot_nt(teacher, proj[...])
    g = student_back(g, save1, s_qkv[1], s_out[1])
    g = student_back(g, save0, s_qkv[0], s_out[0])
    high = g.astype(BF)
    low = (g - high.astype(F32)).astype(BF)
    half = COLS // 2
    for i in range(2):
        table = from_a[i * half * TALL : (i + 1) * half * TALL]
        natural = dot(table, high) + dot(table, low)
        cols = pl.ds(i * half, half)
        grad_ref[0, cols] = natural.reshape(half, TALL, g.shape[1])[:, :ROWS, :]
        copies += fetch((grad_ref.at[0, cols], grad_hbm.at[0, cols], sems.at[1 + i]))
    for copy in copies:
        copy.wait()


VMEM = pl.BlockSpec(memory_space=pltpu.VMEM)
ANY = pl.BlockSpec(memory_space=pl.ANY)
HBM = pl.BlockSpec(memory_space=pltpu.HBM)


def call(kernel, name, outs, specs, args, scratch=(), flops=0, out_space=VMEM):
    shapes = [jax.ShapeDtypeStruct(s, d) for s, d in outs]
    touched = sum(a.size * a.dtype.itemsize for a in args)
    return pl.pallas_call(
        kernel,
        name=name,
        out_shape=shapes,
        in_specs=specs,
        out_specs=[out_space] * len(outs),
        scratch_shapes=list(scratch),
        compiler_params=pltpu.CompilerParams(vmem_limit_bytes=28 << 20),
        cost_estimate=pl.CostEstimate(flops=flops, bytes_accessed=touched, transcendentals=0),
    )(*args)


def buffers(*arrays):
    return [pltpu.VMEM(a.shape, a.dtype) for a in arrays] + [
        pltpu.SemaphoreType.DMA((len(arrays),))
    ]


def swaps(size, start):
    route = {}
    for i in range(start, size, 2):
        j = (i + 1) % size
        route[i], route[j] = j, i
    return sorted(route.items())


def inner_swaps(lat_size, lon_size):
    route = []
    for i in range(lat_size):
        for j in range(lon_size):
            if 0 < i < lat_size - 1:
                to = (i - 1 + 2 * (i % 2)) * lon_size + j
            else:
                to = i * lon_size + (j ^ 1)
            route.append((i * lon_size + j, to))
    return route


def shards(teacher_in, student_in, regions, t_qkv, t_out, s_qkv, s_out, s_proj):
    width, narrow = teacher_in.shape[3], student_in.shape[3]
    lat_size, lon_size = lax.axis_size("lat"), lax.axis_size("lon")
    wide = width + 128
    teacher_in = teacher_in.transpose(0, 2, 1, 3)
    student_in = student_in.transpose(0, 2, 1, 3)
    regions = regions.transpose(2, 0, 1)
    far = lax.ppermute(teacher_in, "grp", [(0, 1), (1, 0)])

    pinned = [
        pltpu.with_memory_space_constraint(jnp.asarray(a), pltpu.HBM)
        for a in (teacher_in, regions, TO_A, A_ROW, A_COL, t_qkv)
    ]
    x, ids, far_ids, q, k, v, to_a, wqkv = call(
        teacher_own, "teacher_own",
        [((NA, width), BF), ((NA, 128), BF), ((NA, 128), BF)] + [((NA, width), BF)] * 3
        + [((NA, NAT), BF), (t_qkv.shape[1:], BF)],
        [HBM] * 6, pinned,
        [pltpu.VMEM((COLS, TALL, width), BF)]
        + buffers(teacher_in, regions, A_ROW, A_COL)[:-1]
        + [pltpu.SemaphoreType.DMA((6,))],
        10**9,
    )
    hidden, rows_1, rows_2 = call(
        teacher_first, "teacher_first",
        [((NA, width), BF)] + [((ROW_SENT, width), BF)] * 2,
        [VMEM] * 10 + [HBM],
        [far, x, ids, far_ids, q, k, v, to_a, ROWS_FROM_A, wqkv]
        + [pltpu.with_memory_space_constraint(t_out, pltpu.HBM)],
        [pltpu.VMEM((COLS, TALL, width), BF)] + buffers(t_out[0]), 3 * 10**9,
    )
    sent = rows_2
    rows_2 = lax.ppermute(rows_2, "lat", swaps(lat_size, 0))
    rows_1 = lax.ppermute(rows_1, ("lat", "lon"), inner_swaps(lat_size, lon_size))

    spread, g0, save0, save1, q, k, v, c_att, west, east = call(
        beside_rows, "beside_rows",
        [((NG, wide), BF), ((NA, narrow), F32), ((NA, SAVE), BF), ((NA, SAVE), BF)]
        + [((NG, width), BF)] * 3 + [((AT["c"][1], width), BF)] + [((COL_SENT, width), BF)] * 2,
        [VMEM] * 10 + [ANY],
        [student_in, ids, to_a, s_qkv, s_out, s_proj, hidden, A_TO_G, t_qkv, PACK_OWN, sent],
        [pltpu.VMEM((COLS, TALL, narrow), BF)], 5 * 10**9,
    )
    cols_1, cols_2 = call(
        send_columns, "send_columns",
        [((COL_SENT, width), BF)] * 2,
        [VMEM] * 6 + [ANY],
        [rows_1, rows_2, FROM_NORTH, FROM_SOUTH, west, east, g0], (), 10**7,
    )
    sent = cols_2
    cols_2 = lax.ppermute(cols_2, "lon", swaps(lon_size, 0))
    cols_1 = lax.ppermute(cols_1, "lon", swaps(lon_size, 1))

    edge, k_edge, v_edge, n_att, s_att = call(
        beside_columns, "beside_columns",
        [((NE_ROWS, wide), BF)] + [((NE_ROWS, width), BF)] * 2 + [((AT["n"][1], width), BF)] * 2,
        [VMEM] * 8 + [ANY],
        [spread, rows_1, rows_2, OPEN_ROWS, t_qkv, q, k, v, sent], (), 2 * 10**9,
    )
    args = [hidden, spread, edge, cols_1, cols_2, q, k, v, k_edge, v_edge, c_att, n_att, s_att]
    args += [OPEN_COLS, FROM_A, G_TO_A, t_qkv, t_out, s_proj, s_qkv, s_out, g0, save0, save1]
    out, grad = call(
        teacher_second, "teacher_second",
        [(teacher_in.shape, BF), (student_in.shape, F32)],
        [VMEM] * len(args), args,
        [
            pltpu.VMEM(teacher_in.shape, BF),
            pltpu.VMEM(student_in.shape, F32),
            pltpu.SemaphoreType.DMA((3,)),
        ],
        6 * 10**9, ANY,
    )
    return out.transpose(0, 2, 1, 3), grad.transpose(0, 2, 1, 3)


def solution(mesh):
    tiles = P("grp", "lat", "lon", None)
    return jax.shard_map(
        shards,
        mesh=mesh,
        in_specs=(tiles, tiles, P(None, "lat", "lon"), P(), P(), P(), P(), P()),
        out_specs=(tiles, tiles),
        check_vma=False,
    )
```

```python
import functools

import jax
import jax.numpy as jnp
import ml_dtypes
import numpy as np
from jax import lax
from jax.experimental import pallas as pl
from jax.experimental.pallas import tpu as pltpu
from jax.sharding import PartitionSpec as P

HEADS_T = 8
HEADS_S = 4
EPS = 1e-06
LOG2E = 1.4426950408889634
SCALE = 10.0 * LOG2E
BF = jnp.bfloat16
F32 = jnp.float32

ROWS, COLS = 24, 12
WIN = 80
NA = 4 * WIN
TALL = 32
NAT = COLS * TALL
PAIR = 128

PARTS = (
    ("nw", (0, 6), (0, 3), 32),
    ("n", (0, 6), (3, 9), 48),
    ("ne", (0, 6), (9, 12), 32),
    ("e", (6, 18), (9, 12), 48),
    ("se", (18, 24), (9, 12), 32),
    ("s", (18, 24), (3, 9), 48),
    ("sw", (18, 24), (0, 3), 32),
    ("w", (6, 18), (0, 3), 48),
    ("c", (6, 18), (3, 9), 80),
)
AT = {}
NG = 0
for _name, _r, _c, _kept in PARTS:
    AT[_name] = (NG, _kept)
    NG += _kept


def _a_slot(r, c):
    return (2 * (r // 12) + c // 6) * WIN + (r % 12) * 6 + c % 6


def _tables():
    to_a = np.zeros((NA, NAT), ml_dtypes.bfloat16)
    a_row = np.zeros((NA, ROWS), ml_dtypes.bfloat16)
    a_col = np.zeros((NA, COLS), ml_dtypes.bfloat16)
    for r in range(ROWS):
        for c in range(COLS):
            slot = _a_slot(r, c)
            to_a[slot, c * TALL + r] = 1
            a_row[slot, r] = 1
            a_col[slot, c] = 1
    a_to_g = np.zeros((NG, NA), ml_dtypes.bfloat16)
    for name, (r0, r1), (c0, c1), _ in PARTS:
        spot = AT[name][0]
        for r in range(r0, r1):
            for c in range(c0, c1):
                a_to_g[spot, _a_slot(r, c)] = 1
                spot += 1
    return to_a, a_row, a_col, a_to_g


TO_A, A_ROW, A_COL, A_TO_G = _tables()
FROM_A = np.ascontiguousarray(TO_A.T)
G_TO_A = np.ascontiguousarray(A_TO_G.T)


def _packing(kept):
    table = np.zeros((128, sum(kept)), ml_dtypes.bfloat16)
    token, start = 0, 0
    for rows in kept:
        count = {32: 18, 48: 36}[rows]
        for i in range(count):
            table[token + i, start + i] = 1
        token, start = token + count, start + rows
    return table


def _corners(start, west, east):
    table = np.zeros((256, ROW_SENT), ml_dtypes.bfloat16)
    for i in range(18):
        table[start + i, west + i] = 1
        table[128 + start + i, east + i] = 1
    return table


PACK_ROWS = _packing((32, 48, 32))
PACK_OWN = np.roll(PACK_ROWS, 18, axis=0)
PACK_COLS = _packing((32, 32, 48, 32, 32))
ROW_TOKENS, ROW_SENT = 72, 80
COL_TOKENS, COL_SENT = 108, 112
FROM_NORTH = _corners(0, 0, 54)
FROM_SOUTH = _corners(90, 0, 54)
OPEN_ROWS = np.ascontiguousarray(PACK_ROWS.T[:, :ROW_SENT])
OPEN_COLS = np.ascontiguousarray(PACK_COLS.T[:, :COL_SENT])


def dot(a, b):
    return jnp.dot(a, b, preferred_element_type=F32)


def dot_nt(a, b):
    return lax.dot_general(a, b, (((1,), (1,)), ((), ())), preferred_element_type=F32)


def dot_tn(a, b):
    return lax.dot_general(a, b, (((0,), (0,)), ((), ())), preferred_element_type=F32)


def head_lanes(rows, h):
    lane = lax.broadcasted_iota(jnp.int32, (rows, PAIR), 1)
    return jnp.where((lane >> 6) == h, 1.0, 0.0).astype(BF)


def head_blocks():
    row = lax.broadcasted_iota(jnp.int32, (2 * PAIR, 2 * PAIR), 0)
    lane = lax.broadcasted_iota(jnp.int32, (2 * PAIR, 2 * PAIR), 1)
    return jnp.where((row >> 6) == (lane >> 6), 1.0, 0.0).astype(BF)


def stack_heads(x):
    return jnp.concatenate([x * head_lanes(1, h) for h in range(2)], axis=0)


def stack_values(v):
    rows = v.shape[0]
    ones = jnp.concatenate([head_lanes(rows, h) for h in range(2)], axis=0)
    return jnp.concatenate([stack_heads(v), ones], axis=1)


def unstack_heads(x):
    n = x.shape[0] // 2
    lane = lax.broadcasted_iota(jnp.int32, (1, PAIR), 1) >> 6
    return jnp.where(lane == 0, x[:n], x[n:])


def head_sums(x, blocks):
    step = blocks.shape[0]
    groups = [dot(x[:, i : i + step].astype(BF), blocks) for i in range(0, x.shape[1], step)]
    return groups[0] if len(groups) == 1 else jnp.concatenate(groups, axis=1)


def unit(x, blocks):
    scale = lax.rsqrt(head_sums(x * x, blocks) + EPS)
    return x * scale, scale


def id_mask(id_query, id_keys):
    keys = jnp.concatenate([id_keys] * 2, axis=0)
    row = dot_nt(jnp.full((8, 128), 1.0 / 128, BF), keys)[0:1]
    return id_query.astype(F32)[:, 0:1] == row


def pairs_of(x):
    return [x[:, i : i + PAIR] for i in range(0, x.shape[1], PAIR)]


def attend(windows):
    scores = [
        [dot_nt(qp, stack_heads(kp)) for qp, kp in zip(pairs_of(q), pairs_of(k))]
        for q, k, _, _ in windows
    ]
    es = [
        [jnp.where(w[3], jnp.exp2(s), 0.0).astype(BF) for s in group]
        for w, group in zip(windows, scores)
    ]
    both = [
        [dot(e, stack_values(vp)) for e, vp in zip(group, pairs_of(w[2]))]
        for w, group in zip(windows, es)
    ]
    return [
        ([b[:, :PAIR] for b in group], [b[:, PAIR:] for b in group], e)
        for group, e in zip(both, es)
    ]


def to_window_order(x_ref, pad_ref, to_a):
    pad_ref[...] = jnp.zeros_like(pad_ref)
    pad_ref[:, 0:ROWS, :] = x_ref[0]
    natural = pad_ref[...].reshape(NAT, x_ref.shape[3])
    return dot(to_a, natural).astype(BF)


def window_ids(reg, a_row, a_col):
    table = (reg + 1).astype(F32).astype(BF)
    picked = (dot(a_col, table) * a_row.astype(F32)).astype(BF)
    return dot(picked, jnp.ones((ROWS, 128), BF)).astype(BF)


def by_level(reg_ref):
    level = lax.axis_index("grp")
    low, high = reg_ref[:, 0, :], reg_ref[:, 1, :]
    own = jnp.where(level == 0, low, high)
    return own, low + high - own


def residual(x, att, w):
    y = dot(att, w)
    r = lax.rsqrt(jnp.mean(y * y, axis=1, keepdims=True) + EPS)
    n = y * r
    return (x.astype(F32) + n).astype(BF), n, r


WIDE = 2 * PAIR
SAVE = 11 * WIDE


def student_layer(x, w_qkv, w_out, ids, save_ref):
    blocks = head_blocks()
    qkv = dot(x, w_qkv)
    q, sq = unit(qkv[:, :WIDE], blocks)
    k, sk = unit(qkv[:, WIDE : 2 * WIDE], blocks)
    q = (q * SCALE).astype(BF)
    k = k.astype(BF)
    v = qkv[:, 2 * WIDE :].astype(BF)
    atts = []
    windows = [slice(w * WIN, (w + 1) * WIN) for w in range(4)]
    found = attend([(q[r], k[r], v[r], id_mask(ids[r], ids[r])) for r in windows])
    for rows, (nums, dens, es) in zip(windows, found):
        z = 1.0 / jnp.concatenate(dens, axis=1)
        att = jnp.concatenate(nums, axis=1) * z
        save_ref[rows, 4 * WIDE : 5 * WIDE] = z.astype(BF)
        for i, e in enumerate(es):
            save_ref[rows, (9 + i) * WIDE : (9 + i) * WIDE + 2 * WIN] = e
        atts.append(att.astype(BF))
    att = jnp.concatenate(atts, axis=0)
    h, n, r = residual(x, att, w_out)
    for i, part in ((0, q), (1, k), (2, v), (3, att), (5, sq), (6, sk), (7, n)):
        save_ref[:, i * WIDE : (i + 1) * WIDE] = part.astype(BF)
    save_ref[:, 8 * WIDE : 9 * WIDE] = jnp.broadcast_to(r, (NA, WIDE)).astype(BF)
    return h


def fetch(*pairs):
    copies = [pltpu.make_async_copy(*pair) for pair in pairs]
    for copy in copies:
        copy.start()
    return copies


def student_back(g, save_ref, w_qkv, w_out):
    blocks = head_blocks()
    part = lambda i: save_ref[:, i * WIDE : (i + 1) * WIDE]
    n, r = part(7).astype(F32), part(8).astype(F32)
    dy = r * (g - n * jnp.mean(g * n, axis=1, keepdims=True))
    datt = dot_nt(dy.astype(BF), w_out) * part(4).astype(F32)
    drop = (datt * part(3).astype(F32)).astype(BF) * jnp.asarray(-1.0, BF)
    datt = datt.astype(BF)
    q, k, v = part(0), part(1), part(2)
    windows = [slice(w * WIN, (w + 1) * WIN) for w in range(4)]
    blocks_of = [(r, slice(i, i + PAIR)) for r in windows for i in range(0, WIDE, PAIR)]
    es = [
        save_ref[r, (9 + i) * WIDE : (9 + i) * WIDE + 2 * WIN] for r in windows for i in range(2)
    ]
    dws = [
        dot_nt(jnp.concatenate([datt[r, p], drop[r, p]], axis=1), stack_values(v[r, p]))
        for r, p in blocks_of
    ]
    dv = [unstack_heads(dot_tn(e, datt[r, p])) for e, (r, p) in zip(es, blocks_of)]
    dss = [(e.astype(F32) * dw).astype(BF) for e, dw in zip(es, dws)]
    dq = [dot(ds, stack_heads(k[r, p])) for ds, (r, p) in zip(dss, blocks_of)]
    dk = [unstack_heads(dot_tn(ds, q[r, p])) for ds, (r, p) in zip(dss, blocks_of)]
    dqs, dks, dvs = [[x[i : i + 2] for i in range(0, len(x), 2)] for x in (dq, dk, dv)]
    dqs, dks, dvs = [[jnp.concatenate(x, axis=1) for x in y] for y in (dqs, dks, dvs)]
    dq = 10.0 * jnp.concatenate(dqs, axis=0)
    dk = (1.0 / LOG2E) * jnp.concatenate(dks, axis=0)
    dv = jnp.concatenate(dvs, axis=0)
    q_unit = q.astype(F32) * (1.0 / SCALE)
    k_unit = k.astype(F32)
    dq = part(5).astype(F32) * (dq - q_unit * head_sums(q_unit * dq, blocks))
    dk = part(6).astype(F32) * (dk - k_unit * head_sums(k_unit * dk, blocks))
    dqkv = jnp.concatenate([dq.astype(BF), dk.astype(BF), dv.astype(BF)], axis=1)
    return g + dot_nt(dqkv, w_qkv)


def teacher_own(
    x_hbm, reg_hbm, to_a_hbm, a_row_hbm, a_col_hbm, t_qkv,
    x_out, id_ref, far_id_ref, q_ref, k_ref, v_ref, to_a, wqkv,
    pad_ref, x_ref, reg_ref, a_row, a_col, sems,
):
    width = x_ref.shape[3]
    copies = fetch(
        (x_hbm, x_ref, sems.at[0]),
        (to_a_hbm, to_a, sems.at[1]),
        (reg_hbm, reg_ref, sems.at[2]),
        (a_row_hbm, a_row, sems.at[3]),
        (a_col_hbm, a_col, sems.at[4]),
        (t_qkv.at[0], wqkv, sems.at[5]),
    )
    blocks = head_blocks()
    copies[0].wait()
    copies[1].wait()
    x = to_window_order(x_ref, pad_ref, to_a[...])
    x_out[...] = x
    for copy in copies[2:5]:
        copy.wait()
    reg, reg_far = by_level(reg_ref)
    id_ref[...] = window_ids(reg, a_row[...], a_col[...])
    far_id_ref[...] = window_ids(reg_far, a_row[...], a_col[...])
    copies[5].wait()
    q_ref[...] = (unit(dot(x, wqkv[:, :width]), blocks)[0] * SCALE).astype(BF)
    k_ref[...] = unit(dot(x, wqkv[:, width : 2 * width]), blocks)[0].astype(BF)
    v_ref[...] = dot(x, wqkv[:, 2 * width :]).astype(BF)


def teacher_first(
    far_ref, x_ref, id_ref, far_id_ref, q_ref, k_ref, v_ref, to_a, rows_from_a, wqkv, t_out,
    h_ref, first_ref, second_ref, pad_ref, wout, sems,
):
    copies = fetch((t_out.at[0], wout, sems.at[0]))
    width = x_ref.shape[1]
    blocks = head_blocks()
    sent_ids = dot(rows_from_a[...], id_ref[...]).astype(BF)
    sent_ids = dot_nt(jnp.full((8, 128), 1.0 / 128, BF), sent_ids)[0:1]
    empty = jnp.zeros((1, width - 128), F32)
    id_rows = [jnp.concatenate([sent_ids[:, i : i + 128], empty], axis=1) for i in (0, 128)]
    far = to_window_order(far_ref, pad_ref, to_a[...])
    k_far = unit(dot(far, wqkv[:, width : 2 * width]), blocks)[0].astype(BF)
    v_far = dot(far, wqkv[:, 2 * width :]).astype(BF)
    windows = []
    for w in range(4):
        rows = slice(w * WIN, (w + 1) * WIN)
        id_keys = jnp.concatenate([id_ref[rows], far_id_ref[rows]], axis=0)
        keys = [
            jnp.concatenate([near[rows], away[rows]], axis=0)
            for near, away in ((k_ref, k_far), (v_ref, v_far))
        ]
        windows.append((q_ref[rows], keys, (id_ref[rows], id_keys)))
    atts = window_attention(windows)
    copies[0].wait()
    h = residual(x_ref[...], jnp.concatenate(atts, axis=0), wout[...])[0]
    h_ref[...] = h
    values = [dot(rows_from_a[i : i + ROW_SENT], h) for i in (0, 128)]
    at = lax.broadcasted_iota(jnp.int32, (ROW_SENT, 1), 0)
    payloads = [jnp.where(at == ROW_TOKENS, row, x) for row, x in zip(id_rows, values)]
    first_ref[...], second_ref[...] = swapped("lat", *payloads)


def swapped(axis, low, high):
    even = lax.rem(lax.axis_index(axis), 2) == 0
    low, high = low.astype(F32), high.astype(F32)
    return jnp.where(even, low, high).astype(BF), jnp.where(even, high, low).astype(BF)


def packed(rows, table, tokens, sent):
    width = rows.shape[1] - 128
    values = dot(table[:sent], rows[:, :width])
    ids = dot(table, rows[:, width:]).astype(BF)
    row = dot_nt(jnp.full((8, 128), 1.0 / 128, BF), ids)[0:1]
    row = jnp.concatenate([row, jnp.zeros((1, width - 128), F32)], axis=1)
    at = lax.broadcasted_iota(jnp.int32, (sent, 1), 0)
    return jnp.where(at == tokens, row, values).astype(BF)


def opened(sent, table, tokens):
    values = dot(table, sent).astype(BF)
    row = sent.astype(F32)[tokens : tokens + 1, : table.shape[1]]
    ids = dot((table.astype(F32) * row).astype(BF), jnp.ones((table.shape[1], 128), BF))
    return jnp.concatenate([values, ids.astype(BF)], axis=1)


def part(x, name):
    start, kept = AT[name]
    return x[start : start + kept]


TO_NORTH = ("nw", "n", "ne")
TO_SOUTH = ("sw", "s", "se")


def _row_table():
    table = np.zeros((256, NA), ml_dtypes.bfloat16)
    for start, names in ((0, TO_NORTH), (128, TO_SOUTH)):
        rows = np.concatenate([A_TO_G[AT[n][0] : AT[n][0] + AT[n][1]] for n in names])
        table[start : start + 128] = PACK_ROWS.astype(np.float32) @ rows.astype(np.float32)
    return table


ROWS_FROM_A = _row_table()
TO_WEST = (("N", "sw"), ("", "nw"), ("", "w"), ("", "sw"), ("S", "nw"))
TO_EAST = (("N", "se"), ("", "ne"), ("", "e"), ("", "se"), ("S", "ne"))
EXTRA = {
    "nw": (("N", "sw"), ("W", "ne"), ("NW", "se")),
    "n": (("N", "s"),),
    "ne": (("N", "se"), ("E", "nw"), ("NE", "sw")),
    "e": (("E", "w"),),
    "se": (("S", "ne"), ("E", "sw"), ("SE", "nw")),
    "s": (("S", "n"),),
    "sw": (("S", "nw"), ("W", "se"), ("SW", "ne")),
    "w": (("W", "e"),),
    "c": (),
}
LATE = ("nw", "ne", "e", "se", "sw", "w")
ORDER = [name for name, *_ in PARTS]


def _spots(items):
    spots, start = {}, 0
    for side, name in items:
        spots[side, name] = start
        start += AT[name][1]
    return spots


OWN = {("", name): AT[name][0] for name in ORDER}
EDGE = _spots([("N", n) for n in TO_SOUTH] + [("S", n) for n in TO_NORTH])
COME = _spots([(s + "E", n) for s, n in TO_WEST] + [(s + "W", n) for s, n in TO_EAST])


def gather(sources, items):
    blocks = []
    for item in items:
        for array, spots in sources:
            if item in spots:
                spot = spots[item]
                blocks.append(array[spot : spot + AT[item[1]][1]])
                break
    return blocks[0] if len(blocks) == 1 else jnp.concatenate(blocks, axis=0)


def window_sums(windows):
    found = attend([(q, k, v, id_mask(*ids)) for q, (k, v), ids in windows])
    return [
        (jnp.concatenate(nums, axis=1), jnp.concatenate(dens, axis=1)) for nums, dens, _ in found
    ]


def window_attention(windows):
    return [(num / den).astype(BF) for num, den in window_sums(windows)]


def beside_rows(
    x_ref, id_ref, to_a, s_qkv, s_out, proj, hidden_ref, a_to_g, t_qkv, pack, after_ref,
    g_ref, g0_ref, save0, save1, q_ref, k_ref, v_ref, att_ref, west_ref, east_ref, pad_ref,
):
    width = hidden_ref.shape[1]
    blocks = head_blocks()
    spread = jnp.concatenate([hidden_ref[...], id_ref[...]], axis=1)
    spread = dot(a_to_g[...], spread).astype(BF)
    g_ref[...] = spread
    x = to_window_order(x_ref, pad_ref, to_a[...])
    h = student_layer(x, s_qkv[0], s_out[0], id_ref[...], save0)
    h = student_layer(h, s_qkv[1], s_out[1], id_ref[...], save1)
    predicted = dot(h, proj[...])
    g0_ref[...] = dot_nt(predicted.astype(BF), proj[...])

    for ref, items in ((west_ref, TO_WEST), (east_ref, TO_EAST)):
        rows = gather([(spread, OWN)], items[1:4])
        ref[...] = packed(rows, pack[...], COL_TOKENS, COL_SENT)

    rows = spread[:, :width]
    q = (unit(dot(rows, t_qkv[1, :, :width]), blocks)[0] * SCALE).astype(BF)
    k = unit(dot(rows, t_qkv[1, :, width : 2 * width]), blocks)[0].astype(BF)
    v = dot(rows, t_qkv[1, :, 2 * width :]).astype(BF)
    q_ref[...] = q
    k_ref[...] = k
    v_ref[...] = v
    ids = part(spread, "c")[:, width:]
    [att_ref[...]] = window_attention([(part(q, "c"), [part(k, "c"), part(v, "c")], (ids, ids))])


def on_map():
    lat = lax.axis_index("lat")
    inside = (lat > 0, lat < lax.axis_size("lat") - 1)
    return [jnp.where(x, 1.0, 0.0) for x in inside]


def send_columns(
    first_ref, second_ref, from_north, from_south, west_ref, east_ref, after_ref,
    out_first, out_second,
):
    rows = swapped("lat", first_ref[...], second_ref[...])
    tables = (from_north[...], from_south[...])
    values = sum(dot(table, sent) for table, sent in zip(tables, rows))
    ids = 0.0
    for table, sent, there in zip(tables, rows, on_map()):
        row = sent.astype(F32)[ROW_TOKENS : ROW_TOKENS + 1, :ROW_SENT] * there
        ids += dot_nt(jnp.broadcast_to(row, (8, ROW_SENT)).astype(BF), table)
    at = lax.broadcasted_iota(jnp.int32, (COL_SENT, 1), 0)
    empty = jnp.zeros((1, first_ref.shape[1] - 128), F32)
    payloads = []
    for i, ref in ((0, west_ref), (128, east_ref)):
        row = jnp.concatenate([ids[0:1, i : i + 128], empty], axis=1)
        corners = jnp.where(at == COL_TOKENS, row, values[i : i + COL_SENT])
        payloads.append((ref[...].astype(F32) + corners).astype(BF))
    out_first[...], out_second[...] = swapped("lon", *payloads)


def beside_columns(
    g_ref, first_ref, second_ref, open_rows, t_qkv, q_ref, k_ref, v_ref, after_ref,
    n_ref, s_ref, num_ref, den_ref,
):
    width = g_ref.shape[1] - 128
    blocks = head_blocks()
    edge = []
    for sent, there in zip(swapped("lat", first_ref[...], second_ref[...]), on_map()):
        rows = opened(sent, open_rows[...], ROW_TOKENS)
        edge.append(jnp.concatenate([rows[:, :width], rows[:, width:] * there.astype(BF)], axis=1))
    edge = jnp.concatenate(edge, axis=0)
    rows = edge[:, :width]
    k = unit(dot(rows, t_qkv[1, :, width : 2 * width]), blocks)[0].astype(BF)
    v = dot(rows, t_qkv[1, :, 2 * width :]).astype(BF)
    windows = []
    for name in ("n", "s") + LATE:
        items = [("", name)] + [item for item in EXTRA[name] if item in EDGE]
        keys = [gather([(own, OWN), (x, EDGE)], items) for own, x in ((k_ref, k), (v_ref, v))]
        ids = [gather([(g_ref, OWN), (edge, EDGE)], some)[:, width:] for some in (items[:1], items)]
        windows.append((part(q_ref, name), keys, ids))
    sums = window_sums(windows)
    for ref, (num, den) in zip((n_ref, s_ref), sums):
        ref[...] = (num / den).astype(BF)
    num_ref[...], den_ref[...] = [jnp.concatenate(x, axis=0) for x in zip(*sums[2:])]


def teacher_second(
    h_ref, g_ref, first_ref, second_ref, q_ref, num_ref, den_ref,
    c_ref, n_ref, s_ref, open_cols, from_a, g_to_a, t_qkv, t_out, proj, s_qkv, s_out,
    g0_ref, save0, save1, out_hbm, grad_hbm, out_ref, grad_ref, sems,
):
    width = h_ref.shape[1]
    blocks = head_blocks()
    west, east = swapped("lon", first_ref[...], second_ref[...])
    came = [opened(sent, open_cols[...], COL_TOKENS) for sent in (east, west)]
    came = jnp.concatenate(came, axis=0)
    rows = came[:, :width]
    k = unit(dot(rows, t_qkv[1, :, width : 2 * width]), blocks)[0].astype(BF)
    v = dot(rows, t_qkv[1, :, 2 * width :]).astype(BF)
    atts = {"c": c_ref[...], "n": n_ref[...], "s": s_ref[...]}
    windows = []
    for name in LATE:
        items = [item for item in EXTRA[name] if item in COME]
        keys = [gather([(new, COME)], items) for new in (k, v)]
        ids = (part(g_ref, name)[:, width:], gather([(came, COME)], items)[:, width:])
        windows.append((part(q_ref, name), keys, ids))
    start = 0
    for name, (num, den) in zip(LATE, window_sums(windows)):
        early = slice(start, start + num.shape[0])
        atts[name] = ((num_ref[early] + num) / (den_ref[early] + den)).astype(BF)
        start += num.shape[0]
    att = jnp.concatenate([atts[name] for name in ORDER], axis=0)
    att = dot(g_to_a[...], att).astype(BF)
    teacher = residual(h_ref[...], att, t_out[1])[0]
    natural = dot(from_a[...], teacher).astype(BF)
    out_ref[0] = natural.reshape(COLS, TALL, width)[:, :ROWS, :]
    copies = fetch((out_ref, out_hbm, sems.at[0]))

    g = g0_ref[...] - dot_nt(teacher, proj[...])
    g = student_back(g, save1, s_qkv[1], s_out[1])
    g = student_back(g, save0, s_qkv[0], s_out[0])
    high = g.astype(BF)
    low = (g - high.astype(F32)).astype(BF)
    half = COLS // 2
    for i in range(2):
        table = from_a[i * half * TALL : (i + 1) * half * TALL]
        natural = dot(table, high) + dot(table, low)
        cols = pl.ds(i * half, half)
        grad_ref[0, cols] = natural.reshape(half, TALL, g.shape[1])[:, :ROWS, :]
        copies += fetch((grad_ref.at[0, cols], grad_hbm.at[0, cols], sems.at[1 + i]))
    for copy in copies:
        copy.wait()


VMEM = pl.BlockSpec(memory_space=pltpu.VMEM)
ANY = pl.BlockSpec(memory_space=pl.ANY)
HBM = pl.BlockSpec(memory_space=pltpu.HBM)


def call(kernel, name, outs, specs, args, scratch=(), flops=0, out_space=VMEM):
    shapes = [jax.ShapeDtypeStruct(s, d) for s, d in outs]
    touched = sum(a.size * a.dtype.itemsize for a in args)
    return pl.pallas_call(
        kernel,
        name=name,
        out_shape=shapes,
        in_specs=specs,
        out_specs=[out_space] * len(outs),
        scratch_shapes=list(scratch),
        compiler_params=pltpu.CompilerParams(vmem_limit_bytes=28 << 20),
        cost_estimate=pl.CostEstimate(flops=flops, bytes_accessed=touched, transcendentals=0),
    )(*args)


def buffers(*arrays):
    return [pltpu.VMEM(a.shape, a.dtype) for a in arrays] + [
        pltpu.SemaphoreType.DMA((len(arrays),))
    ]


def swaps(size, start):
    route = {}
    for i in range(start, size, 2):
        j = (i + 1) % size
        route[i], route[j] = j, i
    return sorted(route.items())


def inner_swaps(lat_size, lon_size):
    route = []
    for i in range(lat_size):
        for j in range(lon_size):
            if 0 < i < lat_size - 1:
                to = (i - 1 + 2 * (i % 2)) * lon_size + j
            else:
                to = i * lon_size + (j ^ 1)
            route.append((i * lon_size + j, to))
    return route


def shards(teacher_in, student_in, regions, t_qkv, t_out, s_qkv, s_out, s_proj):
    width, narrow = teacher_in.shape[3], student_in.shape[3]
    lat_size, lon_size = lax.axis_size("lat"), lax.axis_size("lon")
    wide = width + 128
    teacher_in = teacher_in.transpose(0, 2, 1, 3)
    student_in = student_in.transpose(0, 2, 1, 3)
    regions = regions.transpose(2, 0, 1)
    far = lax.ppermute(teacher_in, "grp", [(0, 1), (1, 0)])

    pinned = [
        pltpu.with_memory_space_constraint(jnp.asarray(a), pltpu.HBM)
        for a in (teacher_in, regions, TO_A, A_ROW, A_COL, t_qkv)
    ]
    x, ids, far_ids, q, k, v, to_a, wqkv = call(
        teacher_own, "teacher_own",
        [((NA, width), BF), ((NA, 128), BF), ((NA, 128), BF)] + [((NA, width), BF)] * 3
        + [((NA, NAT), BF), (t_qkv.shape[1:], BF)],
        [HBM] * 6, pinned,
        [pltpu.VMEM((COLS, TALL, width), BF)]
        + buffers(teacher_in, regions, A_ROW, A_COL)[:-1]
        + [pltpu.SemaphoreType.DMA((6,))],
        10**9,
    )
    hidden, rows_1, rows_2 = call(
        teacher_first, "teacher_first",
        [((NA, width), BF)] + [((ROW_SENT, width), BF)] * 2,
        [VMEM] * 10 + [HBM],
        [far, x, ids, far_ids, q, k, v, to_a, ROWS_FROM_A, wqkv]
        + [pltpu.with_memory_space_constraint(t_out, pltpu.HBM)],
        [pltpu.VMEM((COLS, TALL, width), BF)] + buffers(t_out[0]), 3 * 10**9,
    )
    sent = rows_2
    rows_2 = lax.ppermute(rows_2, "lat", swaps(lat_size, 0))
    rows_1 = lax.ppermute(rows_1, ("lat", "lon"), inner_swaps(lat_size, lon_size))

    spread, g0, save0, save1, q, k, v, c_att, west, east = call(
        beside_rows, "beside_rows",
        [((NG, wide), BF), ((NA, narrow), F32), ((NA, SAVE), BF), ((NA, SAVE), BF)]
        + [((NG, width), BF)] * 3 + [((AT["c"][1], width), BF)] + [((COL_SENT, width), BF)] * 2,
        [VMEM] * 10 + [ANY],
        [student_in, ids, to_a, s_qkv, s_out, s_proj, hidden, A_TO_G, t_qkv, PACK_OWN, sent],
        [pltpu.VMEM((COLS, TALL, narrow), BF)], 5 * 10**9,
    )
    cols_1, cols_2 = call(
        send_columns, "send_columns",
        [((COL_SENT, width), BF)] * 2,
        [VMEM] * 6 + [ANY],
        [rows_1, rows_2, FROM_NORTH, FROM_SOUTH, west, east, g0], (), 10**7,
    )
    sent = cols_2
    cols_2 = lax.ppermute(cols_2, "lon", swaps(lon_size, 0))
    cols_1 = lax.ppermute(cols_1, "lon", swaps(lon_size, 1))

    late = sum(AT[name][1] for name in LATE)
    n_att, s_att, nums, dens = call(
        beside_columns, "beside_columns",
        [((AT["n"][1], width), BF)] * 2 + [((late, width), F32)] * 2,
        [VMEM] * 8 + [ANY],
        [spread, rows_1, rows_2, OPEN_ROWS, t_qkv, q, k, v, sent], (), 2 * 10**9,
    )
    args = [hidden, spread, cols_1, cols_2, q, nums, dens, c_att, n_att, s_att]
    args += [OPEN_COLS, FROM_A, G_TO_A, t_qkv, t_out, s_proj, s_qkv, s_out, g0, save0, save1]
    out, grad = call(
        teacher_second, "teacher_second",
        [(teacher_in.shape, BF), (student_in.shape, F32)],
        [VMEM] * len(args), args,
        [
            pltpu.VMEM(teacher_in.shape, BF),
            pltpu.VMEM(student_in.shape, F32),
            pltpu.SemaphoreType.DMA((3,)),
        ],
        6 * 10**9, ANY,
    )
    return out.transpose(0, 2, 1, 3), grad.transpose(0, 2, 1, 3)


def solution(mesh):
    tiles = P("grp", "lat", "lon", None)
    return jax.shard_map(
        shards,
        mesh=mesh,
        in_specs=(tiles, tiles, P(None, "lat", "lon"), P(), P(), P(), P(), P()),
        out_specs=(tiles, tiles),
        check_vma=False,
    )
```

```python
import functools

import jax
import jax.numpy as jnp
import ml_dtypes
import numpy as np
from jax import lax
from jax.experimental import pallas as pl
from jax.experimental.pallas import tpu as pltpu
from jax.sharding import PartitionSpec as P

HEADS_T = 8
HEADS_S = 4
EPS = 1e-06
LOG2E = 1.4426950408889634
SCALE = 10.0 * LOG2E
BF = jnp.bfloat16
F32 = jnp.float32

ROWS, COLS = 24, 12
WIN = 80
NA = 4 * WIN
TALL = 32
NAT = COLS * TALL
PAIR = 128

PARTS = (
    ("nw", (0, 6), (0, 3), 32),
    ("n", (0, 6), (3, 9), 48),
    ("ne", (0, 6), (9, 12), 32),
    ("e", (6, 18), (9, 12), 48),
    ("se", (18, 24), (9, 12), 32),
    ("s", (18, 24), (3, 9), 48),
    ("sw", (18, 24), (0, 3), 32),
    ("w", (6, 18), (0, 3), 48),
    ("c", (6, 18), (3, 9), 80),
)
AT = {}
NG = 0
for _name, _r, _c, _kept in PARTS:
    AT[_name] = (NG, _kept)
    NG += _kept


def _a_slot(r, c):
    return (2 * (r // 12) + c // 6) * WIN + (r % 12) * 6 + c % 6


def _tables():
    to_a = np.zeros((NA, NAT), ml_dtypes.bfloat16)
    a_row = np.zeros((NA, ROWS), ml_dtypes.bfloat16)
    a_col = np.zeros((NA, COLS), ml_dtypes.bfloat16)
    for r in range(ROWS):
        for c in range(COLS):
            slot = _a_slot(r, c)
            to_a[slot, c * TALL + r] = 1
            a_row[slot, r] = 1
            a_col[slot, c] = 1
    a_to_g = np.zeros((NG, NA), ml_dtypes.bfloat16)
    for name, (r0, r1), (c0, c1), _ in PARTS:
        spot = AT[name][0]
        for r in range(r0, r1):
            for c in range(c0, c1):
                a_to_g[spot, _a_slot(r, c)] = 1
                spot += 1
    return to_a, a_row, a_col, a_to_g


TO_A, A_ROW, A_COL, A_TO_G = _tables()
FROM_A = np.ascontiguousarray(TO_A.T)
G_TO_A = np.ascontiguousarray(A_TO_G.T)


def _packing(kept):
    table = np.zeros((128, sum(kept)), ml_dtypes.bfloat16)
    token, start = 0, 0
    for rows in kept:
        count = {32: 18, 48: 36}[rows]
        for i in range(count):
            table[token + i, start + i] = 1
        token, start = token + count, start + rows
    return table


def _corners(start, west, east):
    table = np.zeros((256, ROW_SENT), ml_dtypes.bfloat16)
    for i in range(18):
        table[start + i, west + i] = 1
        table[128 + start + i, east + i] = 1
    return table


PACK_ROWS = _packing((32, 48, 32))
PACK_OWN = np.roll(PACK_ROWS, 18, axis=0)
PACK_COLS = _packing((32, 32, 48, 32, 32))
ROW_TOKENS, ROW_SENT = 72, 80
COL_TOKENS, COL_SENT = 108, 112
FROM_NORTH = _corners(0, 0, 54)
FROM_SOUTH = _corners(90, 0, 54)
OPEN_ROWS = np.ascontiguousarray(PACK_ROWS.T[:, :ROW_SENT])
OPEN_COLS = np.ascontiguousarray(PACK_COLS.T[:, :COL_SENT])


def dot(a, b):
    return jnp.dot(a, b, preferred_element_type=F32)


def dot_nt(a, b):
    return lax.dot_general(a, b, (((1,), (1,)), ((), ())), preferred_element_type=F32)


def dot_tn(a, b):
    return lax.dot_general(a, b, (((0,), (0,)), ((), ())), preferred_element_type=F32)


def head_lanes(rows, h):
    lane = lax.broadcasted_iota(jnp.int32, (rows, PAIR), 1)
    return jnp.where((lane >> 6) == h, 1.0, 0.0).astype(BF)


def head_blocks():
    row = lax.broadcasted_iota(jnp.int32, (2 * PAIR, 2 * PAIR), 0)
    lane = lax.broadcasted_iota(jnp.int32, (2 * PAIR, 2 * PAIR), 1)
    return jnp.where((row >> 6) == (lane >> 6), 1.0, 0.0).astype(BF)


def stack_heads(x):
    return jnp.concatenate([x * head_lanes(1, h) for h in range(2)], axis=0)


def stack_values(v):
    rows = v.shape[0]
    ones = jnp.concatenate([head_lanes(rows, h) for h in range(2)], axis=0)
    return jnp.concatenate([stack_heads(v), ones], axis=1)


def unstack_heads(x):
    n = x.shape[0] // 2
    lane = lax.broadcasted_iota(jnp.int32, (1, PAIR), 1) >> 6
    return jnp.where(lane == 0, x[:n], x[n:])


def head_sums(x, blocks):
    step = blocks.shape[0]
    groups = [dot(x[:, i : i + step].astype(BF), blocks) for i in range(0, x.shape[1], step)]
    return groups[0] if len(groups) == 1 else jnp.concatenate(groups, axis=1)


def unit(x, blocks):
    scale = lax.rsqrt(head_sums(x * x, blocks) + EPS)
    return x * scale, scale


def id_mask(id_query, id_keys):
    keys = jnp.concatenate([id_keys] * 2, axis=0)
    row = dot_nt(jnp.full((8, 128), 1.0 / 128, BF), keys)[0:1]
    return id_query.astype(F32)[:, 0:1] == row


def pairs_of(x):
    return [x[:, i : i + PAIR] for i in range(0, x.shape[1], PAIR)]


def attend(windows):
    scores = [
        [dot_nt(qp, stack_heads(kp)) for qp, kp in zip(pairs_of(q), pairs_of(k))]
        for q, k, _, _ in windows
    ]
    es = [
        [jnp.where(w[3], jnp.exp2(s), 0.0).astype(BF) for s in group]
        for w, group in zip(windows, scores)
    ]
    both = [
        [dot(e, stack_values(vp)) for e, vp in zip(group, pairs_of(w[2]))]
        for w, group in zip(windows, es)
    ]
    return [
        ([b[:, :PAIR] for b in group], [b[:, PAIR:] for b in group], e)
        for group, e in zip(both, es)
    ]


def to_window_order(x_ref, pad_ref, to_a):
    pad_ref[...] = jnp.zeros_like(pad_ref)
    pad_ref[:, 0:ROWS, :] = x_ref[0]
    natural = pad_ref[...].reshape(NAT, x_ref.shape[3])
    return dot(to_a, natural).astype(BF)


def window_ids(reg, a_row, a_col):
    table = (reg + 1).astype(F32).astype(BF)
    picked = (dot(a_col, table) * a_row.astype(F32)).astype(BF)
    return dot(picked, jnp.ones((ROWS, 128), BF)).astype(BF)


def by_level(reg_ref):
    level = lax.axis_index("grp")
    low, high = reg_ref[:, 0, :], reg_ref[:, 1, :]
    own = jnp.where(level == 0, low, high)
    return own, low + high - own


def residual(x, att, w):
    y = dot(att, w)
    r = lax.rsqrt(jnp.mean(y * y, axis=1, keepdims=True) + EPS)
    n = y * r
    return (x.astype(F32) + n).astype(BF), n, r


WIDE = 2 * PAIR
SAVE = 11 * WIDE


def student_layer(x, w_qkv, w_out, ids, save_ref):
    blocks = head_blocks()
    qkv = dot(x, w_qkv)
    q, sq = unit(qkv[:, :WIDE], blocks)
    k, sk = unit(qkv[:, WIDE : 2 * WIDE], blocks)
    q = (q * SCALE).astype(BF)
    k = k.astype(BF)
    v = qkv[:, 2 * WIDE :].astype(BF)
    atts = []
    windows = [slice(w * WIN, (w + 1) * WIN) for w in range(4)]
    found = attend([(q[r], k[r], v[r], id_mask(ids[r], ids[r])) for r in windows])
    for rows, (nums, dens, es) in zip(windows, found):
        z = 1.0 / jnp.concatenate(dens, axis=1)
        att = jnp.concatenate(nums, axis=1) * z
        save_ref[rows, 4 * WIDE : 5 * WIDE] = z.astype(BF)
        for i, e in enumerate(es):
            save_ref[rows, (9 + i) * WIDE : (9 + i) * WIDE + 2 * WIN] = e
        atts.append(att.astype(BF))
    att = jnp.concatenate(atts, axis=0)
    h, n, r = residual(x, att, w_out)
    for i, part in ((0, q), (1, k), (2, v), (3, att), (5, sq), (6, sk), (7, n)):
        save_ref[:, i * WIDE : (i + 1) * WIDE] = part.astype(BF)
    save_ref[:, 8 * WIDE : 9 * WIDE] = jnp.broadcast_to(r, (NA, WIDE)).astype(BF)
    return h


def fetch(*pairs):
    copies = [pltpu.make_async_copy(*pair) for pair in pairs]
    for copy in copies:
        copy.start()
    return copies


def student_back(g, save_ref, w_qkv, w_out):
    blocks = head_blocks()
    part = lambda i: save_ref[:, i * WIDE : (i + 1) * WIDE]
    n, r = part(7).astype(F32), part(8).astype(F32)
    dy = r * (g - n * jnp.mean(g * n, axis=1, keepdims=True))
    datt = dot_nt(dy.astype(BF), w_out) * part(4).astype(F32)
    drop = (datt * part(3).astype(F32)).astype(BF) * jnp.asarray(-1.0, BF)
    datt = datt.astype(BF)
    q, k, v = part(0), part(1), part(2)
    windows = [slice(w * WIN, (w + 1) * WIN) for w in range(4)]
    blocks_of = [(r, slice(i, i + PAIR)) for r in windows for i in range(0, WIDE, PAIR)]
    es = [
        save_ref[r, (9 + i) * WIDE : (9 + i) * WIDE + 2 * WIN] for r in windows for i in range(2)
    ]
    dws = [
        dot_nt(jnp.concatenate([datt[r, p], drop[r, p]], axis=1), stack_values(v[r, p]))
        for r, p in blocks_of
    ]
    dv = [unstack_heads(dot_tn(e, datt[r, p])) for e, (r, p) in zip(es, blocks_of)]
    dss = [(e.astype(F32) * dw).astype(BF) for e, dw in zip(es, dws)]
    dq = [dot(ds, stack_heads(k[r, p])) for ds, (r, p) in zip(dss, blocks_of)]
    dk = [unstack_heads(dot_tn(ds, q[r, p])) for ds, (r, p) in zip(dss, blocks_of)]
    dqs, dks, dvs = [[x[i : i + 2] for i in range(0, len(x), 2)] for x in (dq, dk, dv)]
    dqs, dks, dvs = [[jnp.concatenate(x, axis=1) for x in y] for y in (dqs, dks, dvs)]
    dq = 10.0 * jnp.concatenate(dqs, axis=0)
    dk = (1.0 / LOG2E) * jnp.concatenate(dks, axis=0)
    dv = jnp.concatenate(dvs, axis=0)
    q_unit = q.astype(F32) * (1.0 / SCALE)
    k_unit = k.astype(F32)
    dq = part(5).astype(F32) * (dq - q_unit * head_sums(q_unit * dq, blocks))
    dk = part(6).astype(F32) * (dk - k_unit * head_sums(k_unit * dk, blocks))
    dqkv = jnp.concatenate([dq.astype(BF), dk.astype(BF), dv.astype(BF)], axis=1)
    return g + dot_nt(dqkv, w_qkv)


def teacher_own(
    x_hbm, reg_hbm, to_a_hbm, a_row_hbm, a_col_hbm, t_qkv,
    x_out, id_ref, far_id_ref, q_ref, k_ref, v_ref, to_a, wqkv,
    pad_ref, x_ref, reg_ref, a_row, a_col, sems,
):
    width = x_ref.shape[3]
    copies = fetch(
        (x_hbm, x_ref, sems.at[0]),
        (to_a_hbm, to_a, sems.at[1]),
        (reg_hbm, reg_ref, sems.at[2]),
        (a_row_hbm, a_row, sems.at[3]),
        (a_col_hbm, a_col, sems.at[4]),
        (t_qkv.at[0], wqkv, sems.at[5]),
    )
    blocks = head_blocks()
    copies[0].wait()
    copies[1].wait()
    x = to_window_order(x_ref, pad_ref, to_a[...])
    x_out[...] = x
    for copy in copies[2:5]:
        copy.wait()
    reg, reg_far = by_level(reg_ref)
    id_ref[...] = window_ids(reg, a_row[...], a_col[...])
    far_id_ref[...] = window_ids(reg_far, a_row[...], a_col[...])
    copies[5].wait()
    q_ref[...] = (unit(dot(x, wqkv[:, :width]), blocks)[0] * SCALE).astype(BF)
    k_ref[...] = unit(dot(x, wqkv[:, width : 2 * width]), blocks)[0].astype(BF)
    v_ref[...] = dot(x, wqkv[:, 2 * width :]).astype(BF)


def teacher_first(
    far_ref, x_ref, id_ref, far_id_ref, q_ref, k_ref, v_ref, to_a, rows_from_a, wqkv, t_out,
    h_ref, first_ref, second_ref, pad_ref, wout, sems,
):
    copies = fetch((t_out.at[0], wout, sems.at[0]))
    width = x_ref.shape[1]
    blocks = head_blocks()
    sent_ids = dot(rows_from_a[...], id_ref[...]).astype(BF)
    sent_ids = dot_nt(jnp.full((8, 128), 1.0 / 128, BF), sent_ids)[0:1]
    empty = jnp.zeros((1, width - 128), F32)
    id_rows = [jnp.concatenate([sent_ids[:, i : i + 128], empty], axis=1) for i in (0, 128)]
    far = to_window_order(far_ref, pad_ref, to_a[...])
    k_far = unit(dot(far, wqkv[:, width : 2 * width]), blocks)[0].astype(BF)
    v_far = dot(far, wqkv[:, 2 * width :]).astype(BF)
    windows = []
    for w in range(4):
        rows = slice(w * WIN, (w + 1) * WIN)
        id_keys = jnp.concatenate([id_ref[rows], far_id_ref[rows]], axis=0)
        keys = [
            jnp.concatenate([near[rows], away[rows]], axis=0)
            for near, away in ((k_ref, k_far), (v_ref, v_far))
        ]
        windows.append((q_ref[rows], keys, (id_ref[rows], id_keys)))
    atts = window_attention(windows)
    copies[0].wait()
    h = residual(x_ref[...], jnp.concatenate(atts, axis=0), wout[...])[0]
    h_ref[...] = h
    values = [dot(rows_from_a[i : i + ROW_SENT], h) for i in (0, 128)]
    at = lax.broadcasted_iota(jnp.int32, (ROW_SENT, 1), 0)
    payloads = [jnp.where(at == ROW_TOKENS, row, x) for row, x in zip(id_rows, values)]
    first_ref[...], second_ref[...] = swapped("lat", *payloads)


def swapped(axis, low, high):
    even = lax.rem(lax.axis_index(axis), 2) == 0
    low, high = low.astype(F32), high.astype(F32)
    return jnp.where(even, low, high).astype(BF), jnp.where(even, high, low).astype(BF)


def packed(rows, table, tokens, sent):
    width = rows.shape[1] - 128
    values = dot(table[:sent], rows[:, :width])
    ids = dot(table, rows[:, width:]).astype(BF)
    row = dot_nt(jnp.full((8, 128), 1.0 / 128, BF), ids)[0:1]
    row = jnp.concatenate([row, jnp.zeros((1, width - 128), F32)], axis=1)
    at = lax.broadcasted_iota(jnp.int32, (sent, 1), 0)
    return jnp.where(at == tokens, row, values).astype(BF)


def opened(sent, table, tokens):
    values = dot(table, sent).astype(BF)
    return jnp.concatenate([values, opened_ids(sent, table, tokens)], axis=1)


def opened_ids(sent, table, tokens):
    row = sent.astype(F32)[tokens : tokens + 1, : table.shape[1]]
    picked = (table.astype(F32) * row).astype(BF)
    return dot(picked, jnp.ones((table.shape[1], 128), BF)).astype(BF)


def part(x, name):
    start, kept = AT[name]
    return x[start : start + kept]


TO_NORTH = ("nw", "n", "ne")
TO_SOUTH = ("sw", "s", "se")


def _row_table():
    table = np.zeros((256, NA), ml_dtypes.bfloat16)
    for start, names in ((0, TO_NORTH), (128, TO_SOUTH)):
        rows = np.concatenate([A_TO_G[AT[n][0] : AT[n][0] + AT[n][1]] for n in names])
        table[start : start + 128] = PACK_ROWS.astype(np.float32) @ rows.astype(np.float32)
    return table


ROWS_FROM_A = _row_table()
TO_WEST = (("N", "sw"), ("", "nw"), ("", "w"), ("", "sw"), ("S", "nw"))
TO_EAST = (("N", "se"), ("", "ne"), ("", "e"), ("", "se"), ("S", "ne"))
EXTRA = {
    "nw": (("N", "sw"), ("W", "ne"), ("NW", "se")),
    "n": (("N", "s"),),
    "ne": (("N", "se"), ("E", "nw"), ("NE", "sw")),
    "e": (("E", "w"),),
    "se": (("S", "ne"), ("E", "sw"), ("SE", "nw")),
    "s": (("S", "n"),),
    "sw": (("S", "nw"), ("W", "se"), ("SW", "ne")),
    "w": (("W", "e"),),
    "c": (),
}
LATE = ("nw", "ne", "e", "se", "sw", "w")
ORDER = [name for name, *_ in PARTS]


def _spots(items):
    spots, start = {}, 0
    for side, name in items:
        spots[side, name] = start
        start += AT[name][1]
    return spots


OWN = {("", name): AT[name][0] for name in ORDER}
EDGE = _spots([("N", n) for n in TO_SOUTH] + [("S", n) for n in TO_NORTH])
COME = _spots([(s + "E", n) for s, n in TO_WEST] + [(s + "W", n) for s, n in TO_EAST])


def gather(sources, items):
    blocks = []
    for item in items:
        for array, spots in sources:
            if item in spots:
                spot = spots[item]
                blocks.append(array[spot : spot + AT[item[1]][1]])
                break
    return blocks[0] if len(blocks) == 1 else jnp.concatenate(blocks, axis=0)


def window_sums(windows):
    found = attend([(q, k, v, id_mask(*ids)) for q, (k, v), ids in windows])
    return [
        (jnp.concatenate(nums, axis=1), jnp.concatenate(dens, axis=1)) for nums, dens, _ in found
    ]


def window_attention(windows):
    return [(num / den).astype(BF) for num, den in window_sums(windows)]


def beside_rows(
    x_ref, id_ref, to_a, s_qkv, s_out, proj, hidden_ref, a_to_g, t_qkv, pack, after_ref,
    g_ref, g0_ref, save0, save1, q_ref, k_ref, v_ref, att_ref, west_ref, east_ref, pad_ref,
):
    width = hidden_ref.shape[1]
    blocks = head_blocks()
    spread = jnp.concatenate([hidden_ref[...], id_ref[...]], axis=1)
    spread = dot(a_to_g[...], spread).astype(BF)
    g_ref[...] = spread
    x = to_window_order(x_ref, pad_ref, to_a[...])
    h = student_layer(x, s_qkv[0], s_out[0], id_ref[...], save0)
    h = student_layer(h, s_qkv[1], s_out[1], id_ref[...], save1)
    predicted = dot(h, proj[...])
    g0_ref[...] = dot_nt(predicted.astype(BF), proj[...])

    for ref, items in ((west_ref, TO_WEST), (east_ref, TO_EAST)):
        rows = gather([(spread, OWN)], items[1:4])
        ref[...] = packed(rows, pack[...], COL_TOKENS, COL_SENT)

    rows = spread[:, :width]
    q = (unit(dot(rows, t_qkv[1, :, :width]), blocks)[0] * SCALE).astype(BF)
    k = unit(dot(rows, t_qkv[1, :, width : 2 * width]), blocks)[0].astype(BF)
    v = dot(rows, t_qkv[1, :, 2 * width :]).astype(BF)
    q_ref[...] = q
    k_ref[...] = k
    v_ref[...] = v
    ids = part(spread, "c")[:, width:]
    [att_ref[...]] = window_attention([(part(q, "c"), [part(k, "c"), part(v, "c")], (ids, ids))])


def on_map():
    lat = lax.axis_index("lat")
    inside = (lat > 0, lat < lax.axis_size("lat") - 1)
    return [jnp.where(x, 1.0, 0.0) for x in inside]


def send_columns(
    first_ref, second_ref, from_north, from_south, west_ref, east_ref, after_ref,
    out_first, out_second,
):
    rows = swapped("lat", first_ref[...], second_ref[...])
    tables = (from_north[...], from_south[...])
    values = sum(dot(table, sent) for table, sent in zip(tables, rows))
    ids = 0.0
    for table, sent, there in zip(tables, rows, on_map()):
        row = sent.astype(F32)[ROW_TOKENS : ROW_TOKENS + 1, :ROW_SENT] * there
        ids += dot_nt(jnp.broadcast_to(row, (8, ROW_SENT)).astype(BF), table)
    at = lax.broadcasted_iota(jnp.int32, (COL_SENT, 1), 0)
    empty = jnp.zeros((1, first_ref.shape[1] - 128), F32)
    payloads = []
    for i, ref in ((0, west_ref), (128, east_ref)):
        row = jnp.concatenate([ids[0:1, i : i + 128], empty], axis=1)
        corners = jnp.where(at == COL_TOKENS, row, values[i : i + COL_SENT])
        payloads.append((ref[...].astype(F32) + corners).astype(BF))
    out_first[...], out_second[...] = swapped("lon", *payloads)


def beside_columns(
    g_ref, first_ref, second_ref, open_rows, t_qkv, q_ref, k_ref, v_ref, after_ref,
    n_ref, s_ref, num_ref, den_ref,
):
    width = g_ref.shape[1] - 128
    blocks = head_blocks()
    edge = []
    for sent, there in zip(swapped("lat", first_ref[...], second_ref[...]), on_map()):
        rows = opened(sent, open_rows[...], ROW_TOKENS)
        edge.append(jnp.concatenate([rows[:, :width], rows[:, width:] * there.astype(BF)], axis=1))
    edge = jnp.concatenate(edge, axis=0)
    rows = edge[:, :width]
    k = unit(dot(rows, t_qkv[1, :, width : 2 * width]), blocks)[0].astype(BF)
    v = dot(rows, t_qkv[1, :, 2 * width :]).astype(BF)
    windows = []
    for name in ("n", "s") + LATE:
        items = [("", name)] + [item for item in EXTRA[name] if item in EDGE]
        keys = [gather([(own, OWN), (x, EDGE)], items) for own, x in ((k_ref, k), (v_ref, v))]
        ids = [gather([(g_ref, OWN), (edge, EDGE)], some)[:, width:] for some in (items[:1], items)]
        windows.append((part(q_ref, name), keys, ids))
    sums = window_sums(windows)
    for ref, (num, den) in zip((n_ref, s_ref), sums):
        ref[...] = (num / den).astype(BF)
    num_ref[...], den_ref[...] = [jnp.concatenate(x, axis=0) for x in zip(*sums[2:])]


def teacher_second(
    h_ref, g_ref, first_ref, second_ref, q_ref, num_ref, den_ref,
    c_ref, n_ref, s_ref, open_cols, from_a, g_to_a, t_qkv, t_out, proj, s_qkv, s_out,
    g0_ref, save0, save1, out_hbm, grad_hbm, out_ref, grad_ref, sems,
):
    width = h_ref.shape[1]
    blocks = head_blocks()
    west, east = swapped("lon", first_ref[...], second_ref[...])
    table = open_cols[...]
    ids_came = jnp.concatenate([opened_ids(x, table, COL_TOKENS) for x in (east, west)], axis=0)
    rows = jnp.concatenate([east, west], axis=0)
    k = unit(dot(rows, t_qkv[1, :, width : 2 * width]), blocks)[0].astype(BF)
    v = dot(rows, t_qkv[1, :, 2 * width :]).astype(BF)
    k, v = [
        jnp.concatenate([dot(table, x[:COL_SENT]), dot(table, x[COL_SENT:])], axis=0).astype(BF)
        for x in (k, v)
    ]
    atts = {"c": c_ref[...], "n": n_ref[...], "s": s_ref[...]}
    windows = []
    for name in LATE:
        items = [item for item in EXTRA[name] if item in COME]
        keys = [gather([(new, COME)], items) for new in (k, v)]
        ids = (part(g_ref, name)[:, width:], gather([(ids_came, COME)], items))
        windows.append((part(q_ref, name), keys, ids))
    start = 0
    for name, (num, den) in zip(LATE, window_sums(windows)):
        early = slice(start, start + num.shape[0])
        atts[name] = ((num_ref[early] + num) / (den_ref[early] + den)).astype(BF)
        start += num.shape[0]
    att = jnp.concatenate([atts[name] for name in ORDER], axis=0)
    att = dot(g_to_a[...], att).astype(BF)
    teacher = residual(h_ref[...], att, t_out[1])[0]
    natural = dot(from_a[...], teacher).astype(BF)
    out_ref[0] = natural.reshape(COLS, TALL, width)[:, :ROWS, :]
    copies = fetch((out_ref, out_hbm, sems.at[0]))

    g = g0_ref[...] - dot_nt(teacher, proj[...])
    g = student_back(g, save1, s_qkv[1], s_out[1])
    g = student_back(g, save0, s_qkv[0], s_out[0])
    high = g.astype(BF)
    low = (g - high.astype(F32)).astype(BF)
    half = COLS // 2
    for i in range(2):
        table = from_a[i * half * TALL : (i + 1) * half * TALL]
        natural = dot(table, high) + dot(table, low)
        cols = pl.ds(i * half, half)
        grad_ref[0, cols] = natural.reshape(half, TALL, g.shape[1])[:, :ROWS, :]
        copies += fetch((grad_ref.at[0, cols], grad_hbm.at[0, cols], sems.at[1 + i]))
    for copy in copies:
        copy.wait()


VMEM = pl.BlockSpec(memory_space=pltpu.VMEM)
ANY = pl.BlockSpec(memory_space=pl.ANY)
HBM = pl.BlockSpec(memory_space=pltpu.HBM)


def call(kernel, name, outs, specs, args, scratch=(), flops=0, out_space=VMEM):
    shapes = [jax.ShapeDtypeStruct(s, d) for s, d in outs]
    touched = sum(a.size * a.dtype.itemsize for a in args)
    return pl.pallas_call(
        kernel,
        name=name,
        out_shape=shapes,
        in_specs=specs,
        out_specs=[out_space] * len(outs),
        scratch_shapes=list(scratch),
        compiler_params=pltpu.CompilerParams(vmem_limit_bytes=28 << 20),
        cost_estimate=pl.CostEstimate(flops=flops, bytes_accessed=touched, transcendentals=0),
    )(*args)


def buffers(*arrays):
    return [pltpu.VMEM(a.shape, a.dtype) for a in arrays] + [
        pltpu.SemaphoreType.DMA((len(arrays),))
    ]


def swaps(size, start):
    route = {}
    for i in range(start, size, 2):
        j = (i + 1) % size
        route[i], route[j] = j, i
    return sorted(route.items())


def inner_swaps(lat_size, lon_size):
    route = []
    for i in range(lat_size):
        for j in range(lon_size):
            if 0 < i < lat_size - 1:
                to = (i - 1 + 2 * (i % 2)) * lon_size + j
            else:
                to = i * lon_size + (j ^ 1)
            route.append((i * lon_size + j, to))
    return route


def shards(teacher_in, student_in, regions, t_qkv, t_out, s_qkv, s_out, s_proj):
    width, narrow = teacher_in.shape[3], student_in.shape[3]
    lat_size, lon_size = lax.axis_size("lat"), lax.axis_size("lon")
    wide = width + 128
    teacher_in = teacher_in.transpose(0, 2, 1, 3)
    student_in = student_in.transpose(0, 2, 1, 3)
    regions = regions.transpose(2, 0, 1)
    far = lax.ppermute(teacher_in, "grp", [(0, 1), (1, 0)])

    pinned = [
        pltpu.with_memory_space_constraint(jnp.asarray(a), pltpu.HBM)
        for a in (teacher_in, regions, TO_A, A_ROW, A_COL, t_qkv)
    ]
    x, ids, far_ids, q, k, v, to_a, wqkv = call(
        teacher_own, "teacher_own",
        [((NA, width), BF), ((NA, 128), BF), ((NA, 128), BF)] + [((NA, width), BF)] * 3
        + [((NA, NAT), BF), (t_qkv.shape[1:], BF)],
        [HBM] * 6, pinned,
        [pltpu.VMEM((COLS, TALL, width), BF)]
        + buffers(teacher_in, regions, A_ROW, A_COL)[:-1]
        + [pltpu.SemaphoreType.DMA((6,))],
        10**9,
    )
    hidden, rows_1, rows_2 = call(
        teacher_first, "teacher_first",
        [((NA, width), BF)] + [((ROW_SENT, width), BF)] * 2,
        [VMEM] * 10 + [HBM],
        [far, x, ids, far_ids, q, k, v, to_a, ROWS_FROM_A, wqkv]
        + [pltpu.with_memory_space_constraint(t_out, pltpu.HBM)],
        [pltpu.VMEM((COLS, TALL, width), BF)] + buffers(t_out[0]), 3 * 10**9,
    )
    sent = rows_2
    rows_2 = lax.ppermute(rows_2, "lat", swaps(lat_size, 0))
    rows_1 = lax.ppermute(rows_1, ("lat", "lon"), inner_swaps(lat_size, lon_size))

    spread, g0, save0, save1, q, k, v, c_att, west, east = call(
        beside_rows, "beside_rows",
        [((NG, wide), BF), ((NA, narrow), F32), ((NA, SAVE), BF), ((NA, SAVE), BF)]
        + [((NG, width), BF)] * 3 + [((AT["c"][1], width), BF)] + [((COL_SENT, width), BF)] * 2,
        [VMEM] * 10 + [ANY],
        [student_in, ids, to_a, s_qkv, s_out, s_proj, hidden, A_TO_G, t_qkv, PACK_OWN, sent],
        [pltpu.VMEM((COLS, TALL, narrow), BF)], 5 * 10**9,
    )
    cols_1, cols_2 = call(
        send_columns, "send_columns",
        [((COL_SENT, width), BF)] * 2,
        [VMEM] * 6 + [ANY],
        [rows_1, rows_2, FROM_NORTH, FROM_SOUTH, west, east, g0], (), 10**7,
    )
    sent = cols_2
    cols_2 = lax.ppermute(cols_2, "lon", swaps(lon_size, 0))
    cols_1 = lax.ppermute(cols_1, "lon", swaps(lon_size, 1))

    late = sum(AT[name][1] for name in LATE)
    n_att, s_att, nums, dens = call(
        beside_columns, "beside_columns",
        [((AT["n"][1], width), BF)] * 2 + [((late, width), F32)] * 2,
        [VMEM] * 8 + [ANY],
        [spread, rows_1, rows_2, OPEN_ROWS, t_qkv, q, k, v, sent], (), 2 * 10**9,
    )
    args = [hidden, spread, cols_1, cols_2, q, nums, dens, c_att, n_att, s_att]
    args += [OPEN_COLS, FROM_A, G_TO_A, t_qkv, t_out, s_proj, s_qkv, s_out, g0, save0, save1]
    out, grad = call(
        teacher_second, "teacher_second",
        [(teacher_in.shape, BF), (student_in.shape, F32)],
        [VMEM] * len(args), args,
        [
            pltpu.VMEM(teacher_in.shape, BF),
            pltpu.VMEM(student_in.shape, F32),
            pltpu.SemaphoreType.DMA((3,)),
        ],
        6 * 10**9, ANY,
    )
    return out.transpose(0, 2, 1, 3), grad.transpose(0, 2, 1, 3)


def solution(mesh):
    tiles = P("grp", "lat", "lon", None)
    return jax.shard_map(
        shards,
        mesh=mesh,
        in_specs=(tiles, tiles, P(None, "lat", "lon"), P(), P(), P(), P(), P()),
        out_specs=(tiles, tiles),
        check_vma=False,
    )
```

```python
import functools

import jax
import jax.numpy as jnp
import ml_dtypes
import numpy as np
from jax import lax
from jax.experimental import pallas as pl
from jax.experimental.pallas import tpu as pltpu
from jax.sharding import PartitionSpec as P

HEADS_T = 8
HEADS_S = 4
EPS = 1e-06
LOG2E = 1.4426950408889634
SCALE = 10.0 * LOG2E
BF = jnp.bfloat16
F32 = jnp.float32

ROWS, COLS = 24, 12
WIN = 80
NA = 4 * WIN
TALL = 32
NAT = COLS * TALL
PAIR = 128

PARTS = (
    ("nw", (0, 6), (0, 3), 32),
    ("n", (0, 6), (3, 9), 48),
    ("ne", (0, 6), (9, 12), 32),
    ("e", (6, 18), (9, 12), 48),
    ("se", (18, 24), (9, 12), 32),
    ("s", (18, 24), (3, 9), 48),
    ("sw", (18, 24), (0, 3), 32),
    ("w", (6, 18), (0, 3), 48),
    ("c", (6, 18), (3, 9), 80),
)
AT = {}
NG = 0
for _name, _r, _c, _kept in PARTS:
    AT[_name] = (NG, _kept)
    NG += _kept


def _a_slot(r, c):
    return (2 * (r // 12) + c // 6) * WIN + (r % 12) * 6 + c % 6


def _tables():
    to_a = np.zeros((NA, NAT), ml_dtypes.bfloat16)
    a_row = np.zeros((NA, ROWS), ml_dtypes.bfloat16)
    a_col = np.zeros((NA, COLS), ml_dtypes.bfloat16)
    for r in range(ROWS):
        for c in range(COLS):
            slot = _a_slot(r, c)
            to_a[slot, c * TALL + r] = 1
            a_row[slot, r] = 1
            a_col[slot, c] = 1
    a_to_g = np.zeros((NG, NA), ml_dtypes.bfloat16)
    for name, (r0, r1), (c0, c1), _ in PARTS:
        spot = AT[name][0]
        for r in range(r0, r1):
            for c in range(c0, c1):
                a_to_g[spot, _a_slot(r, c)] = 1
                spot += 1
    return to_a, a_row, a_col, a_to_g


TO_A, A_ROW, A_COL, A_TO_G = _tables()
FROM_A = np.ascontiguousarray(TO_A.T)
G_TO_A = np.ascontiguousarray(A_TO_G.T)


def _packing(kept):
    table = np.zeros((128, sum(kept)), ml_dtypes.bfloat16)
    token, start = 0, 0
    for rows in kept:
        count = {32: 18, 48: 36}[rows]
        for i in range(count):
            table[token + i, start + i] = 1
        token, start = token + count, start + rows
    return table


def _corners(start, west, east):
    table = np.zeros((256, ROW_SENT), ml_dtypes.bfloat16)
    for i in range(18):
        table[start + i, west + i] = 1
        table[128 + start + i, east + i] = 1
    return table


PACK_ROWS = _packing((32, 48, 32))
PACK_OWN = np.roll(PACK_ROWS, 18, axis=0)
PACK_COLS = _packing((32, 32, 48, 32, 32))
ROW_TOKENS, ROW_SENT = 72, 80
COL_TOKENS, COL_SENT = 108, 112
FROM_NORTH = _corners(0, 0, 54)
FROM_SOUTH = _corners(90, 0, 54)
OPEN_ROWS = np.ascontiguousarray(PACK_ROWS.T[:, :ROW_SENT])
OPEN_COLS = np.ascontiguousarray(PACK_COLS.T[:, :COL_SENT])


def dot(a, b):
    return jnp.dot(a, b, preferred_element_type=F32)


def dot_nt(a, b):
    return lax.dot_general(a, b, (((1,), (1,)), ((), ())), preferred_element_type=F32)


def dot_tn(a, b):
    return lax.dot_general(a, b, (((0,), (0,)), ((), ())), preferred_element_type=F32)


def head_lanes(rows, h):
    lane = lax.broadcasted_iota(jnp.int32, (rows, PAIR), 1)
    return jnp.where((lane >> 6) == h, 1.0, 0.0).astype(BF)


def head_blocks():
    row = lax.broadcasted_iota(jnp.int32, (2 * PAIR, 2 * PAIR), 0)
    lane = lax.broadcasted_iota(jnp.int32, (2 * PAIR, 2 * PAIR), 1)
    return jnp.where((row >> 6) == (lane >> 6), 1.0, 0.0).astype(BF)


def stack_heads(x):
    return jnp.concatenate([x * head_lanes(1, h) for h in range(2)], axis=0)


def stack_values(v):
    rows = v.shape[0]
    ones = jnp.concatenate([head_lanes(rows, h) for h in range(2)], axis=0)
    return jnp.concatenate([stack_heads(v), ones], axis=1)


def unstack_heads(x):
    n = x.shape[0] // 2
    lane = lax.broadcasted_iota(jnp.int32, (1, PAIR), 1) >> 6
    return jnp.where(lane == 0, x[:n], x[n:])


def head_sums(x, blocks):
    step = blocks.shape[0]
    groups = [dot(x[:, i : i + step].astype(BF), blocks) for i in range(0, x.shape[1], step)]
    return groups[0] if len(groups) == 1 else jnp.concatenate(groups, axis=1)


def unit(x, blocks):
    scale = lax.rsqrt(head_sums(x * x, blocks) + EPS)
    return x * scale, scale


def id_mask(id_query, id_keys):
    keys = jnp.concatenate([id_keys] * 2, axis=0)
    row = dot_nt(jnp.full((8, 128), 1.0 / 128, BF), keys)[0:1]
    return id_query.astype(F32)[:, 0:1] == row


def pairs_of(x):
    return [x[:, i : i + PAIR] for i in range(0, x.shape[1], PAIR)]


def attend(windows):
    scores = [
        [dot_nt(qp, stack_heads(kp)) for qp, kp in zip(pairs_of(q), pairs_of(k))]
        for q, k, _, _ in windows
    ]
    es = [
        [jnp.where(w[3], jnp.exp2(s), 0.0).astype(BF) for s in group]
        for w, group in zip(windows, scores)
    ]
    both = [
        [dot(e, stack_values(vp)) for e, vp in zip(group, pairs_of(w[2]))]
        for w, group in zip(windows, es)
    ]
    return [
        ([b[:, :PAIR] for b in group], [b[:, PAIR:] for b in group], e)
        for group, e in zip(both, es)
    ]


def to_window_order(x_ref, pad_ref, to_a):
    pad_ref[...] = jnp.zeros_like(pad_ref)
    pad_ref[:, 0:ROWS, :] = x_ref[0]
    natural = pad_ref[...].reshape(NAT, x_ref.shape[3])
    return dot(to_a, natural).astype(BF)


def window_ids(reg, a_row, a_col):
    table = (reg + 1).astype(F32).astype(BF)
    picked = (dot(a_col, table) * a_row.astype(F32)).astype(BF)
    return dot(picked, jnp.ones((ROWS, 128), BF)).astype(BF)


def by_level(reg_ref):
    level = lax.axis_index("grp")
    low, high = reg_ref[:, 0, :], reg_ref[:, 1, :]
    own = jnp.where(level == 0, low, high)
    return own, low + high - own


def residual(x, att, w):
    y = dot(att, w)
    r = lax.rsqrt(jnp.mean(y * y, axis=1, keepdims=True) + EPS)
    n = y * r
    return (x.astype(F32) + n).astype(BF), n, r


WIDE = 2 * PAIR
SAVE = 11 * WIDE


def student_layer(x, w_qkv, w_out, ids, save_ref):
    blocks = head_blocks()
    qkv = dot(x, w_qkv)
    q, sq = unit(qkv[:, :WIDE], blocks)
    k, sk = unit(qkv[:, WIDE : 2 * WIDE], blocks)
    q = (q * SCALE).astype(BF)
    k = k.astype(BF)
    v = qkv[:, 2 * WIDE :].astype(BF)
    atts = []
    windows = [slice(w * WIN, (w + 1) * WIN) for w in range(4)]
    found = attend([(q[r], k[r], v[r], id_mask(ids[r], ids[r])) for r in windows])
    for rows, (nums, dens, es) in zip(windows, found):
        z = 1.0 / jnp.concatenate(dens, axis=1)
        att = jnp.concatenate(nums, axis=1) * z
        save_ref[rows, 4 * WIDE : 5 * WIDE] = z.astype(BF)
        for i, e in enumerate(es):
            save_ref[rows, (9 + i) * WIDE : (9 + i) * WIDE + 2 * WIN] = e
        atts.append(att.astype(BF))
    att = jnp.concatenate(atts, axis=0)
    h, n, r = residual(x, att, w_out)
    for i, part in ((0, q), (1, k), (2, v), (3, att), (5, sq), (6, sk), (7, n)):
        save_ref[:, i * WIDE : (i + 1) * WIDE] = part.astype(BF)
    save_ref[:, 8 * WIDE : 9 * WIDE] = jnp.broadcast_to(r, (NA, WIDE)).astype(BF)
    return h


def fetch(*pairs):
    copies = [pltpu.make_async_copy(*pair) for pair in pairs]
    for copy in copies:
        copy.start()
    return copies


def student_back(g, save_ref, w_qkv, w_out):
    blocks = head_blocks()
    part = lambda i: save_ref[:, i * WIDE : (i + 1) * WIDE]
    n, r = part(7).astype(F32), part(8).astype(F32)
    dy = r * (g - n * jnp.mean(g * n, axis=1, keepdims=True))
    datt = dot_nt(dy.astype(BF), w_out) * part(4).astype(F32)
    drop = (datt * part(3).astype(F32)).astype(BF) * jnp.asarray(-1.0, BF)
    datt = datt.astype(BF)
    q, k, v = part(0), part(1), part(2)
    windows = [slice(w * WIN, (w + 1) * WIN) for w in range(4)]
    blocks_of = [(r, slice(i, i + PAIR)) for r in windows for i in range(0, WIDE, PAIR)]
    es = [
        save_ref[r, (9 + i) * WIDE : (9 + i) * WIDE + 2 * WIN] for r in windows for i in range(2)
    ]
    dws = [
        dot_nt(jnp.concatenate([datt[r, p], drop[r, p]], axis=1), stack_values(v[r, p]))
        for r, p in blocks_of
    ]
    dv = [unstack_heads(dot_tn(e, datt[r, p])) for e, (r, p) in zip(es, blocks_of)]
    dss = [(e.astype(F32) * dw).astype(BF) for e, dw in zip(es, dws)]
    dq = [dot(ds, stack_heads(k[r, p])) for ds, (r, p) in zip(dss, blocks_of)]
    dk = [unstack_heads(dot_tn(ds, q[r, p])) for ds, (r, p) in zip(dss, blocks_of)]
    dqs, dks, dvs = [[x[i : i + 2] for i in range(0, len(x), 2)] for x in (dq, dk, dv)]
    dqs, dks, dvs = [[jnp.concatenate(x, axis=1) for x in y] for y in (dqs, dks, dvs)]
    dq = 10.0 * jnp.concatenate(dqs, axis=0)
    dk = (1.0 / LOG2E) * jnp.concatenate(dks, axis=0)
    dv = jnp.concatenate(dvs, axis=0)
    q_unit = q.astype(F32) * (1.0 / SCALE)
    k_unit = k.astype(F32)
    dq = part(5).astype(F32) * (dq - q_unit * head_sums(q_unit * dq, blocks))
    dk = part(6).astype(F32) * (dk - k_unit * head_sums(k_unit * dk, blocks))
    dqkv = jnp.concatenate([dq.astype(BF), dk.astype(BF), dv.astype(BF)], axis=1)
    return g + dot_nt(dqkv, w_qkv)


def teacher_own(
    x_hbm, reg_hbm, to_a_hbm, a_row_hbm, a_col_hbm, t_qkv,
    x_out, id_ref, far_id_ref, q_ref, k_ref, v_ref, to_a, wqkv,
    pad_ref, x_ref, reg_ref, a_row, a_col, sems,
):
    width = x_ref.shape[3]
    copies = fetch(
        (x_hbm, x_ref, sems.at[0]),
        (to_a_hbm, to_a, sems.at[1]),
        (reg_hbm, reg_ref, sems.at[2]),
        (a_row_hbm, a_row, sems.at[3]),
        (a_col_hbm, a_col, sems.at[4]),
        (t_qkv.at[0], wqkv, sems.at[5]),
    )
    blocks = head_blocks()
    copies[0].wait()
    copies[1].wait()
    x = to_window_order(x_ref, pad_ref, to_a[...])
    x_out[...] = x
    for copy in copies[2:5]:
        copy.wait()
    reg, reg_far = by_level(reg_ref)
    id_ref[...] = window_ids(reg, a_row[...], a_col[...])
    far_id_ref[...] = window_ids(reg_far, a_row[...], a_col[...])
    copies[5].wait()
    q_ref[...] = (unit(dot(x, wqkv[:, :width]), blocks)[0] * SCALE).astype(BF)
    k_ref[...] = unit(dot(x, wqkv[:, width : 2 * width]), blocks)[0].astype(BF)
    v_ref[...] = dot(x, wqkv[:, 2 * width :]).astype(BF)


def teacher_first(
    far_ref, x_ref, id_ref, far_id_ref, q_ref, k_ref, v_ref, to_a, rows_from_a, wqkv, t_out,
    h_ref, first_ref, second_ref, pad_ref, wout, sems,
):
    copies = fetch((t_out.at[0], wout, sems.at[0]))
    width = x_ref.shape[1]
    blocks = head_blocks()
    sent_ids = dot(rows_from_a[...], id_ref[...]).astype(BF)
    sent_ids = dot_nt(jnp.full((8, 128), 1.0 / 128, BF), sent_ids)[0:1]
    empty = jnp.zeros((1, width - 128), F32)
    id_rows = [jnp.concatenate([sent_ids[:, i : i + 128], empty], axis=1) for i in (0, 128)]
    far = to_window_order(far_ref, pad_ref, to_a[...])
    k_far = unit(dot(far, wqkv[:, width : 2 * width]), blocks)[0].astype(BF)
    v_far = dot(far, wqkv[:, 2 * width :]).astype(BF)
    windows = []
    for w in range(4):
        rows = slice(w * WIN, (w + 1) * WIN)
        id_keys = jnp.concatenate([id_ref[rows], far_id_ref[rows]], axis=0)
        keys = [
            jnp.concatenate([near[rows], away[rows]], axis=0)
            for near, away in ((k_ref, k_far), (v_ref, v_far))
        ]
        windows.append((q_ref[rows], keys, (id_ref[rows], id_keys)))
    atts = window_attention(windows)
    copies[0].wait()
    h = residual(x_ref[...], jnp.concatenate(atts, axis=0), wout[...])[0]
    h_ref[...] = h
    values = [dot(rows_from_a[i : i + ROW_SENT], h) for i in (0, 128)]
    at = lax.broadcasted_iota(jnp.int32, (ROW_SENT, 1), 0)
    payloads = [jnp.where(at == ROW_TOKENS, row, x) for row, x in zip(id_rows, values)]
    first_ref[...], second_ref[...] = swapped("lat", *payloads)


def swapped(axis, low, high):
    even = lax.rem(lax.axis_index(axis), 2) == 0
    low, high = low.astype(F32), high.astype(F32)
    return jnp.where(even, low, high).astype(BF), jnp.where(even, high, low).astype(BF)


def packed(rows, table, tokens, sent):
    width = rows.shape[1] - 128
    values = dot(table[:sent], rows[:, :width])
    ids = dot(table, rows[:, width:]).astype(BF)
    row = dot_nt(jnp.full((8, 128), 1.0 / 128, BF), ids)[0:1]
    row = jnp.concatenate([row, jnp.zeros((1, width - 128), F32)], axis=1)
    at = lax.broadcasted_iota(jnp.int32, (sent, 1), 0)
    return jnp.where(at == tokens, row, values).astype(BF)


def opened(sent, table, tokens):
    values = dot(table, sent).astype(BF)
    return jnp.concatenate([values, opened_ids(sent, table, tokens)], axis=1)


def opened_ids(sent, table, tokens):
    row = sent.astype(F32)[tokens : tokens + 1, : table.shape[1]]
    picked = (table.astype(F32) * row).astype(BF)
    return dot(picked, jnp.ones((table.shape[1], 128), BF)).astype(BF)


def part(x, name):
    start, kept = AT[name]
    return x[start : start + kept]


TO_NORTH = ("nw", "n", "ne")
TO_SOUTH = ("sw", "s", "se")


def _row_table():
    table = np.zeros((256, NA), ml_dtypes.bfloat16)
    for start, names in ((0, TO_NORTH), (128, TO_SOUTH)):
        rows = np.concatenate([A_TO_G[AT[n][0] : AT[n][0] + AT[n][1]] for n in names])
        table[start : start + 128] = PACK_ROWS.astype(np.float32) @ rows.astype(np.float32)
    return table


ROWS_FROM_A = _row_table()
TO_WEST = (("N", "sw"), ("", "nw"), ("", "w"), ("", "sw"), ("S", "nw"))
TO_EAST = (("N", "se"), ("", "ne"), ("", "e"), ("", "se"), ("S", "ne"))
EXTRA = {
    "nw": (("N", "sw"), ("W", "ne"), ("NW", "se")),
    "n": (("N", "s"),),
    "ne": (("N", "se"), ("E", "nw"), ("NE", "sw")),
    "e": (("E", "w"),),
    "se": (("S", "ne"), ("E", "sw"), ("SE", "nw")),
    "s": (("S", "n"),),
    "sw": (("S", "nw"), ("W", "se"), ("SW", "ne")),
    "w": (("W", "e"),),
    "c": (),
}
LATE = ("nw", "ne", "e", "se", "sw", "w")
ORDER = [name for name, *_ in PARTS]


def _spots(items):
    spots, start = {}, 0
    for side, name in items:
        spots[side, name] = start
        start += AT[name][1]
    return spots


OWN = {("", name): AT[name][0] for name in ORDER}
EDGE = _spots([("N", n) for n in TO_SOUTH] + [("S", n) for n in TO_NORTH])
COME = _spots([(s + "E", n) for s, n in TO_WEST] + [(s + "W", n) for s, n in TO_EAST])


def gather(sources, items):
    blocks = []
    for item in items:
        for array, spots in sources:
            if item in spots:
                spot = spots[item]
                blocks.append(array[spot : spot + AT[item[1]][1]])
                break
    return blocks[0] if len(blocks) == 1 else jnp.concatenate(blocks, axis=0)


def window_sums(windows):
    found = attend([(q, k, v, id_mask(*ids)) for q, (k, v), ids in windows])
    return [
        (jnp.concatenate(nums, axis=1), jnp.concatenate(dens, axis=1)) for nums, dens, _ in found
    ]


def window_attention(windows):
    return [(num / den).astype(BF) for num, den in window_sums(windows)]


def beside_rows(
    x_ref, id_ref, to_a, s_qkv, s_out, proj, hidden_ref, a_to_g, t_qkv, pack, after_ref,
    g_ref, g0_ref, save0, save1, q_ref, k_ref, v_ref, att_ref, west_ref, east_ref, pad_ref,
):
    width = hidden_ref.shape[1]
    blocks = head_blocks()
    spread = jnp.concatenate([hidden_ref[...], id_ref[...]], axis=1)
    spread = dot(a_to_g[...], spread).astype(BF)
    g_ref[...] = spread
    x = to_window_order(x_ref, pad_ref, to_a[...])
    h = student_layer(x, s_qkv[0], s_out[0], id_ref[...], save0)
    h = student_layer(h, s_qkv[1], s_out[1], id_ref[...], save1)
    predicted = dot(h, proj[...])
    g0_ref[...] = dot_nt(predicted.astype(BF), proj[...])

    for ref, items in ((west_ref, TO_WEST), (east_ref, TO_EAST)):
        rows = gather([(spread, OWN)], items[1:4])
        ref[...] = packed(rows, pack[...], COL_TOKENS, COL_SENT)

    rows = spread[:, :width]
    q = (unit(dot(rows, t_qkv[1, :, :width]), blocks)[0] * SCALE).astype(BF)
    k = unit(dot(rows, t_qkv[1, :, width : 2 * width]), blocks)[0].astype(BF)
    v = dot(rows, t_qkv[1, :, 2 * width :]).astype(BF)
    q_ref[...] = q
    k_ref[...] = k
    v_ref[...] = v
    ids = part(spread, "c")[:, width:]
    [att_ref[...]] = window_attention([(part(q, "c"), [part(k, "c"), part(v, "c")], (ids, ids))])


def on_map():
    lat = lax.axis_index("lat")
    inside = (lat > 0, lat < lax.axis_size("lat") - 1)
    return [jnp.where(x, 1.0, 0.0) for x in inside]


def send_columns(
    first_ref, second_ref, from_north, from_south, west_ref, east_ref, after_ref,
    out_first, out_second,
):
    rows = swapped("lat", first_ref[...], second_ref[...])
    tables = (from_north[...], from_south[...])
    values = sum(dot(table, sent) for table, sent in zip(tables, rows))
    ids = 0.0
    for table, sent, there in zip(tables, rows, on_map()):
        row = sent.astype(F32)[ROW_TOKENS : ROW_TOKENS + 1, :ROW_SENT] * there
        ids += dot_nt(jnp.broadcast_to(row, (8, ROW_SENT)).astype(BF), table)
    at = lax.broadcasted_iota(jnp.int32, (COL_SENT, 1), 0)
    empty = jnp.zeros((1, first_ref.shape[1] - 128), F32)
    payloads = []
    for i, ref in ((0, west_ref), (128, east_ref)):
        row = jnp.concatenate([ids[0:1, i : i + 128], empty], axis=1)
        corners = jnp.where(at == COL_TOKENS, row, values[i : i + COL_SENT])
        payloads.append((ref[...].astype(F32) + corners).astype(BF))
    out_first[...], out_second[...] = swapped("lon", *payloads)


def beside_columns(
    g_ref, first_ref, second_ref, open_rows, t_qkv, q_ref, k_ref, v_ref, after_ref,
    n_ref, s_ref, num_ref, den_ref,
):
    width = g_ref.shape[1] - 128
    blocks = head_blocks()
    edge = []
    for sent, there in zip(swapped("lat", first_ref[...], second_ref[...]), on_map()):
        rows = opened(sent, open_rows[...], ROW_TOKENS)
        edge.append(jnp.concatenate([rows[:, :width], rows[:, width:] * there.astype(BF)], axis=1))
    edge = jnp.concatenate(edge, axis=0)
    rows = edge[:, :width]
    k = unit(dot(rows, t_qkv[1, :, width : 2 * width]), blocks)[0].astype(BF)
    v = dot(rows, t_qkv[1, :, 2 * width :]).astype(BF)
    windows = []
    for name in ("n", "s") + LATE:
        items = [("", name)] + [item for item in EXTRA[name] if item in EDGE]
        keys = [gather([(own, OWN), (x, EDGE)], items) for own, x in ((k_ref, k), (v_ref, v))]
        ids = [gather([(g_ref, OWN), (edge, EDGE)], some)[:, width:] for some in (items[:1], items)]
        windows.append((part(q_ref, name), keys, ids))
    sums = window_sums(windows)
    for ref, (num, den) in zip((n_ref, s_ref), sums):
        ref[...] = (num / den).astype(BF)
    num_ref[...], den_ref[...] = [jnp.concatenate(x, axis=0) for x in zip(*sums[2:])]


def teacher_second(
    h_ref, g_ref, first_ref, second_ref, q_ref, num_ref, den_ref,
    c_ref, n_ref, s_ref, open_cols, from_a, g_to_a, t_qkv, t_out, proj, s_qkv, s_out,
    g0_ref, save0, save1, out_hbm, grad_hbm, out_ref, grad_ref, sems,
):
    width = h_ref.shape[1]
    blocks = head_blocks()
    west, east = swapped("lon", first_ref[...], second_ref[...])
    table = open_cols[...]
    ids_came = jnp.concatenate([opened_ids(x, table, COL_TOKENS) for x in (east, west)], axis=0)
    rows = jnp.concatenate([east, west], axis=0)
    k = unit(dot(rows, t_qkv[1, :, width : 2 * width]), blocks)[0].astype(BF)
    v = dot(rows, t_qkv[1, :, 2 * width :]).astype(BF)
    k, v = [
        jnp.concatenate([dot(table, x[:COL_SENT]), dot(table, x[COL_SENT:])], axis=0).astype(BF)
        for x in (k, v)
    ]
    atts = {"c": c_ref[...], "n": n_ref[...], "s": s_ref[...]}
    windows = []
    for name in LATE:
        items = [item for item in EXTRA[name] if item in COME]
        keys = [gather([(new, COME)], items) for new in (k, v)]
        ids = (part(g_ref, name)[:, width:], gather([(ids_came, COME)], items))
        windows.append((part(q_ref, name), keys, ids))
    start = 0
    for name, (num, den) in zip(LATE, window_sums(windows)):
        early = slice(start, start + num.shape[0])
        atts[name] = ((num_ref[early] + num) / (den_ref[early] + den)).astype(BF)
        start += num.shape[0]
    att = jnp.concatenate([atts[name] for name in ORDER], axis=0)
    att = dot(g_to_a[...], att).astype(BF)
    teacher = residual(h_ref[...], att, t_out[1])[0]
    natural = dot(from_a[...], teacher).astype(BF)
    out_ref[0] = natural.reshape(COLS, TALL, width)[:, :ROWS, :]

    g = g0_ref[...] - dot_nt(teacher, proj[...])
    g = student_back(g, save1, s_qkv[1], s_out[1])
    copies = fetch((out_ref, out_hbm, sems.at[0]))
    g = student_back(g, save0, s_qkv[0], s_out[0])
    high = g.astype(BF)
    low = (g - high.astype(F32)).astype(BF)
    half = COLS // 2
    for i in range(2):
        table = from_a[i * half * TALL : (i + 1) * half * TALL]
        natural = dot(table, high) + dot(table, low)
        cols = pl.ds(i * half, half)
        grad_ref[0, cols] = natural.reshape(half, TALL, g.shape[1])[:, :ROWS, :]
        copies += fetch((grad_ref.at[0, cols], grad_hbm.at[0, cols], sems.at[1 + i]))
    for copy in copies:
        copy.wait()


VMEM = pl.BlockSpec(memory_space=pltpu.VMEM)
ANY = pl.BlockSpec(memory_space=pl.ANY)
HBM = pl.BlockSpec(memory_space=pltpu.HBM)


def call(kernel, name, outs, specs, args, scratch=(), flops=0, out_space=VMEM):
    shapes = [jax.ShapeDtypeStruct(s, d) for s, d in outs]
    touched = sum(a.size * a.dtype.itemsize for a in args)
    return pl.pallas_call(
        kernel,
        name=name,
        out_shape=shapes,
        in_specs=specs,
        out_specs=[out_space] * len(outs),
        scratch_shapes=list(scratch),
        compiler_params=pltpu.CompilerParams(vmem_limit_bytes=28 << 20),
        cost_estimate=pl.CostEstimate(flops=flops, bytes_accessed=touched, transcendentals=0),
    )(*args)


def buffers(*arrays):
    return [pltpu.VMEM(a.shape, a.dtype) for a in arrays] + [
        pltpu.SemaphoreType.DMA((len(arrays),))
    ]


def swaps(size, start):
    route = {}
    for i in range(start, size, 2):
        j = (i + 1) % size
        route[i], route[j] = j, i
    return sorted(route.items())


def inner_swaps(lat_size, lon_size):
    route = []
    for i in range(lat_size):
        for j in range(lon_size):
            if 0 < i < lat_size - 1:
                to = (i - 1 + 2 * (i % 2)) * lon_size + j
            else:
                to = i * lon_size + (j ^ 1)
            route.append((i * lon_size + j, to))
    return route


def shards(teacher_in, student_in, regions, t_qkv, t_out, s_qkv, s_out, s_proj):
    width, narrow = teacher_in.shape[3], student_in.shape[3]
    lat_size, lon_size = lax.axis_size("lat"), lax.axis_size("lon")
    wide = width + 128
    teacher_in = teacher_in.transpose(0, 2, 1, 3)
    student_in = student_in.transpose(0, 2, 1, 3)
    regions = regions.transpose(2, 0, 1)
    far = lax.ppermute(teacher_in, "grp", [(0, 1), (1, 0)])

    pinned = [
        pltpu.with_memory_space_constraint(jnp.asarray(a), pltpu.HBM)
        for a in (teacher_in, regions, TO_A, A_ROW, A_COL, t_qkv)
    ]
    x, ids, far_ids, q, k, v, to_a, wqkv = call(
        teacher_own, "teacher_own",
        [((NA, width), BF), ((NA, 128), BF), ((NA, 128), BF)] + [((NA, width), BF)] * 3
        + [((NA, NAT), BF), (t_qkv.shape[1:], BF)],
        [HBM] * 6, pinned,
        [pltpu.VMEM((COLS, TALL, width), BF)]
        + buffers(teacher_in, regions, A_ROW, A_COL)[:-1]
        + [pltpu.SemaphoreType.DMA((6,))],
        10**9,
    )
    hidden, rows_1, rows_2 = call(
        teacher_first, "teacher_first",
        [((NA, width), BF)] + [((ROW_SENT, width), BF)] * 2,
        [VMEM] * 10 + [HBM],
        [far, x, ids, far_ids, q, k, v, to_a, ROWS_FROM_A, wqkv]
        + [pltpu.with_memory_space_constraint(t_out, pltpu.HBM)],
        [pltpu.VMEM((COLS, TALL, width), BF)] + buffers(t_out[0]), 3 * 10**9,
    )
    sent = rows_2
    rows_2 = lax.ppermute(rows_2, "lat", swaps(lat_size, 0))
    rows_1 = lax.ppermute(rows_1, ("lat", "lon"), inner_swaps(lat_size, lon_size))

    spread, g0, save0, save1, q, k, v, c_att, west, east = call(
        beside_rows, "beside_rows",
        [((NG, wide), BF), ((NA, narrow), F32), ((NA, SAVE), BF), ((NA, SAVE), BF)]
        + [((NG, width), BF)] * 3 + [((AT["c"][1], width), BF)] + [((COL_SENT, width), BF)] * 2,
        [VMEM] * 10 + [ANY],
        [student_in, ids, to_a, s_qkv, s_out, s_proj, hidden, A_TO_G, t_qkv, PACK_OWN, sent],
        [pltpu.VMEM((COLS, TALL, narrow), BF)], 5 * 10**9,
    )
    cols_1, cols_2 = call(
        send_columns, "send_columns",
        [((COL_SENT, width), BF)] * 2,
        [VMEM] * 6 + [ANY],
        [rows_1, rows_2, FROM_NORTH, FROM_SOUTH, west, east, g0], (), 10**7,
    )
    sent = cols_2
    cols_2 = lax.ppermute(cols_2, "lon", swaps(lon_size, 0))
    cols_1 = lax.ppermute(cols_1, "lon", swaps(lon_size, 1))

    late = sum(AT[name][1] for name in LATE)
    n_att, s_att, nums, dens = call(
        beside_columns, "beside_columns",
        [((AT["n"][1], width), BF)] * 2 + [((late, width), F32)] * 2,
        [VMEM] * 8 + [ANY],
        [spread, rows_1, rows_2, OPEN_ROWS, t_qkv, q, k, v, sent], (), 2 * 10**9,
    )
    args = [hidden, spread, cols_1, cols_2, q, nums, dens, c_att, n_att, s_att]
    args += [OPEN_COLS, FROM_A, G_TO_A, t_qkv, t_out, s_proj, s_qkv, s_out, g0, save0, save1]
    out, grad = call(
        teacher_second, "teacher_second",
        [(teacher_in.shape, BF), (student_in.shape, F32)],
        [VMEM] * len(args), args,
        [
            pltpu.VMEM(teacher_in.shape, BF),
            pltpu.VMEM(student_in.shape, F32),
            pltpu.SemaphoreType.DMA((3,)),
        ],
        6 * 10**9, ANY,
    )
    return out.transpose(0, 2, 1, 3), grad.transpose(0, 2, 1, 3)


def solution(mesh):
    tiles = P("grp", "lat", "lon", None)
    return jax.shard_map(
        shards,
        mesh=mesh,
        in_specs=(tiles, tiles, P(None, "lat", "lon"), P(), P(), P(), P(), P()),
        out_specs=(tiles, tiles),
        check_vma=False,
    )
```
